32 devices in a mesh: dp: 4 (over z), expert: 8 (over y, x, core).
Axes of the slice: x: 2, y: 2, z: 4, core: 2. Of those that a mesh axis runs over, the one named last changes fastest.
Arguments:
- tokens: bfloat16 [2, 2048, 2048], P(None, ('dp', 'expert')), may hold values from -6 to 6
- lengths: int32 [2, 32, 4], P(None, ('dp', 'expert')), may hold values from 1 to 32, 64 in all within a row
- expert_ids: int32 [2, 2048, 8], P(None, ('dp', 'expert')), may hold values from 0 to 15, all different within a row; in each aligned block of 64 rows (0 to 63, 64 to 127, ..., all dimensions but the last counted through in order) at most 40 rows name the same one
- gates: float32 [2, 2048, 8], P(None, ('dp', 'expert')), may hold values from 0.05 to 0.2
- attn_gain: bfloat16 [2048], P(('dp', 'expert')), may hold values from 0.5 to 1.5
- w_qkv: bfloat16 [2048, 6144], P(('dp', 'expert')), may hold values from -0.125 to 0.125
- q_gain: bfloat16 [2048], P(('dp', 'expert')), may hold values from 0.5 to 1.5
- k_gain: bfloat16 [2048], P(('dp', 'expert')), may hold values from 0.5 to 1.5
- w_out: bfloat16 [2048, 2048], P(('dp', 'expert')), may hold values from -0.5 to 0.5
- ffn_gain: bfloat16 [2048], P(('dp', 'expert')), may hold values from 0.5 to 1.5
- expert_in: bfloat16 [16, 2048, 2048], P('expert', 'dp'), may hold values from -0.125 to 0.125
- expert_out: bfloat16 [16, 1024, 2048], P('expert', 'dp'), may hold values from -0.75 to 0.75
- out_grad: bfloat16 [2, 2048, 2048], P(None, ('dp', 'expert')), may hold values from -6 to 6
Outputs:
- out: bfloat16 [2, 2048, 2048], P(None, ('dp', 'expert'))
- grad_tokens: float32 [2, 2048, 2048], P(None, ('dp', 'expert'))
- grad_gates: float32 [2, 2048, 8], P(None, ('dp', 'expert'))
- grad_attn_gain: float32 [2048], P(('dp', 'expert'))
- grad_w_qkv: float32 [2048, 6144], P(('dp', 'expert'))
- grad_q_gain: float32 [2048], P(('dp', 'expert'))
- grad_k_gain: float32 [2048], P(('dp', 'expert'))
- grad_w_out: float32 [2048, 2048], P(('dp', 'expert'))
- grad_ffn_gain: float32 [2048], P(('dp', 'expert'))
- grad_expert_in: float32 [16, 2048, 2048], P('expert', 'dp')
- grad_expert_out: float32 [16, 1024, 2048], P('expert', 'dp')
The draws below stay inside these ranges and needn't reach their ends.
Inputs may be any that keep to these rules, and one draw needn't show every extreme that they name: `expert_ids`: each row names 8 different experts; in each aligned block of 64 rows (one pack) no expert is named by more than 40 rows, and in some block one expert is named by exactly 40 rows. Each pack's 4 lengths sum to 64, and the longest is exactly 32.
All inputs are finite; a program needn't handle non-finite values.
Results may differ from the reference program's by a relative error of at most 0.014.
Values may be sent and summed in bfloat16 or wider, within the bound.
A program may use at most 320 MiB of HBM per device.

```python
import math
import jax
import jax.numpy as jnp
import numpy as np
from jax import lax

D = 2048
HEAD = 128
FF = 1024
TOPK = 8
MB = 2
SEQ = 64
NDOC = 4
EXPERTS = 16
PACKS = 32
TOKENS = 2048
CAP = 40


def shard_levels(stream_key, shape, cuts, least, largest):
    level = 1.0
    for axis_at, blocks in cuts:
        steps = jax.random.uniform(jax.random.fold_in(jax.random.fold_in(stream_key, 6), axis_at), (blocks,), jnp.float32, least / len(cuts), largest / len(cuts))
        level = level * jnp.repeat(jnp.exp(steps), shape[axis_at] // blocks).reshape((-1,) + (1,) * (len(shape) - 1 - axis_at))
    return level


def profile(amount, total, limit, skew):
    portions = [(1 << 20) // math.isqrt(rank ** skew) + 1 for rank in range(2, amount + 1)]
    rest, holding = total - limit - (amount - 1), [1] * (amount - 1)
    while rest > 0:
        movable = [i for i in range(amount - 1) if holding[i] < limit]
        pool, remaining = sum([portions[i] for i in movable]), rest
        for i in movable:
            addition = min(limit - holding[i], max(1, remaining * portions[i] // pool), rest)
            holding[i] = holding[i] + addition
            rest = rest - addition
    return np.array([limit] + holding)


def ragged_sizes(stream_key, number_of, total, limit, lean):
    if number_of == 2:
        one = jax.random.randint(stream_key, (), max(1, total - limit), min(limit, total - 1) + 1)
        return jnp.stack([one, total - one])
    sizes = jnp.asarray(profile(number_of, total, limit, lean), jnp.int32)
    pairs = (number_of - 1) // 2
    donor, receiver = sizes[1:1 + 2 * pairs:2], sizes[2:2 + 2 * pairs:2]
    slack = jnp.minimum(donor - 1, limit - receiver)
    shifted = jax.random.randint(jax.random.fold_in(stream_key, 1), (pairs,), 0, 1 << 20) % (slack + 1)
    sizes = sizes.at[1:1 + 2 * pairs:2].set(donor - shifted).at[2:2 + 2 * pairs:2].set(receiver + shifted)
    return sizes[jax.random.permutation(jax.random.fold_in(stream_key, 2), number_of)]


def assign_block(key, own, number, rows, number_of, top, most, skew):
    sequence = jax.random.permutation(key, number_of)
    packed, common = portions_of(number_of, rows * top, most, skew, True), portions_of(number_of, rows * top, most, skew, False)
    places = jnp.arange(number_of)

    def named(sizes, offset_by):
        used = int((sizes > 0).sum())
        fixed = max(1, used // 4)
        passed = fixed + (places - fixed + offset_by * (used - fixed)) % max(1, number_of - fixed)
        return jnp.zeros((number_of,), jnp.int32).at[sequence[jnp.where(places < fixed, places, passed)]].set(jnp.asarray(sizes, jnp.int32))

    sizes = jnp.where(number % 4 == 0, named(packed, number // 4), named(common, number - number // 4 - 1))
    mixed = jax.random.permutation(jax.random.fold_in(own, 3), number_of)
    donor, receiver = mixed[0:number_of // 2 * 2:2], mixed[1:number_of // 2 * 2:2]
    slack = jnp.minimum(sizes[donor] - 1, most - sizes[receiver]) // 2
    slack = jnp.where((donor == sequence[0]) | (receiver == sequence[0]) | (sizes[receiver] == 0), 0, jnp.maximum(slack, 0))
    passed = jax.random.randint(jax.random.fold_in(own, 4), (number_of // 2,), 0, 1 << 20) % (slack + 1)
    sizes = sizes.at[donor].add(-passed).at[receiver].add(passed)
    items = jnp.searchsorted(jnp.cumsum(sizes), jnp.arange(rows * top), side="right").astype(jnp.int32)
    listing = items.reshape(top, rows).T
    listing = listing[jax.random.permutation(jax.random.fold_in(own, 1), rows)]
    offset_by = jax.random.randint(jax.random.fold_in(own, 2), (rows, 1), 0, top)
    return jnp.take_along_axis(listing, (jnp.arange(top)[None, :] + offset_by) % top, axis=1)


def portions_of(count, total, bound, lean, full):
    portions = [(1 << 20) // math.isqrt(rank ** lean) + 1 for rank in range(1, count + 1)]
    largest = bound if full else min(bound, max(-(-total // count), total * portions[0] // sum(portions)))
    least = 1 if total - largest >= count - 1 else 0
    given, surplus = [largest] + [least] * (count - 1), total - largest - least * (count - 1)
    while surplus > 0:
        free = [i for i in range(1, count) if given[i] < largest] or [i for i in range(1, count) if given[i] < bound]
        mass, budget = sum([portions[i] for i in free]), surplus
        for i in free:
            extra = min(bound - given[i], max(1, budget * portions[i] // mass), surplus)
            given[i] = given[i] + extra
            surplus = surplus - extra
    return np.array(given)


def centred(key, extent, spread, reach, cuts=(), kind=jnp.bfloat16):
    level = shard_levels(key, extent, cuts, -0.22, 0.18) if cuts else 1.0
    entries = jax.random.normal(key, extent, jnp.float32) * spread * level
    return jnp.minimum(jnp.maximum(entries, -reach), reach).astype(kind)


def setup_inputs(seed: int = 0) -> dict:
    splits = jax.random.split(jax.random.key(seed), 14)
    tokens = centred(splits[0], (MB, TOKENS, D), 1.0, 6.0, ((1, 32),))
    lengths = jax.vmap(lambda own: ragged_sizes(own, NDOC, SEQ, SEQ // 2, 2))(jax.random.split(splits[1], MB * PACKS)).reshape((MB, PACKS, NDOC)).astype(jnp.int32)
    expert_ids_keys = jax.random.split(jax.random.fold_in(splits[2], 1), MB * TOKENS // SEQ)
    expert_ids_turns = jax.random.permutation(jax.random.fold_in(splits[2], 3), MB * TOKENS // SEQ)
    expert_ids = jax.vmap(lambda own, number: assign_block(jax.random.fold_in(splits[2], 2), own, number, SEQ, EXPERTS, TOPK, CAP, 2))(expert_ids_keys, expert_ids_turns).reshape((MB, TOKENS, TOPK))
    gates = jnp.clip(0.05 + 0.15 * jax.random.uniform(splits[3], (MB, TOKENS, TOPK), jnp.float32) ** shard_levels(splits[3], (MB, TOKENS, TOPK), ((1, 32),), -0.2, 0.2), 0.05, 0.2)
    attn_gain = jnp.clip(1.0 + 0.1 * jax.random.normal(splits[4], (D,), jnp.float32), 0.5, 1.5).astype(jnp.bfloat16)
    w_qkv = centred(splits[5], (D, 3 * D), D ** -0.5, 0.125, ((0, 32),))
    q_gain = jnp.clip(1.0 + 0.1 * jax.random.normal(splits[6], (D,), jnp.float32), 0.5, 1.5).astype(jnp.bfloat16)
    k_gain = jnp.clip(1.0 + 0.1 * jax.random.normal(splits[7], (D,), jnp.float32), 0.5, 1.5).astype(jnp.bfloat16)
    w_out = centred(splits[8], (D, D), (D // 16) ** -0.5, 0.5, ((0, 32),))
    ffn_gain = jnp.clip(1.0 + 0.1 * jax.random.normal(splits[9], (D,), jnp.float32), 0.5, 1.5).astype(jnp.bfloat16)
    expert_in = centred(splits[10], (EXPERTS, D, 2 * FF), D ** -0.5, 0.125, ((0, 8), (1, 4)))
    expert_out = centred(splits[11], (EXPERTS, FF, D), (FF // 16) ** -0.5, 0.75, ((0, 8), (1, 4)))
    out_grad = centred(splits[12], (MB, TOKENS, D), 1.0, 6.0, ((1, 32),))
    return dict(tokens=tokens, lengths=lengths, expert_ids=expert_ids, gates=gates, attn_gain=attn_gain, w_qkv=w_qkv, q_gain=q_gain, k_gain=k_gain, w_out=w_out, ffn_gain=ffn_gain, expert_in=expert_in, expert_out=expert_out, out_grad=out_grad)


epsilon = 1e-05
base_theta = 10000.0

@jax.custom_vjp
def low(v):
    return lax.optimization_barrier(v.astype(jnp.bfloat16)).astype(jnp.float32)

@jax.custom_vjp
def low_back(v):
    return v

def low_keep(v):
    return (low(v), None)

def low_pass(kept, grad):
    return (grad,)

def back_keep(v):
    return (v, None)

def back_low(kept, grad):
    return (low(grad),)
low.defvjp(low_keep, low_pass)
low_back.defvjp(back_keep, back_low)

def high_dot(left, right):
    return jnp.dot(left, right, precision=lax.Precision.HIGHEST, preferred_element_type=jnp.float32)

def rms_normal(values):
    return values * lax.rsqrt(lax.optimization_barrier(jnp.mean(values * values, axis=-1, keepdims=True)) + epsilon)

def rotate(field, position, turning):
    length = field.shape[0]
    heads = field.reshape(length, -1, HEAD)
    half = HEAD // 2
    ladder = jnp.arange(half, dtype=jnp.float32) * (2.0 / HEAD)
    frequency = jnp.exp(-jnp.log(base_theta) * ladder)
    angle = position.astype(jnp.float32)[:, None] * frequency[None, :]
    cosine = jnp.cos(angle)[:, None, :]
    sine = turning * jnp.sin(angle)[:, None, :]
    first = heads[..., :half]
    second = heads[..., half:]
    turned = jnp.concatenate([first * cosine - second * sine, second * cosine + first * sine], axis=-1)
    return turned.reshape(length, -1)

def layout(doc_lengths, length):
    ends = jnp.cumsum(doc_lengths).astype(jnp.int32)
    starts = (ends - doc_lengths).astype(jnp.int32)
    places = jnp.arange(length, dtype=jnp.int32)
    document = lax.optimization_barrier(jnp.sum((places[:, None] >= ends[None, :]).astype(jnp.int32), axis=1)).astype(jnp.int32)
    member = (places[:, None] >= starts[None, :]) & (places[:, None] < ends[None, :])
    first_place = lax.optimization_barrier(jnp.sum(jnp.where(member, starts[None, :], 0), axis=1)).astype(jnp.int32)
    return (document, (places - first_place).astype(jnp.int32))

def allowed_pairs(document):
    places = jnp.arange(document.shape[0], dtype=jnp.int32)
    return (document[:, None] == document[None, :]) & (places[:, None] >= places[None, :])

def pack_attention(pieces):
    query_raw, key_raw, value_raw, doc_lengths = pieces
    length = query_raw.shape[0]
    document, position = layout(doc_lengths, length)
    query_rows = low(rotate(query_raw, position, 1.0)).reshape(length, -1, HEAD)
    key_rows = low(rotate(key_raw, position, 1.0)).reshape(length, -1, HEAD)
    value_rows = low(value_raw).reshape(length, -1, HEAD)
    scores = jnp.einsum('qhd,khd->hqk', query_rows, key_rows, precision=lax.Precision.HIGHEST)
    scores = low_back(scores * HEAD ** (-0.5))
    scores = jnp.where(allowed_pairs(document)[None], scores, -1e+30)
    highest = lax.optimization_barrier(jnp.max(scores, axis=-1, keepdims=True))
    unnormed = jnp.exp(scores - highest)
    attn_probs = unnormed / lax.optimization_barrier(jnp.sum(unnormed, axis=-1, keepdims=True))
    mixed = jnp.einsum('hqk,khd->qhd', low(attn_probs), value_rows, precision=lax.Precision.HIGHEST)
    return mixed.reshape(length, -1)

def route_tables(expert_ids):
    packs = expert_ids.reshape(-1, SEQ * TOPK).astype(jnp.int32)
    pack_count = packs.shape[0]
    labels = jnp.arange(EXPERTS, dtype=jnp.int32)

    def rank_pack(flat_ids):
        onehot = (flat_ids[:, None] == labels[None, :]).astype(jnp.int32)
        before = (jnp.cumsum(onehot, axis=0) - onehot).astype(jnp.int32)
        return lax.optimization_barrier(jnp.sum(before * onehot, axis=1)).astype(jnp.int32)
    ranks = lax.map(rank_pack, packs)
    pack_base = (jnp.arange(pack_count, dtype=jnp.int32) * CAP)[:, None]
    slot_index = (packs * (pack_count * CAP) + pack_base + ranks).reshape(-1).astype(jnp.int32)
    route_count = slot_index.shape[0]
    filler = jnp.full((EXPERTS * pack_count * CAP,), route_count, jnp.int32)
    route_of_slot = filler.at[slot_index].set(jnp.arange(route_count, dtype=jnp.int32))
    return (slot_index, route_of_slot.reshape(EXPERTS, pack_count * CAP))

def make_forward(lengths, slot_index, route_of_slot):

    def forward(tokens_in, gates, attn_gain, w_qkv, q_gain, k_gain, w_out, ffn_gain, expert_in, expert_out):
        flat_rows = tokens_in.reshape(-1, D)
        row_count = flat_rows.shape[0]
        pack_count = row_count // SEQ
        normed_in = low(rms_normal(flat_rows) * attn_gain)
        projected = low_back(high_dot(normed_in, w_qkv))
        query_full = rms_normal(projected[:, :D]) * q_gain
        key_full = rms_normal(projected[:, D:2 * D]) * k_gain
        value_full = projected[:, 2 * D:]
        attended = lax.map(jax.checkpoint(pack_attention), (query_full.reshape(pack_count, SEQ, D), key_full.reshape(pack_count, SEQ, D), value_full.reshape(pack_count, SEQ, D), lengths.reshape(pack_count, NDOC)))
        attended = low(low_back(attended.reshape(row_count, D)))
        middle = flat_rows + low_back(high_dot(attended, w_out))
        routed_in = low(rms_normal(middle) * ffn_gain)
        padded = jnp.concatenate([routed_in, jnp.zeros((1, D), jnp.float32)], axis=0)

        def expert_run(pieces):
            picks, weight_in, weight_down = pieces
            rows_in = low_back(padded[picks // TOPK])
            gate_up = low_back(high_dot(rows_in, weight_in))
            hidden = low(jax.nn.silu(gate_up[:, :FF]) * gate_up[:, FF:])
            return low(low_back(high_dot(hidden, weight_down)))
        produced = lax.map(jax.checkpoint(expert_run), (route_of_slot, expert_in, expert_out)).reshape(-1, D)
        slot_rows = slot_index.reshape(row_count, TOPK)
        gate_rows = gates.reshape(row_count, TOPK)
        mixture = jnp.zeros((row_count, D), jnp.float32)
        for column in range(TOPK):
            mixture = mixture + gate_rows[:, column:column + 1] * produced[slot_rows[:, column]]
        return (middle + mixture).reshape(tokens_in.shape)
    return forward

def reference(tokens, lengths, expert_ids, gates, attn_gain, w_qkv, q_gain, k_gain, w_out, ffn_gain, expert_in, expert_out, out_grad):
    single = jnp.float32
    slot_index, route_of_slot = route_tables(expert_ids)
    forward = make_forward(lengths, slot_index, route_of_slot)
    primal, pullback = jax.vjp(forward, tokens.astype(single), gates.astype(single), attn_gain.astype(single), w_qkv.astype(single), q_gain.astype(single), k_gain.astype(single), w_out.astype(single), ffn_gain.astype(single), expert_in.astype(single), expert_out.astype(single))
    gradients = pullback(out_grad.astype(single))
    return (primal.astype(jnp.bfloat16), gradients[0], gradients[1], gradients[2], gradients[3], gradients[4], gradients[5], gradients[6], gradients[7], gradients[8], gradients[9])
```

```python
import jax
import jax.numpy as jnp
from jax import lax
from jax.sharding import PartitionSpec as P

HEAD = 128
epsilon = 1e-05
base_theta = 10000.0
masked_score = -1e30
single = jnp.float32
narrow = jnp.bfloat16


def normalize(values):
    factor = lax.rsqrt(jnp.mean(values * values, axis=-1, keepdims=True) + epsilon)
    return (values * factor, factor)


def rms_back(upstream, normal, factor, gain):
    weighted = upstream * gain
    inner = jnp.mean(weighted * normal, axis=-1, keepdims=True)
    return (factor * (weighted - normal * inner), jnp.sum(upstream * normal, axis=0))


def angles(position):
    half = HEAD // 2
    ladder = jnp.arange(half, dtype=single) * (2.0 / HEAD)
    frequency = jnp.exp(-jnp.log(base_theta) * ladder)
    angle = position.astype(single)[:, None] * frequency[None, :]
    return (jnp.cos(angle)[:, None, :], jnp.sin(angle)[:, None, :])


def rotate(field, cosine, sine):
    length = field.shape[0]
    heads = field.reshape(length, -1, HEAD)
    half = HEAD // 2
    first = heads[..., :half]
    second = heads[..., half:]
    turned = jnp.concatenate(
        [first * cosine - second * sine, second * cosine + first * sine], axis=-1
    )
    return turned.reshape(length, -1)


def layout(doc_lengths, length):
    packs, count = doc_lengths.shape
    upto = jnp.arange(count)[None, :] <= jnp.arange(count)[:, None]
    ends = jnp.sum(jnp.where(upto[None], doc_lengths[:, None, :], 0), axis=2)
    starts = ends - doc_lengths
    places = jnp.arange(length, dtype=jnp.int32)[None, :, None]
    document = jnp.sum((places >= ends[:, None, :]).astype(jnp.int32), axis=2)
    member = (places >= starts[:, None, :]) & (places < ends[:, None, :])
    first_place = jnp.sum(jnp.where(member, starts[:, None, :], 0), axis=2)
    document = document + (count + 1) * jnp.arange(packs, dtype=jnp.int32)[:, None]
    return (document.reshape(-1), (places[..., 0] - first_place).reshape(-1))


def contract_rows(left, right, kind=single):
    return lax.dot_general(left, right, (((0,), (0,)), ((), ())), preferred_element_type=kind)


def contract_last(left, right, kind=single):
    return lax.dot_general(left, right, (((1,), (1,)), ((), ())), preferred_element_type=kind)


def core_groups():
    return [[2 * chip + core for chip in range(lax.axis_size("expert") // 2)] for core in range(2)]


def chip_groups():
    return [[2 * chip, 2 * chip + 1] for chip in range(lax.axis_size("expert") // 2)]


def gather_alike(block):
    column = lax.all_gather(block, "dp", axis=0)
    return lax.all_gather(column, "expert", axis=1, axis_index_groups=core_groups())


def scatter_alike(blocks):
    column = lax.psum_scatter(
        blocks, "expert", scatter_dimension=1, axis_index_groups=core_groups()
    )
    return lax.psum_scatter(column, "dp", scatter_dimension=0)


def fetch_weights(expert_in, expert_out):
    depth = lax.axis_size("dp")
    held, rows, columns = expert_in.shape
    part = columns // (2 * depth)
    cut = expert_in.reshape(held, rows, 2, depth, part)
    turned = lax.all_to_all(cut, "dp", split_axis=3, concat_axis=1, tiled=True)
    both = lax.all_gather(turned[:, :, :, 0], "expert", axis=0, axis_index_groups=chip_groups())
    weight_in = both.transpose(2, 3, 0, 1, 4).reshape(depth * rows, 4 * held * part)
    weight_down = lax.all_gather(
        expert_out, "expert", axis=0, axis_index_groups=chip_groups()
    ).reshape(-1, expert_out.shape[2])
    return (weight_in, weight_down)


def return_weights(grad_in, grad_down, held):
    depth = lax.axis_size("dp")
    rows, columns = grad_in.shape
    part = columns // (4 * held)
    cut = grad_in.reshape(rows, 2, 2, held, part)
    own = lax.psum_scatter(cut, "expert", scatter_dimension=2, axis_index_groups=chip_groups())
    own = own.reshape(depth, rows // depth, 2, held, part)
    turned = lax.all_to_all(own, "dp", split_axis=0, concat_axis=0)
    share_in = turned.transpose(3, 1, 2, 0, 4).reshape(held, rows // depth, 2 * depth * part)
    down = grad_down.reshape(2, held, part, grad_down.shape[1])
    share_down = lax.psum_scatter(
        down, "expert", scatter_dimension=0, axis_index_groups=chip_groups()
    )
    return (share_in, share_down)


def expert_round(mid_rows, up_rows, gate, weight_in, weight_down):
    count = gate.shape[1]
    part = weight_down.shape[0] // count
    wide = jnp.broadcast_to(gate[:, :, None], gate.shape + (part,)).reshape(gate.shape[0], -1)
    gate_up = jnp.dot(mid_rows, weight_in, preferred_element_type=single)
    hidden_units = gate_up.shape[1] // 2
    gate_part = gate_up[:, :hidden_units]
    up_part = gate_up[:, hidden_units:]
    sigmoid = jax.nn.sigmoid(gate_part)
    activated = gate_part * sigmoid
    hidden = activated * up_part
    back = contract_last(up_rows, weight_down)
    scaled = (wide * hidden).astype(narrow)
    piece_out = jnp.dot(scaled, weight_down, preferred_element_type=narrow)
    piece_gates = jnp.sum((hidden * back).reshape(-1, count, part), axis=2)
    grad_hidden = wide * back
    grad_gate = grad_hidden * up_part * sigmoid * (1.0 + gate_part * (1.0 - sigmoid))
    grad_up = grad_hidden * activated
    grad_gate_up = jnp.concatenate([grad_gate, grad_up], axis=1).astype(narrow)
    piece_mid = contract_last(grad_gate_up, weight_in, narrow)
    return (piece_out, piece_mid, piece_gates, grad_gate_up, scaled)


def expert_rounds(mid_rows, up_rows, gate, weight_in, weight_down):
    total = mid_rows.shape[0]
    rounds = max(1, total // 2048)

    def one(sums, pieces):
        mid, up, weights = pieces
        piece_out, piece_mid, piece_gates, grad_gate_up, scaled = expert_round(
            mid, up, weights, weight_in, weight_down
        )
        grads = (contract_rows(mid, grad_gate_up), contract_rows(scaled, up))
        return (jax.tree.map(jnp.add, sums, grads), (piece_out, piece_mid, piece_gates))

    if rounds == 1:
        piece_out, piece_mid, piece_gates, grad_gate_up, scaled = expert_round(
            mid_rows, up_rows, gate, weight_in, weight_down
        )
        grads = (contract_rows(mid_rows, grad_gate_up, narrow), contract_rows(scaled, up_rows, narrow))
        return (piece_out, piece_mid, piece_gates) + grads
    start = (jnp.zeros(weight_in.shape, single), jnp.zeros(weight_down.shape, single))
    cut = jax.tree.map(lambda a: a.reshape(rounds, total // rounds, -1), (mid_rows, up_rows, gate))
    sums, made = lax.scan(one, start, cut)
    made = jax.tree.map(lambda a: a.reshape(total, -1), made)
    return made + (sums[0].astype(narrow), sums[1].astype(narrow))


def local(
    tokens,
    lengths,
    expert_ids,
    gates,
    attn_gain,
    w_qkv,
    q_gain,
    k_gain,
    w_out,
    ffn_gain,
    expert_in,
    expert_out,
    out_grad,
):
    micro_count, seq_len, model_width = tokens.shape
    rows = micro_count * seq_len
    depth = lax.axis_size("dp")
    owners = lax.axis_size("expert")
    held = expert_in.shape[0]
    experts = owners * held
    chip_experts = 2 * held
    everyone = ("dp", "expert")
    gain_rows = jnp.stack([attn_gain, q_gain, k_gain, ffn_gain]).astype(single)
    gains = lax.all_gather(gain_rows, everyone, axis=1, tiled=True)
    gain_attn, gain_query, gain_key, gain_ffn = gains[0], gains[1], gains[2], gains[3]
    weight_qkv = lax.all_gather(w_qkv, everyone, axis=0, tiled=True)
    weight_out = lax.all_gather(w_out, everyone, axis=0, tiled=True)
    weight_in, weight_down = fetch_weights(expert_in, expert_out)

    inputs = tokens.reshape(rows, model_width).astype(single)
    upstream = out_grad.reshape(rows, model_width)
    ids = expert_ids.reshape(rows, -1)
    gate_rows = gates.reshape(rows, -1)
    onehot = (ids[:, :, None] == jnp.arange(experts, dtype=jnp.int32)).astype(single)
    dense = jnp.sum(onehot * gate_rows[:, :, None], axis=1)

    normal_in, factor_in = normalize(inputs)
    normed_in = (normal_in * gain_attn).astype(narrow)
    projected = jnp.dot(normed_in, weight_qkv, preferred_element_type=single)
    normal_q, factor_q = normalize(projected[:, :model_width])
    normal_k, factor_k = normalize(projected[:, model_width : 2 * model_width])
    document, position = layout(lengths[:, 0], seq_len)
    cosine, sine = angles(position)
    query_rows = rotate(normal_q * gain_query, cosine, sine).astype(narrow).reshape(rows, -1, HEAD)
    key_rows = rotate(normal_k * gain_key, cosine, sine).astype(narrow).reshape(rows, -1, HEAD)
    value_rows = projected[:, 2 * model_width :].astype(narrow).reshape(rows, -1, HEAD)
    places = jnp.arange(rows, dtype=jnp.int32)
    allowed = (document[:, None] == document[None, :]) & (places[:, None] >= places[None, :])
    raw = jnp.einsum("qhd,khd->hqk", query_rows, key_rows, preferred_element_type=single)
    scores = jnp.where(allowed[None], raw * HEAD ** (-0.5), masked_score)
    highest = jnp.max(scores, axis=-1, keepdims=True)
    unnormed = jnp.exp(scores - highest)
    probs = unnormed / jnp.sum(unnormed, axis=-1, keepdims=True)
    attn_probs = probs.astype(narrow)
    attended = (
        jnp.einsum("hqk,khd->qhd", attn_probs, value_rows, preferred_element_type=single)
        .reshape(rows, model_width)
        .astype(narrow)
    )
    middle = inputs + jnp.dot(attended, weight_out, preferred_element_type=single)
    normal_mid, factor_mid = normalize(middle)
    routed_in = (normal_mid * gain_ffn).astype(narrow)

    chip = lax.axis_index("expert") // 2
    up_rows = gather_alike(upstream).reshape(-1, model_width)
    mid_rows = gather_alike(routed_in).reshape(-1, model_width)
    every_gate = gather_alike(dense.T)
    mine = lax.dynamic_slice_in_dim(every_gate, chip * chip_experts, chip_experts, axis=2)
    gate = mine.transpose(0, 1, 3, 2).reshape(-1, chip_experts)
    piece_out, piece_mid, piece_gates, grad_in_part, grad_down_part = expert_rounds(
        mid_rows, up_rows, gate, weight_in, weight_down
    )

    chips = owners // 2
    mixture = scatter_alike(piece_out.reshape(depth, chips, rows, model_width)).astype(single)
    grad_routed = scatter_alike(piece_mid.reshape(depth, chips, rows, model_width)).astype(single)
    by_gate = piece_gates.reshape(depth, chips, rows, chip_experts).transpose(0, 1, 3, 2)
    spread = jnp.zeros((depth, chips, experts, rows), single)
    spread = lax.dynamic_update_slice_in_dim(spread, by_gate, chip * chip_experts, axis=2)
    gate_table = scatter_alike(spread).T
    grad_gates = jnp.sum(onehot * gate_table[:, None, :], axis=2)
    results = (middle + mixture).astype(narrow)

    grad_mid, piece_ffn = rms_back(grad_routed, normal_mid, factor_mid, gain_ffn)
    grad_middle = upstream.astype(single) + grad_mid
    grad_branch = grad_middle.astype(narrow)
    grad_out_part = contract_rows(attended, grad_branch, narrow)
    grad_attended = contract_last(grad_branch, weight_out).astype(narrow).reshape(rows, -1, HEAD)
    grad_probs = jnp.einsum("qhd,khd->hqk", grad_attended, value_rows, preferred_element_type=single)
    inner = jnp.sum(grad_probs * probs, axis=-1, keepdims=True)
    grad_scores = (probs * (grad_probs - inner)).astype(narrow)
    grad_query = jnp.einsum(
        "hqk,khd->qhd", grad_scores, key_rows, preferred_element_type=single
    ) * HEAD ** (-0.5)
    grad_key = jnp.einsum(
        "hqk,qhd->khd", grad_scores, query_rows, preferred_element_type=single
    ) * HEAD ** (-0.5)
    grad_value = jnp.einsum("hqk,qhd->khd", attn_probs, grad_attended, preferred_element_type=single)
    grad_q_raw, piece_query = rms_back(
        rotate(grad_query.reshape(rows, model_width), cosine, -sine), normal_q, factor_q, gain_query
    )
    grad_k_raw, piece_key = rms_back(
        rotate(grad_key.reshape(rows, model_width), cosine, -sine), normal_k, factor_k, gain_key
    )
    grad_qkv = jnp.concatenate(
        [grad_q_raw, grad_k_raw, grad_value.reshape(rows, model_width)], axis=1
    ).astype(narrow)
    grad_qkv_part = contract_rows(normed_in, grad_qkv, narrow)
    grad_normed = contract_last(grad_qkv, weight_qkv)
    grad_input, piece_attn = rms_back(grad_normed, normal_in, factor_in, gain_attn)
    grad_tokens = grad_middle + grad_input

    pieces = jnp.stack([piece_attn, piece_query, piece_key, piece_ffn])
    gain_sums = lax.psum_scatter(pieces, everyone, scatter_dimension=1, tiled=True)
    grad_qkv_share = lax.psum_scatter(grad_qkv_part, everyone, scatter_dimension=0, tiled=True)
    grad_out_share = lax.psum_scatter(grad_out_part, everyone, scatter_dimension=0, tiled=True)
    share_in, share_down = return_weights(grad_in_part, grad_down_part, held)
    shape = (micro_count, seq_len, model_width)
    return (
        results.reshape(shape),
        grad_tokens.reshape(shape),
        grad_gates.reshape(expert_ids.shape),
        gain_sums[0],
        grad_qkv_share.astype(single),
        gain_sums[1],
        gain_sums[2],
        grad_out_share.astype(single),
        gain_sums[3],
        share_in.astype(single),
        share_down.astype(single),
    )


def solution(mesh):
    by_rows = P(None, ("dp", "expert"), None)
    flat = P(("dp", "expert"))
    split = P(("dp", "expert"), None)
    held = P("expert", "dp", None)
    return jax.shard_map(
        local,
        mesh=mesh,
        in_specs=(
            by_rows, by_rows, by_rows, by_rows, flat, split, flat, flat, split, flat, held, held, by_rows,
        ),
        out_specs=(by_rows, by_rows, by_rows, flat, split, flat, flat, split, flat, held, held),
        check_vma=False,
    )
```

```python
import jax
import jax.numpy as jnp
from jax import lax
from jax.experimental import pallas as pl
from jax.experimental.pallas import tpu as pltpu
from jax.sharding import PartitionSpec as P

HEAD = 128
epsilon = 1e-05
base_theta = 10000.0
masked_score = -1e30
single = jnp.float32
narrow = jnp.bfloat16


def normalize(values):
    factor = lax.rsqrt(jnp.mean(values * values, axis=-1, keepdims=True) + epsilon)
    return (values * factor, factor)


def rms_back(upstream, normal, factor, gain):
    weighted = upstream * gain
    inner = jnp.mean(weighted * normal, axis=-1, keepdims=True)
    return (factor * (weighted - normal * inner), jnp.sum(upstream * normal, axis=0))


def angles(position):
    half = HEAD // 2
    ladder = jnp.arange(half, dtype=single) * (2.0 / HEAD)
    frequency = jnp.exp(-jnp.log(base_theta) * ladder)
    angle = position.astype(single)[:, None] * frequency[None, :]
    return (jnp.cos(angle)[:, None, :], jnp.sin(angle)[:, None, :])


def rotate(field, cosine, sine):
    length = field.shape[0]
    heads = field.reshape(length, -1, HEAD)
    half = HEAD // 2
    first = heads[..., :half]
    second = heads[..., half:]
    turned = jnp.concatenate(
        [first * cosine - second * sine, second * cosine + first * sine], axis=-1
    )
    return turned.reshape(length, -1)


def layout(doc_lengths, length):
    packs, count = doc_lengths.shape
    upto = jnp.arange(count)[None, :] <= jnp.arange(count)[:, None]
    ends = jnp.sum(jnp.where(upto[None], doc_lengths[:, None, :], 0), axis=2)
    starts = ends - doc_lengths
    places = jnp.arange(length, dtype=jnp.int32)[None, :, None]
    document = jnp.sum((places >= ends[:, None, :]).astype(jnp.int32), axis=2)
    member = (places >= starts[:, None, :]) & (places < ends[:, None, :])
    first_place = jnp.sum(jnp.where(member, starts[:, None, :], 0), axis=2)
    document = document + (count + 1) * jnp.arange(packs, dtype=jnp.int32)[:, None]
    return (document.reshape(-1), (places[..., 0] - first_place).reshape(-1))


def contract_rows(left, right, kind=single):
    return lax.dot_general(left, right, (((0,), (0,)), ((), ())), preferred_element_type=kind)


def contract_last(left, right, kind=single):
    return lax.dot_general(left, right, (((1,), (1,)), ((), ())), preferred_element_type=kind)


def core_groups():
    return [[2 * chip + core for chip in range(lax.axis_size("expert") // 2)] for core in range(2)]


def chip_groups():
    return [[2 * chip, 2 * chip + 1] for chip in range(lax.axis_size("expert") // 2)]


def gather_alike(block):
    column = lax.all_gather(block, "dp", axis=0)
    return lax.all_gather(column, "expert", axis=1, axis_index_groups=core_groups())


def scatter_alike(blocks):
    column = lax.psum_scatter(
        blocks, "expert", scatter_dimension=1, axis_index_groups=core_groups()
    )
    return lax.psum_scatter(column, "dp", scatter_dimension=0)


def fetch_weights(expert_in, expert_out):
    depth = lax.axis_size("dp")
    held, rows, columns = expert_in.shape
    part = columns // (2 * depth)
    cut = expert_in.reshape(held, rows, 2, depth, part)
    turned = lax.all_to_all(cut, "dp", split_axis=3, concat_axis=1, tiled=True)
    both = lax.all_gather(turned[:, :, :, 0], "expert", axis=0, axis_index_groups=chip_groups())
    weight_in = both.transpose(2, 3, 0, 1, 4).reshape(depth * rows, 4 * held * part)
    weight_down = lax.all_gather(
        expert_out, "expert", axis=0, axis_index_groups=chip_groups()
    ).reshape(-1, expert_out.shape[2])
    return (weight_in, weight_down)


def return_weights(grad_in, grad_down, held):
    depth = lax.axis_size("dp")
    rows, columns = grad_in.shape
    part = columns // (4 * held)
    cut = grad_in.reshape(rows, 2, 2, held, part)
    own = lax.psum_scatter(cut, "expert", scatter_dimension=2, axis_index_groups=chip_groups())
    own = own.reshape(depth, rows // depth, 2, held, part)
    turned = lax.all_to_all(own, "dp", split_axis=0, concat_axis=0)
    share_in = turned.transpose(3, 1, 2, 0, 4).reshape(held, rows // depth, 2 * depth * part)
    down = grad_down.reshape(2, held, part, grad_down.shape[1])
    share_down = lax.psum_scatter(
        down, "expert", scatter_dimension=0, axis_index_groups=chip_groups()
    )
    return (share_in, share_down)


def expert_round(mid_rows, up_rows, gate, weight_in, weight_down):
    count = gate.shape[1]
    part = weight_down.shape[0] // count
    wide = jnp.broadcast_to(gate[:, :, None], gate.shape + (part,)).reshape(gate.shape[0], -1)
    gate_up = jnp.dot(mid_rows, weight_in, preferred_element_type=single)
    hidden_units = gate_up.shape[1] // 2
    gate_part = gate_up[:, :hidden_units]
    up_part = gate_up[:, hidden_units:]
    sigmoid = jax.nn.sigmoid(gate_part)
    activated = gate_part * sigmoid
    hidden = activated * up_part
    back = contract_last(up_rows, weight_down)
    scaled = (wide * hidden).astype(narrow)
    piece_out = jnp.dot(scaled, weight_down, preferred_element_type=narrow)
    piece_gates = jnp.sum((hidden * back).reshape(-1, count, part), axis=2)
    grad_hidden = wide * back
    grad_gate = grad_hidden * up_part * sigmoid * (1.0 + gate_part * (1.0 - sigmoid))
    grad_up = grad_hidden * activated
    grad_gate_up = jnp.concatenate([grad_gate, grad_up], axis=1).astype(narrow)
    piece_mid = contract_last(grad_gate_up, weight_in, narrow)
    return (piece_out, piece_mid, piece_gates, grad_gate_up, scaled)


def expert_rounds(mid_rows, up_rows, gate, weight_in, weight_down):
    total = mid_rows.shape[0]
    rounds = max(1, total // 2048)

    def one(sums, pieces):
        mid, up, weights = pieces
        piece_out, piece_mid, piece_gates, grad_gate_up, scaled = expert_round(
            mid, up, weights, weight_in, weight_down
        )
        grads = (contract_rows(mid, grad_gate_up), contract_rows(scaled, up))
        return (jax.tree.map(jnp.add, sums, grads), (piece_out, piece_mid, piece_gates))

    if rounds == 1:
        piece_out, piece_mid, piece_gates, grad_gate_up, scaled = expert_round(
            mid_rows, up_rows, gate, weight_in, weight_down
        )
        grads = (contract_rows(mid_rows, grad_gate_up, narrow), contract_rows(scaled, up_rows, narrow))
        return (piece_out, piece_mid, piece_gates) + grads
    start = (jnp.zeros(weight_in.shape, single), jnp.zeros(weight_down.shape, single))
    cut = jax.tree.map(lambda a: a.reshape(rounds, total // rounds, -1), (mid_rows, up_rows, gate))
    sums, made = lax.scan(one, start, cut)
    made = jax.tree.map(lambda a: a.reshape(total, -1), made)
    return made + (sums[0].astype(narrow), sums[1].astype(narrow))


MESH = pl.DeviceIdType.MESH
HBM = pl.BlockSpec(memory_space=pl.ANY)
DEPTH = 4
RING = 4


def ring_turn(number):
    high = lax.div(number, 2)
    return number + high * (1 - 2 * lax.rem(number, 2))


class Here:
    def __init__(self):
        number = lax.axis_index("expert")
        self.z = lax.axis_index("dp")
        self.core = lax.rem(number, 2)
        self.chip = lax.div(number, 2)
        self.q = ring_turn(self.chip)

    def chip_at(self, turn):
        return ring_turn(lax.rem(self.q + turn + RING, RING))

    def beside(self, turn):
        return (self.z, 2 * self.chip_at(turn) + self.core)

    def above(self, steps):
        return (lax.rem(self.z + steps + DEPTH, DEPTH), 2 * self.chip + self.core)

    def sibling(self):
        return (self.z, 2 * self.chip + 1 - self.core)

    def meet(self):
        barrier = pltpu.get_barrier_semaphore()
        others = [self.beside(1), self.beside(-1), self.sibling()]
        others += [self.above(steps) for steps in range(1, DEPTH)]
        for other in others:
            pl.semaphore_signal(barrier, inc=1, device_id=other, device_id_type=MESH)
        pl.semaphore_wait(barrier, len(others))


def remote(source, target, sent, arrived, device):
    return pltpu.make_async_remote_copy(
        src_ref=source,
        dst_ref=target,
        send_sem=sent,
        recv_sem=arrived,
        device_id=device,
        device_id_type=MESH,
    )


GATHER_SEMS = [
    pltpu.SemaphoreType.DMA((2, 2, DEPTH - 1)),
    pltpu.SemaphoreType.DMA((2, DEPTH, 2, 2)),
    pltpu.SemaphoreType.DMA((2, DEPTH)),
    pltpu.SemaphoreType.DMA((1,)),
]


class Gather:
    def __init__(self, here, source, whole, halves, shared, sems):
        self.here, self.source, self.whole, self.halves, self.shared = here, source, whole, halves, shared
        self.line, self.ring, self.pair, self.own = sems

    def block(self, z, turn):
        chip = self.here.chip_at(turn)
        return self.whole.at[z, chip, self.here.core] if self.shared else self.whole.at[z, chip]

    def keep(self):
        return pltpu.make_async_copy(self.source, self.block(self.here.z, 0), self.own.at[0])

    def along(self, step, way, first):
        z = self.here.z - step + 1 if way == 0 else self.here.z + step - 1
        block = self.block(z, 0)
        return remote(
            self.source if first else block,
            block,
            self.line.at[0, way, step - 1],
            self.line.at[1, way, step - 1],
            self.here.above(1 if way == 0 else -1),
        )

    def round(self, z, way, first=False):
        turn = 1 if way == 0 else -1
        block = self.block(z, 0)
        return remote(
            self.source if first else block,
            block,
            self.ring.at[0, z, way, 0],
            self.ring.at[1, z, way, 0],
            self.here.beside(turn),
        )

    def heard(self, z, way):
        block = self.block(z, -1 if way == 0 else 1)
        return remote(
            block, block, self.ring.at[0, z, way, 0], self.ring.at[1, z, way, 0], self.here.beside(1)
        )

    def onward(self, z, way, mine):
        if self.halves[way] is None:
            return None
        turn = (-1 if mine else -2) if way == 0 else (1 if mine else 2)
        block = self.block(z, turn).at[pl.ds(*self.halves[way])]
        return remote(
            block,
            block,
            self.ring.at[0, z, way, 1],
            self.ring.at[1, z, way, 1],
            self.here.beside(1 if way == 0 else -1),
        )

    def swap(self, z, mine):
        core = self.here.core if mine else 1 - self.here.core
        part = self.whole.at[z, :, core]
        return remote(part, part, self.pair.at[0, z], self.pair.at[1, z], self.here.sibling())


def start(copy):
    if copy is not None:
        copy.start()


def run_gather(here, items, between=()):
    places = [(0, 0)] + [(step, way) for step in range(1, DEPTH) for way in (0, 1)]

    def when(step, way, body):
        z = here.z - step if way == 0 else here.z + step
        if step == 0:
            body(z)
        else:
            pl.when(z >= 0 if way == 0 else z < DEPTH)(lambda: body(z))

    def depart(step, way, item):
        ahead = here.z + 1 < DEPTH if way == 0 else here.z >= 1
        pl.when(ahead)(lambda: item.along(step + 1, way, step == 0).start())

    for item in items:
        item.keep().start()
        for way in (0, 1):
            depart(0, way, item)
        for way in (0, 1):
            item.round(here.z, way, True).start()

    def second(z):
        for item in items:
            for way in (0, 1):
                item.heard(z, way).wait_recv()
                start(item.onward(z, way, True))

    def third(z):
        for item in items:
            for way in (0, 1):
                copy = item.onward(z, way, False)
                if copy is not None:
                    copy.wait_recv()
            if item.shared:
                item.swap(z, True).start()

    for step in range(1, DEPTH):
        for way in (0, 1):

            def first(z, step=step, way=way):
                for item in items:
                    block = item.block(z, 0)
                    remote(
                        block, block, item.line.at[0, way, step - 1], item.line.at[1, way, step - 1], here.above(1)
                    ).wait_recv()
                    if step + 1 < DEPTH:
                        depart(step, way, item)
                    for side in (0, 1):
                        item.round(z, side).start()

            when(step, way, first)
        if step == 1:
            for item in items:
                item.keep().wait()
        if step <= len(between):
            between[step - 1]()
        for before, way in places:
            if before == step - 1:
                when(before, way, second)
        for before, way in places:
            if before == step - 2:
                when(before, way, third)
    for before, way in places:
        if before == DEPTH - 1:
            when(before, way, second)
    for late in (DEPTH - 2, DEPTH - 1):
        for before, way in places:
            if before == late:
                when(before, way, third)

    def settle(z):
        for item in items:
            for way in (0, 1):
                item.round(z, way).wait_send()
                copy = item.onward(z, way, True)
                if copy is not None:
                    copy.wait_send()
            if item.shared:
                item.swap(z, True).wait_send()
                item.swap(z, False).wait_recv()

    for step, way in places:
        when(step, way, settle)
    for item in items:
        for step in range(DEPTH - 1):
            for way in (0, 1):

                def sent(z, step=step, way=way, item=item):
                    ahead = here.z + 1 < DEPTH if way == 0 else here.z >= 1
                    pl.when(ahead)(lambda: item.along(step + 1, way, step == 0).wait_send())

                when(step, way, sent)


class Recut:
    def __init__(self, here, source_in, source_out, whole_in, whole_out, sems):
        self.here, self.source_in, self.source_out = here, source_in, source_out
        self.whole_in, self.whole_out = whole_in, whole_out
        self.cut, self.pair, self.down, self.own = sems
        self.held, self.rows, columns = source_in.shape
        self.hidden = columns // 2
        self.part = self.hidden // DEPTH

    def pieces(self, steps, arriving):
        here, copies = self.here, []
        mine = lax.rem(here.z + DEPTH - steps, DEPTH) if arriving else here.z
        away = lax.rem(here.z + steps, DEPTH)
        for side in range(2):
            for expert in range(self.held):
                columns = side * self.held * 2 * self.part + (here.core * self.held + expert) * self.part
                target = self.whole_in.at[
                    pl.ds(pl.multiple_of(mine * self.rows, 16), self.rows),
                    pl.ds(pl.multiple_of(columns, 128), self.part),
                ]
                source = self.source_in.at[
                    expert, :, pl.ds(pl.multiple_of(side * self.hidden + away * self.part, 128), self.part)
                ]
                spot = (steps, side * self.held + expert)
                if steps == 0:
                    copies.append(pltpu.make_async_copy(source, target, self.own.at[spot[1]]))
                else:
                    copies.append(
                        remote(
                            target if arriving else source,
                            target,
                            self.cut.at[(0,) + spot],
                            self.cut.at[(1,) + spot],
                            here.above(steps),
                        )
                    )
        return copies

    def across(self, steps, mine):
        here, copies = self.here, []
        core = here.core if mine else 1 - here.core
        row = lax.rem(here.z + DEPTH - steps, DEPTH)
        width = self.held * self.part
        for side in range(2):
            spot = self.whole_in.at[
                pl.ds(pl.multiple_of(row * self.rows, 16), self.rows),
                pl.ds(pl.multiple_of(side * 2 * width + core * width, 128), width),
            ]
            copies.append(
                remote(spot, spot, self.pair.at[0, steps, side], self.pair.at[1, steps, side], here.sibling())
            )
        return copies

    def lower(self, mine):
        here = self.here
        core = here.core if mine else 1 - here.core
        spot = self.whole_out.at[pl.ds(core * self.held, self.held)]
        return remote(
            self.source_out if mine else spot, spot, self.down.at[0], self.down.at[1], here.sibling()
        )

    def lower_own(self):
        return pltpu.make_async_copy(
            self.source_out, self.whole_out.at[pl.ds(self.here.core * self.held, self.held)], self.own.at[4]
        )

    def begin(self):
        for copy in self.pieces(0, False):
            copy.start()
        self.lower_own().start()
        self.lower(True).start()
        for steps in range(1, DEPTH):
            for copy in self.pieces(steps, False):
                copy.start()

    def relay(self):
        for steps in range(DEPTH):
            for copy in self.pieces(steps, True):
                copy.wait() if steps == 0 else copy.wait_recv()
            for copy in self.across(steps, True):
                copy.start()

    def end(self):
        self.lower_own().wait()
        self.lower(True).wait_send()
        self.lower(False).wait_recv()
        for steps in range(DEPTH):
            if steps:
                for copy in self.pieces(steps, False):
                    copy.wait_send()
            for copy in self.across(steps, True):
                copy.wait_send()
            for copy in self.across(steps, False):
                copy.wait_recv()


RECUT_SEMS = [
    pltpu.SemaphoreType.DMA((2, DEPTH, 4)),
    pltpu.SemaphoreType.DMA((2, DEPTH, 2)),
    pltpu.SemaphoreType.DMA((2,)),
    pltpu.SemaphoreType.DMA((5,)),
]


def halves_of(rows, split=True):
    return ((0, rows // 2), (rows // 2, rows - rows // 2)) if split else ((0, rows), None)


def first_gather_kernel(wq, wo, up, small, ein, eout, wq_all, wo_all, up_all, small_all, win, wout, *sems):
    here = Here()
    here.meet()
    items = []
    for number, (source, whole, halves, shared) in enumerate(
        (
            (small, small_all, halves_of(small.shape[0], False), True),
            (wq, wq_all, halves_of(wq.shape[0]), True),
            (wo, wo_all, halves_of(wo.shape[0]), True),
            (up, up_all, halves_of(up.shape[0]), False),
        )
    ):
        items.append(Gather(here, source, whole, halves, shared, sems[4 * number : 4 * number + 4]))
    recut = Recut(here, ein, eout, win, wout, sems[16:20])
    run_gather(here, items, (recut.begin,))
    recut.relay()
    recut.end()


def first_gather(wq, wo, up, small, ein, eout):
    def whole(array, shared):
        lead = (DEPTH, RING, 2) if shared else (DEPTH, RING)
        return jax.ShapeDtypeStruct(lead + array.shape, array.dtype)

    held, rows, columns = ein.shape
    return pl.pallas_call(
        first_gather_kernel,
        out_shape=(
            whole(wq, True),
            whole(wo, True),
            whole(up, False),
            whole(small, True),
            jax.ShapeDtypeStruct((DEPTH * rows, columns), ein.dtype),
            jax.ShapeDtypeStruct((2 * held,) + eout.shape[1:], eout.dtype),
        ),
        in_specs=[HBM] * 6,
        out_specs=(HBM,) * 6,
        scratch_shapes=GATHER_SEMS * 4 + RECUT_SEMS,
        compiler_params=pltpu.CompilerParams(collective_id=1, has_side_effects=True),
        name="bring",
    )(wq, wo, up, small, ein, eout)


def row_gather_kernel(rows, whole, *sems):
    here = Here()
    here.meet()
    run_gather(here, [Gather(here, rows, whole, halves_of(rows.shape[0]), False, sems)])


def row_gather(rows):
    return pl.pallas_call(
        row_gather_kernel,
        out_shape=jax.ShapeDtypeStruct((DEPTH, RING) + rows.shape, rows.dtype),
        in_specs=[HBM],
        out_specs=HBM,
        scratch_shapes=GATHER_SEMS,
        compiler_params=pltpu.CompilerParams(collective_id=2, has_side_effects=True),
        name="spread",
    )(rows)


def add_up(target, terms, rows, columns):
    high = 16 if rows % 16 == 0 else 8
    wide = min(columns, 1024)
    across = columns // wide

    def piece(number, carry):
        row = pl.multiple_of(lax.div(number, across) * high, high)
        column = pl.multiple_of(lax.rem(number, across) * wide, 128)
        spot = (pl.ds(row, high), pl.ds(column, wide))
        total = terms[0][spot].astype(single)
        for term in terms[1:]:
            total = total + term[spot].astype(single)
        target[spot] = total.astype(target.dtype)
        return carry

    lax.fori_loop(0, (rows // high) * across, piece, 0)


SUM_SEMS = [
    pltpu.SemaphoreType.DMA((2, DEPTH, 2)),
    pltpu.SemaphoreType.DMA((2, DEPTH, 2)),
    pltpu.SemaphoreType.DMA((2, 2, DEPTH)),
    pltpu.SemaphoreType.DMA((DEPTH, RING, 2)),
]


def sum_scratch(rows, columns, kind, halves, paired):
    high = max(size for _, size in filter(None, halves))
    kept = RING if paired else RING - 1
    made = [
        pltpu.VMEM((DEPTH, kept, rows, columns), kind),
        pltpu.VMEM((DEPTH, 2, high, columns), kind),
        pltpu.VMEM((DEPTH, 2, rows, columns), kind),
        pltpu.VMEM((2, DEPTH, rows, columns), kind),
    ] + SUM_SEMS
    if paired:
        made += [pltpu.VMEM((DEPTH, RING, rows, columns), kind), pltpu.SemaphoreType.DMA((2, DEPTH, 2))]
    return made


class Sum:
    def __init__(self, here, sources, target, halves, paired, scratch):
        self.here, self.sources, self.target, self.halves, self.paired = here, sources, target, halves, paired
        self.mine, self.half, self.full, self.column = scratch[:4]
        self.half_sem, self.full_sem, self.line_sem, self.load_sem = scratch[4:8]
        if paired:
            self.other, self.pair_sem = scratch[8:10]
        self.rows, self.columns = self.mine.shape[2:]

    def kept(self, z, turn):
        return self.mine.at[z, turn if self.paired else {0: 0, 1: 1, 3: 2}[turn]]

    def raw(self, part, z, turn):
        chip = self.here.chip_at(turn)
        return part.at[z, chip, self.here.core] if self.paired else part.at[z, chip]

    def spots(self):
        at, made = 0, []
        for part in self.sources:
            made.append((part, pl.ds(at, part.shape[-1])))
            at += part.shape[-1]
        return made

    def loads(self, z, turn):
        return [
            pltpu.make_async_copy(
                self.raw(part, z, turn), self.kept(z, turn).at[:, spot], self.load_sem.at[z, turn, number]
            )
            for number, (part, spot) in enumerate(self.spots())
        ]

    def swaps(self, z, mine):
        return [
            remote(
                part.at[z, :, 1 - self.here.core] if mine else self.other.at[z, :, :, spot],
                self.other.at[z, :, :, spot],
                self.pair_sem.at[0, z, number],
                self.pair_sem.at[1, z, number],
                self.here.sibling(),
            )
            for number, (part, spot) in enumerate(self.spots())
        ]

    def toss(self, z, way):
        if self.halves[way] is None:
            return None
        rows = pl.ds(*self.halves[way])
        source = (self.kept(z, 2) if self.paired else self.raw(self.sources[0], z, 2)).at[rows]
        return remote(
            source,
            self.half.at[z, way, pl.ds(0, self.halves[way][1])],
            self.half_sem.at[0, z, way],
            self.half_sem.at[1, z, way],
            self.here.beside(1 if way == 0 else -1),
        )

    def pass_on(self, z, way):
        return remote(
            self.kept(z, 1 if way == 0 else 3),
            self.full.at[z, way],
            self.full_sem.at[0, z, way],
            self.full_sem.at[1, z, way],
            self.here.beside(1 if way == 0 else -1),
        )

    def climb(self, z, way, up):
        return remote(
            self.kept(z, 0),
            self.column.at[way, z],
            self.line_sem.at[0, way, z],
            self.line_sem.at[1, way, z],
            self.here.above(2 * up - 1),
        )

    def begin(self, z):
        if self.paired:
            for copy in self.swaps(z, True):
                copy.start()
        for turn in (2, 1, 3, 0):
            if turn != 2 or self.paired:
                for copy in self.loads(z, turn):
                    copy.start()
        if not self.paired:
            for way in (0, 1):
                start(self.toss(z, way))

    def merge(self, z):
        if not self.paired:
            return
        for copy in self.swaps(z, False):
            copy.wait_recv()
        for turn in (2, 1, 3, 0):
            for copy in self.loads(z, turn):
                copy.wait()
            kept = self.kept(z, turn)
            add_up(kept, [kept, self.other.at[z, self.here.chip_at(turn)]], self.rows, self.columns)
            if turn == 2:
                for way in (0, 1):
                    start(self.toss(z, way))

    def second(self, z):
        for way, turn in ((0, 1), (1, 3)):
            if not self.paired:
                for copy in self.loads(z, turn):
                    copy.wait()
            copy = self.toss(z, way)
            if copy is not None:
                copy.wait_recv()
                begin, size = self.halves[way]
                rows = self.kept(z, turn).at[pl.ds(begin, size)]
                add_up(rows, [rows, self.half.at[z, way, pl.ds(0, size)]], size, self.columns)
            self.pass_on(z, way).start()

    def third(self, z, last):
        here = self.here
        if not self.paired:
            for copy in self.loads(z, 0):
                copy.wait()
        for way in (0, 1):
            self.pass_on(z, way).wait_recv()
        kept = self.kept(z, 0)
        terms = [kept, self.full.at[z, 0], self.full.at[z, 1]]
        if last:
            below, above = self.column.at[0, z], self.column.at[1, z]

            @pl.when(here.z == 0)
            def _():
                self.climb(z, 1, 0).wait_recv()
                add_up(self.target, terms + [above], self.rows, self.columns)

            @pl.when(here.z == DEPTH - 1)
            def _():
                self.climb(z, 0, 0).wait_recv()
                add_up(self.target, terms + [below], self.rows, self.columns)

            @pl.when((here.z > 0) & (here.z < DEPTH - 1))
            def _():
                for way in (0, 1):
                    self.climb(z, way, 0).wait_recv()
                add_up(self.target, terms + [below, above], self.rows, self.columns)

            return
        up = (z > here.z).astype(jnp.int32)
        way = 1 - up
        follows = up * here.z + way * (DEPTH - 1 - here.z)

        @pl.when(follows > 0)
        def _():
            self.climb(z, way, up).wait_recv()
            add_up(kept, terms + [self.column.at[way, z]], self.rows, self.columns)

        @pl.when(follows == 0)
        def _():
            add_up(kept, terms, self.rows, self.columns)

        self.climb(z, way, up).start()

    def end(self, z, last):
        if self.paired:
            for copy in self.swaps(z, True):
                copy.wait_send()
        for way in (0, 1):
            copy = self.toss(z, way)
            if copy is not None:
                copy.wait_send()
            self.pass_on(z, way).wait_send()
        if not last:
            up = (z > self.here.z).astype(jnp.int32)
            self.climb(z, 1 - up, up).wait_send()


def far_first(here, number):
    high = lax.div(here.z, 2)
    inner = lax.rem(lax.div(here.z + 1, 2), 2)
    low = (DEPTH - 1 - number) + inner * (0, -2, 1, 1)[number]
    return low + high * (DEPTH - 1 - 2 * low)


def run_sum(here, items, before=None, between=None):
    order = [far_first(here, number) for number in range(DEPTH)]
    for z in order:
        for item in items:
            item.begin(z)
    if before is not None:
        before()
    for item in items:
        item.merge(order[0])
    for number, z in enumerate(order):
        for item in items:
            item.second(z)
        if number + 1 < DEPTH:
            for item in items:
                item.merge(order[number + 1])
        if number == 0 and between is not None:
            between()
        if number:
            for item in items:
                item.third(order[number - 1], False)
    for item in items:
        item.third(order[-1], True)
    for number, z in enumerate(order):
        for item in items:
            item.end(z, number == DEPTH - 1)


class Share:
    def __init__(self, here, source, target, sems, held):
        self.here, self.source, self.target, self.sems, self.held = here, source, target, sems, held
        self.rows = target.shape[1]
        self.part = source.shape[1] // held

    def pieces(self, steps, arriving):
        here = self.here
        origin = lax.rem(here.z + DEPTH - steps, DEPTH) if arriving else here.z
        away = lax.rem(here.z + steps, DEPTH)
        copies = []
        for expert in range(self.held):
            target = self.target.at[expert, :, pl.ds(pl.multiple_of(origin * self.part, 128), self.part)]
            source = self.source.at[
                pl.ds(pl.multiple_of(away * self.rows, 16), self.rows), pl.ds(expert * self.part, self.part)
            ]
            if steps == 0:
                copies.append(pltpu.make_async_copy(source, target, self.sems.at[0, 0, expert]))
            else:
                copies.append(
                    remote(
                        target if arriving else source,
                        target,
                        self.sems.at[0, steps, expert],
                        self.sems.at[1, steps, expert],
                        here.above(steps),
                    )
                )
        return copies

    def begin(self):
        for steps in range(DEPTH):
            for copy in self.pieces(steps, False):
                copy.start()

    def end(self):
        for steps in range(DEPTH):
            for copy in self.pieces(steps, False):
                copy.wait() if steps == 0 else copy.wait_send()
            if steps:
                for copy in self.pieces(steps, True):
                    copy.wait_recv()


def row_sum_kernel(
    out, mid, gate, gin, gdown, out_sum, mid_sum, gate_sum, gate_half, up_half, down_sum, *scratch
):
    here = Here()
    here.meet()
    rows, slots = out.shape[2], gate.shape[2]
    items = [
        Sum(here, [mid], mid_sum, halves_of(rows), False, scratch[0:8]),
        Sum(here, [out], out_sum, halves_of(rows), False, scratch[8:16]),
        Sum(here, [gate], gate_sum, halves_of(slots, False), False, scratch[16:24]),
    ]
    other_in, other_down, own_in, own_down, sems, loads, share_sems = scratch[24:31]
    width = own_in.shape[2]
    tall = own_down.shape[0]
    swaps, kept = [], []
    for side in range(2):
        for core, into in ((1 - here.core, swaps), (here.core, kept)):
            source = gin.at[:, pl.ds(pl.multiple_of(side * 2 * width + core * width, 128), width)]
            into.append((source, side))
    copies = [
        remote(source, other_in.at[side], sems.at[0, side], sems.at[1, side], here.sibling())
        for source, side in swaps
    ]
    copies.append(
        remote(
            gdown.at[pl.ds(pl.multiple_of((1 - here.core) * tall, 16), tall)],
            other_down,
            sems.at[0, 2],
            sems.at[1, 2],
            here.sibling(),
        )
    )
    fetched = [pltpu.make_async_copy(source, own_in.at[side], loads.at[side]) for source, side in kept]
    fetched.append(
        pltpu.make_async_copy(
            gdown.at[pl.ds(pl.multiple_of(here.core * tall, 16), tall)], own_down, loads.at[2]
        )
    )
    held = 2
    share = Share(here, own_in.at[0], gate_half, share_sems, held)

    def before():
        for copy in copies + fetched:
            copy.start()

    def between():
        for side in range(2):
            copies[side].wait_recv()
            fetched[side].wait()
            target = own_in.at[0] if side == 0 else up_half
            add_up(target, [own_in.at[side], other_in.at[side]], own_in.shape[1], width)
            if side == 0:
                share.begin()
        copies[2].wait_recv()
        fetched[2].wait()
        add_up(down_sum, [own_down, other_down], tall, own_down.shape[1])

    run_sum(here, items, before, between)
    share.end()
    for copy in copies:
        copy.wait_send()


def row_sum(out, mid, gate, gin, gdown, held):
    rows, columns = out.shape[2:]
    slots = gate.shape[2]
    deep, wide = gin.shape
    width = wide // 4
    tall = gdown.shape[0] // 2
    vmem = pl.BlockSpec(memory_space=pltpu.VMEM)
    return pl.pallas_call(
        row_sum_kernel,
        out_shape=(
            jax.ShapeDtypeStruct((rows, columns), single),
            jax.ShapeDtypeStruct((rows, columns), single),
            jax.ShapeDtypeStruct(gate.shape[2:], single),
            jax.ShapeDtypeStruct((held, deep // DEPTH, wide // 2), narrow),
            jax.ShapeDtypeStruct((deep, width), narrow),
            jax.ShapeDtypeStruct((tall, columns), single),
        ),
        in_specs=[HBM] * 5,
        out_specs=(vmem, vmem, vmem, HBM, vmem, vmem),
        scratch_shapes=sum_scratch(rows, columns, narrow, halves_of(rows), False) * 2
        + sum_scratch(slots, gate.shape[3], single, halves_of(slots, False), False)
        + [
            pltpu.VMEM((2, deep, width), narrow),
            pltpu.VMEM((tall, columns), narrow),
            pltpu.VMEM((2, deep, width), narrow),
            pltpu.VMEM((tall, columns), narrow),
            pltpu.SemaphoreType.DMA((2, 3)),
            pltpu.SemaphoreType.DMA((3,)),
            pltpu.SemaphoreType.DMA((2, DEPTH, 2)),
        ],
        compiler_params=pltpu.CompilerParams(
            collective_id=3, has_side_effects=True, vmem_limit_bytes=62 * 2**20
        ),
        name="collect",
    )(out, mid, gate, gin, gdown)


def last_sum_kernel(gq, go, small, up_half, q_sum, small_sum, up_share, *scratch):
    here = Here()
    here.meet()
    rows = gq.shape[3]
    items = [
        Sum(here, [gq, go], q_sum, halves_of(rows), True, scratch[0:10]),
        Sum(here, [small], small_sum, halves_of(small.shape[3], False), True, scratch[10:20]),
    ]
    share = Share(here, up_half, up_share, scratch[20], 2)
    run_sum(here, items, share.begin)
    share.end()


def last_sum(gq, go, small, up_half, held):
    rows = gq.shape[3]
    columns = gq.shape[4] + go.shape[4]
    vmem = pl.BlockSpec(memory_space=pltpu.VMEM)
    deep, width = up_half.shape
    return pl.pallas_call(
        last_sum_kernel,
        out_shape=(
            jax.ShapeDtypeStruct((rows, columns), single),
            jax.ShapeDtypeStruct(small.shape[3:], single),
            jax.ShapeDtypeStruct((held, deep // DEPTH, DEPTH * width // held), narrow),
        ),
        in_specs=[HBM] * 4,
        out_specs=(vmem, vmem, HBM),
        scratch_shapes=sum_scratch(rows, columns, narrow, halves_of(rows), True)
        + sum_scratch(small.shape[3], small.shape[4], single, halves_of(small.shape[3], False), True)
        + [pltpu.SemaphoreType.DMA((2, DEPTH, 2))],
        compiler_params=pltpu.CompilerParams(
            collective_id=4, has_side_effects=True, vmem_limit_bytes=62 * 2**20
        ),
        name="deliver",
    )(gq, go, small, up_half)


def by_kernels():
    return lax.axis_size("dp") == DEPTH and lax.axis_size("expert") == 2 * RING


def bring_all(w_qkv, w_out, upstream, dense, gain_rows, expert_in, expert_out):
    width = upstream.shape[1]
    share = gain_rows.shape[1]
    if by_kernels():
        experts, rows = dense.shape[1], dense.shape[0]
        small = jnp.concatenate([dense.T, jnp.pad(gain_rows, ((0, 4), (0, rows - share)))], axis=0)
        wq, wo, up, all_small, weight_in, weight_down = first_gather(
            w_qkv, w_out, upstream, small, expert_in, expert_out
        )
        gains = all_small[:, :, :, experts : experts + 4, :share].transpose(3, 0, 1, 2, 4).reshape(4, -1)
        core = lax.rem(lax.axis_index("expert"), 2)
        every_gate = lax.dynamic_index_in_dim(all_small, core, axis=2, keepdims=False)[:, :, :experts]
        return (
            wq.reshape(-1, w_qkv.shape[1]),
            wo.reshape(-1, w_out.shape[1]),
            up.reshape(-1, width),
            every_gate,
            gains,
            weight_in,
            weight_down.reshape(-1, width),
        )
    everyone = ("dp", "expert")
    weight_in, weight_down = fetch_weights(expert_in, expert_out)
    return (
        lax.all_gather(w_qkv, everyone, axis=0, tiled=True),
        lax.all_gather(w_out, everyone, axis=0, tiled=True),
        gather_alike(upstream).reshape(-1, width),
        gather_alike(dense.T),
        lax.all_gather(gain_rows, everyone, axis=1, tiled=True),
        weight_in,
        weight_down,
    )


def spread_rows(block):
    every = row_gather(block) if by_kernels() else gather_alike(block)
    return every.reshape(-1, block.shape[1])


def collect_all(out, mid, gate, grad_in, grad_down, held):
    if by_kernels():
        return row_sum(out, mid, gate, grad_in, grad_down, held)
    return (
        scatter_alike(out).astype(single),
        scatter_alike(mid).astype(single),
        scatter_alike(gate),
        grad_in,
        grad_down,
    )


def deliver_all(pieces, grad_qkv, grad_out, half_way, held):
    owners = lax.axis_size("dp") * lax.axis_size("expert")
    share = pieces.shape[1] // owners
    if by_kernels():
        gate_half, up_half, down = half_way
        lead = (DEPTH, RING, 2)
        small = pieces.reshape(4, owners, share).transpose(1, 0, 2)
        small = jnp.pad(small, ((0, 0), (0, 4), (0, 128 - share))).reshape(lead + (8, 128))
        shares, gains, up_share = last_sum(
            grad_qkv.reshape(lead + (-1,) + grad_qkv.shape[1:]),
            grad_out.reshape(lead + (-1,) + grad_out.shape[1:]),
            small,
            up_half,
            held,
        )
        wide = grad_qkv.shape[1]
        return (
            gains[:4, :share],
            shares[:, :wide],
            shares[:, wide:],
            jnp.concatenate([gate_half, up_share], axis=2).astype(single),
            down.reshape(held, -1, down.shape[1]),
        )
    everyone = ("dp", "expert")
    share_in, share_down = return_weights(*half_way, held)
    return (
        lax.psum_scatter(pieces, everyone, scatter_dimension=1, tiled=True),
        lax.psum_scatter(grad_qkv, everyone, scatter_dimension=0, tiled=True).astype(single),
        lax.psum_scatter(grad_out, everyone, scatter_dimension=0, tiled=True).astype(single),
        share_in.astype(single),
        share_down.astype(single),
    )


def local(
    tokens,
    lengths,
    expert_ids,
    gates,
    attn_gain,
    w_qkv,
    q_gain,
    k_gain,
    w_out,
    ffn_gain,
    expert_in,
    expert_out,
    out_grad,
):
    micro_count, seq_len, model_width = tokens.shape
    rows = micro_count * seq_len
    depth = lax.axis_size("dp")
    owners = lax.axis_size("expert")
    held = expert_in.shape[0]
    experts = owners * held
    chip_experts = 2 * held
    inputs = tokens.reshape(rows, model_width).astype(single)
    upstream = out_grad.reshape(rows, model_width)
    ids = expert_ids.reshape(rows, -1)
    gate_rows = gates.reshape(rows, -1)
    onehot = (ids[:, :, None] == jnp.arange(experts, dtype=jnp.int32)).astype(single)
    dense = jnp.sum(onehot * gate_rows[:, :, None], axis=1)
    gain_rows = jnp.stack([attn_gain, q_gain, k_gain, ffn_gain]).astype(single)
    weight_qkv, weight_out, up_rows, every_gate, gains, weight_in, weight_down = bring_all(
        w_qkv, w_out, upstream, dense, gain_rows, expert_in, expert_out
    )
    gain_attn, gain_query, gain_key, gain_ffn = gains[0], gains[1], gains[2], gains[3]

    normal_in, factor_in = normalize(inputs)
    normed_in = (normal_in * gain_attn).astype(narrow)
    projected = jnp.dot(normed_in, weight_qkv, preferred_element_type=single)
    normal_q, factor_q = normalize(projected[:, :model_width])
    normal_k, factor_k = normalize(projected[:, model_width : 2 * model_width])
    document, position = layout(lengths[:, 0], seq_len)
    cosine, sine = angles(position)
    query_rows = rotate(normal_q * gain_query, cosine, sine).astype(narrow).reshape(rows, -1, HEAD)
    key_rows = rotate(normal_k * gain_key, cosine, sine).astype(narrow).reshape(rows, -1, HEAD)
    value_rows = projected[:, 2 * model_width :].astype(narrow).reshape(rows, -1, HEAD)
    places = jnp.arange(rows, dtype=jnp.int32)
    allowed = (document[:, None] == document[None, :]) & (places[:, None] >= places[None, :])
    raw = jnp.einsum("qhd,khd->hqk", query_rows, key_rows, preferred_element_type=single)
    scores = jnp.where(allowed[None], raw * HEAD ** (-0.5), masked_score)
    highest = jnp.max(scores, axis=-1, keepdims=True)
    unnormed = jnp.exp(scores - highest)
    probs = unnormed / jnp.sum(unnormed, axis=-1, keepdims=True)
    attn_probs = probs.astype(narrow)
    attended = (
        jnp.einsum("hqk,khd->qhd", attn_probs, value_rows, preferred_element_type=single)
        .reshape(rows, model_width)
        .astype(narrow)
    )
    middle = inputs + jnp.dot(attended, weight_out, preferred_element_type=single)
    normal_mid, factor_mid = normalize(middle)
    routed_in = (normal_mid * gain_ffn).astype(narrow)

    chip = lax.axis_index("expert") // 2
    mid_rows = spread_rows(routed_in)
    mine = lax.dynamic_slice_in_dim(every_gate, chip * chip_experts, chip_experts, axis=2)
    gate = mine.transpose(0, 1, 3, 2).reshape(-1, chip_experts)
    piece_out, piece_mid, piece_gates, grad_in_part, grad_down_part = expert_rounds(
        mid_rows, up_rows, gate, weight_in, weight_down
    )

    chips = owners // 2
    by_gate = piece_gates.reshape(depth, chips, rows, chip_experts).transpose(0, 1, 3, 2)
    spread = jnp.zeros((depth, chips, experts, rows), single)
    spread = lax.dynamic_update_slice_in_dim(spread, by_gate, chip * chip_experts, axis=2)
    mixture, grad_routed, gate_table, *half_way = collect_all(
        piece_out.reshape(depth, chips, rows, model_width),
        piece_mid.reshape(depth, chips, rows, model_width),
        spread,
        grad_in_part,
        grad_down_part,
        held,
    )
    gate_table = gate_table.T
    grad_gates = jnp.sum(onehot * gate_table[:, None, :], axis=2)
    results = (middle + mixture).astype(narrow)

    grad_mid, piece_ffn = rms_back(grad_routed, normal_mid, factor_mid, gain_ffn)
    grad_middle = upstream.astype(single) + grad_mid
    grad_branch = grad_middle.astype(narrow)
    grad_out_part = contract_rows(attended, grad_branch, narrow)
    grad_attended = contract_last(grad_branch, weight_out).astype(narrow).reshape(rows, -1, HEAD)
    grad_probs = jnp.einsum("qhd,khd->hqk", grad_attended, value_rows, preferred_element_type=single)
    inner = jnp.sum(grad_probs * probs, axis=-1, keepdims=True)
    grad_scores = (probs * (grad_probs - inner)).astype(narrow)
    grad_query = jnp.einsum(
        "hqk,khd->qhd", grad_scores, key_rows, preferred_element_type=single
    ) * HEAD ** (-0.5)
    grad_key = jnp.einsum(
        "hqk,qhd->khd", grad_scores, query_rows, preferred_element_type=single
    ) * HEAD ** (-0.5)
    grad_value = jnp.einsum("hqk,qhd->khd", attn_probs, grad_attended, preferred_element_type=single)
    grad_q_raw, piece_query = rms_back(
        rotate(grad_query.reshape(rows, model_width), cosine, -sine), normal_q, factor_q, gain_query
    )
    grad_k_raw, piece_key = rms_back(
        rotate(grad_key.reshape(rows, model_width), cosine, -sine), normal_k, factor_k, gain_key
    )
    grad_qkv = jnp.concatenate(
        [grad_q_raw, grad_k_raw, grad_value.reshape(rows, model_width)], axis=1
    ).astype(narrow)
    grad_qkv_part = contract_rows(normed_in, grad_qkv, narrow)
    grad_normed = contract_last(grad_qkv, weight_qkv)
    grad_input, piece_attn = rms_back(grad_normed, normal_in, factor_in, gain_attn)
    grad_tokens = grad_middle + grad_input

    pieces = jnp.stack([piece_attn, piece_query, piece_key, piece_ffn])
    gain_sums, grad_qkv_share, grad_out_share, share_in, share_down = deliver_all(
        pieces, grad_qkv_part, grad_out_part, half_way, held
    )
    shape = (micro_count, seq_len, model_width)
    return (
        results.reshape(shape),
        grad_tokens.reshape(shape),
        grad_gates.reshape(expert_ids.shape),
        gain_sums[0],
        grad_qkv_share,
        gain_sums[1],
        gain_sums[2],
        grad_out_share,
        gain_sums[3],
        share_in,
        share_down,
    )


def solution(mesh):
    by_rows = P(None, ("dp", "expert"), None)
    flat = P(("dp", "expert"))
    split = P(("dp", "expert"), None)
    held = P("expert", "dp", None)
    return jax.shard_map(
        local,
        mesh=mesh,
        in_specs=(
            by_rows, by_rows, by_rows, by_rows, flat, split, flat, flat, split, flat, held, held, by_rows,
        ),
        out_specs=(by_rows, by_rows, by_rows, flat, split, flat, flat, split, flat, held, held),
        check_vma=False,
    )
```

```python
import jax
import jax.numpy as jnp
from jax import lax
from jax.experimental import pallas as pl
from jax.experimental.pallas import tpu as pltpu
from jax.sharding import PartitionSpec as P

HEAD = 128
epsilon = 1e-05
base_theta = 10000.0
masked_score = -1e30
single = jnp.float32
narrow = jnp.bfloat16


def normalize(values):
    factor = lax.rsqrt(jnp.mean(values * values, axis=-1, keepdims=True) + epsilon)
    return (values * factor, factor)


def rms_back(upstream, normal, factor, gain):
    weighted = upstream * gain
    inner = jnp.mean(weighted * normal, axis=-1, keepdims=True)
    return (factor * (weighted - normal * inner), jnp.sum(upstream * normal, axis=0))


def angles(position):
    half = HEAD // 2
    ladder = jnp.arange(half, dtype=single) * (2.0 / HEAD)
    frequency = jnp.exp(-jnp.log(base_theta) * ladder)
    angle = position.astype(single)[:, None] * frequency[None, :]
    return (jnp.cos(angle)[:, None, :], jnp.sin(angle)[:, None, :])


def rotate(field, cosine, sine):
    length = field.shape[0]
    heads = field.reshape(length, -1, HEAD)
    half = HEAD // 2
    first = heads[..., :half]
    second = heads[..., half:]
    turned = jnp.concatenate(
        [first * cosine - second * sine, second * cosine + first * sine], axis=-1
    )
    return turned.reshape(length, -1)


def layout(doc_lengths, length):
    packs, count = doc_lengths.shape
    upto = jnp.arange(count)[None, :] <= jnp.arange(count)[:, None]
    ends = jnp.sum(jnp.where(upto[None], doc_lengths[:, None, :], 0), axis=2)
    starts = ends - doc_lengths
    places = jnp.arange(length, dtype=jnp.int32)[None, :, None]
    document = jnp.sum((places >= ends[:, None, :]).astype(jnp.int32), axis=2)
    member = (places >= starts[:, None, :]) & (places < ends[:, None, :])
    first_place = jnp.sum(jnp.where(member, starts[:, None, :], 0), axis=2)
    document = document + (count + 1) * jnp.arange(packs, dtype=jnp.int32)[:, None]
    return (document.reshape(-1), (places[..., 0] - first_place).reshape(-1))


def contract_rows(left, right, kind=single):
    return lax.dot_general(left, right, (((0,), (0,)), ((), ())), preferred_element_type=kind)


def contract_last(left, right, kind=single):
    return lax.dot_general(left, right, (((1,), (1,)), ((), ())), preferred_element_type=kind)


def core_groups():
    return [[2 * chip + core for chip in range(lax.axis_size("expert") // 2)] for core in range(2)]


def chip_groups():
    return [[2 * chip, 2 * chip + 1] for chip in range(lax.axis_size("expert") // 2)]


def gather_alike(block):
    column = lax.all_gather(block, "dp", axis=0)
    return lax.all_gather(column, "expert", axis=1, axis_index_groups=core_groups())


def scatter_alike(blocks):
    column = lax.psum_scatter(
        blocks, "expert", scatter_dimension=1, axis_index_groups=core_groups()
    )
    return lax.psum_scatter(column, "dp", scatter_dimension=0)


def fetch_weights(expert_in, expert_out):
    depth = lax.axis_size("dp")
    held, rows, columns = expert_in.shape
    part = columns // (2 * depth)
    cut = expert_in.reshape(held, rows, 2, depth, part)
    turned = lax.all_to_all(cut, "dp", split_axis=3, concat_axis=1, tiled=True)
    both = lax.all_gather(turned[:, :, :, 0], "expert", axis=0, axis_index_groups=chip_groups())
    weight_in = both.transpose(2, 3, 0, 1, 4).reshape(depth * rows, 4 * held * part)
    weight_down = lax.all_gather(
        expert_out, "expert", axis=0, axis_index_groups=chip_groups()
    ).reshape(-1, expert_out.shape[2])
    return (weight_in, weight_down)


def return_weights(grad_in, grad_down, held):
    depth = lax.axis_size("dp")
    rows, columns = grad_in.shape
    part = columns // (4 * held)
    cut = grad_in.reshape(rows, 2, 2, held, part)
    own = lax.psum_scatter(cut, "expert", scatter_dimension=2, axis_index_groups=chip_groups())
    own = own.reshape(depth, rows // depth, 2, held, part)
    turned = lax.all_to_all(own, "dp", split_axis=0, concat_axis=0)
    share_in = turned.transpose(3, 1, 2, 0, 4).reshape(held, rows // depth, 2 * depth * part)
    down = grad_down.reshape(2, held, part, grad_down.shape[1])
    share_down = lax.psum_scatter(
        down, "expert", scatter_dimension=0, axis_index_groups=chip_groups()
    )
    return (share_in, share_down)


def expert_round(mid_rows, up_rows, gate, weight_in, weight_down):
    count = gate.shape[1]
    part = weight_down.shape[0] // count
    wide = jnp.broadcast_to(gate[:, :, None], gate.shape + (part,)).reshape(gate.shape[0], -1)
    gate_up = jnp.dot(mid_rows, weight_in, preferred_element_type=single)
    hidden_units = gate_up.shape[1] // 2
    gate_part = gate_up[:, :hidden_units]
    up_part = gate_up[:, hidden_units:]
    sigmoid = jax.nn.sigmoid(gate_part)
    activated = gate_part * sigmoid
    hidden = activated * up_part
    back = contract_last(up_rows, weight_down)
    scaled = (wide * hidden).astype(narrow)
    piece_out = jnp.dot(scaled, weight_down, preferred_element_type=narrow)
    piece_gates = jnp.sum((hidden * back).reshape(-1, count, part), axis=2)
    grad_hidden = wide * back
    grad_gate = grad_hidden * up_part * sigmoid * (1.0 + gate_part * (1.0 - sigmoid))
    grad_up = grad_hidden * activated
    grad_gate_up = jnp.concatenate([grad_gate, grad_up], axis=1).astype(narrow)
    piece_mid = contract_last(grad_gate_up, weight_in, narrow)
    return (piece_out, piece_mid, piece_gates, grad_gate_up, scaled)


def expert_rounds(mid_rows, up_rows, gate, weight_in, weight_down):
    total = mid_rows.shape[0]
    rounds = max(1, total // 2048)

    def one(sums, pieces):
        mid, up, weights = pieces
        piece_out, piece_mid, piece_gates, grad_gate_up, scaled = expert_round(
            mid, up, weights, weight_in, weight_down
        )
        grads = (contract_rows(mid, grad_gate_up), contract_rows(scaled, up))
        return (jax.tree.map(jnp.add, sums, grads), (piece_out, piece_mid, piece_gates))

    if rounds == 1:
        piece_out, piece_mid, piece_gates, grad_gate_up, scaled = expert_round(
            mid_rows, up_rows, gate, weight_in, weight_down
        )
        grads = (contract_rows(mid_rows, grad_gate_up, narrow), contract_rows(scaled, up_rows, narrow))
        return (piece_out, piece_mid, piece_gates) + grads
    start = (jnp.zeros(weight_in.shape, single), jnp.zeros(weight_down.shape, single))
    cut = jax.tree.map(lambda a: a.reshape(rounds, total // rounds, -1), (mid_rows, up_rows, gate))
    sums, made = lax.scan(one, start, cut)
    made = jax.tree.map(lambda a: a.reshape(total, -1), made)
    return made + (sums[0].astype(narrow), sums[1].astype(narrow))


MESH = pl.DeviceIdType.MESH
HBM = pl.BlockSpec(memory_space=pl.ANY)
DEPTH = 4
RING = 4


def ring_turn(number):
    high = lax.div(number, 2)
    return number + high * (1 - 2 * lax.rem(number, 2))


class Here:
    def __init__(self):
        number = lax.axis_index("expert")
        self.z = lax.axis_index("dp")
        self.core = lax.rem(number, 2)
        self.chip = lax.div(number, 2)
        self.q = ring_turn(self.chip)

    def chip_at(self, turn):
        return ring_turn(lax.rem(self.q + turn + RING, RING))

    def beside(self, turn):
        return (self.z, 2 * self.chip_at(turn) + self.core)

    def above(self, steps):
        return (lax.rem(self.z + steps + DEPTH, DEPTH), 2 * self.chip + self.core)

    def sibling(self):
        return (self.z, 2 * self.chip + 1 - self.core)

    def meet(self):
        barrier = pltpu.get_barrier_semaphore()
        others = [self.beside(1), self.beside(-1), self.sibling()]
        others += [self.above(steps) for steps in range(1, DEPTH)]
        for other in others:
            pl.semaphore_signal(barrier, inc=1, device_id=other, device_id_type=MESH)
        pl.semaphore_wait(barrier, len(others))


def remote(source, target, sent, arrived, device):
    return pltpu.make_async_remote_copy(
        src_ref=source,
        dst_ref=target,
        send_sem=sent,
        recv_sem=arrived,
        device_id=device,
        device_id_type=MESH,
    )


GATHER_SEMS = [
    pltpu.SemaphoreType.DMA((2, 2, DEPTH - 1)),
    pltpu.SemaphoreType.DMA((2, DEPTH, 2, 2)),
    pltpu.SemaphoreType.DMA((2, DEPTH)),
    pltpu.SemaphoreType.DMA((1,)),
]


class Gather:
    def __init__(self, here, source, whole, halves, shared, sems):
        self.here, self.source, self.whole, self.halves, self.shared = here, source, whole, halves, shared
        self.line, self.ring, self.pair, self.own = sems

    def block(self, z, turn):
        chip = self.here.chip_at(turn)
        return self.whole.at[z, chip, self.here.core] if self.shared else self.whole.at[z, chip]

    def keep(self):
        return pltpu.make_async_copy(self.source, self.block(self.here.z, 0), self.own.at[0])

    def along(self, step, way, first):
        z = self.here.z - step + 1 if way == 0 else self.here.z + step - 1
        block = self.block(z, 0)
        return remote(
            self.source if first else block,
            block,
            self.line.at[0, way, step - 1],
            self.line.at[1, way, step - 1],
            self.here.above(1 if way == 0 else -1),
        )

    def round(self, z, way, first=False):
        turn = 1 if way == 0 else -1
        block = self.block(z, 0)
        return remote(
            self.source if first else block,
            block,
            self.ring.at[0, z, way, 0],
            self.ring.at[1, z, way, 0],
            self.here.beside(turn),
        )

    def heard(self, z, way):
        block = self.block(z, -1 if way == 0 else 1)
        return remote(
            block, block, self.ring.at[0, z, way, 0], self.ring.at[1, z, way, 0], self.here.beside(1)
        )

    def onward(self, z, way, mine):
        if self.halves[way] is None:
            return None
        turn = (-1 if mine else -2) if way == 0 else (1 if mine else 2)
        block = self.block(z, turn).at[pl.ds(*self.halves[way])]
        return remote(
            block,
            block,
            self.ring.at[0, z, way, 1],
            self.ring.at[1, z, way, 1],
            self.here.beside(1 if way == 0 else -1),
        )

    def swap(self, z, mine):
        core = self.here.core if mine else 1 - self.here.core
        part = self.whole.at[z, :, core]
        return remote(part, part, self.pair.at[0, z], self.pair.at[1, z], self.here.sibling())


def start(copy):
    if copy is not None:
        copy.start()


def gather_third(item, z):
    for way in (0, 1):
        copy = item.onward(z, way, False)
        if copy is not None:
            copy.wait_recv()


class Rounds:
    def __init__(self, here, items):
        self.here, self.items = here, items
        for item in items:
            item.keep().start()
            for way in (0, 1):
                self.depart(0, way, item)
            for way in (0, 1):
                item.round(here.z, way, True).start()

    def depart(self, step, way, item):
        here = self.here
        ahead = here.z + 1 < DEPTH if way == 0 else here.z >= 1
        pl.when(ahead)(lambda: item.along(step + 1, way, step == 0).start())

    def places(self, step, body):
        here = self.here
        if step == 0:
            body(here.z, 0)
            return
        pl.when(here.z >= step)(lambda: body(here.z - step, 0))
        pl.when(here.z + step < DEPTH)(lambda: body(here.z + step, 1))

    def service(self, step):
        items, here = self.items, self.here

        def first(z, way):
            for item in items:
                block = item.block(z, 0)
                remote(
                    block, block, item.line.at[0, way, step], item.line.at[1, way, step], here.above(1)
                ).wait_recv()
                if step + 2 < DEPTH:
                    self.depart(step + 1, way, item)
                for side in (0, 1):
                    item.round(z, side).start()

        def second(z, way):
            for item in items:
                for side in (0, 1):
                    item.heard(z, side).wait_recv()
                    start(item.onward(z, side, True))

        if step + 1 < DEPTH:
            self.places(step + 1, first)
        if step == 0:
            for item in items:
                item.keep().wait()
        self.places(step, second)

    def third(self, step):
        def body(z, way):
            for item in self.items:
                gather_third(item, z)
                if item.shared:
                    item.swap(z, True).start()

        self.places(step, body)

    def finish(self):
        def settle(z, way):
            for item in self.items:
                for side in (0, 1):
                    item.round(z, side).wait_send()
                    copy = item.onward(z, side, True)
                    if copy is not None:
                        copy.wait_send()
                if item.shared:
                    item.swap(z, True).wait_send()
                    item.swap(z, False).wait_recv()

        for step in range(DEPTH):
            self.places(step, settle)
        here = self.here
        for item in self.items:
            for step in range(DEPTH - 1):
                for way in (0, 1):

                    def sent(z, side, step=step, way=way, item=item):
                        if step and side != way:
                            return
                        ahead = here.z + 1 < DEPTH if way == 0 else here.z >= 1
                        pl.when(ahead)(lambda: item.along(step + 1, way, step == 0).wait_send())

                    self.places(step, sent)


class Recut:
    def __init__(self, here, source_in, source_out, whole_in, whole_out, sems):
        self.here, self.source_in, self.source_out = here, source_in, source_out
        self.whole_in, self.whole_out = whole_in, whole_out
        self.cut, self.pair, self.down, self.own = sems
        self.held, self.rows, columns = source_in.shape
        self.hidden = columns // 2
        self.part = self.hidden // DEPTH

    def pieces(self, steps, arriving):
        here, copies = self.here, []
        mine = lax.rem(here.z + DEPTH - steps, DEPTH) if arriving else here.z
        away = lax.rem(here.z + steps, DEPTH)
        for side in range(2):
            for expert in range(self.held):
                columns = side * self.held * 2 * self.part + (here.core * self.held + expert) * self.part
                target = self.whole_in.at[
                    pl.ds(pl.multiple_of(mine * self.rows, 16), self.rows),
                    pl.ds(pl.multiple_of(columns, 128), self.part),
                ]
                source = self.source_in.at[
                    expert, :, pl.ds(pl.multiple_of(side * self.hidden + away * self.part, 128), self.part)
                ]
                spot = (steps, side * self.held + expert)
                if steps == 0:
                    copies.append(pltpu.make_async_copy(source, target, self.own.at[spot[1]]))
                else:
                    copies.append(
                        remote(
                            target if arriving else source,
                            target,
                            self.cut.at[(0,) + spot],
                            self.cut.at[(1,) + spot],
                            here.above(steps),
                        )
                    )
        return copies

    def across(self, steps, mine):
        here, copies = self.here, []
        core = here.core if mine else 1 - here.core
        row = lax.rem(here.z + DEPTH - steps, DEPTH)
        width = self.held * self.part
        for side in range(2):
            spot = self.whole_in.at[
                pl.ds(pl.multiple_of(row * self.rows, 16), self.rows),
                pl.ds(pl.multiple_of(side * 2 * width + core * width, 128), width),
            ]
            copies.append(
                remote(spot, spot, self.pair.at[0, steps, side], self.pair.at[1, steps, side], here.sibling())
            )
        return copies

    def lower(self, mine):
        here = self.here
        core = here.core if mine else 1 - here.core
        spot = self.whole_out.at[pl.ds(core * self.held, self.held)]
        return remote(
            self.source_out if mine else spot, spot, self.down.at[0], self.down.at[1], here.sibling()
        )

    def lower_own(self):
        return pltpu.make_async_copy(
            self.source_out, self.whole_out.at[pl.ds(self.here.core * self.held, self.held)], self.own.at[4]
        )

    def begin(self):
        for copy in self.pieces(0, False):
            copy.start()
        self.lower_own().start()
        self.lower(True).start()
        for steps in range(1, DEPTH):
            for copy in self.pieces(steps, False):
                copy.start()

    def relay(self):
        for steps in range(DEPTH):
            for copy in self.pieces(steps, True):
                copy.wait() if steps == 0 else copy.wait_recv()
            for copy in self.across(steps, True):
                copy.start()

    def end(self):
        self.lower_own().wait()
        self.lower(True).wait_send()
        self.lower(False).wait_recv()
        for steps in range(DEPTH):
            if steps:
                for copy in self.pieces(steps, False):
                    copy.wait_send()
            for copy in self.across(steps, True):
                copy.wait_send()
            for copy in self.across(steps, False):
                copy.wait_recv()


RECUT_SEMS = [
    pltpu.SemaphoreType.DMA((2, DEPTH, 4)),
    pltpu.SemaphoreType.DMA((2, DEPTH, 2)),
    pltpu.SemaphoreType.DMA((2,)),
    pltpu.SemaphoreType.DMA((5,)),
]


def halves_of(rows, split=True):
    return ((0, rows // 2), (rows // 2, rows - rows // 2)) if split else ((0, rows), None)


def first_gather_kernel(wq, wo, up, small, ein, eout, wq_all, wo_all, up_all, small_all, win, wout, *sems):
    here = Here()
    here.meet()
    items = []
    for number, (source, whole, halves, shared) in enumerate(
        (
            (small, small_all, halves_of(small.shape[0], False), True),
            (wq, wq_all, halves_of(wq.shape[0]), True),
            (wo, wo_all, halves_of(wo.shape[0]), True),
            (up, up_all, halves_of(up.shape[0]), False),
        )
    ):
        items.append(Gather(here, source, whole, halves, shared, sems[4 * number : 4 * number + 4]))
    recut = Recut(here, ein, eout, win, wout, sems[16:20])
    rounds = Rounds(here, items)
    for step in range(DEPTH):
        rounds.service(step)
        if step == 0:
            recut.begin()
        else:
            rounds.third(step - 1)
    rounds.third(DEPTH - 1)
    recut.relay()
    rounds.finish()
    recut.end()


def first_gather(wq, wo, up, small, ein, eout):
    def whole(array, shared):
        lead = (DEPTH, RING, 2) if shared else (DEPTH, RING)
        return jax.ShapeDtypeStruct(lead + array.shape, array.dtype)

    held, rows, columns = ein.shape
    return pl.pallas_call(
        first_gather_kernel,
        out_shape=(
            whole(wq, True),
            whole(wo, True),
            whole(up, False),
            whole(small, True),
            jax.ShapeDtypeStruct((DEPTH * rows, columns), ein.dtype),
            jax.ShapeDtypeStruct((2 * held,) + eout.shape[1:], eout.dtype),
        ),
        in_specs=[HBM] * 6,
        out_specs=(HBM,) * 6,
        scratch_shapes=GATHER_SEMS * 4 + RECUT_SEMS,
        compiler_params=pltpu.CompilerParams(collective_id=1, has_side_effects=True),
        name="bring",
    )(wq, wo, up, small, ein, eout)

def add_up(target, terms, rows, columns):
    high = 16 if rows % 16 == 0 else 8
    wide = min(columns, 1024)
    across = columns // wide

    def piece(number, carry):
        row = pl.multiple_of(lax.div(number, across) * high, high)
        column = pl.multiple_of(lax.rem(number, across) * wide, 128)
        spot = (pl.ds(row, high), pl.ds(column, wide))
        total = terms[0][spot].astype(single)
        for term in terms[1:]:
            total = total + term[spot].astype(single)
        target[spot] = total.astype(target.dtype)
        return carry

    lax.fori_loop(0, (rows // high) * across, piece, 0)


SUM_SEMS = [
    pltpu.SemaphoreType.DMA((2, DEPTH, 2)),
    pltpu.SemaphoreType.DMA((2, DEPTH, 2)),
    pltpu.SemaphoreType.DMA((2, 2, DEPTH)),
    pltpu.SemaphoreType.DMA((DEPTH, RING, 2)),
]


def sum_scratch(rows, columns, kind, halves, paired=False, made=False):
    high = max(size for _, size in filter(None, halves))
    kept = RING if paired or made else RING - 1
    scratch = [
        pltpu.VMEM((DEPTH, kept, rows, columns), kind),
        pltpu.VMEM((DEPTH, 2, high, columns), kind),
        pltpu.VMEM((DEPTH, 2, rows, columns), kind),
        pltpu.VMEM((DEPTH + 1, rows, columns), kind),
    ] + SUM_SEMS
    if paired:
        scratch += [pltpu.VMEM((DEPTH, RING, rows, columns), kind), pltpu.SemaphoreType.DMA((2, DEPTH, 2))]
    return scratch


class Sum:
    def __init__(self, here, sources, target, halves, paired, scratch):
        self.here, self.sources, self.target, self.halves, self.paired = here, sources, target, halves, paired
        self.mine, self.half, self.full, self.column = scratch[:4]
        self.half_sem, self.full_sem, self.line_sem, self.load_sem = scratch[4:8]
        if paired:
            self.other, self.pair_sem = scratch[8:10]
        self.rows, self.columns = self.mine.shape[2:]

    def kept(self, z, turn):
        if self.sources is None:
            return self.mine.at[z, self.here.chip_at(turn)]
        return self.mine.at[z, turn if self.paired else {0: 0, 1: 1, 3: 2}[turn]]

    def raw(self, part, z, turn):
        chip = self.here.chip_at(turn)
        return part.at[z, chip, self.here.core] if self.paired else part.at[z, chip]

    def spots(self):
        at, spots = 0, []
        for part in self.sources or []:
            spots.append((part, pl.ds(at, part.shape[-1])))
            at += part.shape[-1]
        return spots

    def loads(self, z, turn):
        return [
            pltpu.make_async_copy(
                self.raw(part, z, turn), self.kept(z, turn).at[:, spot], self.load_sem.at[z, turn, number]
            )
            for number, (part, spot) in enumerate(self.spots())
        ]

    def swaps(self, z, mine):
        return [
            remote(
                part.at[z, :, 1 - self.here.core] if mine else self.other.at[z, :, :, spot],
                self.other.at[z, :, :, spot],
                self.pair_sem.at[0, z, number],
                self.pair_sem.at[1, z, number],
                self.here.sibling(),
            )
            for number, (part, spot) in enumerate(self.spots())
        ]

    def toss(self, z, way):
        if self.halves[way] is None:
            return None
        rows = pl.ds(*self.halves[way])
        loaded = self.sources is not None and not self.paired
        source = (self.raw(self.sources[0], z, 2) if loaded else self.kept(z, 2)).at[rows]
        return remote(
            source,
            self.half.at[z, way, pl.ds(0, self.halves[way][1])],
            self.half_sem.at[0, z, way],
            self.half_sem.at[1, z, way],
            self.here.beside(1 if way == 0 else -1),
        )

    def pass_on(self, z, way):
        return remote(
            self.kept(z, 1 if way == 0 else 3),
            self.full.at[z, way],
            self.full_sem.at[0, z, way],
            self.full_sem.at[1, z, way],
            self.here.beside(1 if way == 0 else -1),
        )

    def climb(self, z, way, up, slot=None):
        if slot is None:
            down_to_owner = way * (z == self.here.z - 1).astype(jnp.int32)
            slot = z + down_to_owner * (DEPTH - z)
        return remote(
            self.kept(z, 0),
            self.column.at[slot],
            self.line_sem.at[0, way, z],
            self.line_sem.at[1, way, z],
            self.here.above(2 * up - 1),
        )

    def begin(self, z):
        if self.paired:
            for copy in self.swaps(z, True):
                copy.start()
        for turn in (2, 1, 3, 0):
            if turn != 2 or self.paired:
                for copy in self.loads(z, turn):
                    copy.start()
        if not self.paired:
            for way in (0, 1):
                start(self.toss(z, way))

    def merge(self, z):
        if not self.paired:
            return
        for copy in self.swaps(z, False):
            copy.wait_recv()
        for turn in (2, 1, 3, 0):
            for copy in self.loads(z, turn):
                copy.wait()
            kept = self.kept(z, turn)
            add_up(kept, [kept, self.other.at[z, self.here.chip_at(turn)]], self.rows, self.columns)
            if turn == 2:
                for way in (0, 1):
                    start(self.toss(z, way))

    def second(self, z):
        for way, turn in ((0, 1), (1, 3)):
            if not self.paired:
                for copy in self.loads(z, turn):
                    copy.wait()
            copy = self.toss(z, way)
            if copy is not None:
                copy.wait_recv()
                begin, size = self.halves[way]
                rows = self.kept(z, turn).at[pl.ds(begin, size)]
                add_up(rows, [rows, self.half.at[z, way, pl.ds(0, size)]], size, self.columns)
            self.pass_on(z, way).start()

    def third(self, z, last):
        here = self.here
        if not self.paired:
            for copy in self.loads(z, 0):
                copy.wait()
        for way in (0, 1):
            self.pass_on(z, way).wait_recv()
        kept = self.kept(z, 0)
        terms = [kept, self.full.at[z, 0], self.full.at[z, 1]]
        if last:
            below, above = self.column.at[z], self.column.at[DEPTH]

            @pl.when(here.z == 0)
            def _():
                self.climb(z, 1, 0, DEPTH).wait_recv()
                add_up(self.target, terms + [above], self.rows, self.columns)

            @pl.when(here.z == DEPTH - 1)
            def _():
                self.climb(z, 0, 0, z).wait_recv()
                add_up(self.target, terms + [below], self.rows, self.columns)

            @pl.when((here.z > 0) & (here.z < DEPTH - 1))
            def _():
                self.climb(z, 0, 0, z).wait_recv()
                self.climb(z, 1, 0, DEPTH).wait_recv()
                add_up(self.target, terms + [below, above], self.rows, self.columns)

            return
        up = (z > here.z).astype(jnp.int32)
        way = 1 - up
        follows = up * here.z + way * (DEPTH - 1 - here.z)

        @pl.when(follows > 0)
        def _():
            self.climb(z, way, up, z).wait_recv()
            add_up(kept, terms + [self.column.at[z]], self.rows, self.columns)

        @pl.when(follows == 0)
        def _():
            add_up(kept, terms, self.rows, self.columns)

        self.climb(z, way, up).start()

    def end(self, z, last):
        if self.paired:
            for copy in self.swaps(z, True):
                copy.wait_send()
        for way in (0, 1):
            copy = self.toss(z, way)
            if copy is not None:
                copy.wait_send()
            self.pass_on(z, way).wait_send()
        if not last:
            up = (z > self.here.z).astype(jnp.int32)
            self.climb(z, 1 - up, up).wait_send()


def far_first(here, number):
    high = lax.div(here.z, 2)
    inner = lax.rem(lax.div(here.z + 1, 2), 2)
    low = (DEPTH - 1 - number) + inner * (0, -2, 1, 1)[number]
    return low + high * (DEPTH - 1 - 2 * low)


def run_sum(here, items, before=None, between=None):
    order = [far_first(here, number) for number in range(DEPTH)]
    for z in order:
        for item in items:
            item.begin(z)
    if before is not None:
        before()
    for item in items:
        item.merge(order[0])
    for number, z in enumerate(order):
        for item in items:
            item.second(z)
        if number + 1 < DEPTH:
            for item in items:
                item.merge(order[number + 1])
        if number == 0 and between is not None:
            between()
        if number:
            for item in items:
                item.third(order[number - 1], False)
    for item in items:
        item.third(order[-1], True)
    for number, z in enumerate(order):
        for item in items:
            item.end(z, number == DEPTH - 1)


class Share:
    def __init__(self, here, source, target, sems, held):
        self.here, self.source, self.target, self.sems, self.held = here, source, target, sems, held
        self.rows = target.shape[1]
        self.part = source.shape[1] // held

    def pieces(self, steps, arriving):
        here = self.here
        origin = lax.rem(here.z + DEPTH - steps, DEPTH) if arriving else here.z
        away = lax.rem(here.z + steps, DEPTH)
        copies = []
        for expert in range(self.held):
            target = self.target.at[expert, :, pl.ds(pl.multiple_of(origin * self.part, 128), self.part)]
            source = self.source.at[
                pl.ds(pl.multiple_of(away * self.rows, 16), self.rows), pl.ds(expert * self.part, self.part)
            ]
            if steps == 0:
                copies.append(pltpu.make_async_copy(source, target, self.sems.at[0, 0, expert]))
            else:
                copies.append(
                    remote(
                        target if arriving else source,
                        target,
                        self.sems.at[0, steps, expert],
                        self.sems.at[1, steps, expert],
                        here.above(steps),
                    )
                )
        return copies

    def begin(self):
        for steps in range(DEPTH):
            for copy in self.pieces(steps, False):
                copy.start()

    def end(self):
        for steps in range(DEPTH):
            for copy in self.pieces(steps, False):
                copy.wait() if steps == 0 else copy.wait_send()
            if steps:
                for copy in self.pieces(steps, True):
                    copy.wait_recv()


def row_sum_kernel(
    out, gin, gdown, out_sum, gate_half, up_half, down_sum, *scratch
):
    here = Here()
    here.meet()
    items = [Sum(here, [out], out_sum, halves_of(out.shape[2]), False, scratch[0:8])]
    other_in, other_down, own_in, own_down, sems, loads, share_sems = scratch[8:15]
    width = own_in.shape[2]
    tall = own_down.shape[0]
    swaps, kept = [], []
    for side in range(2):
        for core, into in ((1 - here.core, swaps), (here.core, kept)):
            source = gin.at[:, pl.ds(pl.multiple_of(side * 2 * width + core * width, 128), width)]
            into.append((source, side))
    copies = [
        remote(source, other_in.at[side], sems.at[0, side], sems.at[1, side], here.sibling())
        for source, side in swaps
    ]
    copies.append(
        remote(
            gdown.at[pl.ds(pl.multiple_of((1 - here.core) * tall, 16), tall)],
            other_down,
            sems.at[0, 2],
            sems.at[1, 2],
            here.sibling(),
        )
    )
    fetched = [pltpu.make_async_copy(source, own_in.at[side], loads.at[side]) for source, side in kept]
    fetched.append(
        pltpu.make_async_copy(
            gdown.at[pl.ds(pl.multiple_of(here.core * tall, 16), tall)], own_down, loads.at[2]
        )
    )
    held = 2
    share = Share(here, own_in.at[0], gate_half, share_sems, held)

    def before():
        for copy in copies + fetched:
            copy.start()

    def between():
        for side in range(2):
            copies[side].wait_recv()
            fetched[side].wait()
            target = own_in.at[0] if side == 0 else up_half
            add_up(target, [own_in.at[side], other_in.at[side]], own_in.shape[1], width)
            if side == 0:
                share.begin()
        copies[2].wait_recv()
        fetched[2].wait()
        add_up(down_sum, [own_down, other_down], tall, own_down.shape[1])

    run_sum(here, items, before, between)
    share.end()
    for copy in copies:
        copy.wait_send()


def row_sum(out, gin, gdown, held):
    rows, columns = out.shape[2:]
    deep, wide = gin.shape
    width = wide // 4
    tall = gdown.shape[0] // 2
    vmem = pl.BlockSpec(memory_space=pltpu.VMEM)
    return pl.pallas_call(
        row_sum_kernel,
        out_shape=(
            jax.ShapeDtypeStruct((rows, columns), single),
            jax.ShapeDtypeStruct((held, deep // DEPTH, wide // 2), narrow),
            jax.ShapeDtypeStruct((deep, width), narrow),
            jax.ShapeDtypeStruct((tall, columns), single),
        ),
        in_specs=[HBM] * 3,
        out_specs=(vmem, HBM, vmem, vmem),
        scratch_shapes=sum_scratch(rows, columns, narrow, halves_of(rows))
        + [
            pltpu.VMEM((2, deep, width), narrow),
            pltpu.VMEM((tall, columns), narrow),
            pltpu.VMEM((2, deep, width), narrow),
            pltpu.VMEM((tall, columns), narrow),
            pltpu.SemaphoreType.DMA((2, 3)),
            pltpu.SemaphoreType.DMA((3,)),
            pltpu.SemaphoreType.DMA((2, DEPTH, 2)),
        ],
        compiler_params=pltpu.CompilerParams(
            collective_id=3, has_side_effects=True, vmem_limit_bytes=62 * 2**20
        ),
        name="collect",
    )(out, gin, gdown)


def last_sum_kernel(gq, go, small, up_half, q_sum, small_sum, up_share, *scratch):
    here = Here()
    here.meet()
    rows = gq.shape[3]
    items = [
        Sum(here, [gq, go], q_sum, halves_of(rows), True, scratch[0:10]),
        Sum(here, [small], small_sum, halves_of(small.shape[3], False), True, scratch[10:20]),
    ]
    share = Share(here, up_half, up_share, scratch[20], 2)
    run_sum(here, items, share.begin)
    share.end()


def last_sum(gq, go, small, up_half, held):
    rows = gq.shape[3]
    columns = gq.shape[4] + go.shape[4]
    vmem = pl.BlockSpec(memory_space=pltpu.VMEM)
    deep, width = up_half.shape
    return pl.pallas_call(
        last_sum_kernel,
        out_shape=(
            jax.ShapeDtypeStruct((rows, columns), single),
            jax.ShapeDtypeStruct(small.shape[3:], single),
            jax.ShapeDtypeStruct((held, deep // DEPTH, DEPTH * width // held), narrow),
        ),
        in_specs=[HBM] * 4,
        out_specs=(vmem, vmem, HBM),
        scratch_shapes=sum_scratch(rows, columns, narrow, halves_of(rows), True)
        + sum_scratch(small.shape[3], small.shape[4], single, halves_of(small.shape[3], False), True)
        + [pltpu.SemaphoreType.DMA((2, DEPTH, 2))],
        compiler_params=pltpu.CompilerParams(
            collective_id=4, has_side_effects=True, vmem_limit_bytes=62 * 2**20
        ),
        name="deliver",
    )(gq, go, small, up_half)

def near_first(here, number):
    high = lax.div(here.z, 2)
    inner = lax.rem(lax.div(here.z + 1, 2), 2)
    low = number + inner * (1, -1, 0, 0)[number]
    return low + high * (DEPTH - 1 - 2 * low)


TILE = 256


class Tiles:
    def __init__(self, stage, sems):
        self.stage, self.sems = stage, sems

    def run(self, first, last, count, target, make):
        def store(number):
            slot = lax.rem(number, 2)
            rows = pl.ds(pl.multiple_of(number * TILE, TILE), TILE)
            return pltpu.make_async_copy(self.stage.at[slot], target.at[rows], self.sems.at[slot])

        def body(number, carry):
            pl.when(number >= 2)(lambda: store(number - 2).wait())
            make(number, self.stage.at[lax.rem(number, 2)])
            store(number).start()
            return carry

        lax.fori_loop(first, last, body, 0)
        if last == count:
            for number in (count - 2, count - 1):
                store(number).wait()


def experts_kernel(
    rows, ups, gates, win, wout, mid_sum, gate_sum, out, gin, gdown, rows_all, *scratch
):
    here = Here()
    here.meet()
    (
        w_in, w_out, grads, scaled, row_plane, up_plane, gate_plane, served, strip, stage, loads, strip_sems, stage_sems
    ) = scratch[:13]
    gather = Gather(here, rows, rows_all, halves_of(rows.shape[0]), False, scratch[13:17])
    mids = Sum(here, None, mid_sum, halves_of(rows.shape[0]), False, scratch[17:25])
    tables = Sum(here, None, gate_sum, halves_of(gate_sum.shape[0], False), False, scratch[25:33])
    block, width = rows.shape
    plane = RING * block
    hidden = w_out.shape[0]
    chunk = hidden // 4
    column = lax.broadcasted_iota(jnp.int32, (plane, 128), 1)
    fetch_in = pltpu.make_async_copy(win, w_in, loads.at[0])
    fetch_out = pltpu.make_async_copy(wout, w_out, loads.at[1])
    fetch_in.start()
    fetch_out.start()

    def fetch_plane(number):
        z = near_first(here, number)
        return (
            pltpu.make_async_copy(ups.at[z], up_plane.at[number % 2], loads.at[2 + number % 2]),
            pltpu.make_async_copy(gates.at[z], gate_plane.at[number % 2], loads.at[4 + number % 2]),
        )

    def fetch_rows(number):
        return pltpu.make_async_copy(rows_all.at[near_first(here, number)], row_plane, loads.at[6])

    def hidden_units(number):
        z = near_first(here, number)
        fetch_rows(number).start()
        for copy in fetch_plane(number):
            copy.wait()
        if number == 0:
            fetch_in.wait()
            fetch_out.wait()
        fetch_rows(number).wait()
        served[...] = jnp.zeros_like(served)
        at = pl.ds(pl.multiple_of(z * plane, plane), plane)

        def one(expert, carry):
            mid = row_plane[...].reshape(plane, width)
            up_rows = up_plane[number % 2]
            spot = pl.ds(pl.multiple_of(expert * chunk, chunk), chunk)
            spot_up = pl.ds(pl.multiple_of(hidden + expert * chunk, chunk), chunk)
            gate = jnp.sum(jnp.where(column == expert, gate_plane[number % 2], 0.0), axis=1, keepdims=True)
            gate_part = jnp.dot(mid, w_in[:, spot], preferred_element_type=single)
            up_part = jnp.dot(mid, w_in[:, spot_up], preferred_element_type=single)
            back = contract_last(up_rows, w_out[spot])
            sigmoid = 1.0 / (1.0 + jnp.exp(-gate_part))
            activated = gate_part * sigmoid
            units = activated * up_part
            scaled[at, spot] = (gate * units).astype(narrow)
            total = jnp.sum(units * back, axis=1, keepdims=True)
            served[...] += jnp.where(column == here.chip * 4 + expert, total, 0.0)
            grad = gate * back
            grads[at, spot] = (grad * up_part * (sigmoid * (1.0 + gate_part * (1.0 - sigmoid)))).astype(narrow)
            grads[at, spot_up] = (grad * activated).astype(narrow)
            return carry

        lax.fori_loop(0, 4, one, 0)
        for chip in range(RING):
            turned = jnp.transpose(served[chip * block : (chip + 1) * block])
            tables.mine[z, chip] = turned[: tables.rows]

    def row_grads(z):
        at = pl.ds(pl.multiple_of(z * plane, plane), plane)

        def one(number, carry):
            spot = pl.ds(pl.multiple_of(number * TILE, TILE), TILE)
            made = contract_last(grads[at], w_in[spot]).astype(narrow)
            for chip in range(RING):
                mids.mine[z, chip, :, spot] = made[chip * block : (chip + 1) * block]
            return carry

        lax.fori_loop(0, width // TILE, one, 0)

    for copy in fetch_plane(0):
        copy.start()
    rounds = Rounds(here, [gather])
    for number in range(DEPTH):
        rounds.service(number)
        gather_third(gather, near_first(here, number))
        if number + 1 < DEPTH:
            for copy in fetch_plane(number + 1):
                copy.start()
        hidden_units(number)

    tiles = Tiles(stage, stage_sems)
    strips = width // TILE

    def fetch_strip(number):
        spot = pl.ds(pl.multiple_of(number * TILE, TILE), TILE)
        slot = lax.rem(number, 2)
        return pltpu.make_async_copy(rows_all.at[:, :, :, spot], strip.at[slot], strip_sems.at[slot])

    def columns_of(result, stage, step=512):
        for begin in range(0, width, step):
            stage[:, begin : begin + step] = result(begin, step).astype(narrow)

    def grad_in(number, stage):
        slot = lax.rem(number, 2)
        fetch_strip(number).wait()
        pl.when(number + 1 < strips)(lambda: fetch_strip(number + 1).start())
        left = strip[slot].reshape(DEPTH * plane, TILE)
        columns_of(lambda begin, step: contract_rows(left, grads[:, begin : begin + step]), stage)

    def outputs(number, stage):
        at = pl.ds(pl.multiple_of(number * TILE, TILE), TILE)
        left = scaled[at]
        columns_of(
            lambda begin, step: jnp.dot(left, w_out[:, begin : begin + step], preferred_element_type=single),
            stage,
        )

    def grad_down(number, stage):
        at = pl.ds(pl.multiple_of(number * TILE, TILE), TILE)
        left = scaled[:, at]
        columns_of(lambda begin, step: contract_rows(left, w_in[:, begin : begin + step]), stage)

    fetch_strip(0).start()
    order = [far_first(here, number) for number in range(DEPTH)]
    items = [mids, tables]
    high = DEPTH * plane // TILE
    work = [
        lambda: tiles.run(0, 2, strips, gin, grad_in),
        lambda: tiles.run(2, 4, strips, gin, grad_in),
        lambda: tiles.run(4, 6, strips, gin, grad_in),
        lambda: tiles.run(6, strips, strips, gin, grad_in),
    ]
    for number, z in enumerate(order):
        row_grads(z)
        for item in items:
            for way in (0, 1):
                start(item.toss(z, way))
        if number:
            for item in items:
                item.second(order[number - 1])
        if number > 1:
            for item in items:
                item.third(order[number - 2], False)
        if number + 1 < DEPTH:
            work[number]()
    again = [
        pltpu.make_async_copy(ups.at[z], w_in.at[pl.ds(z * plane, plane)], loads.at[7 + z]) for z in range(DEPTH)
    ]
    for copy in again:
        copy.start()
    work[DEPTH - 1]()
    for item in items:
        item.second(order[DEPTH - 1])
        item.third(order[DEPTH - 2], False)
    tiles.run(0, high, high, out, outputs)
    for item in items:
        item.third(order[DEPTH - 1], True)
    for copy in again:
        copy.wait()
    tiles.run(0, hidden // TILE, hidden // TILE, gdown, grad_down)
    for number, z in enumerate(order):
        for item in items:
            item.end(z, number == DEPTH - 1)
    rounds.finish()


def experts_round(rows, ups, gates, win, wout, experts):
    block, width = rows.shape
    plane = RING * block
    hidden = wout.shape[0]
    total = DEPTH * plane
    vmem = pl.BlockSpec(memory_space=pltpu.VMEM)
    return pl.pallas_call(
        experts_kernel,
        out_shape=(
            jax.ShapeDtypeStruct((block, width), single),
            jax.ShapeDtypeStruct((experts, block), single),
            jax.ShapeDtypeStruct((total, width), narrow),
            jax.ShapeDtypeStruct((width, 2 * hidden), narrow),
            jax.ShapeDtypeStruct((hidden, width), narrow),
            jax.ShapeDtypeStruct((DEPTH, RING, block, width), narrow),
        ),
        in_specs=[HBM] * 5,
        out_specs=(vmem, vmem) + (HBM,) * 4,
        scratch_shapes=[
            pltpu.VMEM((width, 2 * hidden), narrow),
            pltpu.VMEM((hidden, width), narrow),
            pltpu.VMEM((total, 2 * hidden), narrow),
            pltpu.VMEM((total, hidden), narrow),
            pltpu.VMEM((RING, block, width), narrow),
            pltpu.VMEM((2, plane, width), narrow),
            pltpu.VMEM((2, plane, 128), single),
            pltpu.VMEM((plane, 128), single),
            pltpu.VMEM((2, DEPTH, RING, block, TILE), narrow),
            pltpu.VMEM((2, TILE, width), narrow),
            pltpu.SemaphoreType.DMA((11,)),
            pltpu.SemaphoreType.DMA((2,)),
            pltpu.SemaphoreType.DMA((2,)),
        ]
        + GATHER_SEMS
        + sum_scratch(block, width, narrow, halves_of(block), made=True)
        + sum_scratch(experts, block, single, halves_of(experts, False), made=True),
        compiler_params=pltpu.CompilerParams(
            collective_id=2, has_side_effects=True, vmem_limit_bytes=62 * 2**20
        ),
        name="experts",
    )(rows, ups, gates, win, wout)


def by_kernels():
    return lax.axis_size("dp") == DEPTH and lax.axis_size("expert") == 2 * RING


def bring_all(w_qkv, w_out, upstream, dense, gain_rows, expert_in, expert_out):
    width = upstream.shape[1]
    share = gain_rows.shape[1]
    if by_kernels():
        experts, rows = dense.shape[1], dense.shape[0]
        small = jnp.concatenate([dense.T, jnp.pad(gain_rows, ((0, 4), (0, rows - share)))], axis=0)
        wq, wo, up, all_small, weight_in, weight_down = first_gather(
            w_qkv, w_out, upstream, small, expert_in, expert_out
        )
        gains = all_small[:, :, :, experts : experts + 4, :share].transpose(3, 0, 1, 2, 4).reshape(4, -1)
        core = lax.rem(lax.axis_index("expert"), 2)
        every_gate = lax.dynamic_index_in_dim(all_small, core, axis=2, keepdims=False)[:, :, :experts]
        return (
            wq.reshape(-1, w_qkv.shape[1]),
            wo.reshape(-1, w_out.shape[1]),
            up.reshape(-1, width),
            every_gate,
            gains,
            weight_in,
            weight_down.reshape(-1, width),
        )
    everyone = ("dp", "expert")
    weight_in, weight_down = fetch_weights(expert_in, expert_out)
    return (
        lax.all_gather(w_qkv, everyone, axis=0, tiled=True),
        lax.all_gather(w_out, everyone, axis=0, tiled=True),
        gather_alike(upstream).reshape(-1, width),
        gather_alike(dense.T),
        lax.all_gather(gain_rows, everyone, axis=1, tiled=True),
        weight_in,
        weight_down,
    )


def experts_all(routed_in, up_rows, every_gate, weight_in, weight_down, held):
    depth = lax.axis_size("dp")
    owners = lax.axis_size("expert")
    chips = owners // 2
    experts = owners * held
    chip_experts = 2 * held
    rows, width = routed_in.shape
    chip = lax.axis_index("expert") // 2
    mine = lax.dynamic_slice_in_dim(every_gate, chip * chip_experts, chip_experts, axis=2)
    gate = mine.transpose(0, 1, 3, 2)
    if by_kernels():
        gate = jnp.pad(gate.reshape(DEPTH, -1, chip_experts), ((0, 0), (0, 0), (0, 128 - chip_experts)))
        ups = up_rows.reshape(DEPTH, -1, width)
        grad_routed, table, out, grad_in, grad_down, _ = experts_round(
            routed_in, ups, gate, weight_in, weight_down, experts
        )
        mixture, *half_way = row_sum(out.reshape(DEPTH, RING, rows, width), grad_in, grad_down, held)
        return (mixture, grad_routed, table, half_way)
    mid_rows = gather_alike(routed_in).reshape(-1, width)
    out, mid, served, grad_in, grad_down = expert_rounds(
        mid_rows, up_rows, gate.reshape(-1, chip_experts), weight_in, weight_down
    )
    by_gate = served.reshape(depth, chips, rows, chip_experts).transpose(0, 1, 3, 2)
    spread = jnp.zeros((depth, chips, experts, rows), single)
    spread = lax.dynamic_update_slice_in_dim(spread, by_gate, chip * chip_experts, axis=2)
    return (
        scatter_alike(out.reshape(depth, chips, rows, width)).astype(single),
        scatter_alike(mid.reshape(depth, chips, rows, width)).astype(single),
        scatter_alike(spread),
        (grad_in, grad_down),
    )


def deliver_all(pieces, grad_qkv, grad_out, half_way, held):
    owners = lax.axis_size("dp") * lax.axis_size("expert")
    share = pieces.shape[1] // owners
    if by_kernels():
        gate_half, up_half, down = half_way
        lead = (DEPTH, RING, 2)
        small = pieces.reshape(4, owners, share).transpose(1, 0, 2)
        small = jnp.pad(small, ((0, 0), (0, 4), (0, 128 - share))).reshape(lead + (8, 128))
        shares, gains, up_share = last_sum(
            grad_qkv.reshape(lead + (-1,) + grad_qkv.shape[1:]),
            grad_out.reshape(lead + (-1,) + grad_out.shape[1:]),
            small,
            up_half,
            held,
        )
        wide = grad_qkv.shape[1]
        return (
            gains[:4, :share],
            shares[:, :wide],
            shares[:, wide:],
            jnp.concatenate([gate_half, up_share], axis=2).astype(single),
            down.reshape(held, -1, down.shape[1]),
        )
    everyone = ("dp", "expert")
    share_in, share_down = return_weights(*half_way, held)
    return (
        lax.psum_scatter(pieces, everyone, scatter_dimension=1, tiled=True),
        lax.psum_scatter(grad_qkv, everyone, scatter_dimension=0, tiled=True).astype(single),
        lax.psum_scatter(grad_out, everyone, scatter_dimension=0, tiled=True).astype(single),
        share_in.astype(single),
        share_down.astype(single),
    )


def local(
    tokens,
    lengths,
    expert_ids,
    gates,
    attn_gain,
    w_qkv,
    q_gain,
    k_gain,
    w_out,
    ffn_gain,
    expert_in,
    expert_out,
    out_grad,
):
    micro_count, seq_len, model_width = tokens.shape
    rows = micro_count * seq_len
    held = expert_in.shape[0]
    experts = lax.axis_size("expert") * held
    inputs = tokens.reshape(rows, model_width).astype(single)
    upstream = out_grad.reshape(rows, model_width)
    ids = expert_ids.reshape(rows, -1)
    gate_rows = gates.reshape(rows, -1)
    onehot = (ids[:, :, None] == jnp.arange(experts, dtype=jnp.int32)).astype(single)
    dense = jnp.sum(onehot * gate_rows[:, :, None], axis=1)
    gain_rows = jnp.stack([attn_gain, q_gain, k_gain, ffn_gain]).astype(single)
    weight_qkv, weight_out, up_rows, every_gate, gains, weight_in, weight_down = bring_all(
        w_qkv, w_out, upstream, dense, gain_rows, expert_in, expert_out
    )
    gain_attn, gain_query, gain_key, gain_ffn = gains[0], gains[1], gains[2], gains[3]

    normal_in, factor_in = normalize(inputs)
    normed_in = (normal_in * gain_attn).astype(narrow)
    projected = jnp.dot(normed_in, weight_qkv, preferred_element_type=single)
    normal_q, factor_q = normalize(projected[:, :model_width])
    normal_k, factor_k = normalize(projected[:, model_width : 2 * model_width])
    document, position = layout(lengths[:, 0], seq_len)
    cosine, sine = angles(position)
    query_rows = rotate(normal_q * gain_query, cosine, sine).astype(narrow).reshape(rows, -1, HEAD)
    key_rows = rotate(normal_k * gain_key, cosine, sine).astype(narrow).reshape(rows, -1, HEAD)
    value_rows = projected[:, 2 * model_width :].astype(narrow).reshape(rows, -1, HEAD)
    places = jnp.arange(rows, dtype=jnp.int32)
    allowed = (document[:, None] == document[None, :]) & (places[:, None] >= places[None, :])
    raw = jnp.einsum("qhd,khd->hqk", query_rows, key_rows, preferred_element_type=single)
    scores = jnp.where(allowed[None], raw * HEAD ** (-0.5), masked_score)
    highest = jnp.max(scores, axis=-1, keepdims=True)
    unnormed = jnp.exp(scores - highest)
    probs = unnormed / jnp.sum(unnormed, axis=-1, keepdims=True)
    attn_probs = probs.astype(narrow)
    attended = (
        jnp.einsum("hqk,khd->qhd", attn_probs, value_rows, preferred_element_type=single)
        .reshape(rows, model_width)
        .astype(narrow)
    )
    middle = inputs + jnp.dot(attended, weight_out, preferred_element_type=single)
    normal_mid, factor_mid = normalize(middle)
    routed_in = (normal_mid * gain_ffn).astype(narrow)

    mixture, grad_routed, gate_table, half_way = experts_all(
        routed_in, up_rows, every_gate, weight_in, weight_down, held
    )
    grad_gates = jnp.sum(onehot * gate_table.T[:, None, :], axis=2)
    results = (middle + mixture).astype(narrow)

    grad_mid, piece_ffn = rms_back(grad_routed, normal_mid, factor_mid, gain_ffn)
    grad_middle = upstream.astype(single) + grad_mid
    grad_branch = grad_middle.astype(narrow)
    grad_out_part = contract_rows(attended, grad_branch, narrow)
    grad_attended = contract_last(grad_branch, weight_out).astype(narrow).reshape(rows, -1, HEAD)
    grad_probs = jnp.einsum("qhd,khd->hqk", grad_attended, value_rows, preferred_element_type=single)
    inner = jnp.sum(grad_probs * probs, axis=-1, keepdims=True)
    grad_scores = (probs * (grad_probs - inner)).astype(narrow)
    grad_query = jnp.einsum(
        "hqk,khd->qhd", grad_scores, key_rows, preferred_element_type=single
    ) * HEAD ** (-0.5)
    grad_key = jnp.einsum(
        "hqk,qhd->khd", grad_scores, query_rows, preferred_element_type=single
    ) * HEAD ** (-0.5)
    grad_value = jnp.einsum("hqk,qhd->khd", attn_probs, grad_attended, preferred_element_type=single)
    grad_q_raw, piece_query = rms_back(
        rotate(grad_query.reshape(rows, model_width), cosine, -sine), normal_q, factor_q, gain_query
    )
    grad_k_raw, piece_key = rms_back(
        rotate(grad_key.reshape(rows, model_width), cosine, -sine), normal_k, factor_k, gain_key
    )
    grad_qkv = jnp.concatenate(
        [grad_q_raw, grad_k_raw, grad_value.reshape(rows, model_width)], axis=1
    ).astype(narrow)
    grad_qkv_part = contract_rows(normed_in, grad_qkv, narrow)
    grad_normed = contract_last(grad_qkv, weight_qkv)
    grad_input, piece_attn = rms_back(grad_normed, normal_in, factor_in, gain_attn)
    grad_tokens = grad_middle + grad_input

    pieces = jnp.stack([piece_attn, piece_query, piece_key, piece_ffn])
    gain_sums, grad_qkv_share, grad_out_share, share_in, share_down = deliver_all(
        pieces, grad_qkv_part, grad_out_part, half_way, held
    )
    shape = (micro_count, seq_len, model_width)
    return (
        results.reshape(shape),
        grad_tokens.reshape(shape),
        grad_gates.reshape(expert_ids.shape),
        gain_sums[0],
        grad_qkv_share,
        gain_sums[1],
        gain_sums[2],
        grad_out_share,
        gain_sums[3],
        share_in,
        share_down,
    )


def solution(mesh):
    by_rows = P(None, ("dp", "expert"), None)
    flat = P(("dp", "expert"))
    split = P(("dp", "expert"), None)
    held = P("expert", "dp", None)
    return jax.shard_map(
        local,
        mesh=mesh,
        in_specs=(
            by_rows, by_rows, by_rows, by_rows, flat, split, flat, flat, split, flat, held, held, by_rows,
        ),
        out_specs=(by_rows, by_rows, by_rows, flat, split, flat, flat, split, flat, held, held),
        check_vma=False,
    )
```

```python
import jax
import jax.numpy as jnp
from jax import lax
from jax.experimental import pallas as pl
from jax.experimental.pallas import tpu as pltpu
from jax.sharding import PartitionSpec as P

HEAD = 128
epsilon = 1e-05
base_theta = 10000.0
masked_score = -1e30
single = jnp.float32
narrow = jnp.bfloat16


def normalize(values):
    factor = lax.rsqrt(jnp.mean(values * values, axis=-1, keepdims=True) + epsilon)
    return (values * factor, factor)


def rms_back(upstream, normal, factor, gain):
    weighted = upstream * gain
    inner = jnp.mean(weighted * normal, axis=-1, keepdims=True)
    return (factor * (weighted - normal * inner), jnp.sum(upstream * normal, axis=0))


def angles(position):
    half = HEAD // 2
    ladder = jnp.arange(half, dtype=single) * (2.0 / HEAD)
    frequency = jnp.exp(-jnp.log(base_theta) * ladder)
    angle = position.astype(single)[:, None] * frequency[None, :]
    return (jnp.cos(angle)[:, None, :], jnp.sin(angle)[:, None, :])


def rotate(field, cosine, sine):
    length = field.shape[0]
    heads = field.reshape(length, -1, HEAD)
    half = HEAD // 2
    first = heads[..., :half]
    second = heads[..., half:]
    turned = jnp.concatenate(
        [first * cosine - second * sine, second * cosine + first * sine], axis=-1
    )
    return turned.reshape(length, -1)


def layout(doc_lengths, length):
    packs, count = doc_lengths.shape
    upto = jnp.arange(count)[None, :] <= jnp.arange(count)[:, None]
    ends = jnp.sum(jnp.where(upto[None], doc_lengths[:, None, :], 0), axis=2)
    starts = ends - doc_lengths
    places = jnp.arange(length, dtype=jnp.int32)[None, :, None]
    document = jnp.sum((places >= ends[:, None, :]).astype(jnp.int32), axis=2)
    member = (places >= starts[:, None, :]) & (places < ends[:, None, :])
    first_place = jnp.sum(jnp.where(member, starts[:, None, :], 0), axis=2)
    document = document + (count + 1) * jnp.arange(packs, dtype=jnp.int32)[:, None]
    return (document.reshape(-1), (places[..., 0] - first_place).reshape(-1))


def contract_rows(left, right, kind=single):
    return lax.dot_general(left, right, (((0,), (0,)), ((), ())), preferred_element_type=kind)


def contract_last(left, right, kind=single):
    return lax.dot_general(left, right, (((1,), (1,)), ((), ())), preferred_element_type=kind)


def core_groups():
    return [[2 * chip + core for chip in range(lax.axis_size("expert") // 2)] for core in range(2)]


def chip_groups():
    return [[2 * chip, 2 * chip + 1] for chip in range(lax.axis_size("expert") // 2)]


def gather_alike(block):
    column = lax.all_gather(block, "dp", axis=0)
    return lax.all_gather(column, "expert", axis=1, axis_index_groups=core_groups())


def scatter_alike(blocks):
    column = lax.psum_scatter(
        blocks, "expert", scatter_dimension=1, axis_index_groups=core_groups()
    )
    return lax.psum_scatter(column, "dp", scatter_dimension=0)


def fetch_weights(expert_in, expert_out):
    depth = lax.axis_size("dp")
    held, rows, columns = expert_in.shape
    part = columns // (2 * depth)
    cut = expert_in.reshape(held, rows, 2, depth, part)
    turned = lax.all_to_all(cut, "dp", split_axis=3, concat_axis=1, tiled=True)
    both = lax.all_gather(turned[:, :, :, 0], "expert", axis=0, axis_index_groups=chip_groups())
    weight_in = both.transpose(2, 3, 0, 1, 4).reshape(depth * rows, 4 * held * part)
    weight_down = lax.all_gather(
        expert_out, "expert", axis=0, axis_index_groups=chip_groups()
    ).reshape(-1, expert_out.shape[2])
    return (weight_in, weight_down)


def return_weights(grad_in, grad_down, held):
    depth = lax.axis_size("dp")
    rows, columns = grad_in.shape
    part = columns // (4 * held)
    cut = grad_in.reshape(rows, 2, 2, held, part)
    own = lax.psum_scatter(cut, "expert", scatter_dimension=2, axis_index_groups=chip_groups())
    own = own.reshape(depth, rows // depth, 2, held, part)
    turned = lax.all_to_all(own, "dp", split_axis=0, concat_axis=0)
    share_in = turned.transpose(3, 1, 2, 0, 4).reshape(held, rows // depth, 2 * depth * part)
    down = grad_down.reshape(2, held, part, grad_down.shape[1])
    share_down = lax.psum_scatter(
        down, "expert", scatter_dimension=0, axis_index_groups=chip_groups()
    )
    return (share_in, share_down)


def expert_round(mid_rows, up_rows, gate, weight_in, weight_down):
    count = gate.shape[1]
    part = weight_down.shape[0] // count
    wide = jnp.broadcast_to(gate[:, :, None], gate.shape + (part,)).reshape(gate.shape[0], -1)
    gate_up = jnp.dot(mid_rows, weight_in, preferred_element_type=single)
    hidden_units = gate_up.shape[1] // 2
    gate_part = gate_up[:, :hidden_units]
    up_part = gate_up[:, hidden_units:]
    sigmoid = jax.nn.sigmoid(gate_part)
    activated = gate_part * sigmoid
    hidden = activated * up_part
    back = contract_last(up_rows, weight_down)
    scaled = (wide * hidden).astype(narrow)
    piece_out = jnp.dot(scaled, weight_down, preferred_element_type=narrow)
    piece_gates = jnp.sum((hidden * back).reshape(-1, count, part), axis=2)
    grad_hidden = wide * back
    grad_gate = grad_hidden * up_part * sigmoid * (1.0 + gate_part * (1.0 - sigmoid))
    grad_up = grad_hidden * activated
    grad_gate_up = jnp.concatenate([grad_gate, grad_up], axis=1).astype(narrow)
    piece_mid = contract_last(grad_gate_up, weight_in, narrow)
    return (piece_out, piece_mid, piece_gates, grad_gate_up, scaled)


def expert_rounds(mid_rows, up_rows, gate, weight_in, weight_down):
    total = mid_rows.shape[0]
    rounds = max(1, total // 2048)

    def one(sums, pieces):
        mid, up, weights = pieces
        piece_out, piece_mid, piece_gates, grad_gate_up, scaled = expert_round(
            mid, up, weights, weight_in, weight_down
        )
        grads = (contract_rows(mid, grad_gate_up), contract_rows(scaled, up))
        return (jax.tree.map(jnp.add, sums, grads), (piece_out, piece_mid, piece_gates))

    if rounds == 1:
        piece_out, piece_mid, piece_gates, grad_gate_up, scaled = expert_round(
            mid_rows, up_rows, gate, weight_in, weight_down
        )
        grads = (contract_rows(mid_rows, grad_gate_up, narrow), contract_rows(scaled, up_rows, narrow))
        return (piece_out, piece_mid, piece_gates) + grads
    start = (jnp.zeros(weight_in.shape, single), jnp.zeros(weight_down.shape, single))
    cut = jax.tree.map(lambda a: a.reshape(rounds, total // rounds, -1), (mid_rows, up_rows, gate))
    sums, made = lax.scan(one, start, cut)
    made = jax.tree.map(lambda a: a.reshape(total, -1), made)
    return made + (sums[0].astype(narrow), sums[1].astype(narrow))


MESH = pl.DeviceIdType.MESH
HBM = pl.BlockSpec(memory_space=pl.ANY)
DEPTH = 4
RING = 4


def ring_turn(number):
    high = lax.div(number, 2)
    return number + high * (1 - 2 * lax.rem(number, 2))


class Here:
    def __init__(self):
        number = lax.axis_index("expert")
        self.z = lax.axis_index("dp")
        self.core = lax.rem(number, 2)
        self.chip = lax.div(number, 2)
        self.q = ring_turn(self.chip)

    def chip_at(self, turn):
        return ring_turn(lax.rem(self.q + turn + RING, RING))

    def beside(self, turn):
        return (self.z, 2 * self.chip_at(turn) + self.core)

    def above(self, steps):
        return (lax.rem(self.z + steps + DEPTH, DEPTH), 2 * self.chip + self.core)

    def sibling(self):
        return (self.z, 2 * self.chip + 1 - self.core)

    def meet(self):
        barrier = pltpu.get_barrier_semaphore()
        others = [self.beside(1), self.beside(-1), self.sibling()]
        others += [self.above(steps) for steps in range(1, DEPTH)]
        for other in others:
            pl.semaphore_signal(barrier, inc=1, device_id=other, device_id_type=MESH)
        pl.semaphore_wait(barrier, len(others))


def remote(source, target, sent, arrived, device):
    return pltpu.make_async_remote_copy(
        src_ref=source,
        dst_ref=target,
        send_sem=sent,
        recv_sem=arrived,
        device_id=device,
        device_id_type=MESH,
    )


GATHER_SEMS = [
    pltpu.SemaphoreType.DMA((2, 2, DEPTH - 1)),
    pltpu.SemaphoreType.DMA((2, DEPTH, 2, 2)),
    pltpu.SemaphoreType.DMA((2, DEPTH)),
    pltpu.SemaphoreType.DMA((1,)),
]


class Gather:
    def __init__(self, here, source, whole, halves, shared, sems):
        self.here, self.source, self.whole, self.halves, self.shared = here, source, whole, halves, shared
        self.line, self.ring, self.pair, self.own = sems

    def block(self, z, turn):
        chip = self.here.chip_at(turn)
        return self.whole.at[z, chip, self.here.core] if self.shared else self.whole.at[z, chip]

    def keep(self):
        return pltpu.make_async_copy(self.source, self.block(self.here.z, 0), self.own.at[0])

    def along(self, step, way, first):
        z = self.here.z - step + 1 if way == 0 else self.here.z + step - 1
        block = self.block(z, 0)
        return remote(
            self.source if first else block,
            block,
            self.line.at[0, way, step - 1],
            self.line.at[1, way, step - 1],
            self.here.above(1 if way == 0 else -1),
        )

    def round(self, z, way, first=False):
        turn = 1 if way == 0 else -1
        block = self.block(z, 0)
        return remote(
            self.source if first else block,
            block,
            self.ring.at[0, z, way, 0],
            self.ring.at[1, z, way, 0],
            self.here.beside(turn),
        )

    def heard(self, z, way):
        block = self.block(z, -1 if way == 0 else 1)
        return remote(
            block, block, self.ring.at[0, z, way, 0], self.ring.at[1, z, way, 0], self.here.beside(1)
        )

    def onward(self, z, way, mine):
        if self.halves[way] is None:
            return None
        turn = (-1 if mine else -2) if way == 0 else (1 if mine else 2)
        block = self.block(z, turn).at[pl.ds(*self.halves[way])]
        return remote(
            block,
            block,
            self.ring.at[0, z, way, 1],
            self.ring.at[1, z, way, 1],
            self.here.beside(1 if way == 0 else -1),
        )

    def swap(self, z, mine):
        core = self.here.core if mine else 1 - self.here.core
        part = self.whole.at[z, :, core]
        return remote(part, part, self.pair.at[0, z], self.pair.at[1, z], self.here.sibling())


def start(copy):
    if copy is not None:
        copy.start()


def gather_third(item, z):
    for way in (0, 1):
        copy = item.onward(z, way, False)
        if copy is not None:
            copy.wait_recv()


class Rounds:
    def __init__(self, here, items):
        self.here, self.items = here, items
        for item in items:
            item.keep().start()
            for way in (0, 1):
                self.depart(0, way, item)
            for way in (0, 1):
                item.round(here.z, way, True).start()

    def depart(self, step, way, item):
        here = self.here
        ahead = here.z + 1 < DEPTH if way == 0 else here.z >= 1
        pl.when(ahead)(lambda: item.along(step + 1, way, step == 0).start())

    def places(self, step, body):
        here = self.here
        if step == 0:
            body(here.z, 0)
            return
        pl.when(here.z >= step)(lambda: body(here.z - step, 0))
        pl.when(here.z + step < DEPTH)(lambda: body(here.z + step, 1))

    def service(self, step):
        items, here = self.items, self.here

        def first(z, way):
            for item in items:
                block = item.block(z, 0)
                remote(
                    block, block, item.line.at[0, way, step], item.line.at[1, way, step], here.above(1)
                ).wait_recv()
                if step + 2 < DEPTH:
                    self.depart(step + 1, way, item)
                for side in (0, 1):
                    item.round(z, side).start()

        def second(z, way):
            for item in items:
                for side in (0, 1):
                    item.heard(z, side).wait_recv()
                    start(item.onward(z, side, True))

        if step + 1 < DEPTH:
            self.places(step + 1, first)
        if step == 0:
            for item in items:
                item.keep().wait()
        self.places(step, second)

    def third(self, step):
        def body(z, way):
            for item in self.items:
                gather_third(item, z)
                if item.shared:
                    item.swap(z, True).start()

        self.places(step, body)

    def finish(self):
        def settle(z, way):
            for item in self.items:
                for side in (0, 1):
                    item.round(z, side).wait_send()
                    copy = item.onward(z, side, True)
                    if copy is not None:
                        copy.wait_send()
                if item.shared:
                    item.swap(z, True).wait_send()
                    item.swap(z, False).wait_recv()

        for step in range(DEPTH):
            self.places(step, settle)
        here = self.here
        for item in self.items:
            for step in range(DEPTH - 1):
                for way in (0, 1):

                    def sent(z, side, step=step, way=way, item=item):
                        if step and side != way:
                            return
                        ahead = here.z + 1 < DEPTH if way == 0 else here.z >= 1
                        pl.when(ahead)(lambda: item.along(step + 1, way, step == 0).wait_send())

                    self.places(step, sent)


class Recut:
    def __init__(self, here, source_in, source_out, whole_in, whole_out, sems):
        self.here, self.source_in, self.source_out = here, source_in, source_out
        self.whole_in, self.whole_out = whole_in, whole_out
        self.cut, self.pair, self.down, self.own = sems
        self.held, self.rows, columns = source_in.shape
        self.hidden = columns // 2
        self.part = self.hidden // DEPTH

    def pieces(self, steps, arriving):
        here, copies = self.here, []
        mine = lax.rem(here.z + DEPTH - steps, DEPTH) if arriving else here.z
        away = lax.rem(here.z + steps, DEPTH)
        for side in range(2):
            for expert in range(self.held):
                columns = side * self.held * 2 * self.part + (here.core * self.held + expert) * self.part
                target = self.whole_in.at[
                    pl.ds(pl.multiple_of(mine * self.rows, 16), self.rows),
                    pl.ds(pl.multiple_of(columns, 128), self.part),
                ]
                source = self.source_in.at[
                    expert, :, pl.ds(pl.multiple_of(side * self.hidden + away * self.part, 128), self.part)
                ]
                spot = (steps, side * self.held + expert)
                if steps == 0:
                    copies.append(pltpu.make_async_copy(source, target, self.own.at[spot[1]]))
                else:
                    copies.append(
                        remote(
                            target if arriving else source,
                            target,
                            self.cut.at[(0,) + spot],
                            self.cut.at[(1,) + spot],
                            here.above(steps),
                        )
                    )
        return copies

    def across(self, steps, mine):
        here, copies = self.here, []
        core = here.core if mine else 1 - here.core
        row = lax.rem(here.z + DEPTH - steps, DEPTH)
        width = self.held * self.part
        for side in range(2):
            spot = self.whole_in.at[
                pl.ds(pl.multiple_of(row * self.rows, 16), self.rows),
                pl.ds(pl.multiple_of(side * 2 * width + core * width, 128), width),
            ]
            copies.append(
                remote(spot, spot, self.pair.at[0, steps, side], self.pair.at[1, steps, side], here.sibling())
            )
        return copies

    def lower(self, mine):
        here = self.here
        core = here.core if mine else 1 - here.core
        spot = self.whole_out.at[pl.ds(core * self.held, self.held)]
        return remote(
            self.source_out if mine else spot, spot, self.down.at[0], self.down.at[1], here.sibling()
        )

    def lower_own(self):
        return pltpu.make_async_copy(
            self.source_out, self.whole_out.at[pl.ds(self.here.core * self.held, self.held)], self.own.at[4]
        )

    def begin(self):
        for copy in self.pieces(0, False):
            copy.start()
        self.lower_own().start()
        self.lower(True).start()
        for steps in range(1, DEPTH):
            for copy in self.pieces(steps, False):
                copy.start()

    def relay(self):
        for steps in range(DEPTH):
            for copy in self.pieces(steps, True):
                copy.wait() if steps == 0 else copy.wait_recv()
            for copy in self.across(steps, True):
                copy.start()

    def end(self):
        self.lower_own().wait()
        self.lower(True).wait_send()
        self.lower(False).wait_recv()
        for steps in range(DEPTH):
            if steps:
                for copy in self.pieces(steps, False):
                    copy.wait_send()
            for copy in self.across(steps, True):
                copy.wait_send()
            for copy in self.across(steps, False):
                copy.wait_recv()


RECUT_SEMS = [
    pltpu.SemaphoreType.DMA((2, DEPTH, 4)),
    pltpu.SemaphoreType.DMA((2, DEPTH, 2)),
    pltpu.SemaphoreType.DMA((2,)),
    pltpu.SemaphoreType.DMA((5,)),
]


def halves_of(rows, split=True):
    return ((0, rows // 2), (rows // 2, rows - rows // 2)) if split else ((0, rows), None)


def first_gather_kernel(wq, wo, up, small, ein, eout, wq_all, wo_all, up_all, small_all, win, wout, *sems):
    here = Here()
    here.meet()
    items = []
    for number, (source, whole, halves, shared) in enumerate(
        (
            (small, small_all, halves_of(small.shape[0], False), True),
            (wq, wq_all, halves_of(wq.shape[0]), True),
            (wo, wo_all, halves_of(wo.shape[0]), True),
            (up, up_all, halves_of(up.shape[0]), False),
        )
    ):
        items.append(Gather(here, source, whole, halves, shared, sems[4 * number : 4 * number + 4]))
    recut = Recut(here, ein, eout, win, wout, sems[16:20])
    rounds = Rounds(here, items)
    for step in range(DEPTH):
        rounds.service(step)
        if step == 0:
            recut.begin()
        else:
            rounds.third(step - 1)
    rounds.third(DEPTH - 1)
    recut.relay()
    rounds.finish()
    recut.end()


def first_gather(wq, wo, up, small, ein, eout):
    def whole(array, shared):
        lead = (DEPTH, RING, 2) if shared else (DEPTH, RING)
        return jax.ShapeDtypeStruct(lead + array.shape, array.dtype)

    held, rows, columns = ein.shape
    return pl.pallas_call(
        first_gather_kernel,
        out_shape=(
            whole(wq, True),
            whole(wo, True),
            whole(up, False),
            whole(small, True),
            jax.ShapeDtypeStruct((DEPTH * rows, columns), ein.dtype),
            jax.ShapeDtypeStruct((2 * held,) + eout.shape[1:], eout.dtype),
        ),
        in_specs=[HBM] * 6,
        out_specs=(HBM,) * 6,
        scratch_shapes=GATHER_SEMS * 4 + RECUT_SEMS,
        compiler_params=pltpu.CompilerParams(collective_id=1, has_side_effects=True),
        name="bring",
    )(wq, wo, up, small, ein, eout)

def add_up(target, terms, rows, columns):
    high = 16 if rows % 16 == 0 else 8
    wide = min(columns, 1024)
    across = columns // wide

    def piece(number, carry):
        row = pl.multiple_of(lax.div(number, across) * high, high)
        column = pl.multiple_of(lax.rem(number, across) * wide, 128)
        spot = (pl.ds(row, high), pl.ds(column, wide))
        total = terms[0][spot].astype(single)
        for term in terms[1:]:
            total = total + term[spot].astype(single)
        target[spot] = total.astype(target.dtype)
        return carry

    lax.fori_loop(0, (rows // high) * across, piece, 0)


SUM_SEMS = [
    pltpu.SemaphoreType.DMA((2, DEPTH, 2)),
    pltpu.SemaphoreType.DMA((2, DEPTH, 2)),
    pltpu.SemaphoreType.DMA((2, 2, DEPTH)),
    pltpu.SemaphoreType.DMA((DEPTH, RING, 2)),
]


def sum_scratch(rows, columns, kind, halves, paired=False, made=False):
    high = max(size for _, size in filter(None, halves))
    kept = RING if paired or made else RING - 1
    scratch = [
        pltpu.VMEM((DEPTH, kept, rows, columns), kind),
        pltpu.VMEM((DEPTH, 2, high, columns), kind),
        pltpu.VMEM((DEPTH, 2, rows, columns), kind),
        pltpu.VMEM((DEPTH + 1, rows, columns), kind),
    ] + SUM_SEMS
    if paired:
        scratch += [pltpu.VMEM((DEPTH, RING, rows, columns), kind), pltpu.SemaphoreType.DMA((2, DEPTH, 2))]
    return scratch


class Sum:
    def __init__(self, here, sources, target, halves, paired, scratch):
        self.here, self.sources, self.target, self.halves, self.paired = here, sources, target, halves, paired
        self.mine, self.half, self.full, self.column = scratch[:4]
        self.half_sem, self.full_sem, self.line_sem, self.load_sem = scratch[4:8]
        if paired:
            self.other, self.pair_sem = scratch[8:10]
        self.rows, self.columns = self.mine.shape[2:]

    def kept(self, z, turn):
        if self.sources is None:
            return self.mine.at[z, self.here.chip_at(turn)]
        return self.mine.at[z, turn if self.paired else {0: 0, 1: 1, 3: 2}[turn]]

    def raw(self, part, z, turn):
        chip = self.here.chip_at(turn)
        return part.at[z, chip, self.here.core] if self.paired else part.at[z, chip]

    def spots(self):
        at, spots = 0, []
        for part in self.sources or []:
            spots.append((part, pl.ds(at, part.shape[-1])))
            at += part.shape[-1]
        return spots

    def loads(self, z, turn):
        return [
            pltpu.make_async_copy(
                self.raw(part, z, turn), self.kept(z, turn).at[:, spot], self.load_sem.at[z, turn, number]
            )
            for number, (part, spot) in enumerate(self.spots())
        ]

    def swaps(self, z, mine):
        return [
            remote(
                part.at[z, :, 1 - self.here.core] if mine else self.other.at[z, :, :, spot],
                self.other.at[z, :, :, spot],
                self.pair_sem.at[0, z, number],
                self.pair_sem.at[1, z, number],
                self.here.sibling(),
            )
            for number, (part, spot) in enumerate(self.spots())
        ]

    def toss(self, z, way):
        if self.halves[way] is None:
            return None
        rows = pl.ds(*self.halves[way])
        loaded = self.sources is not None and not self.paired
        source = (self.raw(self.sources[0], z, 2) if loaded else self.kept(z, 2)).at[rows]
        return remote(
            source,
            self.half.at[z, way, pl.ds(0, self.halves[way][1])],
            self.half_sem.at[0, z, way],
            self.half_sem.at[1, z, way],
            self.here.beside(1 if way == 0 else -1),
        )

    def pass_on(self, z, way):
        return remote(
            self.kept(z, 1 if way == 0 else 3),
            self.full.at[z, way],
            self.full_sem.at[0, z, way],
            self.full_sem.at[1, z, way],
            self.here.beside(1 if way == 0 else -1),
        )

    def climb(self, z, way, up, slot=None):
        if slot is None:
            down_to_owner = way * (z == self.here.z - 1).astype(jnp.int32)
            slot = z + down_to_owner * (DEPTH - z)
        return remote(
            self.kept(z, 0),
            self.column.at[slot],
            self.line_sem.at[0, way, z],
            self.line_sem.at[1, way, z],
            self.here.above(2 * up - 1),
        )

    def begin(self, z):
        if self.paired:
            for copy in self.swaps(z, True):
                copy.start()
        for turn in (2, 1, 3, 0):
            if turn != 2 or self.paired:
                for copy in self.loads(z, turn):
                    copy.start()
        if not self.paired:
            for way in (0, 1):
                start(self.toss(z, way))

    def merge(self, z):
        if not self.paired:
            return
        for copy in self.swaps(z, False):
            copy.wait_recv()
        for turn in (2, 1, 3, 0):
            for copy in self.loads(z, turn):
                copy.wait()
            kept = self.kept(z, turn)
            add_up(kept, [kept, self.other.at[z, self.here.chip_at(turn)]], self.rows, self.columns)
            if turn == 2:
                for way in (0, 1):
                    start(self.toss(z, way))

    def second(self, z):
        for way, turn in ((0, 1), (1, 3)):
            if not self.paired:
                for copy in self.loads(z, turn):
                    copy.wait()
            copy = self.toss(z, way)
            if copy is not None:
                copy.wait_recv()
                begin, size = self.halves[way]
                rows = self.kept(z, turn).at[pl.ds(begin, size)]
                add_up(rows, [rows, self.half.at[z, way, pl.ds(0, size)]], size, self.columns)
        for way in (0, 1):
            self.pass_on(z, way).start()

    def third(self, z, last):
        here = self.here
        if not self.paired:
            for copy in self.loads(z, 0):
                copy.wait()
        for way in (0, 1):
            self.pass_on(z, way).wait_recv()
        kept = self.kept(z, 0)
        terms = [kept, self.full.at[z, 0], self.full.at[z, 1]]
        if last:
            below, above = self.column.at[z], self.column.at[DEPTH]

            @pl.when(here.z == 0)
            def _():
                self.climb(z, 1, 0, DEPTH).wait_recv()
                add_up(self.target, terms + [above], self.rows, self.columns)

            @pl.when(here.z == DEPTH - 1)
            def _():
                self.climb(z, 0, 0, z).wait_recv()
                add_up(self.target, terms + [below], self.rows, self.columns)

            @pl.when((here.z > 0) & (here.z < DEPTH - 1))
            def _():
                self.climb(z, 0, 0, z).wait_recv()
                self.climb(z, 1, 0, DEPTH).wait_recv()
                add_up(self.target, terms + [below, above], self.rows, self.columns)

            return
        up = (z > here.z).astype(jnp.int32)
        way = 1 - up
        follows = up * here.z + way * (DEPTH - 1 - here.z)

        @pl.when(follows > 0)
        def _():
            self.climb(z, way, up, z).wait_recv()
            add_up(kept, terms + [self.column.at[z]], self.rows, self.columns)

        @pl.when(follows == 0)
        def _():
            add_up(kept, terms, self.rows, self.columns)

        self.climb(z, way, up).start()

    def end(self, z, last):
        if self.paired:
            for copy in self.swaps(z, True):
                copy.wait_send()
        for way in (0, 1):
            copy = self.toss(z, way)
            if copy is not None:
                copy.wait_send()
            self.pass_on(z, way).wait_send()
        if not last:
            up = (z > self.here.z).astype(jnp.int32)
            self.climb(z, 1 - up, up).wait_send()


def far_first(here, number):
    high = lax.div(here.z, 2)
    inner = lax.rem(lax.div(here.z + 1, 2), 2)
    low = (DEPTH - 1 - number) + inner * (0, -2, 1, 1)[number]
    return low + high * (DEPTH - 1 - 2 * low)


def run_sum(here, items):
    order = [far_first(here, number) for number in range(DEPTH)]
    for z in order:
        for item in items:
            item.begin(z)
    for item in items:
        item.merge(order[0])
    for number, z in enumerate(order):
        for item in items:
            item.second(z)
        if number + 1 < DEPTH:
            for item in items:
                item.merge(order[number + 1])
        if number:
            for item in items:
                item.third(order[number - 1], False)
    for item in items:
        item.third(order[-1], True)
    for number, z in enumerate(order):
        for item in items:
            item.end(z, number == DEPTH - 1)


def last_sum_kernel(gq, go, small, q_sum, small_sum, *scratch):
    here = Here()
    here.meet()
    items = [
        Sum(here, [gq, go], q_sum, halves_of(gq.shape[3]), True, scratch[0:10]),
        Sum(here, [small], small_sum, halves_of(small.shape[3], False), True, scratch[10:20]),
    ]
    run_sum(here, items)


def last_sum(gq, go, small):
    rows = gq.shape[3]
    columns = gq.shape[4] + go.shape[4]
    vmem = pl.BlockSpec(memory_space=pltpu.VMEM)
    return pl.pallas_call(
        last_sum_kernel,
        out_shape=(
            jax.ShapeDtypeStruct((rows, columns), single),
            jax.ShapeDtypeStruct(small.shape[3:], single),
        ),
        in_specs=[HBM] * 3,
        out_specs=(vmem, vmem),
        scratch_shapes=sum_scratch(rows, columns, narrow, halves_of(rows), paired=True)
        + sum_scratch(small.shape[3], small.shape[4], single, halves_of(small.shape[3], False), paired=True),
        compiler_params=pltpu.CompilerParams(
            collective_id=4, has_side_effects=True, vmem_limit_bytes=62 * 2**20
        ),
        name="deliver",
    )(gq, go, small)

def near_first(here, number):
    high = lax.div(here.z, 2)
    inner = lax.rem(lax.div(here.z + 1, 2), 2)
    low = number + inner * (1, -1, 0, 0)[number]
    return low + high * (DEPTH - 1 - 2 * low)


TILE = 256


class Tiles:
    def __init__(self, here, stage, count, sems, parts, targets):
        self.here, self.stage, self.count = here, stage, count
        self.kept, self.sent, self.came = sems
        self.parts, self.targets = parts, targets

    def copies(self, number, keep=True, give=True):
        slot = lax.rem(number, 2)
        own, other = self.targets
        made = []
        for piece, (mine, theirs, spot) in enumerate(self.parts(number, self.stage.at[slot])):
            if keep:
                made.append(pltpu.make_async_copy(mine, own.at[spot], self.kept.at[slot, piece]))
            if give:
                sems = (self.sent.at[slot, piece], self.came.at[number, piece])
                made.append(remote(theirs, other.at[spot], *sems, self.here.sibling()))
        return made

    def settle(self, number):
        for copy in self.copies(number, give=False):
            copy.wait()
        for copy in self.copies(number, keep=False):
            copy.wait_send()

    def run(self, first, last, make):
        def body(number, carry):
            pl.when(number >= 2)(lambda: self.settle(number - 2))
            make(number, self.stage.at[lax.rem(number, 2)])
            for copy in self.copies(number):
                copy.start()
            return carry

        lax.fori_loop(first, last, body, 0)
        if last == self.count:
            for number in (last - 2, last - 1):
                self.settle(number)

    def heard(self):
        for number in range(self.count):
            for copy in self.copies(number, keep=False):
                copy.wait_recv()


def experts_kernel(
    rows, ups, gates, win, wout, mid_sum, gate_sum, out_sum, gin, gin_other, gdown, gdown_other, rows_all, *scratch
):
    here = Here()
    here.meet()
    (
        w_in, w_out, grads, scaled, row_plane, up_plane, gate_plane, served, strip, stage, loads, strip_sems
    ) = scratch[:12]
    gather = Gather(here, rows, rows_all, halves_of(rows.shape[0]), False, scratch[12:16])
    mids = Sum(here, None, mid_sum, halves_of(rows.shape[0]), False, scratch[16:24])
    outs = Sum(here, None, out_sum, halves_of(rows.shape[0]), False, scratch[16:19] + scratch[24:29])
    tables = Sum(here, None, gate_sum, halves_of(gate_sum.shape[0], False), False, scratch[29:37])
    in_sems, down_sems = scratch[37:40], scratch[40:43]
    block, width = rows.shape
    plane = RING * block
    hidden = w_out.shape[0]
    chunk = hidden // 4
    column = lax.broadcasted_iota(jnp.int32, (plane, 128), 1)
    fetch_in = pltpu.make_async_copy(win, w_in, loads.at[0])
    fetch_out = pltpu.make_async_copy(wout, w_out, loads.at[1])
    fetch_in.start()
    fetch_out.start()

    def fetch_plane(number):
        z = near_first(here, number)
        return (
            pltpu.make_async_copy(ups.at[z], up_plane.at[number % 2], loads.at[2 + number % 2]),
            pltpu.make_async_copy(gates.at[z], gate_plane.at[number % 2], loads.at[4 + number % 2]),
        )

    def fetch_rows(number):
        return pltpu.make_async_copy(rows_all.at[near_first(here, number)], row_plane, loads.at[6])

    def hidden_units(number):
        z = near_first(here, number)
        fetch_rows(number).start()
        for copy in fetch_plane(number):
            copy.wait()
        if number == 0:
            fetch_in.wait()
            fetch_out.wait()
        fetch_rows(number).wait()
        served[...] = jnp.zeros_like(served)
        at = pl.ds(pl.multiple_of(z * plane, plane), plane)

        def one(expert, carry):
            mid = row_plane[...].reshape(plane, width)
            up_rows = up_plane[number % 2]
            spot = pl.ds(pl.multiple_of(expert * chunk, chunk), chunk)
            spot_up = pl.ds(pl.multiple_of(hidden + expert * chunk, chunk), chunk)
            gate = jnp.sum(jnp.where(column == expert, gate_plane[number % 2], 0.0), axis=1, keepdims=True)
            gate_part = jnp.dot(mid, w_in[:, spot], preferred_element_type=single)
            up_part = jnp.dot(mid, w_in[:, spot_up], preferred_element_type=single)
            back = contract_last(up_rows, w_out[spot])
            sigmoid = 1.0 / (1.0 + jnp.exp(-gate_part))
            activated = gate_part * sigmoid
            units = activated * up_part
            scaled[at, spot] = (gate * units).astype(narrow)
            total = jnp.sum(units * back, axis=1, keepdims=True)
            served[...] += jnp.where(column == here.chip * 4 + expert, total, 0.0)
            grad = gate * back
            grads[at, spot] = (grad * up_part * (sigmoid * (1.0 + gate_part * (1.0 - sigmoid)))).astype(narrow)
            grads[at, spot_up] = (grad * activated).astype(narrow)
            return carry

        lax.fori_loop(0, 4, one, 0)
        for chip in range(RING):
            turned = jnp.transpose(served[chip * block : (chip + 1) * block])
            tables.mine[z, chip] = turned[: tables.rows]

    def row_grads(z):
        at = pl.ds(pl.multiple_of(z * plane, plane), plane)

        def one(number, carry):
            spot = pl.ds(pl.multiple_of(number * TILE, TILE), TILE)
            made = contract_last(grads[at], w_in[spot]).astype(narrow)
            for chip in range(RING):
                mids.mine[z, chip, :, spot] = made[chip * block : (chip + 1) * block]
            return carry

        lax.fori_loop(0, width // TILE, one, 0)

    def products(z):
        at = pl.ds(pl.multiple_of(z * plane, plane), plane)

        def one(number, carry):
            spot = pl.ds(pl.multiple_of(number * TILE, TILE), TILE)
            made = jnp.dot(scaled[at], w_out[:, spot], preferred_element_type=single).astype(narrow)
            for chip in range(RING):
                outs.mine[z, chip, :, spot] = made[chip * block : (chip + 1) * block]
            return carry

        lax.fori_loop(0, width // TILE, one, 0)

    for copy in fetch_plane(0):
        copy.start()
    rounds = Rounds(here, [gather])
    rounds.service(0)
    for number in range(DEPTH):
        if number + 1 < DEPTH:
            rounds.service(number + 1)
        gather_third(gather, near_first(here, number))
        if number + 1 < DEPTH:
            for copy in fetch_plane(number + 1):
                copy.start()
        hidden_units(number)

    strips = width // TILE

    def fetch_strip(number):
        spot = pl.ds(pl.multiple_of(number * TILE, TILE), TILE)
        slot = lax.rem(number, 2)
        return pltpu.make_async_copy(rows_all.at[:, :, :, spot], strip.at[slot], strip_sems.at[slot])

    def columns_of(result, stage, step=512):
        for begin in range(0, width, step):
            stage[:, begin : begin + step] = result(begin, step).astype(narrow)

    def grad_in(number, stage):
        slot = lax.rem(number, 2)
        fetch_strip(number).wait()
        pl.when(number + 1 < strips)(lambda: fetch_strip(number + 1).start())
        left = strip[slot].reshape(DEPTH * plane, TILE)
        columns_of(lambda begin, step: contract_rows(left, grads[:, begin : begin + step]), stage)

    def grad_in_parts(number, stage):
        share = hidden // 2
        at = pl.ds(pl.multiple_of(number * TILE, TILE), TILE)
        for side in range(2):
            mine, theirs = (
                stage.at[:, pl.ds(pl.multiple_of(side * hidden + core * share, 128), share)]
                for core in (here.core, 1 - here.core)
            )
            yield mine, theirs, (at, pl.ds(side * share, share))

    def grad_down(number, stage):
        half = tall // 2
        core = here.core + (1 - lax.div(number, half)) * (1 - 2 * here.core)
        at = core * half + lax.rem(number, half)
        left = scaled[:, pl.ds(pl.multiple_of(at * TILE, TILE), TILE)]
        columns_of(lambda begin, step: contract_rows(left, w_in[:, begin : begin + step]), stage)

    tall = hidden // TILE
    tiles_in = Tiles(here, stage, strips, in_sems, grad_in_parts, (gin, gin_other))

    def grad_down_store(number, away):
        slot = lax.rem(number, 2)
        rest = lax.rem(number, tall // 2)
        spot = pl.ds(pl.multiple_of(rest * TILE, TILE), TILE)
        kept, sent, came = down_sems
        if away:
            return remote(stage.at[slot], gdown_other.at[spot], sent.at[slot, 0], came.at[rest, 0], here.sibling())
        return pltpu.make_async_copy(stage.at[slot], gdown.at[spot], kept.at[slot, 0])

    def grads_down(away):
        first = 0 if away else tall // 2

        def body(number, carry):
            grad_down(number, stage.at[lax.rem(number, 2)])
            grad_down_store(number, away).start()
            return carry

        lax.fori_loop(first, first + tall // 2, body, 0)
        for number in range(first, first + tall // 2):
            copy = grad_down_store(number, away)
            copy.wait_send() if away else copy.wait()

    again = [
        pltpu.make_async_copy(ups.at[z], w_in.at[pl.ds(z * plane, plane)], loads.at[7 + z]) for z in range(DEPTH)
    ]

    def again_wait():
        for copy in again:
            copy.wait()

    fetch_strip(0).start()
    order = [far_first(here, number) for number in range(DEPTH)]
    steps = [([mids, tables], z, number == DEPTH - 1) for number, z in enumerate(order)]
    steps += [([outs], z, number == DEPTH - 1) for number, z in enumerate(order)]
    each = strips // DEPTH
    for number, (items, z, last) in enumerate(steps):
        if number < DEPTH:
            row_grads(z)
        else:
            mids.end(z, last)
            products(z)
        for item in items:
            for way in (0, 1):
                start(item.toss(z, way))
        if number:
            for item in steps[number - 1][0]:
                item.second(steps[number - 1][1])
        if number > 1:
            before, place, final = steps[number - 2]
            for item in before:
                item.third(place, final)
        if number == DEPTH - 1:
            for copy in again:
                copy.start()
        if number < DEPTH:
            tiles_in.run(number * each, (number + 1) * each, grad_in)
        elif number == DEPTH:
            again_wait()
            grads_down(True)
        elif number == DEPTH + 1:
            grads_down(False)
    outs.second(order[-1])
    outs.third(order[-2], False)
    outs.third(order[-1], True)
    for number, z in enumerate(order):
        outs.end(z, number == DEPTH - 1)
        tables.end(z, number == DEPTH - 1)
    tiles_in.heard()
    for number in range(tall // 2):
        grad_down_store(number, True).wait_recv()
    rounds.finish()


def experts_round(rows, ups, gates, win, wout, experts):
    block, width = rows.shape
    plane = RING * block
    hidden = wout.shape[0]
    total = DEPTH * plane
    vmem = pl.BlockSpec(memory_space=pltpu.VMEM)
    return pl.pallas_call(
        experts_kernel,
        out_shape=(
            jax.ShapeDtypeStruct((block, width), single),
            jax.ShapeDtypeStruct((experts, block), single),
            jax.ShapeDtypeStruct((block, width), single),
            jax.ShapeDtypeStruct((width, hidden), narrow),
            jax.ShapeDtypeStruct((width, hidden), narrow),
            jax.ShapeDtypeStruct((hidden // 2, width), narrow),
            jax.ShapeDtypeStruct((hidden // 2, width), narrow),
            jax.ShapeDtypeStruct((DEPTH, RING, block, width), narrow),
        ),
        in_specs=[HBM] * 5,
        out_specs=(vmem, vmem, vmem) + (HBM,) * 5,
        scratch_shapes=[
            pltpu.VMEM((width, 2 * hidden), narrow),
            pltpu.VMEM((hidden, width), narrow),
            pltpu.VMEM((total, 2 * hidden), narrow),
            pltpu.VMEM((total, hidden), narrow),
            pltpu.VMEM((RING, block, width), narrow),
            pltpu.VMEM((2, plane, width), narrow),
            pltpu.VMEM((2, plane, 128), single),
            pltpu.VMEM((plane, 128), single),
            pltpu.VMEM((2, DEPTH, RING, block, TILE), narrow),
            pltpu.VMEM((2, TILE, width), narrow),
            pltpu.SemaphoreType.DMA((11,)),
            pltpu.SemaphoreType.DMA((2,)),
        ]
        + GATHER_SEMS
        + sum_scratch(block, width, narrow, halves_of(block), made=True)
        + [pltpu.VMEM((DEPTH + 1, block, width), narrow)]
        + SUM_SEMS
        + sum_scratch(experts, block, single, halves_of(experts, False), made=True)
        + [
            pltpu.SemaphoreType.DMA((2, 2)),
            pltpu.SemaphoreType.DMA((2, 2)),
            pltpu.SemaphoreType.DMA((width // TILE, 2)),
        ]
        + [
            pltpu.SemaphoreType.DMA((2, 1)),
            pltpu.SemaphoreType.DMA((2, 1)),
            pltpu.SemaphoreType.DMA((hidden // TILE, 1)),
        ],
        compiler_params=pltpu.CompilerParams(
            collective_id=2, has_side_effects=True, vmem_limit_bytes=62 * 2**20
        ),
        name="experts",
    )(rows, ups, gates, win, wout)


def by_kernels():
    return lax.axis_size("dp") == DEPTH and lax.axis_size("expert") == 2 * RING


def bring_all(w_qkv, w_out, upstream, dense, gain_rows, expert_in, expert_out):
    width = upstream.shape[1]
    share = gain_rows.shape[1]
    if by_kernels():
        experts, rows = dense.shape[1], dense.shape[0]
        small = jnp.concatenate([dense.T, jnp.pad(gain_rows, ((0, 4), (0, rows - share)))], axis=0)
        wq, wo, up, all_small, weight_in, weight_down = first_gather(
            w_qkv, w_out, upstream, small, expert_in, expert_out
        )
        gains = all_small[:, :, :, experts : experts + 4, :share].transpose(3, 0, 1, 2, 4).reshape(4, -1)
        core = lax.rem(lax.axis_index("expert"), 2)
        every_gate = lax.dynamic_index_in_dim(all_small, core, axis=2, keepdims=False)[:, :, :experts]
        return (
            wq.reshape(-1, w_qkv.shape[1]),
            wo.reshape(-1, w_out.shape[1]),
            up.reshape(-1, width),
            every_gate,
            gains,
            weight_in,
            weight_down.reshape(-1, width),
        )
    everyone = ("dp", "expert")
    weight_in, weight_down = fetch_weights(expert_in, expert_out)
    return (
        lax.all_gather(w_qkv, everyone, axis=0, tiled=True),
        lax.all_gather(w_out, everyone, axis=0, tiled=True),
        gather_alike(upstream).reshape(-1, width),
        gather_alike(dense.T),
        lax.all_gather(gain_rows, everyone, axis=1, tiled=True),
        weight_in,
        weight_down,
    )


def return_halves(half_way, held):
    grad_in, grad_in_other, grad_down, grad_down_other = half_way
    total = (grad_in.astype(single) + grad_in_other.astype(single)).astype(narrow)
    rows, columns = total.shape
    cut = total.reshape(DEPTH, rows // DEPTH, columns)
    turned = lax.all_to_all(cut, "dp", split_axis=0, concat_axis=0, tiled=True)
    part = columns // (2 * held)
    share = jnp.stack(
        [
            jnp.concatenate(
                [
                    turned[z, :, (side * held + expert) * part : (side * held + expert + 1) * part]
                    for side in range(2)
                    for z in range(DEPTH)
                ],
                axis=1,
            )
            for expert in range(held)
        ]
    )
    down = grad_down.astype(single) + grad_down_other.astype(single)
    return (
        share.astype(single),
        down.reshape(held, -1, down.shape[1]),
    )


def experts_all(routed_in, up_rows, every_gate, weight_in, weight_down, held):
    depth = lax.axis_size("dp")
    owners = lax.axis_size("expert")
    chips = owners // 2
    experts = owners * held
    chip_experts = 2 * held
    rows, width = routed_in.shape
    chip = lax.axis_index("expert") // 2
    mine = lax.dynamic_slice_in_dim(every_gate, chip * chip_experts, chip_experts, axis=2)
    gate = mine.transpose(0, 1, 3, 2)
    if by_kernels():
        gate = jnp.pad(gate.reshape(DEPTH, -1, chip_experts), ((0, 0), (0, 0), (0, 128 - chip_experts)))
        ups = up_rows.reshape(DEPTH, -1, width)
        grad_routed, table, mixture, *half_way, _ = experts_round(
            routed_in, ups, gate, weight_in, weight_down, experts
        )
        return (mixture, grad_routed, table, return_halves(half_way, held))
    mid_rows = gather_alike(routed_in).reshape(-1, width)
    out, mid, served, grad_in, grad_down = expert_rounds(
        mid_rows, up_rows, gate.reshape(-1, chip_experts), weight_in, weight_down
    )
    by_gate = served.reshape(depth, chips, rows, chip_experts).transpose(0, 1, 3, 2)
    spread = jnp.zeros((depth, chips, experts, rows), single)
    spread = lax.dynamic_update_slice_in_dim(spread, by_gate, chip * chip_experts, axis=2)
    return (
        scatter_alike(out.reshape(depth, chips, rows, width)).astype(single),
        scatter_alike(mid.reshape(depth, chips, rows, width)).astype(single),
        scatter_alike(spread),
        [share.astype(single) for share in return_weights(grad_in, grad_down, held)],
    )


def deliver_all(pieces, grad_qkv, grad_out):
    owners = lax.axis_size("dp") * lax.axis_size("expert")
    share = pieces.shape[1] // owners
    if by_kernels():
        lead = (DEPTH, RING, 2)
        small = pieces.reshape(4, owners, share).transpose(1, 0, 2)
        small = jnp.pad(small, ((0, 0), (0, 4), (0, 128 - share))).reshape(lead + (8, 128))
        shares, gains = last_sum(
            grad_qkv.reshape(lead + (-1,) + grad_qkv.shape[1:]),
            grad_out.reshape(lead + (-1,) + grad_out.shape[1:]),
            small,
        )
        wide = grad_qkv.shape[1]
        return (
            gains[:4, :share],
            shares[:, :wide],
            shares[:, wide:],
        )
    everyone = ("dp", "expert")
    return (
        lax.psum_scatter(pieces, everyone, scatter_dimension=1, tiled=True),
        lax.psum_scatter(grad_qkv, everyone, scatter_dimension=0, tiled=True).astype(single),
        lax.psum_scatter(grad_out, everyone, scatter_dimension=0, tiled=True).astype(single),
    )


def local(
    tokens,
    lengths,
    expert_ids,
    gates,
    attn_gain,
    w_qkv,
    q_gain,
    k_gain,
    w_out,
    ffn_gain,
    expert_in,
    expert_out,
    out_grad,
):
    micro_count, seq_len, model_width = tokens.shape
    rows = micro_count * seq_len
    held = expert_in.shape[0]
    experts = lax.axis_size("expert") * held
    inputs = tokens.reshape(rows, model_width).astype(single)
    upstream = out_grad.reshape(rows, model_width)
    ids = expert_ids.reshape(rows, -1)
    gate_rows = gates.reshape(rows, -1)
    onehot = (ids[:, :, None] == jnp.arange(experts, dtype=jnp.int32)).astype(single)
    dense = jnp.sum(onehot * gate_rows[:, :, None], axis=1)
    gain_rows = jnp.stack([attn_gain, q_gain, k_gain, ffn_gain]).astype(single)
    weight_qkv, weight_out, up_rows, every_gate, gains, weight_in, weight_down = bring_all(
        w_qkv, w_out, upstream, dense, gain_rows, expert_in, expert_out
    )
    gain_attn, gain_query, gain_key, gain_ffn = gains[0], gains[1], gains[2], gains[3]

    normal_in, factor_in = normalize(inputs)
    normed_in = (normal_in * gain_attn).astype(narrow)
    projected = jnp.dot(normed_in, weight_qkv, preferred_element_type=single)
    normal_q, factor_q = normalize(projected[:, :model_width])
    normal_k, factor_k = normalize(projected[:, model_width : 2 * model_width])
    document, position = layout(lengths[:, 0], seq_len)
    cosine, sine = angles(position)
    query_rows = rotate(normal_q * gain_query, cosine, sine).astype(narrow).reshape(rows, -1, HEAD)
    key_rows = rotate(normal_k * gain_key, cosine, sine).astype(narrow).reshape(rows, -1, HEAD)
    value_rows = projected[:, 2 * model_width :].astype(narrow).reshape(rows, -1, HEAD)
    places = jnp.arange(rows, dtype=jnp.int32)
    allowed = (document[:, None] == document[None, :]) & (places[:, None] >= places[None, :])
    raw = jnp.einsum("qhd,khd->hqk", query_rows, key_rows, preferred_element_type=single)
    scores = jnp.where(allowed[None], raw * HEAD ** (-0.5), masked_score)
    highest = jnp.max(scores, axis=-1, keepdims=True)
    unnormed = jnp.exp(scores - highest)
    probs = unnormed / jnp.sum(unnormed, axis=-1, keepdims=True)
    attn_probs = probs.astype(narrow)
    attended = (
        jnp.einsum("hqk,khd->qhd", attn_probs, value_rows, preferred_element_type=single)
        .reshape(rows, model_width)
        .astype(narrow)
    )
    middle = inputs + jnp.dot(attended, weight_out, preferred_element_type=single)
    normal_mid, factor_mid = normalize(middle)
    routed_in = (normal_mid * gain_ffn).astype(narrow)

    mixture, grad_routed, gate_table, (share_in, share_down) = experts_all(
        routed_in, up_rows, every_gate, weight_in, weight_down, held
    )
    grad_gates = jnp.sum(onehot * gate_table.T[:, None, :], axis=2)
    results = (middle + mixture).astype(narrow)

    grad_mid, piece_ffn = rms_back(grad_routed, normal_mid, factor_mid, gain_ffn)
    grad_middle = upstream.astype(single) + grad_mid
    grad_branch = grad_middle.astype(narrow)
    grad_out_part = contract_rows(attended, grad_branch, narrow)
    grad_attended = contract_last(grad_branch, weight_out).astype(narrow).reshape(rows, -1, HEAD)
    grad_probs = jnp.einsum("qhd,khd->hqk", grad_attended, value_rows, preferred_element_type=single)
    inner = jnp.sum(grad_probs * probs, axis=-1, keepdims=True)
    grad_scores = (probs * (grad_probs - inner)).astype(narrow)
    grad_query = jnp.einsum(
        "hqk,khd->qhd", grad_scores, key_rows, preferred_element_type=single
    ) * HEAD ** (-0.5)
    grad_key = jnp.einsum(
        "hqk,qhd->khd", grad_scores, query_rows, preferred_element_type=single
    ) * HEAD ** (-0.5)
    grad_value = jnp.einsum("hqk,qhd->khd", attn_probs, grad_attended, preferred_element_type=single)
    grad_q_raw, piece_query = rms_back(
        rotate(grad_query.reshape(rows, model_width), cosine, -sine), normal_q, factor_q, gain_query
    )
    grad_k_raw, piece_key = rms_back(
        rotate(grad_key.reshape(rows, model_width), cosine, -sine), normal_k, factor_k, gain_key
    )
    grad_qkv = jnp.concatenate(
        [grad_q_raw, grad_k_raw, grad_value.reshape(rows, model_width)], axis=1
    ).astype(narrow)
    grad_qkv_part = contract_rows(normed_in, grad_qkv, narrow)
    grad_normed = contract_last(grad_qkv, weight_qkv)
    grad_input, piece_attn = rms_back(grad_normed, normal_in, factor_in, gain_attn)
    grad_tokens = grad_middle + grad_input

    pieces = jnp.stack([piece_attn, piece_query, piece_key, piece_ffn])
    gain_sums, grad_qkv_share, grad_out_share = deliver_all(pieces, grad_qkv_part, grad_out_part)
    shape = (micro_count, seq_len, model_width)
    return (
        results.reshape(shape),
        grad_tokens.reshape(shape),
        grad_gates.reshape(expert_ids.shape),
        gain_sums[0],
        grad_qkv_share,
        gain_sums[1],
        gain_sums[2],
        grad_out_share,
        gain_sums[3],
        share_in,
        share_down,
    )


def solution(mesh):
    by_rows = P(None, ("dp", "expert"), None)
    flat = P(("dp", "expert"))
    split = P(("dp", "expert"), None)
    held = P("expert", "dp", None)
    return jax.shard_map(
        local,
        mesh=mesh,
        in_specs=(
            by_rows, by_rows, by_rows, by_rows, flat, split, flat, flat, split, flat, held, held, by_rows,
        ),
        out_specs=(by_rows, by_rows, by_rows, flat, split, flat, flat, split, flat, held, held),
        check_vma=False,
    )
```

```python
import jax
import jax.numpy as jnp
from jax import lax
from jax.experimental import pallas as pl
from jax.experimental.pallas import tpu as pltpu
from jax.sharding import PartitionSpec as P

HEAD = 128
epsilon = 1e-05
base_theta = 10000.0
masked_score = -1e30
single = jnp.float32
narrow = jnp.bfloat16


def normalize(values):
    factor = lax.rsqrt(jnp.mean(values * values, axis=-1, keepdims=True) + epsilon)
    return (values * factor, factor)


def rms_back(upstream, normal, factor, gain):
    weighted = upstream * gain
    inner = jnp.mean(weighted * normal, axis=-1, keepdims=True)
    return (factor * (weighted - normal * inner), jnp.sum(upstream * normal, axis=0))


def angles(position):
    half = HEAD // 2
    ladder = jnp.arange(half, dtype=single) * (2.0 / HEAD)
    frequency = jnp.exp(-jnp.log(base_theta) * ladder)
    angle = position.astype(single)[:, None] * frequency[None, :]
    return (jnp.cos(angle)[:, None, :], jnp.sin(angle)[:, None, :])


def rotate(field, cosine, sine):
    length = field.shape[0]
    heads = field.reshape(length, -1, HEAD)
    half = HEAD // 2
    first = heads[..., :half]
    second = heads[..., half:]
    turned = jnp.concatenate(
        [first * cosine - second * sine, second * cosine + first * sine], axis=-1
    )
    return turned.reshape(length, -1)


def layout(doc_lengths, length):
    packs, count = doc_lengths.shape
    upto = jnp.arange(count)[None, :] <= jnp.arange(count)[:, None]
    ends = jnp.sum(jnp.where(upto[None], doc_lengths[:, None, :], 0), axis=2)
    starts = ends - doc_lengths
    places = jnp.arange(length, dtype=jnp.int32)[None, :, None]
    document = jnp.sum((places >= ends[:, None, :]).astype(jnp.int32), axis=2)
    member = (places >= starts[:, None, :]) & (places < ends[:, None, :])
    first_place = jnp.sum(jnp.where(member, starts[:, None, :], 0), axis=2)
    document = document + (count + 1) * jnp.arange(packs, dtype=jnp.int32)[:, None]
    return (document.reshape(-1), (places[..., 0] - first_place).reshape(-1))


def contract_rows(left, right, kind=single):
    return lax.dot_general(left, right, (((0,), (0,)), ((), ())), preferred_element_type=kind)


def contract_last(left, right, kind=single):
    return lax.dot_general(left, right, (((1,), (1,)), ((), ())), preferred_element_type=kind)


def core_groups():
    return [[2 * chip + core for chip in range(lax.axis_size("expert") // 2)] for core in range(2)]


def chip_groups():
    return [[2 * chip, 2 * chip + 1] for chip in range(lax.axis_size("expert") // 2)]


def gather_alike(block):
    column = lax.all_gather(block, "dp", axis=0)
    return lax.all_gather(column, "expert", axis=1, axis_index_groups=core_groups())


def scatter_alike(blocks):
    column = lax.psum_scatter(
        blocks, "expert", scatter_dimension=1, axis_index_groups=core_groups()
    )
    return lax.psum_scatter(column, "dp", scatter_dimension=0)


def fetch_weights(expert_in, expert_out):
    depth = lax.axis_size("dp")
    held, rows, columns = expert_in.shape
    part = columns // (2 * depth)
    cut = expert_in.reshape(held, rows, 2, depth, part)
    turned = lax.all_to_all(cut, "dp", split_axis=3, concat_axis=1, tiled=True)
    both = lax.all_gather(turned[:, :, :, 0], "expert", axis=0, axis_index_groups=chip_groups())
    weight_in = both.transpose(2, 3, 0, 1, 4).reshape(depth * rows, 4 * held * part)
    weight_down = lax.all_gather(
        expert_out, "expert", axis=0, axis_index_groups=chip_groups()
    ).reshape(-1, expert_out.shape[2])
    return (weight_in, weight_down)


def return_weights(grad_in, grad_down, held):
    depth = lax.axis_size("dp")
    rows, columns = grad_in.shape
    part = columns // (4 * held)
    cut = grad_in.reshape(rows, 2, 2, held, part)
    own = lax.psum_scatter(cut, "expert", scatter_dimension=2, axis_index_groups=chip_groups())
    own = own.reshape(depth, rows // depth, 2, held, part)
    turned = lax.all_to_all(own, "dp", split_axis=0, concat_axis=0)
    share_in = turned.transpose(3, 1, 2, 0, 4).reshape(held, rows // depth, 2 * depth * part)
    down = grad_down.reshape(2, held, part, grad_down.shape[1])
    share_down = lax.psum_scatter(
        down, "expert", scatter_dimension=0, axis_index_groups=chip_groups()
    )
    return (share_in, share_down)


def expert_round(mid_rows, up_rows, gate, weight_in, weight_down):
    count = gate.shape[1]
    part = weight_down.shape[0] // count
    wide = jnp.broadcast_to(gate[:, :, None], gate.shape + (part,)).reshape(gate.shape[0], -1)
    gate_up = jnp.dot(mid_rows, weight_in, preferred_element_type=single)
    hidden_units = gate_up.shape[1] // 2
    gate_part = gate_up[:, :hidden_units]
    up_part = gate_up[:, hidden_units:]
    sigmoid = jax.nn.sigmoid(gate_part)
    activated = gate_part * sigmoid
    hidden = activated * up_part
    back = contract_last(up_rows, weight_down)
    scaled = (wide * hidden).astype(narrow)
    piece_out = jnp.dot(scaled, weight_down, preferred_element_type=narrow)
    piece_gates = jnp.sum((hidden * back).reshape(-1, count, part), axis=2)
    grad_hidden = wide * back
    grad_gate = grad_hidden * up_part * sigmoid * (1.0 + gate_part * (1.0 - sigmoid))
    grad_up = grad_hidden * activated
    grad_gate_up = jnp.concatenate([grad_gate, grad_up], axis=1).astype(narrow)
    piece_mid = contract_last(grad_gate_up, weight_in, narrow)
    return (piece_out, piece_mid, piece_gates, grad_gate_up, scaled)


def expert_rounds(mid_rows, up_rows, gate, weight_in, weight_down):
    total = mid_rows.shape[0]
    rounds = max(1, total // 2048)

    def one(sums, pieces):
        mid, up, weights = pieces
        piece_out, piece_mid, piece_gates, grad_gate_up, scaled = expert_round(
            mid, up, weights, weight_in, weight_down
        )
        grads = (contract_rows(mid, grad_gate_up), contract_rows(scaled, up))
        return (jax.tree.map(jnp.add, sums, grads), (piece_out, piece_mid, piece_gates))

    if rounds == 1:
        piece_out, piece_mid, piece_gates, grad_gate_up, scaled = expert_round(
            mid_rows, up_rows, gate, weight_in, weight_down
        )
        grads = (contract_rows(mid_rows, grad_gate_up, narrow), contract_rows(scaled, up_rows, narrow))
        return (piece_out, piece_mid, piece_gates) + grads
    start = (jnp.zeros(weight_in.shape, single), jnp.zeros(weight_down.shape, single))
    cut = jax.tree.map(lambda a: a.reshape(rounds, total // rounds, -1), (mid_rows, up_rows, gate))
    sums, made = lax.scan(one, start, cut)
    made = jax.tree.map(lambda a: a.reshape(total, -1), made)
    return made + (sums[0].astype(narrow), sums[1].astype(narrow))


MESH = pl.DeviceIdType.MESH
HBM = pl.BlockSpec(memory_space=pl.ANY)
DEPTH = 4
RING = 4


def ring_turn(number):
    high = lax.div(number, 2)
    return number + high * (1 - 2 * lax.rem(number, 2))


class Here:
    def __init__(self):
        number = lax.axis_index("expert")
        self.z = lax.axis_index("dp")
        self.core = lax.rem(number, 2)
        self.chip = lax.div(number, 2)
        self.q = ring_turn(self.chip)

    def chip_at(self, turn):
        return ring_turn(lax.rem(self.q + turn + RING, RING))

    def beside(self, turn):
        return (self.z, 2 * self.chip_at(turn) + self.core)

    def above(self, steps):
        return (lax.rem(self.z + steps + DEPTH, DEPTH), 2 * self.chip + self.core)

    def sibling(self):
        return (self.z, 2 * self.chip + 1 - self.core)

    def meet(self):
        barrier = pltpu.get_barrier_semaphore()
        others = [self.beside(1), self.beside(-1), self.sibling()]
        others += [self.above(steps) for steps in range(1, DEPTH)]
        for other in others:
            pl.semaphore_signal(barrier, inc=1, device_id=other, device_id_type=MESH)
        pl.semaphore_wait(barrier, len(others))


def remote(source, target, sent, arrived, device):
    return pltpu.make_async_remote_copy(
        src_ref=source,
        dst_ref=target,
        send_sem=sent,
        recv_sem=arrived,
        device_id=device,
        device_id_type=MESH,
    )


GATHER_SEMS = [
    pltpu.SemaphoreType.DMA((2, 2, DEPTH - 1)),
    pltpu.SemaphoreType.DMA((2, DEPTH, 2, 2)),
    pltpu.SemaphoreType.DMA((2, DEPTH)),
    pltpu.SemaphoreType.DMA((1,)),
]


class Gather:
    def __init__(self, here, source, whole, halves, shared, sems):
        self.here, self.source, self.whole, self.halves, self.shared = here, source, whole, halves, shared
        self.line, self.ring, self.pair, self.own = sems

    def block(self, z, turn):
        chip = self.here.chip_at(turn)
        return self.whole.at[z, chip, self.here.core] if self.shared else self.whole.at[z, chip]

    def keep(self):
        return pltpu.make_async_copy(self.source, self.block(self.here.z, 0), self.own.at[0])

    def along(self, step, way, first):
        z = self.here.z - step + 1 if way == 0 else self.here.z + step - 1
        block = self.block(z, 0)
        return remote(
            self.source if first else block,
            block,
            self.line.at[0, way, step - 1],
            self.line.at[1, way, step - 1],
            self.here.above(1 if way == 0 else -1),
        )

    def round(self, z, way, first=False):
        turn = 1 if way == 0 else -1
        block = self.block(z, 0)
        return remote(
            self.source if first else block,
            block,
            self.ring.at[0, z, way, 0],
            self.ring.at[1, z, way, 0],
            self.here.beside(turn),
        )

    def heard(self, z, way):
        block = self.block(z, -1 if way == 0 else 1)
        return remote(
            block, block, self.ring.at[0, z, way, 0], self.ring.at[1, z, way, 0], self.here.beside(1)
        )

    def onward(self, z, way, mine):
        if self.halves[way] is None:
            return None
        turn = (-1 if mine else -2) if way == 0 else (1 if mine else 2)
        block = self.block(z, turn).at[pl.ds(*self.halves[way])]
        return remote(
            block,
            block,
            self.ring.at[0, z, way, 1],
            self.ring.at[1, z, way, 1],
            self.here.beside(1 if way == 0 else -1),
        )

    def swap(self, z, mine):
        core = self.here.core if mine else 1 - self.here.core
        part = self.whole.at[z, :, core]
        return remote(part, part, self.pair.at[0, z], self.pair.at[1, z], self.here.sibling())


def start(copy):
    if copy is not None:
        copy.start()


def gather_third(item, z):
    for way in (0, 1):
        copy = item.onward(z, way, False)
        if copy is not None:
            copy.wait_recv()


class Rounds:
    def __init__(self, here, items):
        self.here, self.items = here, items
        for item in items:
            item.keep().start()
            for way in (0, 1):
                self.depart(0, way, item)
            for way in (0, 1):
                item.round(here.z, way, True).start()

    def depart(self, step, way, item):
        here = self.here
        ahead = here.z + 1 < DEPTH if way == 0 else here.z >= 1
        pl.when(ahead)(lambda: item.along(step + 1, way, step == 0).start())

    def places(self, step, body):
        here = self.here
        if step == 0:
            body(here.z, 0)
            return
        pl.when(here.z >= step)(lambda: body(here.z - step, 0))
        pl.when(here.z + step < DEPTH)(lambda: body(here.z + step, 1))

    def service(self, step):
        items, here = self.items, self.here

        def first(z, way):
            for item in items:
                block = item.block(z, 0)
                remote(
                    block, block, item.line.at[0, way, step], item.line.at[1, way, step], here.above(1)
                ).wait_recv()
                if step + 2 < DEPTH:
                    self.depart(step + 1, way, item)
                for side in (0, 1):
                    item.round(z, side).start()

        def second(z, way):
            for item in items:
                for side in (0, 1):
                    item.heard(z, side).wait_recv()
                    start(item.onward(z, side, True))

        if step + 1 < DEPTH:
            self.places(step + 1, first)
        if step == 0:
            for item in items:
                item.keep().wait()
        self.places(step, second)

    def third(self, step):
        def body(z, way):
            for item in self.items:
                gather_third(item, z)
                if item.shared:
                    item.swap(z, True).start()

        self.places(step, body)

    def finish(self):
        def settle(z, way):
            for item in self.items:
                for side in (0, 1):
                    item.round(z, side).wait_send()
                    copy = item.onward(z, side, True)
                    if copy is not None:
                        copy.wait_send()
                if item.shared:
                    item.swap(z, True).wait_send()
                    item.swap(z, False).wait_recv()

        for step in range(DEPTH):
            self.places(step, settle)
        here = self.here
        for item in self.items:
            for step in range(DEPTH - 1):
                for way in (0, 1):

                    def sent(z, side, step=step, way=way, item=item):
                        if step and side != way:
                            return
                        ahead = here.z + 1 < DEPTH if way == 0 else here.z >= 1
                        pl.when(ahead)(lambda: item.along(step + 1, way, step == 0).wait_send())

                    self.places(step, sent)


class Recut:
    def __init__(self, here, source_in, source_out, whole_in, whole_out, sems):
        self.here, self.source_in, self.source_out = here, source_in, source_out
        self.whole_in, self.whole_out = whole_in, whole_out
        self.cut, self.pair, self.down, self.own = sems
        self.held, self.rows, columns = source_in.shape
        self.hidden = columns // 2
        self.part = self.hidden // DEPTH

    def pieces(self, steps, arriving):
        here, copies = self.here, []
        mine = lax.rem(here.z + DEPTH - steps, DEPTH) if arriving else here.z
        away = lax.rem(here.z + steps, DEPTH)
        for side in range(2):
            for expert in range(self.held):
                columns = side * self.held * 2 * self.part + (here.core * self.held + expert) * self.part
                target = self.whole_in.at[
                    pl.ds(pl.multiple_of(mine * self.rows, 16), self.rows),
                    pl.ds(pl.multiple_of(columns, 128), self.part),
                ]
                source = self.source_in.at[
                    expert, :, pl.ds(pl.multiple_of(side * self.hidden + away * self.part, 128), self.part)
                ]
                spot = (steps, side * self.held + expert)
                if steps == 0:
                    copies.append(pltpu.make_async_copy(source, target, self.own.at[spot[1]]))
                else:
                    copies.append(
                        remote(
                            target if arriving else source,
                            target,
                            self.cut.at[(0,) + spot],
                            self.cut.at[(1,) + spot],
                            here.above(steps),
                        )
                    )
        return copies

    def across(self, steps, mine):
        here, copies = self.here, []
        core = here.core if mine else 1 - here.core
        row = lax.rem(here.z + DEPTH - steps, DEPTH)
        width = self.held * self.part
        for side in range(2):
            spot = self.whole_in.at[
                pl.ds(pl.multiple_of(row * self.rows, 16), self.rows),
                pl.ds(pl.multiple_of(side * 2 * width + core * width, 128), width),
            ]
            copies.append(
                remote(spot, spot, self.pair.at[0, steps, side], self.pair.at[1, steps, side], here.sibling())
            )
        return copies

    def lower(self, mine):
        here = self.here
        core = here.core if mine else 1 - here.core
        spot = self.whole_out.at[pl.ds(core * self.held, self.held)]
        return remote(
            self.source_out if mine else spot, spot, self.down.at[0], self.down.at[1], here.sibling()
        )

    def lower_own(self):
        return pltpu.make_async_copy(
            self.source_out, self.whole_out.at[pl.ds(self.here.core * self.held, self.held)], self.own.at[4]
        )

    def begin(self):
        for copy in self.pieces(0, False):
            copy.start()
        self.lower_own().start()
        self.lower(True).start()
        for steps in range(1, DEPTH):
            for copy in self.pieces(steps, False):
                copy.start()

    def relay(self):
        for steps in range(DEPTH):
            for copy in self.pieces(steps, True):
                copy.wait() if steps == 0 else copy.wait_recv()
            for copy in self.across(steps, True):
                copy.start()

    def end(self):
        self.lower_own().wait()
        self.lower(True).wait_send()
        self.lower(False).wait_recv()
        for steps in range(DEPTH):
            if steps:
                for copy in self.pieces(steps, False):
                    copy.wait_send()
            for copy in self.across(steps, True):
                copy.wait_send()
            for copy in self.across(steps, False):
                copy.wait_recv()


RECUT_SEMS = [
    pltpu.SemaphoreType.DMA((2, DEPTH, 4)),
    pltpu.SemaphoreType.DMA((2, DEPTH, 2)),
    pltpu.SemaphoreType.DMA((2,)),
    pltpu.SemaphoreType.DMA((5,)),
]


def halves_of(rows, split=True):
    return ((0, rows // 2), (rows // 2, rows - rows // 2)) if split else ((0, rows), None)


def first_gather_kernel(wq, wo, up, small, ein, eout, wq_all, wo_all, up_all, small_all, win, wout, *sems):
    here = Here()
    here.meet()
    items = []
    for number, (source, whole, halves, shared) in enumerate(
        (
            (small, small_all, halves_of(small.shape[0], False), True),
            (wq, wq_all, halves_of(wq.shape[0]), True),
            (wo, wo_all, halves_of(wo.shape[0]), True),
            (up, up_all, halves_of(up.shape[0]), False),
        )
    ):
        items.append(Gather(here, source, whole, halves, shared, sems[4 * number : 4 * number + 4]))
    recut = Recut(here, ein, eout, win, wout, sems[16:20])
    rounds = Rounds(here, items)
    for step in range(DEPTH):
        rounds.service(step)
        if step == 0:
            recut.begin()
        else:
            rounds.third(step - 1)
    rounds.third(DEPTH - 1)
    recut.relay()
    rounds.finish()
    recut.end()


def first_gather(wq, wo, up, small, ein, eout):
    def whole(array, shared):
        lead = (DEPTH, RING, 2) if shared else (DEPTH, RING)
        return jax.ShapeDtypeStruct(lead + array.shape, array.dtype)

    held, rows, columns = ein.shape
    return pl.pallas_call(
        first_gather_kernel,
        out_shape=(
            whole(wq, True),
            whole(wo, True),
            whole(up, False),
            whole(small, True),
            jax.ShapeDtypeStruct((DEPTH * rows, columns), ein.dtype),
            jax.ShapeDtypeStruct((2 * held,) + eout.shape[1:], eout.dtype),
        ),
        in_specs=[HBM] * 6,
        out_specs=(HBM,) * 6,
        scratch_shapes=GATHER_SEMS * 4 + RECUT_SEMS,
        compiler_params=pltpu.CompilerParams(collective_id=1, has_side_effects=True),
        name="bring",
    )(wq, wo, up, small, ein, eout)

def add_up(target, terms, rows, columns):
    high = 16 if rows % 16 == 0 else 8
    wide = min(columns, 1024)
    across = columns // wide

    def piece(number, carry):
        row = pl.multiple_of(lax.div(number, across) * high, high)
        column = pl.multiple_of(lax.rem(number, across) * wide, 128)
        spot = (pl.ds(row, high), pl.ds(column, wide))
        total = terms[0][spot].astype(single)
        for term in terms[1:]:
            total = total + term[spot].astype(single)
        target[spot] = total.astype(target.dtype)
        return carry

    lax.fori_loop(0, (rows // high) * across, piece, 0)


SUM_SEMS = [
    pltpu.SemaphoreType.DMA((2, DEPTH, 2)),
    pltpu.SemaphoreType.DMA((2, DEPTH, 2)),
    pltpu.SemaphoreType.DMA((2, 2, DEPTH)),
    pltpu.SemaphoreType.DMA((DEPTH, RING, 2)),
]


def sum_scratch(rows, columns, kind, halves, paired=False, made=False):
    high = max(size for _, size in filter(None, halves))
    kept = RING if paired or made else RING - 1
    scratch = [
        pltpu.VMEM((DEPTH, kept, rows, columns), kind),
        pltpu.VMEM((DEPTH, 2, high, columns), kind),
        pltpu.VMEM((DEPTH, 2, rows, columns), kind),
        pltpu.VMEM((DEPTH + 1, rows, columns), kind),
    ] + SUM_SEMS
    if paired:
        scratch += [pltpu.VMEM((DEPTH, RING, rows, columns), kind), pltpu.SemaphoreType.DMA((2, DEPTH, 2))]
    return scratch


class Sum:
    def __init__(self, here, sources, target, halves, paired, scratch):
        self.here, self.sources, self.halves, self.paired = here, sources, halves, paired
        self.target = target if isinstance(target, list) else [(target, 0, target.shape[0])]
        self.mine, self.half, self.full, self.column = scratch[:4]
        self.half_sem, self.full_sem, self.line_sem, self.load_sem = scratch[4:8]
        if paired:
            self.other, self.pair_sem = scratch[8:10]
        self.rows, self.columns = self.mine.shape[2:]

    def kept(self, z, turn):
        if self.sources is None:
            return self.mine.at[z, self.here.chip_at(turn)]
        return self.mine.at[z, turn if self.paired else {0: 0, 1: 1, 3: 2}[turn]]

    def raw(self, part, z, turn):
        chip = self.here.chip_at(turn)
        return part.at[z, chip, self.here.core] if self.paired else part.at[z, chip]

    def spots(self):
        at, spots = 0, []
        for part in self.sources or []:
            spots.append((part, pl.ds(at, part.shape[-1])))
            at += part.shape[-1]
        return spots

    def loads(self, z, turn):
        return [
            pltpu.make_async_copy(
                self.raw(part, z, turn), self.kept(z, turn).at[:, spot], self.load_sem.at[z, turn, number]
            )
            for number, (part, spot) in enumerate(self.spots())
        ]

    def swaps(self, z, mine):
        return [
            remote(
                part.at[z, :, 1 - self.here.core] if mine else self.other.at[z, :, :, spot],
                self.other.at[z, :, :, spot],
                self.pair_sem.at[0, z, number],
                self.pair_sem.at[1, z, number],
                self.here.sibling(),
            )
            for number, (part, spot) in enumerate(self.spots())
        ]

    def toss(self, z, way):
        if self.halves[way] is None:
            return None
        rows = pl.ds(*self.halves[way])
        loaded = self.sources is not None and not self.paired
        source = (self.raw(self.sources[0], z, 2) if loaded else self.kept(z, 2)).at[rows]
        return remote(
            source,
            self.half.at[z, way, pl.ds(0, self.halves[way][1])],
            self.half_sem.at[0, z, way],
            self.half_sem.at[1, z, way],
            self.here.beside(1 if way == 0 else -1),
        )

    def pass_on(self, z, way):
        return remote(
            self.kept(z, 1 if way == 0 else 3),
            self.full.at[z, way],
            self.full_sem.at[0, z, way],
            self.full_sem.at[1, z, way],
            self.here.beside(1 if way == 0 else -1),
        )

    def climb(self, z, way, up, slot=None):
        if slot is None:
            down_to_owner = way * (z == self.here.z - 1).astype(jnp.int32)
            slot = z + down_to_owner * (DEPTH - z)
        return remote(
            self.kept(z, 0),
            self.column.at[slot],
            self.line_sem.at[0, way, z],
            self.line_sem.at[1, way, z],
            self.here.above(2 * up - 1),
        )

    def begin(self, z):
        if self.paired:
            for copy in self.swaps(z, True):
                copy.start()
        for turn in (2, 1, 3, 0):
            if turn != 2 or self.paired:
                for copy in self.loads(z, turn):
                    copy.start()
        if not self.paired:
            for way in (0, 1):
                start(self.toss(z, way))

    def merge(self, z):
        if not self.paired:
            return
        for copy in self.swaps(z, False):
            copy.wait_recv()
        for turn in (2, 1, 3, 0):
            for copy in self.loads(z, turn):
                copy.wait()
            kept = self.kept(z, turn)
            add_up(kept, [kept, self.other.at[z, self.here.chip_at(turn)]], self.rows, self.columns)
            if turn == 2:
                for way in (0, 1):
                    start(self.toss(z, way))

    def second(self, z):
        for way, turn in ((0, 1), (1, 3)):
            if not self.paired:
                for copy in self.loads(z, turn):
                    copy.wait()
            copy = self.toss(z, way)
            if copy is not None:
                copy.wait_recv()
                begin, size = self.halves[way]
                rows = self.kept(z, turn).at[pl.ds(begin, size)]
                add_up(rows, [rows, self.half.at[z, way, pl.ds(0, size)]], size, self.columns)
        for way in (0, 1):
            self.pass_on(z, way).start()

    def third(self, z, last):
        here = self.here
        if not self.paired:
            for copy in self.loads(z, 0):
                copy.wait()
        for way in (0, 1):
            self.pass_on(z, way).wait_recv()
        kept = self.kept(z, 0)
        terms = [kept, self.full.at[z, 0], self.full.at[z, 1]]
        if last:
            self.arrive(z, terms)
            return
        up = (z > here.z).astype(jnp.int32)
        way = 1 - up
        follows = up * here.z + way * (DEPTH - 1 - here.z)

        @pl.when(follows > 0)
        def _():
            self.climb(z, way, up, z).wait_recv()
            add_up(kept, terms + [self.column.at[z]], self.rows, self.columns)

        @pl.when(follows == 0)
        def _():
            add_up(kept, terms, self.rows, self.columns)

        self.climb(z, way, up).start()

    def own_part(self, z):
        for way in (0, 1):
            self.pass_on(z, way).wait_recv()
        [(target, _, rows)] = self.target
        add_up(target, [self.kept(z, 0), self.full.at[z, 0], self.full.at[z, 1]], rows, self.columns)

    def own_rest(self, z):
        self.arrive(z, [self.target[0][0]])

    def arrive(self, z, terms):
        here = self.here
        below, above = self.column.at[z], self.column.at[DEPTH]

        def total(more):
            for target, row, rows in self.target:
                part = [term.at[pl.ds(row, rows)] for term in terms + more]
                add_up(target, part, rows, self.columns)

        @pl.when(here.z == 0)
        def _():
            self.climb(z, 1, 0, DEPTH).wait_recv()
            total([above])

        @pl.when(here.z == DEPTH - 1)
        def _():
            self.climb(z, 0, 0, z).wait_recv()
            total([below])

        @pl.when((here.z > 0) & (here.z < DEPTH - 1))
        def _():
            self.climb(z, 0, 0, z).wait_recv()
            self.climb(z, 1, 0, DEPTH).wait_recv()
            total([below, above])

    def end(self, z, last):
        if self.paired:
            for copy in self.swaps(z, True):
                copy.wait_send()
        for way in (0, 1):
            copy = self.toss(z, way)
            if copy is not None:
                copy.wait_send()
            self.pass_on(z, way).wait_send()
        if not last:
            up = (z > self.here.z).astype(jnp.int32)
            self.climb(z, 1 - up, up).wait_send()


def far_first(here, number):
    high = lax.div(here.z, 2)
    inner = lax.rem(lax.div(here.z + 1, 2), 2)
    low = (DEPTH - 1 - number) + inner * (0, -2, 1, 1)[number]
    return low + high * (DEPTH - 1 - 2 * low)


def last_sum_kernel(
    normed, grad, attended, branch, small, q_sum, o_sum, small_sum, left, left_out, right, sems, *scratch
):
    here = Here()
    here.meet()
    block, width = normed.shape
    share = q_sum.shape[0]
    wide = grad.shape[1]
    sides = wide // width
    moved = [
        (normed, left, None),
        (grad, right, pl.ds(0, wide)),
        (attended, left_out, None),
        (branch, right, pl.ds(wide, width)),
    ]
    copies = []
    for number, (source, target, spot) in enumerate(moved):
        own, other = (target.at[core] if spot is None else target.at[core, :, spot] for core in (0, 1))
        copies.append(
            (
                pltpu.make_async_copy(source, own, sems.at[number]),
                remote(source, other, sems.at[4 + number], sems.at[8 + number], here.sibling()),
            )
        )
    for kept, sent in copies:
        sent.start()
        kept.start()
    targets = [(q_sum.at[:, pl.ds(side * width, width)], side * share, share) for side in range(sides)]
    targets.append((o_sum, sides * share, share))
    big = Sum(here, None, targets, halves_of((sides + 1) * share), False, scratch[0:8])
    few = Sum(here, [small], small_sum, halves_of(small.shape[3], False), True, scratch[8:18])
    order = [far_first(here, number) for number in range(DEPTH)]
    for z in order:
        few.begin(z)
    for kept, sent in copies:
        kept.wait()
        sent.wait_recv()
    step = 512
    each = width // step
    rows = RING * 2 * share

    def make(z):
        at = pl.ds(pl.multiple_of(z * rows, rows), rows)

        def piece(number, source):
            spot = pl.ds(pl.multiple_of(number * step, step), step)
            turned = source[:, :, at].reshape(2 * block, rows)
            made = contract_rows(turned, right[:, :, spot].reshape(2 * block, step))
            made = made.reshape(RING, 2, share, step)
            mine = jnp.where(here.core == 0, made[:, 0], made[:, 1]).astype(narrow)
            row = pl.multiple_of(lax.div(number, each) * share, share)
            column = pl.multiple_of(lax.rem(number, each) * step, step)
            for chip in range(RING):
                big.mine[z, chip, pl.ds(row, share), pl.ds(column, step)] = mine[chip]

        def qkv(number, carry):
            piece(number, left)
            return carry

        def out(number, carry):
            piece(number, left_out)
            return carry

        lax.fori_loop(0, sides * each, qkv, 0)
        lax.fori_loop(sides * each, (sides + 1) * each, out, 0)

    items = [big, few]
    for number, z in enumerate(order):
        make(z)
        for way in (0, 1):
            start(big.toss(z, way))
        few.merge(z)
        if number:
            for item in items:
                item.second(order[number - 1])
        if number > 1:
            for item in items:
                item.third(order[number - 2], False)
    for item in items:
        item.second(order[-1])
    for item in items:
        item.third(order[-2], False)
    for item in items:
        item.third(order[-1], True)
    for number, z in enumerate(order):
        for item in items:
            item.end(z, number == DEPTH - 1)
    for kept, sent in copies:
        sent.wait_send()


def last_sum(normed, grad, attended, branch, small, share):
    block, width = normed.shape
    wide = grad.shape[1]
    rows = (wide // width + 1) * share
    vmem = pl.BlockSpec(memory_space=pltpu.VMEM)
    return pl.pallas_call(
        last_sum_kernel,
        out_shape=(
            jax.ShapeDtypeStruct((share, wide), single),
            jax.ShapeDtypeStruct((share, width), single),
            jax.ShapeDtypeStruct(small.shape[3:], single),
        ),
        in_specs=[HBM] * 5,
        out_specs=(vmem, vmem, vmem),
        scratch_shapes=[
            pltpu.VMEM((2, block, width), narrow),
            pltpu.VMEM((2, block, width), narrow),
            pltpu.VMEM((2, block, wide + width), narrow),
            pltpu.SemaphoreType.DMA((12,)),
        ]
        + sum_scratch(rows, width, narrow, halves_of(rows), made=True)
        + sum_scratch(small.shape[3], small.shape[4], single, halves_of(small.shape[3], False), paired=True),
        compiler_params=pltpu.CompilerParams(
            collective_id=4, has_side_effects=True, vmem_limit_bytes=62 * 2**20
        ),
        name="deliver",
    )(normed, grad, attended, branch, small)

def near_first(here, number):
    high = lax.div(here.z, 2)
    inner = lax.rem(lax.div(here.z + 1, 2), 2)
    low = number + inner * (1, -1, 0, 0)[number]
    return low + high * (DEPTH - 1 - 2 * low)


TILE = 256


class Tiles:
    def __init__(self, here, stage, count, sems, parts, targets):
        self.here, self.stage, self.count = here, stage, count
        self.kept, self.sent, self.came = sems
        self.parts, self.targets = parts, targets

    def copies(self, number, keep=True, give=True):
        slot = lax.rem(number, 2)
        own, other = self.targets
        made = []
        for piece, (mine, theirs, spot) in enumerate(self.parts(number, self.stage.at[slot])):
            if keep:
                made.append(pltpu.make_async_copy(mine, own.at[spot], self.kept.at[slot, piece]))
            if give:
                sems = (self.sent.at[slot, piece], self.came.at[number, piece])
                made.append(remote(theirs, other.at[spot], *sems, self.here.sibling()))
        return made

    def settle(self, number):
        for copy in self.copies(number, give=False):
            copy.wait()
        for copy in self.copies(number, keep=False):
            copy.wait_send()

    def run(self, first, last, make):
        def body(number, carry):
            pl.when(number >= 2)(lambda: self.settle(number - 2))
            make(number, self.stage.at[lax.rem(number, 2)])
            for copy in self.copies(number):
                copy.start()
            return carry

        lax.fori_loop(first, last, body, 0)
        if last == self.count:
            for number in (last - 2, last - 1):
                self.settle(number)

    def heard(self):
        for number in range(self.count):
            for copy in self.copies(number, keep=False):
                copy.wait_recv()


def experts_kernel(
    rows, ups, gates, win, wout, mid_sum, gate_sum, out_sum, gin, gin_other, gdown, gdown_other, rows_all, *scratch
):
    here = Here()
    here.meet()
    (
        w_in, w_out, grads, scaled, row_plane, up_plane, gate_plane, served, strip, stage, loads, strip_sems
    ) = scratch[:12]
    gather = Gather(here, rows, rows_all, halves_of(rows.shape[0]), False, scratch[12:16])
    mids = Sum(here, None, mid_sum, halves_of(rows.shape[0]), False, scratch[16:24])
    outs = Sum(here, None, out_sum, halves_of(rows.shape[0]), False, scratch[16:19] + scratch[24:29])
    tables = Sum(here, None, gate_sum, halves_of(gate_sum.shape[0], False), False, scratch[29:37])
    in_sems, down_sems = scratch[37:40], scratch[40:43]
    block, width = rows.shape
    plane = RING * block
    hidden = w_out.shape[0]
    chunk = hidden // 4
    column = lax.broadcasted_iota(jnp.int32, (plane, 128), 1)
    fetch_in = pltpu.make_async_copy(win, w_in, loads.at[0])
    fetch_out = pltpu.make_async_copy(wout, w_out, loads.at[1])
    fetch_in.start()
    fetch_out.start()

    def fetch_plane(number):
        z = near_first(here, number)
        return (
            pltpu.make_async_copy(ups.at[z], up_plane.at[number % 2], loads.at[2 + number % 2]),
            pltpu.make_async_copy(gates.at[z], gate_plane.at[number % 2], loads.at[4 + number % 2]),
        )

    def fetch_rows(number):
        return pltpu.make_async_copy(rows_all.at[near_first(here, number)], row_plane, loads.at[6])

    def hidden_units(number):
        z = near_first(here, number)
        fetch_rows(number).start()
        for copy in fetch_plane(number):
            copy.wait()
        if number == 0:
            fetch_in.wait()
            fetch_out.wait()
        fetch_rows(number).wait()
        served[...] = jnp.zeros_like(served)
        at = pl.ds(pl.multiple_of(z * plane, plane), plane)

        def one(expert, carry):
            mid = row_plane[...].reshape(plane, width)
            up_rows = up_plane[number % 2]
            spot = pl.ds(pl.multiple_of(expert * chunk, chunk), chunk)
            spot_up = pl.ds(pl.multiple_of(hidden + expert * chunk, chunk), chunk)
            gate = jnp.sum(jnp.where(column == expert, gate_plane[number % 2], 0.0), axis=1, keepdims=True)
            gate_part = jnp.dot(mid, w_in[:, spot], preferred_element_type=single)
            up_part = jnp.dot(mid, w_in[:, spot_up], preferred_element_type=single)
            back = contract_last(up_rows, w_out[spot])
            sigmoid = 1.0 / (1.0 + jnp.exp(-gate_part))
            activated = gate_part * sigmoid
            units = activated * up_part
            scaled[at, spot] = (gate * units).astype(narrow)
            total = jnp.sum(units * back, axis=1, keepdims=True)
            served[...] += jnp.where(column == here.chip * 4 + expert, total, 0.0)
            grad = gate * back
            grads[at, spot] = (grad * up_part * (sigmoid * (1.0 + gate_part * (1.0 - sigmoid)))).astype(narrow)
            grads[at, spot_up] = (grad * activated).astype(narrow)
            return carry

        lax.fori_loop(0, 4, one, 0)
        for chip in range(RING):
            turned = jnp.transpose(served[chip * block : (chip + 1) * block])
            tables.mine[z, chip] = turned[: tables.rows]

    def row_grads(z):
        at = pl.ds(pl.multiple_of(z * plane, plane), plane)

        def one(number, carry):
            spot = pl.ds(pl.multiple_of(number * TILE, TILE), TILE)
            made = contract_last(grads[at], w_in[spot]).astype(narrow)
            for chip in range(RING):
                mids.mine[z, chip, :, spot] = made[chip * block : (chip + 1) * block]
            return carry

        lax.fori_loop(0, width // TILE, one, 0)

    def products(z):
        at = pl.ds(pl.multiple_of(z * plane, plane), plane)

        def one(number, carry):
            spot = pl.ds(pl.multiple_of(number * TILE, TILE), TILE)
            made = jnp.dot(scaled[at], w_out[:, spot], preferred_element_type=single).astype(narrow)
            for chip in range(RING):
                outs.mine[z, chip, :, spot] = made[chip * block : (chip + 1) * block]
            return carry

        lax.fori_loop(0, width // TILE, one, 0)

    strips = width // TILE

    def fetch_strip(number):
        spot = pl.ds(pl.multiple_of(number * TILE, TILE), TILE)
        slot = lax.rem(number, 2)
        return pltpu.make_async_copy(rows_all.at[:, :, :, spot], strip.at[slot], strip_sems.at[slot])

    def columns_of(result, stage, step=512):
        for begin in range(0, width, step):
            stage[:, begin : begin + step] = result(begin, step).astype(narrow)

    def grad_in(number, stage):
        slot = lax.rem(number, 2)
        fetch_strip(number).wait()
        pl.when(number + 1 < strips)(lambda: fetch_strip(number + 1).start())
        left = strip[slot].reshape(DEPTH * plane, TILE)
        columns_of(lambda begin, step: contract_rows(left, grads[:, begin : begin + step]), stage)

    def grad_in_parts(number, stage):
        share = hidden // 2
        at = pl.ds(pl.multiple_of(number * TILE, TILE), TILE)
        for side in range(2):
            mine, theirs = (
                stage.at[:, pl.ds(pl.multiple_of(side * hidden + core * share, 128), share)]
                for core in (here.core, 1 - here.core)
            )
            yield mine, theirs, (at, pl.ds(side * share, share))

    def grad_down(number, stage):
        half = tall // 2
        core = here.core + (1 - lax.div(number, half)) * (1 - 2 * here.core)
        at = core * half + lax.rem(number, half)
        left = scaled[:, pl.ds(pl.multiple_of(at * TILE, TILE), TILE)]
        columns_of(lambda begin, step: contract_rows(left, w_in[:, begin : begin + step]), stage)

    tall = hidden // TILE
    tiles_in = Tiles(here, stage, strips, in_sems, grad_in_parts, (gin, gin_other))

    def grad_down_store(number, away):
        slot = lax.rem(number, 2)
        rest = lax.rem(number, tall // 2)
        spot = pl.ds(pl.multiple_of(rest * TILE, TILE), TILE)
        kept, sent, came = down_sems
        if away:
            return remote(stage.at[slot], gdown_other.at[spot], sent.at[slot, 0], came.at[rest, 0], here.sibling())
        return pltpu.make_async_copy(stage.at[slot], gdown.at[spot], kept.at[slot, 0])

    def grads_down(away):
        first = 0 if away else tall // 2

        def body(number, carry):
            grad_down(number, stage.at[lax.rem(number, 2)])
            grad_down_store(number, away).start()
            return carry

        lax.fori_loop(first, first + tall // 2, body, 0)
        for number in range(first, first + tall // 2):
            copy = grad_down_store(number, away)
            copy.wait_send() if away else copy.wait()

    again = [
        pltpu.make_async_copy(ups.at[z], w_in.at[pl.ds(z * plane, plane)], loads.at[7 + z]) for z in range(DEPTH)
    ]

    def again_wait():
        for copy in again:
            copy.wait()

    order = [far_first(here, number) for number in range(DEPTH)]
    first = [mids, tables]
    steps = [(first, z, False) for z in [here.z] + order[:-1]]
    steps += [([outs], z, number == DEPTH - 1) for number, z in enumerate(order)]

    def begin(number):
        items, z, last = steps[number]
        if number < DEPTH:
            row_grads(z)
        else:
            mids.end(z, last)
            products(z)
        for item in items:
            for way in (0, 1):
                start(item.toss(z, way))

    def second(number):
        for item in steps[number][0]:
            item.second(steps[number][1])

    def third(number):
        items, z, last = steps[number]
        for item in items:
            item.own_part(z) if number == 0 else item.third(z, last)

    for copy in fetch_plane(0):
        copy.start()
    rounds = Rounds(here, [gather])
    rounds.service(0)
    for number in range(DEPTH):
        if number + 1 < DEPTH:
            rounds.service(number + 1)
        if number == DEPTH - 1:
            second(0)
        gather_third(gather, near_first(here, number))
        if number + 1 < DEPTH:
            for copy in fetch_plane(number + 1):
                copy.start()
        hidden_units(number)
        if number == 1:
            begin(0)
    fetch_strip(0).start()
    ends = [0] + [strips * (number + 1) // (DEPTH - 1) for number in range(DEPTH - 1)]
    for number in range(1, 2 * DEPTH):
        begin(number)
        if number > 1:
            second(number - 1)
            third(number - 2)
        if number == DEPTH - 1:
            for copy in again:
                copy.start()
        if number < DEPTH:
            tiles_in.run(ends[number - 1], ends[number], grad_in)
        elif number == DEPTH:
            again_wait()
            grads_down(True)
        elif number == DEPTH + 1:
            grads_down(False)
        elif number == DEPTH + 2:
            for item in first:
                item.own_rest(here.z)
    outs.second(order[-1])
    outs.third(order[-2], False)
    outs.third(order[-1], True)
    for number, z in enumerate(order):
        outs.end(z, number == DEPTH - 1)
        tables.end(z, number == DEPTH - 1)
    tiles_in.heard()
    for number in range(tall // 2):
        grad_down_store(number, True).wait_recv()
    rounds.finish()


def experts_round(rows, ups, gates, win, wout, experts):
    block, width = rows.shape
    plane = RING * block
    hidden = wout.shape[0]
    total = DEPTH * plane
    vmem = pl.BlockSpec(memory_space=pltpu.VMEM)
    return pl.pallas_call(
        experts_kernel,
        out_shape=(
            jax.ShapeDtypeStruct((block, width), single),
            jax.ShapeDtypeStruct((experts, block), single),
            jax.ShapeDtypeStruct((block, width), single),
            jax.ShapeDtypeStruct((width, hidden), narrow),
            jax.ShapeDtypeStruct((width, hidden), narrow),
            jax.ShapeDtypeStruct((hidden // 2, width), narrow),
            jax.ShapeDtypeStruct((hidden // 2, width), narrow),
            jax.ShapeDtypeStruct((DEPTH, RING, block, width), narrow),
        ),
        in_specs=[HBM] * 5,
        out_specs=(vmem, vmem, vmem) + (HBM,) * 5,
        scratch_shapes=[
            pltpu.VMEM((width, 2 * hidden), narrow),
            pltpu.VMEM((hidden, width), narrow),
            pltpu.VMEM((total, 2 * hidden), narrow),
            pltpu.VMEM((total, hidden), narrow),
            pltpu.VMEM((RING, block, width), narrow),
            pltpu.VMEM((2, plane, width), narrow),
            pltpu.VMEM((2, plane, 128), single),
            pltpu.VMEM((plane, 128), single),
            pltpu.VMEM((2, DEPTH, RING, block, TILE), narrow),
            pltpu.VMEM((2, TILE, width), narrow),
            pltpu.SemaphoreType.DMA((11,)),
            pltpu.SemaphoreType.DMA((2,)),
        ]
        + GATHER_SEMS
        + sum_scratch(block, width, narrow, halves_of(block), made=True)
        + [pltpu.VMEM((DEPTH + 1, block, width), narrow)]
        + SUM_SEMS
        + sum_scratch(experts, block, single, halves_of(experts, False), made=True)
        + [
            pltpu.SemaphoreType.DMA((2, 2)),
            pltpu.SemaphoreType.DMA((2, 2)),
            pltpu.SemaphoreType.DMA((width // TILE, 2)),
        ]
        + [
            pltpu.SemaphoreType.DMA((2, 1)),
            pltpu.SemaphoreType.DMA((2, 1)),
            pltpu.SemaphoreType.DMA((hidden // TILE, 1)),
        ],
        compiler_params=pltpu.CompilerParams(
            collective_id=2, has_side_effects=True, vmem_limit_bytes=62 * 2**20
        ),
        name="experts",
    )(rows, ups, gates, win, wout)

def turn_kernel(source, target):
    target[...] = source[...].astype(target.dtype)


def turn_back(turned, held):
    planes, rows, columns = turned.shape
    part = columns // (2 * held)
    return pl.pallas_call(
        turn_kernel,
        out_shape=jax.ShapeDtypeStruct((held, rows, 2 * planes * part), single),
        grid=(held, 2, planes),
        in_specs=[pl.BlockSpec((1, rows, part), lambda expert, side, z: (z, 0, side * held + expert))],
        out_specs=pl.BlockSpec((1, rows, part), lambda expert, side, z: (expert, 0, side * planes + z)),
        cost_estimate=pl.CostEstimate(flops=0, bytes_accessed=6 * turned.size, transcendentals=0),
        name="turn",
    )(turned)


def by_kernels():
    return lax.axis_size("dp") == DEPTH and lax.axis_size("expert") == 2 * RING


def bring_all(w_qkv, w_out, upstream, dense, gain_rows, expert_in, expert_out):
    width = upstream.shape[1]
    share = gain_rows.shape[1]
    if by_kernels():
        experts, rows = dense.shape[1], dense.shape[0]
        small = jnp.concatenate([dense.T, jnp.pad(gain_rows, ((0, 4), (0, rows - share)))], axis=0)
        wq, wo, up, all_small, weight_in, weight_down = first_gather(
            w_qkv, w_out, upstream, small, expert_in, expert_out
        )
        gains = all_small[:, :, :, experts : experts + 4, :share].transpose(3, 0, 1, 2, 4).reshape(4, -1)
        core = lax.rem(lax.axis_index("expert"), 2)
        every_gate = lax.dynamic_index_in_dim(all_small, core, axis=2, keepdims=False)[:, :, :experts]
        return (
            wq.reshape(-1, w_qkv.shape[1]),
            wo.reshape(-1, w_out.shape[1]),
            up.reshape(-1, width),
            every_gate,
            gains,
            weight_in,
            weight_down.reshape(-1, width),
        )
    everyone = ("dp", "expert")
    weight_in, weight_down = fetch_weights(expert_in, expert_out)
    return (
        lax.all_gather(w_qkv, everyone, axis=0, tiled=True),
        lax.all_gather(w_out, everyone, axis=0, tiled=True),
        gather_alike(upstream).reshape(-1, width),
        gather_alike(dense.T),
        lax.all_gather(gain_rows, everyone, axis=1, tiled=True),
        weight_in,
        weight_down,
    )


def return_halves(half_way, held):
    grad_in, grad_in_other, grad_down, grad_down_other = half_way
    total = (grad_in.astype(single) + grad_in_other.astype(single)).astype(narrow)
    rows, columns = total.shape
    cut = total.reshape(DEPTH, rows // DEPTH, columns)
    turned = lax.all_to_all(cut, "dp", split_axis=0, concat_axis=0, tiled=True)
    down = grad_down.astype(single) + grad_down_other.astype(single)
    return (
        turn_back(turned, held),
        down.reshape(held, -1, down.shape[1]),
    )


def experts_all(routed_in, up_rows, every_gate, weight_in, weight_down, held):
    depth = lax.axis_size("dp")
    owners = lax.axis_size("expert")
    chips = owners // 2
    experts = owners * held
    chip_experts = 2 * held
    rows, width = routed_in.shape
    chip = lax.axis_index("expert") // 2
    mine = lax.dynamic_slice_in_dim(every_gate, chip * chip_experts, chip_experts, axis=2)
    gate = mine.transpose(0, 1, 3, 2)
    if by_kernels():
        gate = jnp.pad(gate.reshape(DEPTH, -1, chip_experts), ((0, 0), (0, 0), (0, 128 - chip_experts)))
        ups = up_rows.reshape(DEPTH, -1, width)
        grad_routed, table, mixture, *half_way, _ = experts_round(
            routed_in, ups, gate, weight_in, weight_down, experts
        )
        return (mixture, grad_routed, table, return_halves(half_way, held))
    mid_rows = gather_alike(routed_in).reshape(-1, width)
    out, mid, served, grad_in, grad_down = expert_rounds(
        mid_rows, up_rows, gate.reshape(-1, chip_experts), weight_in, weight_down
    )
    by_gate = served.reshape(depth, chips, rows, chip_experts).transpose(0, 1, 3, 2)
    spread = jnp.zeros((depth, chips, experts, rows), single)
    spread = lax.dynamic_update_slice_in_dim(spread, by_gate, chip * chip_experts, axis=2)
    return (
        scatter_alike(out.reshape(depth, chips, rows, width)).astype(single),
        scatter_alike(mid.reshape(depth, chips, rows, width)).astype(single),
        scatter_alike(spread),
        [share.astype(single) for share in return_weights(grad_in, grad_down, held)],
    )


def deliver_all(pieces, normed, grad_qkv, attended, branch):
    owners = lax.axis_size("dp") * lax.axis_size("expert")
    share = pieces.shape[1] // owners
    if by_kernels():
        small = pieces.reshape(4, owners, share).transpose(1, 0, 2)
        small = jnp.pad(small, ((0, 0), (0, 4), (0, 128 - share))).reshape(DEPTH, RING, 2, 8, 128)
        share_qkv, share_out, gains = last_sum(normed, grad_qkv, attended, branch, small, share)
        return (gains[:4, :share], share_qkv, share_out)
    everyone = ("dp", "expert")
    return (
        lax.psum_scatter(pieces, everyone, scatter_dimension=1, tiled=True),
        *(
            lax.psum_scatter(
                contract_rows(left, right, narrow), everyone, scatter_dimension=0, tiled=True
            ).astype(single)
            for left, right in ((normed, grad_qkv), (attended, branch))
        ),
    )


def local(
    tokens,
    lengths,
    expert_ids,
    gates,
    attn_gain,
    w_qkv,
    q_gain,
    k_gain,
    w_out,
    ffn_gain,
    expert_in,
    expert_out,
    out_grad,
):
    micro_count, seq_len, model_width = tokens.shape
    rows = micro_count * seq_len
    held = expert_in.shape[0]
    experts = lax.axis_size("expert") * held
    inputs = tokens.reshape(rows, model_width).astype(single)
    upstream = out_grad.reshape(rows, model_width)
    ids = expert_ids.reshape(rows, -1)
    gate_rows = gates.reshape(rows, -1)
    onehot = (ids[:, :, None] == jnp.arange(experts, dtype=jnp.int32)).astype(single)
    dense = jnp.sum(onehot * gate_rows[:, :, None], axis=1)
    gain_rows = jnp.stack([attn_gain, q_gain, k_gain, ffn_gain]).astype(single)
    weight_qkv, weight_out, up_rows, every_gate, gains, weight_in, weight_down = bring_all(
        w_qkv, w_out, upstream, dense, gain_rows, expert_in, expert_out
    )
    gain_attn, gain_query, gain_key, gain_ffn = gains[0], gains[1], gains[2], gains[3]

    normal_in, factor_in = normalize(inputs)
    normed_in = (normal_in * gain_attn).astype(narrow)
    projected = jnp.dot(normed_in, weight_qkv, preferred_element_type=single)
    normal_q, factor_q = normalize(projected[:, :model_width])
    normal_k, factor_k = normalize(projected[:, model_width : 2 * model_width])
    document, position = layout(lengths[:, 0], seq_len)
    cosine, sine = angles(position)
    query_rows = rotate(normal_q * gain_query, cosine, sine).astype(narrow).reshape(rows, -1, HEAD)
    key_rows = rotate(normal_k * gain_key, cosine, sine).astype(narrow).reshape(rows, -1, HEAD)
    value_rows = projected[:, 2 * model_width :].astype(narrow).reshape(rows, -1, HEAD)
    places = jnp.arange(rows, dtype=jnp.int32)
    allowed = (document[:, None] == document[None, :]) & (places[:, None] >= places[None, :])
    raw = jnp.einsum("qhd,khd->hqk", query_rows, key_rows, preferred_element_type=single)
    scores = jnp.where(allowed[None], raw * HEAD ** (-0.5), masked_score)
    highest = jnp.max(scores, axis=-1, keepdims=True)
    unnormed = jnp.exp(scores - highest)
    probs = unnormed / jnp.sum(unnormed, axis=-1, keepdims=True)
    attn_probs = probs.astype(narrow)
    attended = (
        jnp.einsum("hqk,khd->qhd", attn_probs, value_rows, preferred_element_type=single)
        .reshape(rows, model_width)
        .astype(narrow)
    )
    middle = inputs + jnp.dot(attended, weight_out, preferred_element_type=single)
    normal_mid, factor_mid = normalize(middle)
    routed_in = (normal_mid * gain_ffn).astype(narrow)

    mixture, grad_routed, gate_table, (share_in, share_down) = experts_all(
        routed_in, up_rows, every_gate, weight_in, weight_down, held
    )
    grad_gates = jnp.sum(onehot * gate_table.T[:, None, :], axis=2)
    results = (middle + mixture).astype(narrow)

    grad_mid, piece_ffn = rms_back(grad_routed, normal_mid, factor_mid, gain_ffn)
    grad_middle = upstream.astype(single) + grad_mid
    grad_branch = grad_middle.astype(narrow)
    grad_attended = contract_last(grad_branch, weight_out).astype(narrow).reshape(rows, -1, HEAD)
    grad_probs = jnp.einsum("qhd,khd->hqk", grad_attended, value_rows, preferred_element_type=single)
    inner = jnp.sum(grad_probs * probs, axis=-1, keepdims=True)
    grad_scores = (probs * (grad_probs - inner)).astype(narrow)
    grad_query = jnp.einsum(
        "hqk,khd->qhd", grad_scores, key_rows, preferred_element_type=single
    ) * HEAD ** (-0.5)
    grad_key = jnp.einsum(
        "hqk,qhd->khd", grad_scores, query_rows, preferred_element_type=single
    ) * HEAD ** (-0.5)
    grad_value = jnp.einsum("hqk,qhd->khd", attn_probs, grad_attended, preferred_element_type=single)
    grad_q_raw, piece_query = rms_back(
        rotate(grad_query.reshape(rows, model_width), cosine, -sine), normal_q, factor_q, gain_query
    )
    grad_k_raw, piece_key = rms_back(
        rotate(grad_key.reshape(rows, model_width), cosine, -sine), normal_k, factor_k, gain_key
    )
    grad_qkv = jnp.concatenate(
        [grad_q_raw, grad_k_raw, grad_value.reshape(rows, model_width)], axis=1
    ).astype(narrow)
    grad_normed = contract_last(grad_qkv, weight_qkv)
    grad_input, piece_attn = rms_back(grad_normed, normal_in, factor_in, gain_attn)
    grad_tokens = grad_middle + grad_input

    pieces = jnp.stack([piece_attn, piece_query, piece_key, piece_ffn])
    gain_sums, grad_qkv_share, grad_out_share = deliver_all(
        pieces, normed_in, grad_qkv, attended, grad_branch
    )
    shape = (micro_count, seq_len, model_width)
    return (
        results.reshape(shape),
        grad_tokens.reshape(shape),
        grad_gates.reshape(expert_ids.shape),
        gain_sums[0],
        grad_qkv_share,
        gain_sums[1],
        gain_sums[2],
        grad_out_share,
        gain_sums[3],
        share_in,
        share_down,
    )


def solution(mesh):
    by_rows = P(None, ("dp", "expert"), None)
    flat = P(("dp", "expert"))
    split = P(("dp", "expert"), None)
    held = P("expert", "dp", None)
    return jax.shard_map(
        local,
        mesh=mesh,
        in_specs=(
            by_rows, by_rows, by_rows, by_rows, flat, split, flat, flat, split, flat, held, held, by_rows,
        ),
        out_specs=(by_rows, by_rows, by_rows, flat, split, flat, flat, split, flat, held, held),
        check_vma=False,
    )
```

```python
import jax
import jax.numpy as jnp
from jax import lax
from jax.experimental import pallas as pl
from jax.experimental.pallas import tpu as pltpu
from jax.sharding import PartitionSpec as P

HEAD = 128
epsilon = 1e-05
base_theta = 10000.0
masked_score = -1e30
single = jnp.float32
narrow = jnp.bfloat16


def normalize(values):
    factor = lax.rsqrt(jnp.mean(values * values, axis=-1, keepdims=True) + epsilon)
    return (values * factor, factor)


def rms_back(upstream, normal, factor, gain):
    weighted = upstream * gain
    inner = jnp.mean(weighted * normal, axis=-1, keepdims=True)
    return (factor * (weighted - normal * inner), jnp.sum(upstream * normal, axis=0))


def angles(position):
    half = HEAD // 2
    ladder = jnp.arange(half, dtype=single) * (2.0 / HEAD)
    frequency = jnp.exp(-jnp.log(base_theta) * ladder)
    angle = position.astype(single)[:, None] * frequency[None, :]
    return (jnp.cos(angle)[:, None, :], jnp.sin(angle)[:, None, :])


def rotate(field, cosine, sine):
    length = field.shape[0]
    heads = field.reshape(length, -1, HEAD)
    half = HEAD // 2
    first = heads[..., :half]
    second = heads[..., half:]
    turned = jnp.concatenate(
        [first * cosine - second * sine, second * cosine + first * sine], axis=-1
    )
    return turned.reshape(length, -1)


def layout(doc_lengths, length):
    packs, count = doc_lengths.shape
    upto = jnp.arange(count)[None, :] <= jnp.arange(count)[:, None]
    ends = jnp.sum(jnp.where(upto[None], doc_lengths[:, None, :], 0), axis=2)
    starts = ends - doc_lengths
    places = jnp.arange(length, dtype=jnp.int32)[None, :, None]
    document = jnp.sum((places >= ends[:, None, :]).astype(jnp.int32), axis=2)
    member = (places >= starts[:, None, :]) & (places < ends[:, None, :])
    first_place = jnp.sum(jnp.where(member, starts[:, None, :], 0), axis=2)
    document = document + (count + 1) * jnp.arange(packs, dtype=jnp.int32)[:, None]
    return (document.reshape(-1), (places[..., 0] - first_place).reshape(-1))


def contract_rows(left, right, kind=single):
    return lax.dot_general(left, right, (((0,), (0,)), ((), ())), preferred_element_type=kind)


def contract_last(left, right, kind=single):
    return lax.dot_general(left, right, (((1,), (1,)), ((), ())), preferred_element_type=kind)


def core_groups():
    return [[2 * chip + core for chip in range(lax.axis_size("expert") // 2)] for core in range(2)]


def chip_groups():
    return [[2 * chip, 2 * chip + 1] for chip in range(lax.axis_size("expert") // 2)]


def gather_alike(block):
    column = lax.all_gather(block, "dp", axis=0)
    return lax.all_gather(column, "expert", axis=1, axis_index_groups=core_groups())


def scatter_alike(blocks):
    column = lax.psum_scatter(
        blocks, "expert", scatter_dimension=1, axis_index_groups=core_groups()
    )
    return lax.psum_scatter(column, "dp", scatter_dimension=0)


def fetch_weights(expert_in, expert_out):
    depth = lax.axis_size("dp")
    held, rows, columns = expert_in.shape
    part = columns // (2 * depth)
    cut = expert_in.reshape(held, rows, 2, depth, part)
    turned = lax.all_to_all(cut, "dp", split_axis=3, concat_axis=1, tiled=True)
    both = lax.all_gather(turned[:, :, :, 0], "expert", axis=0, axis_index_groups=chip_groups())
    weight_in = both.transpose(2, 3, 0, 1, 4).reshape(depth * rows, 4 * held * part)
    weight_down = lax.all_gather(
        expert_out, "expert", axis=0, axis_index_groups=chip_groups()
    ).reshape(-1, expert_out.shape[2])
    return (weight_in, weight_down)


def return_weights(grad_in, grad_down, held):
    depth = lax.axis_size("dp")
    rows, columns = grad_in.shape
    part = columns // (4 * held)
    cut = grad_in.reshape(rows, 2, 2, held, part)
    own = lax.psum_scatter(cut, "expert", scatter_dimension=2, axis_index_groups=chip_groups())
    own = own.reshape(depth, rows // depth, 2, held, part)
    turned = lax.all_to_all(own, "dp", split_axis=0, concat_axis=0)
    share_in = turned.transpose(3, 1, 2, 0, 4).reshape(held, rows // depth, 2 * depth * part)
    down = grad_down.reshape(2, held, part, grad_down.shape[1])
    share_down = lax.psum_scatter(
        down, "expert", scatter_dimension=0, axis_index_groups=chip_groups()
    )
    return (share_in, share_down)


def expert_round(mid_rows, up_rows, gate, weight_in, weight_down):
    count = gate.shape[1]
    part = weight_down.shape[0] // count
    wide = jnp.broadcast_to(gate[:, :, None], gate.shape + (part,)).reshape(gate.shape[0], -1)
    gate_up = jnp.dot(mid_rows, weight_in, preferred_element_type=single)
    hidden_units = gate_up.shape[1] // 2
    gate_part = gate_up[:, :hidden_units]
    up_part = gate_up[:, hidden_units:]
    sigmoid = jax.nn.sigmoid(gate_part)
    activated = gate_part * sigmoid
    hidden = activated * up_part
    back = contract_last(up_rows, weight_down)
    scaled = (wide * hidden).astype(narrow)
    piece_out = jnp.dot(scaled, weight_down, preferred_element_type=narrow)
    piece_gates = jnp.sum((hidden * back).reshape(-1, count, part), axis=2)
    grad_hidden = wide * back
    grad_gate = grad_hidden * up_part * sigmoid * (1.0 + gate_part * (1.0 - sigmoid))
    grad_up = grad_hidden * activated
    grad_gate_up = jnp.concatenate([grad_gate, grad_up], axis=1).astype(narrow)
    piece_mid = contract_last(grad_gate_up, weight_in, narrow)
    return (piece_out, piece_mid, piece_gates, grad_gate_up, scaled)


def expert_rounds(mid_rows, up_rows, gate, weight_in, weight_down):
    total = mid_rows.shape[0]
    rounds = max(1, total // 2048)

    def one(sums, pieces):
        mid, up, weights = pieces
        piece_out, piece_mid, piece_gates, grad_gate_up, scaled = expert_round(
            mid, up, weights, weight_in, weight_down
        )
        grads = (contract_rows(mid, grad_gate_up), contract_rows(scaled, up))
        return (jax.tree.map(jnp.add, sums, grads), (piece_out, piece_mid, piece_gates))

    if rounds == 1:
        piece_out, piece_mid, piece_gates, grad_gate_up, scaled = expert_round(
            mid_rows, up_rows, gate, weight_in, weight_down
        )
        grads = (contract_rows(mid_rows, grad_gate_up, narrow), contract_rows(scaled, up_rows, narrow))
        return (piece_out, piece_mid, piece_gates) + grads
    start = (jnp.zeros(weight_in.shape, single), jnp.zeros(weight_down.shape, single))
    cut = jax.tree.map(lambda a: a.reshape(rounds, total // rounds, -1), (mid_rows, up_rows, gate))
    sums, made = lax.scan(one, start, cut)
    made = jax.tree.map(lambda a: a.reshape(total, -1), made)
    return made + (sums[0].astype(narrow), sums[1].astype(narrow))


MESH = pl.DeviceIdType.MESH
HBM = pl.BlockSpec(memory_space=pl.ANY)
DEPTH = 4
RING = 4


def ring_turn(number):
    high = lax.div(number, 2)
    return number + high * (1 - 2 * lax.rem(number, 2))


class Here:
    def __init__(self):
        number = lax.axis_index("expert")
        self.z = lax.axis_index("dp")
        self.core = lax.rem(number, 2)
        self.chip = lax.div(number, 2)
        self.q = ring_turn(self.chip)

    def chip_at(self, turn):
        return ring_turn(lax.rem(self.q + turn + RING, RING))

    def beside(self, turn):
        return (self.z, 2 * self.chip_at(turn) + self.core)

    def above(self, steps):
        return (lax.rem(self.z + steps + DEPTH, DEPTH), 2 * self.chip + self.core)

    def sibling(self):
        return (self.z, 2 * self.chip + 1 - self.core)

    def meet(self):
        barrier = pltpu.get_barrier_semaphore()
        others = [self.beside(1), self.beside(-1), self.sibling()]
        others += [self.above(steps) for steps in range(1, DEPTH)]
        for other in others:
            pl.semaphore_signal(barrier, inc=1, device_id=other, device_id_type=MESH)
        pl.semaphore_wait(barrier, len(others))


def remote(source, target, sent, arrived, device):
    return pltpu.make_async_remote_copy(
        src_ref=source,
        dst_ref=target,
        send_sem=sent,
        recv_sem=arrived,
        device_id=device,
        device_id_type=MESH,
    )


GATHER_SEMS = [
    pltpu.SemaphoreType.DMA((2, 2, DEPTH - 1)),
    pltpu.SemaphoreType.DMA((2, DEPTH, 2, 2)),
    pltpu.SemaphoreType.DMA((2, DEPTH)),
    pltpu.SemaphoreType.DMA((1,)),
]


class Gather:
    def __init__(self, here, source, whole, halves, shared, sems):
        self.here, self.source, self.whole, self.halves, self.shared = here, source, whole, halves, shared
        self.line, self.ring, self.pair, self.own = sems

    def block(self, z, turn):
        chip = self.here.chip_at(turn)
        return self.whole.at[z, chip, self.here.core] if self.shared else self.whole.at[z, chip]

    def keep(self):
        return pltpu.make_async_copy(self.source, self.block(self.here.z, 0), self.own.at[0])

    def along(self, step, way, first):
        z = self.here.z - step + 1 if way == 0 else self.here.z + step - 1
        block = self.block(z, 0)
        return remote(
            self.source if first else block,
            block,
            self.line.at[0, way, step - 1],
            self.line.at[1, way, step - 1],
            self.here.above(1 if way == 0 else -1),
        )

    def round(self, z, way, first=False):
        turn = 1 if way == 0 else -1
        block = self.block(z, 0)
        return remote(
            self.source if first else block,
            block,
            self.ring.at[0, z, way, 0],
            self.ring.at[1, z, way, 0],
            self.here.beside(turn),
        )

    def heard(self, z, way):
        block = self.block(z, -1 if way == 0 else 1)
        return remote(
            block, block, self.ring.at[0, z, way, 0], self.ring.at[1, z, way, 0], self.here.beside(1)
        )

    def onward(self, z, way, mine):
        if self.halves[way] is None:
            return None
        turn = (-1 if mine else -2) if way == 0 else (1 if mine else 2)
        block = self.block(z, turn).at[pl.ds(*self.halves[way])]
        return remote(
            block,
            block,
            self.ring.at[0, z, way, 1],
            self.ring.at[1, z, way, 1],
            self.here.beside(1 if way == 0 else -1),
        )

    def swap(self, z, mine):
        core = self.here.core if mine else 1 - self.here.core
        part = self.whole.at[z, :, core]
        return remote(part, part, self.pair.at[0, z], self.pair.at[1, z], self.here.sibling())


def start(copy):
    if copy is not None:
        copy.start()


def gather_third(item, z):
    for way in (0, 1):
        copy = item.onward(z, way, False)
        if copy is not None:
            copy.wait_recv()


class Rounds:
    def __init__(self, here, items):
        self.here, self.items = here, items
        for item in items:
            item.keep().start()
            for way in (0, 1):
                self.depart(0, way, item)
            for way in (0, 1):
                item.round(here.z, way, True).start()

    def depart(self, step, way, item):
        here = self.here
        ahead = here.z + 1 < DEPTH if way == 0 else here.z >= 1
        pl.when(ahead)(lambda: item.along(step + 1, way, step == 0).start())

    def places(self, step, body):
        here = self.here
        if step == 0:
            body(here.z, 0)
            return
        pl.when(here.z >= step)(lambda: body(here.z - step, 0))
        pl.when(here.z + step < DEPTH)(lambda: body(here.z + step, 1))

    def service(self, step, between=None):
        items, here = self.items, self.here

        def first(z, way):
            for item in items:
                block = item.block(z, 0)
                remote(
                    block, block, item.line.at[0, way, step], item.line.at[1, way, step], here.above(1)
                ).wait_recv()
                if step + 2 < DEPTH:
                    self.depart(step + 1, way, item)
                for side in (0, 1):
                    item.round(z, side).start()

        def second(z, way):
            for item in items:
                for side in (0, 1):
                    item.heard(z, side).wait_recv()
                    start(item.onward(z, side, True))

        if step + 1 < DEPTH:
            self.places(step + 1, first)
        if between is not None:
            between()
        if step == 0:
            for item in items:
                item.keep().wait()
        self.places(step, second)

    def third(self, step):
        def body(z, way):
            for item in self.items:
                gather_third(item, z)
                if item.shared:
                    item.swap(z, True).start()

        self.places(step, body)

    def finish(self):
        def settle(z, way):
            for item in self.items:
                for side in (0, 1):
                    item.round(z, side).wait_send()
                    copy = item.onward(z, side, True)
                    if copy is not None:
                        copy.wait_send()
                if item.shared:
                    item.swap(z, True).wait_send()
                    item.swap(z, False).wait_recv()

        for step in range(DEPTH):
            self.places(step, settle)
        here = self.here
        for item in self.items:
            for step in range(DEPTH - 1):
                for way in (0, 1):

                    def sent(z, side, step=step, way=way, item=item):
                        if step and side != way:
                            return
                        ahead = here.z + 1 < DEPTH if way == 0 else here.z >= 1
                        pl.when(ahead)(lambda: item.along(step + 1, way, step == 0).wait_send())

                    self.places(step, sent)


class Recut:
    def __init__(self, here, source_in, source_out, whole_in, whole_out, sems):
        self.here, self.source_in, self.source_out = here, source_in, source_out
        self.whole_in, self.whole_out = whole_in, whole_out
        self.cut, self.pair, self.down, self.own = sems
        self.held, self.rows, columns = source_in.shape
        self.hidden = columns // 2
        self.part = self.hidden // DEPTH

    def pieces(self, steps, arriving):
        here, copies = self.here, []
        mine = lax.rem(here.z + DEPTH - steps, DEPTH) if arriving else here.z
        away = lax.rem(here.z + steps, DEPTH)
        for side in range(2):
            for expert in range(self.held):
                columns = side * self.held * 2 * self.part + (here.core * self.held + expert) * self.part
                target = self.whole_in.at[
                    pl.ds(pl.multiple_of(mine * self.rows, 16), self.rows),
                    pl.ds(pl.multiple_of(columns, 128), self.part),
                ]
                source = self.source_in.at[
                    expert, :, pl.ds(pl.multiple_of(side * self.hidden + away * self.part, 128), self.part)
                ]
                spot = (steps, side * self.held + expert)
                if steps == 0:
                    copies.append(pltpu.make_async_copy(source, target, self.own.at[spot[1]]))
                else:
                    copies.append(
                        remote(
                            target if arriving else source,
                            target,
                            self.cut.at[(0,) + spot],
                            self.cut.at[(1,) + spot],
                            here.above(steps),
                        )
                    )
        return copies

    def across(self, steps, mine):
        here, copies = self.here, []
        core = here.core if mine else 1 - here.core
        row = lax.rem(here.z + DEPTH - steps, DEPTH)
        width = self.held * self.part
        for side in range(2):
            spot = self.whole_in.at[
                pl.ds(pl.multiple_of(row * self.rows, 16), self.rows),
                pl.ds(pl.multiple_of(side * 2 * width + core * width, 128), width),
            ]
            copies.append(
                remote(spot, spot, self.pair.at[0, steps, side], self.pair.at[1, steps, side], here.sibling())
            )
        return copies

    def lower(self, mine):
        here = self.here
        core = here.core if mine else 1 - here.core
        spot = self.whole_out.at[pl.ds(core * self.held, self.held)]
        return remote(
            self.source_out if mine else spot, spot, self.down.at[0], self.down.at[1], here.sibling()
        )

    def lower_own(self):
        return pltpu.make_async_copy(
            self.source_out, self.whole_out.at[pl.ds(self.here.core * self.held, self.held)], self.own.at[4]
        )

    def begin(self):
        for copy in self.pieces(0, False):
            copy.start()
        self.lower_own().start()
        self.lower(True).start()
        for steps in range(1, DEPTH):
            for copy in self.pieces(steps, False):
                copy.start()

    def relay(self):
        for steps in range(DEPTH):
            for copy in self.pieces(steps, True):
                copy.wait() if steps == 0 else copy.wait_recv()
            for copy in self.across(steps, True):
                copy.start()

    def end(self):
        self.lower_own().wait()
        self.lower(True).wait_send()
        self.lower(False).wait_recv()
        for steps in range(DEPTH):
            if steps:
                for copy in self.pieces(steps, False):
                    copy.wait_send()
            for copy in self.across(steps, True):
                copy.wait_send()
            for copy in self.across(steps, False):
                copy.wait_recv()


RECUT_SEMS = [
    pltpu.SemaphoreType.DMA((2, DEPTH, 4)),
    pltpu.SemaphoreType.DMA((2, DEPTH, 2)),
    pltpu.SemaphoreType.DMA((2,)),
    pltpu.SemaphoreType.DMA((5,)),
]


def halves_of(rows, split=True):
    return ((0, rows // 2), (rows // 2, rows - rows // 2)) if split else ((0, rows), None)


def first_gather_kernel(wq, wo, up, small, ein, eout, wq_all, wo_all, up_all, small_all, win, wout, *sems):
    here = Here()
    here.meet()
    items = []
    for number, (source, whole, halves, shared) in enumerate(
        (
            (small, small_all, halves_of(small.shape[0], False), True),
            (wq, wq_all, halves_of(wq.shape[0]), True),
            (wo, wo_all, halves_of(wo.shape[0]), True),
            (up, up_all, halves_of(up.shape[0]), False),
        )
    ):
        items.append(Gather(here, source, whole, halves, shared, sems[4 * number : 4 * number + 4]))
    recut = Recut(here, ein, eout, win, wout, sems[16:20])
    rounds = Rounds(here, items)
    for step in range(DEPTH):
        rounds.service(step, recut.begin if step == 1 else None)
        if step:
            rounds.third(step - 1)
    rounds.third(DEPTH - 1)
    recut.relay()
    rounds.finish()
    recut.end()


def first_gather(wq, wo, up, small, ein, eout):
    def whole(array, shared):
        lead = (DEPTH, RING, 2) if shared else (DEPTH, RING)
        return jax.ShapeDtypeStruct(lead + array.shape, array.dtype)

    held, rows, columns = ein.shape
    return pl.pallas_call(
        first_gather_kernel,
        out_shape=(
            whole(wq, True),
            whole(wo, True),
            whole(up, False),
            whole(small, True),
            jax.ShapeDtypeStruct((DEPTH * rows, columns), ein.dtype),
            jax.ShapeDtypeStruct((2 * held,) + eout.shape[1:], eout.dtype),
        ),
        in_specs=[HBM] * 6,
        out_specs=(HBM,) * 6,
        scratch_shapes=GATHER_SEMS * 4 + RECUT_SEMS,
        compiler_params=pltpu.CompilerParams(collective_id=1, has_side_effects=True),
        name="bring",
    )(wq, wo, up, small, ein, eout)

TILE = 256


def add_up(target, terms, rows, columns):
    high = 16 if rows % 16 == 0 else 8
    wide = min(columns, 1024)
    across = columns // wide

    def piece(number, carry):
        row = pl.multiple_of(lax.div(number, across) * high, high)
        column = pl.multiple_of(lax.rem(number, across) * wide, 128)
        spot = (pl.ds(row, high), pl.ds(column, wide))
        total = terms[0][spot].astype(single)
        for term in terms[1:]:
            total = total + term[spot].astype(single)
        target[spot] = total.astype(target.dtype)
        return carry

    lax.fori_loop(0, (rows // high) * across, piece, 0)


SUM_SEMS = [
    pltpu.SemaphoreType.DMA((2, DEPTH, 2)),
    pltpu.SemaphoreType.DMA((2, DEPTH, 2)),
    pltpu.SemaphoreType.DMA((2, 2, DEPTH)),
    pltpu.SemaphoreType.DMA((DEPTH, RING, 2)),
]


def sum_scratch(rows, columns, kind, halves, paired=False, made=False):
    high = max(size for _, size in filter(None, halves))
    kept = RING if paired or made else RING - 1
    scratch = [
        pltpu.VMEM((DEPTH, kept, rows, columns), kind),
        pltpu.VMEM((DEPTH, 2, high, columns), kind),
        pltpu.VMEM((DEPTH, 2, rows, columns), kind),
        pltpu.VMEM((DEPTH + 1, rows, columns), kind),
    ] + SUM_SEMS
    if paired:
        scratch += [pltpu.VMEM((DEPTH, RING, rows, columns), kind), pltpu.SemaphoreType.DMA((2, DEPTH, 2))]
    return scratch


class Sum:
    def __init__(self, here, sources, target, halves, paired, scratch):
        self.here, self.sources, self.halves, self.paired = here, sources, halves, paired
        self.target = target if isinstance(target, list) else [(target, 0, target.shape[0])]
        self.mine, self.half, self.full, self.column = scratch[:4]
        self.half_sem, self.full_sem, self.line_sem, self.load_sem = scratch[4:8]
        if paired:
            self.other, self.pair_sem = scratch[8:10]
        self.rows, self.columns = self.mine.shape[2:]

    def kept(self, z, turn):
        if self.sources is None:
            return self.mine.at[z, self.here.chip_at(turn)]
        return self.mine.at[z, turn if self.paired else {0: 0, 1: 1, 3: 2}[turn]]

    def raw(self, part, z, turn):
        chip = self.here.chip_at(turn)
        return part.at[z, chip, self.here.core] if self.paired else part.at[z, chip]

    def spots(self):
        at, spots = 0, []
        for part in self.sources or []:
            spots.append((part, pl.ds(at, part.shape[-1])))
            at += part.shape[-1]
        return spots

    def loads(self, z, turn):
        return [
            pltpu.make_async_copy(
                self.raw(part, z, turn), self.kept(z, turn).at[:, spot], self.load_sem.at[z, turn, number]
            )
            for number, (part, spot) in enumerate(self.spots())
        ]

    def swaps(self, z, mine):
        return [
            remote(
                part.at[z, :, 1 - self.here.core] if mine else self.other.at[z, :, :, spot],
                self.other.at[z, :, :, spot],
                self.pair_sem.at[0, z, number],
                self.pair_sem.at[1, z, number],
                self.here.sibling(),
            )
            for number, (part, spot) in enumerate(self.spots())
        ]

    def toss(self, z, way):
        if self.halves[way] is None:
            return None
        rows = pl.ds(*self.halves[way])
        loaded = self.sources is not None and not self.paired
        source = (self.raw(self.sources[0], z, 2) if loaded else self.kept(z, 2)).at[rows]
        return remote(
            source,
            self.half.at[z, way, pl.ds(0, self.halves[way][1])],
            self.half_sem.at[0, z, way],
            self.half_sem.at[1, z, way],
            self.here.beside(1 if way == 0 else -1),
        )

    def pass_on(self, z, way):
        return remote(
            self.kept(z, 1 if way == 0 else 3),
            self.full.at[z, way],
            self.full_sem.at[0, z, way],
            self.full_sem.at[1, z, way],
            self.here.beside(1 if way == 0 else -1),
        )

    def climb(self, z, way, up, slot=None):
        if slot is None:
            down_to_owner = way * (z == self.here.z - 1).astype(jnp.int32)
            slot = z + down_to_owner * (DEPTH - z)
        return remote(
            self.kept(z, 0),
            self.column.at[slot],
            self.line_sem.at[0, way, z],
            self.line_sem.at[1, way, z],
            self.here.above(2 * up - 1),
        )

    def begin(self, z):
        if self.paired:
            for copy in self.swaps(z, True):
                copy.start()
        for turn in (2, 1, 3, 0):
            if turn != 2 or self.paired:
                for copy in self.loads(z, turn):
                    copy.start()
        if not self.paired:
            for way in (0, 1):
                start(self.toss(z, way))

    def merge(self, z):
        if not self.paired:
            return
        for copy in self.swaps(z, False):
            copy.wait_recv()
        for turn in (2, 1, 3, 0):
            for copy in self.loads(z, turn):
                copy.wait()
            kept = self.kept(z, turn)
            add_up(kept, [kept, self.other.at[z, self.here.chip_at(turn)]], self.rows, self.columns)
            if turn == 2:
                for way in (0, 1):
                    start(self.toss(z, way))

    def second(self, z):
        for way, turn in ((0, 1), (1, 3)):
            if not self.paired:
                for copy in self.loads(z, turn):
                    copy.wait()
            copy = self.toss(z, way)
            if copy is not None:
                copy.wait_recv()
                begin, size = self.halves[way]
                rows = self.kept(z, turn).at[pl.ds(begin, size)]
                add_up(rows, [rows, self.half.at[z, way, pl.ds(0, size)]], size, self.columns)
        for way in (0, 1):
            self.pass_on(z, way).start()

    def third(self, z, last):
        here = self.here
        if not self.paired:
            for copy in self.loads(z, 0):
                copy.wait()
        for way in (0, 1):
            self.pass_on(z, way).wait_recv()
        kept = self.kept(z, 0)
        terms = [kept, self.full.at[z, 0], self.full.at[z, 1]]
        if last:
            self.arrive(z, terms)
            return
        up = (z > here.z).astype(jnp.int32)
        way = 1 - up
        follows = up * here.z + way * (DEPTH - 1 - here.z)

        @pl.when(follows > 0)
        def _():
            self.climb(z, way, up, z).wait_recv()
            add_up(kept, terms + [self.column.at[z]], self.rows, self.columns)

        @pl.when(follows == 0)
        def _():
            add_up(kept, terms, self.rows, self.columns)

        self.climb(z, way, up).start()

    def own_part(self, z):
        for way in (0, 1):
            self.pass_on(z, way).wait_recv()
        [(target, _, rows)] = self.target
        add_up(target, [self.kept(z, 0), self.full.at[z, 0], self.full.at[z, 1]], rows, self.columns)

    def own_rest(self, z):
        self.arrive(z, [self.target[0][0]])

    def arrive(self, z, terms):
        here = self.here
        below, above = self.column.at[z], self.column.at[DEPTH]

        def total(more):
            for target, row, rows in self.target:
                part = [term.at[pl.ds(row, rows)] for term in terms + more]
                add_up(target, part, rows, self.columns)

        @pl.when(here.z == 0)
        def _():
            self.climb(z, 1, 0, DEPTH).wait_recv()
            total([above])

        @pl.when(here.z == DEPTH - 1)
        def _():
            self.climb(z, 0, 0, z).wait_recv()
            total([below])

        @pl.when((here.z > 0) & (here.z < DEPTH - 1))
        def _():
            self.climb(z, 0, 0, z).wait_recv()
            self.climb(z, 1, 0, DEPTH).wait_recv()
            total([below, above])

    def end(self, z, last):
        if self.paired:
            for copy in self.swaps(z, True):
                copy.wait_send()
        for way in (0, 1):
            copy = self.toss(z, way)
            if copy is not None:
                copy.wait_send()
            self.pass_on(z, way).wait_send()
        if not last:
            up = (z > self.here.z).astype(jnp.int32)
            self.climb(z, 1 - up, up).wait_send()


def far_first(here, number):
    high = lax.div(here.z, 2)
    inner = lax.rem(lax.div(here.z + 1, 2), 2)
    low = (DEPTH - 1 - number) + inner * (0, -2, 1, 1)[number]
    return low + high * (DEPTH - 1 - 2 * low)


class Share:
    def __init__(self, here, source, target, sems):
        self.here, self.source, self.target, self.sems = here, source, target, sems
        self.held, self.rows, columns = target.shape
        self.part = columns // (2 * DEPTH)

    def pieces(self, steps, arriving):
        here = self.here
        origin = lax.rem(here.z + DEPTH - steps, DEPTH) if arriving else here.z
        away = lax.rem(here.z + steps, DEPTH)
        copies = []
        for number in range(2 * self.held):
            side, expert = divmod(number, self.held)
            column = (side * DEPTH + origin) * self.part
            target = self.target.at[expert, :, pl.ds(pl.multiple_of(column, 128), self.part)]
            source = self.source.at[
                pl.ds(pl.multiple_of(away * self.rows, 16), self.rows), pl.ds(number * self.part, self.part)
            ]
            if steps == 0:
                copies.append(pltpu.make_async_copy(source, target, self.sems.at[0, 0, number]))
            else:
                sems = (self.sems.at[0, steps, number], self.sems.at[1, steps, number])
                copies.append(remote(target if arriving else source, target, *sems, here.above(steps)))
        return copies

    def begin(self):
        for steps in range(DEPTH):
            for copy in self.pieces(steps, False):
                copy.start()

    def end(self):
        for steps in range(DEPTH):
            for copy in self.pieces(steps, False):
                copy.wait() if steps == 0 else copy.wait_send()
            if steps:
                for copy in self.pieces(steps, True):
                    copy.wait_recv()


def last_sum_kernel(
    normed,
    grad,
    attended,
    branch,
    gin_sum,
    weight,
    tokens,
    grad_middle,
    gain,
    pieces,
    q_sum,
    o_sum,
    gains,
    grad_tokens,
    share_in,
    left,
    left_out,
    right,
    sems,
    panel,
    panel_sems,
    back,
    piece,
    few_sum,
    few_other,
    pair_sems,
    share_sems,
    *scratch,
):
    here = Here()
    here.meet()
    block, width = normed.shape
    share = q_sum.shape[0]
    wide = grad.shape[1]
    sides = wide // width
    moved = [
        (normed, left, None),
        (grad, right, pl.ds(0, wide)),
        (attended, left_out, None),
        (branch, right, pl.ds(wide, width)),
    ]
    copies = []
    for number, (source, target, spot) in enumerate(moved):
        own, other = (target.at[core] if spot is None else target.at[core, :, spot] for core in (0, 1))
        copies.append(
            (
                pltpu.make_async_copy(source, own, sems.at[number]),
                remote(source, other, sems.at[4 + number], sems.at[8 + number], here.sibling()),
            )
        )
    for kept, sent in copies:
        sent.start()
        kept.start()
    back_share = Share(here, gin_sum, share_in, share_sems)
    back_share.begin()
    targets = [(q_sum.at[:, pl.ds(side * width, width)], side * share, share) for side in range(sides)]
    targets.append((o_sum, sides * share, share))
    big = Sum(here, None, targets, halves_of((sides + 1) * share), False, scratch[0:8])
    few = Sum(here, None, few_sum, halves_of(few_sum.shape[0], False), False, scratch[8:16])
    order = [far_first(here, number) for number in range(DEPTH)]

    def fetch_panel(number):
        slot = lax.rem(number, 2)
        rows = pl.ds(pl.multiple_of(number * TILE, TILE), TILE)
        return pltpu.make_async_copy(weight.at[rows], panel.at[slot], panel_sems.at[slot])

    panels = width // TILE
    fetch_panel(0).start()
    for kept, sent in copies:
        kept.wait()
        sent.wait_recv()
    step = 512
    each = width // step
    rows = RING * 2 * share

    def make(z):
        at = pl.ds(pl.multiple_of(z * rows, rows), rows)

        def one(number, source):
            spot = pl.ds(pl.multiple_of(number * step, step), step)
            turned = source[:, :, at].reshape(2 * block, rows)
            made = contract_rows(turned, right[:, :, spot].reshape(2 * block, step))
            made = made.reshape(RING, 2, share, step)
            mine = jnp.where(here.core == 0, made[:, 0], made[:, 1]).astype(narrow)
            row = pl.multiple_of(lax.div(number, each) * share, share)
            column = pl.multiple_of(lax.rem(number, each) * step, step)
            for chip in range(RING):
                big.mine[z, chip, pl.ds(row, share), pl.ds(column, step)] = mine[chip]

        def qkv(number, carry):
            one(number, left)
            return carry

        def out(number, carry):
            one(number, left_out)
            return carry

        lax.fori_loop(0, sides * each, qkv, 0)
        lax.fori_loop(sides * each, (sides + 1) * each, out, 0)

    def through(first, last):
        def body(number, carry):
            fetch_panel(number).wait()
            pl.when(number + 1 < panels)(lambda: fetch_panel(number + 1).start())
            spot = pl.ds(pl.multiple_of(number * TILE, TILE), TILE)
            back[:, spot] = contract_last(right[0, :, 0:wide], panel[lax.rem(number, 2)])
            return carry

        lax.fori_loop(first, last, body, 0)

    def norm_back():
        piece[...] = pieces[...]
        high = 16

        def body(number, carry):
            at = pl.ds(pl.multiple_of(number * high, high), high)
            values = tokens[at].astype(single)
            factor = lax.rsqrt(jnp.mean(values * values, axis=-1, keepdims=True) + epsilon)
            normal = values * factor
            upstream = back[at]
            weighted = upstream * gain[...]
            inner = jnp.mean(weighted * normal, axis=-1, keepdims=True)
            grad_tokens[at] = grad_middle[at] + factor * (weighted - normal * inner)
            piece[0:1] += jnp.sum(upstream * normal, axis=0, keepdims=True)
            return carry

        lax.fori_loop(0, block // high, body, 0)
        for z in range(DEPTH):
            for chip in range(RING):
                begin = (z * RING + chip) * 2 * share
                few.mine[z, chip] = piece[:, begin : begin + 2 * share]

    for number, z in enumerate(order):
        make(z)
        for way in (0, 1):
            start(big.toss(z, way))
        if number:
            big.second(order[number - 1])
        if number > 1:
            big.third(order[number - 2], False)
        if number < 2:
            through(number * panels // 2, (number + 1) * panels // 2)
        if number == 2:
            norm_back()
            for place in order:
                start(few.toss(place, 0))
    big.second(order[-1])
    for z in order:
        few.second(z)
    big.third(order[-2], False)
    for z in order[:-1]:
        few.third(z, False)
    big.third(order[-1], True)
    few.third(order[-1], True)
    swap = remote(few_sum, few_other, pair_sems.at[0], pair_sems.at[1], here.sibling())
    swap.start()
    swap.wait_recv()
    gains[...] = few_sum[...] + few_other[...]
    swap.wait_send()
    for number, z in enumerate(order):
        for item in (big, few):
            item.end(z, number == DEPTH - 1)
    for kept, sent in copies:
        sent.wait_send()
    back_share.end()


def last_sum(normed, grad, attended, branch, gin_sum, weight, tokens, grad_middle, gain, pieces, share, held):
    block, width = normed.shape
    wide = grad.shape[1]
    rows = (wide // width + 1) * share
    vmem = pl.BlockSpec(memory_space=pltpu.VMEM)
    few = (pieces.shape[0], 2 * share)
    return pl.pallas_call(
        last_sum_kernel,
        out_shape=(
            jax.ShapeDtypeStruct((share, wide), single),
            jax.ShapeDtypeStruct((share, width), single),
            jax.ShapeDtypeStruct(few, single),
            jax.ShapeDtypeStruct((block, width), single),
            jax.ShapeDtypeStruct((held, gin_sum.shape[0] // DEPTH, DEPTH * gin_sum.shape[1] // held), narrow),
        ),
        in_specs=[HBM] * 6 + [vmem] * 4,
        out_specs=(vmem, vmem, vmem, vmem, HBM),
        scratch_shapes=[
            pltpu.VMEM((2, block, width), narrow),
            pltpu.VMEM((2, block, width), narrow),
            pltpu.VMEM((2, block, wide + width), narrow),
            pltpu.SemaphoreType.DMA((12,)),
            pltpu.VMEM((2, TILE, wide), narrow),
            pltpu.SemaphoreType.DMA((2,)),
            pltpu.VMEM((block, width), single),
            pltpu.VMEM(pieces.shape, single),
            pltpu.VMEM(few, single),
            pltpu.VMEM(few, single),
            pltpu.SemaphoreType.DMA((2,)),
            pltpu.SemaphoreType.DMA((2, DEPTH, 2 * held)),
        ]
        + sum_scratch(rows, width, narrow, halves_of(rows), made=True)
        + sum_scratch(few[0], few[1], single, halves_of(few[0], False), made=True),
        compiler_params=pltpu.CompilerParams(
            collective_id=4, has_side_effects=True, vmem_limit_bytes=62 * 2**20
        ),
        name="deliver",
    )(normed, grad, attended, branch, gin_sum, weight, tokens, grad_middle, gain, pieces)

def near_first(here, number):
    high = lax.div(here.z, 2)
    inner = lax.rem(lax.div(here.z + 1, 2), 2)
    low = number + inner * (1, -1, 0, 0)[number]
    return low + high * (DEPTH - 1 - 2 * low)


class Tiles:
    def __init__(self, here, stage, count, sems, parts, targets):
        self.here, self.stage, self.count = here, stage, count
        self.kept, self.sent, self.came = sems
        self.parts, self.targets = parts, targets

    def copies(self, number, keep=True, give=True):
        slot = lax.rem(number, 2)
        own, other = self.targets
        made = []
        for piece, (mine, theirs, spot) in enumerate(self.parts(number, self.stage.at[slot])):
            if keep:
                made.append(pltpu.make_async_copy(mine, own.at[spot], self.kept.at[slot, piece]))
            if give:
                sems = (self.sent.at[slot, piece], self.came.at[number, piece])
                made.append(remote(theirs, other.at[spot], *sems, self.here.sibling()))
        return made

    def settle(self, number):
        for copy in self.copies(number, give=False):
            copy.wait()
        for copy in self.copies(number, keep=False):
            copy.wait_send()

    def run(self, first, last, make):
        def body(number, carry):
            pl.when(number >= 2)(lambda: self.settle(number - 2))
            make(number, self.stage.at[lax.rem(number, 2)])
            for copy in self.copies(number):
                copy.start()
            return carry

        lax.fori_loop(first, last, body, 0)
        if last == self.count:
            for number in (last - 2, last - 1):
                self.settle(number)

    def heard(self):
        for number in range(self.count):
            for copy in self.copies(number, keep=False):
                copy.wait_recv()


def experts_kernel(
    rows, ups, gates, win, wout, mid_sum, gate_sum, out_sum, gin_sum, gdown, gdown_other, gin, gin_other, rows_all, *scratch
):
    here = Here()
    here.meet()
    (
        w_in, w_out, grads, scaled, row_plane, up_plane, gate_plane, served, strip, stage, loads, strip_sems
    ) = scratch[:12]
    gather = Gather(here, rows, rows_all, halves_of(rows.shape[0]), False, scratch[12:16])
    mids = Sum(here, None, mid_sum, halves_of(rows.shape[0]), False, scratch[16:24])
    outs = Sum(here, None, out_sum, halves_of(rows.shape[0]), False, scratch[16:19] + scratch[24:29])
    tables = Sum(here, None, gate_sum, halves_of(gate_sum.shape[0], False), False, scratch[29:37])
    in_sems, down_sems = scratch[37:40], scratch[40:43]
    block, width = rows.shape
    plane = RING * block
    hidden = w_out.shape[0]
    chunk = hidden // 4
    column = lax.broadcasted_iota(jnp.int32, (plane, 128), 1)
    fetch_in = pltpu.make_async_copy(win, w_in, loads.at[0])
    fetch_out = pltpu.make_async_copy(wout, w_out, loads.at[1])
    fetch_in.start()
    fetch_out.start()

    def fetch_plane(number):
        z = near_first(here, number)
        return (
            pltpu.make_async_copy(ups.at[z], up_plane.at[number % 2], loads.at[2 + number % 2]),
            pltpu.make_async_copy(gates.at[z], gate_plane.at[number % 2], loads.at[4 + number % 2]),
        )

    def fetch_rows(number):
        return pltpu.make_async_copy(rows_all.at[near_first(here, number)], row_plane, loads.at[6])

    def hidden_units(number):
        z = near_first(here, number)
        fetch_rows(number).start()
        for copy in fetch_plane(number):
            copy.wait()
        if number == 0:
            fetch_in.wait()
            fetch_out.wait()
        fetch_rows(number).wait()
        served[...] = jnp.zeros_like(served)
        at = pl.ds(pl.multiple_of(z * plane, plane), plane)

        def one(expert, carry):
            mid = row_plane[...].reshape(plane, width)
            up_rows = up_plane[number % 2]
            spot = pl.ds(pl.multiple_of(expert * chunk, chunk), chunk)
            spot_up = pl.ds(pl.multiple_of(hidden + expert * chunk, chunk), chunk)
            gate = jnp.sum(jnp.where(column == expert, gate_plane[number % 2], 0.0), axis=1, keepdims=True)
            gate_part = jnp.dot(mid, w_in[:, spot], preferred_element_type=single)
            up_part = jnp.dot(mid, w_in[:, spot_up], preferred_element_type=single)
            back = contract_last(up_rows, w_out[spot])
            sigmoid = 1.0 / (1.0 + jnp.exp(-gate_part))
            activated = gate_part * sigmoid
            units = activated * up_part
            scaled[at, spot] = (gate * units).astype(narrow)
            total = jnp.sum(units * back, axis=1, keepdims=True)
            served[...] += jnp.where(column == here.chip * 4 + expert, total, 0.0)
            grad = gate * back
            grads[at, spot] = (grad * up_part * (sigmoid * (1.0 + gate_part * (1.0 - sigmoid)))).astype(narrow)
            grads[at, spot_up] = (grad * activated).astype(narrow)
            return carry

        lax.fori_loop(0, 4, one, 0)
        for chip in range(RING):
            turned = jnp.transpose(served[chip * block : (chip + 1) * block])
            tables.mine[z, chip] = turned[: tables.rows]

    def row_grads(z):
        at = pl.ds(pl.multiple_of(z * plane, plane), plane)

        def one(number, carry):
            spot = pl.ds(pl.multiple_of(number * TILE, TILE), TILE)
            made = contract_last(grads[at], w_in[spot]).astype(narrow)
            for chip in range(RING):
                mids.mine[z, chip, :, spot] = made[chip * block : (chip + 1) * block]
            return carry

        lax.fori_loop(0, width // TILE, one, 0)

    def products(z):
        at = pl.ds(pl.multiple_of(z * plane, plane), plane)

        def one(number, carry):
            spot = pl.ds(pl.multiple_of(number * TILE, TILE), TILE)
            made = jnp.dot(scaled[at], w_out[:, spot], preferred_element_type=single).astype(narrow)
            for chip in range(RING):
                outs.mine[z, chip, :, spot] = made[chip * block : (chip + 1) * block]
            return carry

        lax.fori_loop(0, width // TILE, one, 0)

    strips = width // TILE

    def fetch_strip(number):
        spot = pl.ds(pl.multiple_of(number * TILE, TILE), TILE)
        slot = lax.rem(number, 2)
        return pltpu.make_async_copy(rows_all.at[:, :, :, spot], strip.at[slot], strip_sems.at[slot])

    def columns_of(result, stage, step=512):
        for begin in range(0, width, step):
            stage[:, begin : begin + step] = result(begin, step).astype(narrow)

    def grad_in(number, stage):
        slot = lax.rem(number, 2)
        fetch_strip(number).wait()
        pl.when(number + 1 < strips)(lambda: fetch_strip(number + 1).start())
        left = strip[slot].reshape(DEPTH * plane, TILE)
        columns_of(lambda begin, step: contract_rows(left, grads[:, begin : begin + step]), stage)

    def grad_in_parts(number, stage):
        share = hidden // 2
        at = pl.ds(pl.multiple_of(number * TILE, TILE), TILE)
        for side in range(2):
            mine, theirs = (
                stage.at[:, pl.ds(pl.multiple_of(side * hidden + core * share, 128), share)]
                for core in (here.core, 1 - here.core)
            )
            yield mine, theirs, (at, pl.ds(side * share, share))

    def grad_down(number, stage):
        half = tall // 2
        core = here.core + (1 - lax.div(number, half)) * (1 - 2 * here.core)
        at = core * half + lax.rem(number, half)
        left = scaled[:, pl.ds(pl.multiple_of(at * TILE, TILE), TILE)]
        columns_of(lambda begin, step: contract_rows(left, w_in[:, begin : begin + step]), stage)

    tall = hidden // TILE
    tiles_in = Tiles(here, stage, strips, in_sems, grad_in_parts, (gin, gin_other))

    def grad_down_store(number, away):
        slot = lax.rem(number, 2)
        rest = lax.rem(number, tall // 2)
        spot = pl.ds(pl.multiple_of(rest * TILE, TILE), TILE)
        kept, sent, came = down_sems
        if away:
            return remote(stage.at[slot], gdown_other.at[spot], sent.at[slot, 0], came.at[rest, 0], here.sibling())
        return pltpu.make_async_copy(stage.at[slot], gdown.at[spot], kept.at[slot, 0])

    def grads_down(away):
        first = 0 if away else tall // 2

        def body(number, carry):
            grad_down(number, stage.at[lax.rem(number, 2)])
            grad_down_store(number, away).start()
            return carry

        lax.fori_loop(first, first + tall // 2, body, 0)
        for number in range(first, first + tall // 2):
            copy = grad_down_store(number, away)
            copy.wait_send() if away else copy.wait()

    def add_cores():
        half = hidden
        adds, puts = scratch[43], scratch[44]

        def fetch(number):
            slot = lax.rem(number, 2)
            at = pl.ds(pl.multiple_of(number * TILE, TILE), TILE)
            return [
                pltpu.make_async_copy(
                    source.at[at], stage.at[slot, :, pl.ds(side * half, half)], adds.at[slot, side]
                )
                for side, source in enumerate((gin, gin_other))
            ]

        def put(number):
            slot = lax.rem(number, 2)
            at = pl.ds(pl.multiple_of(number * TILE, TILE), TILE)
            return pltpu.make_async_copy(stage.at[slot, :, pl.ds(0, half)], gin_sum.at[at], puts.at[slot])

        def start_fetch(number):
            for copy in fetch(number):
                copy.start()

        def body(number, carry):
            for copy in fetch(number):
                copy.wait()
            pl.when(number >= 1)(lambda: put(number - 1).wait())
            pl.when(number + 1 < strips)(lambda: start_fetch(number + 1))
            slot = lax.rem(number, 2)
            own = stage.at[slot, :, pl.ds(0, half)]
            add_up(own, [own, stage.at[slot, :, pl.ds(half, half)]], TILE, half)
            put(number).start()
            return carry

        start_fetch(0)
        lax.fori_loop(0, strips, body, 0)
        put(strips - 1).wait()

    again = [
        pltpu.make_async_copy(ups.at[z], w_in.at[pl.ds(z * plane, plane)], loads.at[7 + z]) for z in range(DEPTH)
    ]

    def again_wait():
        for copy in again:
            copy.wait()

    order = [far_first(here, number) for number in range(DEPTH)]
    first = [mids, tables]
    steps = [(first, z, False) for z in [here.z] + order[:-1]]
    steps += [([outs], z, number == DEPTH - 1) for number, z in enumerate(order)]

    def begin(number):
        items, z, last = steps[number]
        if number < DEPTH:
            row_grads(z)
        else:
            mids.end(z, last)
            products(z)
        for item in items:
            for way in (0, 1):
                start(item.toss(z, way))

    def second(number):
        for item in steps[number][0]:
            item.second(steps[number][1])

    def third(number):
        items, z, last = steps[number]
        for item in items:
            item.own_part(z) if number == 0 else item.third(z, last)

    for copy in fetch_plane(0):
        copy.start()
    rounds = Rounds(here, [gather])
    rounds.service(0)
    for number in range(DEPTH):
        if number + 1 < DEPTH:
            rounds.service(number + 1)
        if number == DEPTH - 1:
            second(0)
        gather_third(gather, near_first(here, number))
        if number + 1 < DEPTH:
            for copy in fetch_plane(number + 1):
                copy.start()
        hidden_units(number)
        if number == 1:
            begin(0)
    fetch_strip(0).start()
    ends = [0] + [strips * (number + 1) // (DEPTH - 1) for number in range(DEPTH - 1)]
    for number in range(1, 2 * DEPTH):
        begin(number)
        if number > 1:
            second(number - 1)
            third(number - 2)
        if number == DEPTH - 1:
            for copy in again:
                copy.start()
        if number < DEPTH:
            tiles_in.run(ends[number - 1], ends[number], grad_in)
        elif number == DEPTH:
            again_wait()
            grads_down(True)
        elif number == DEPTH + 1:
            grads_down(False)
        elif number == DEPTH + 2:
            for item in first:
                item.own_rest(here.z)
            tiles_in.heard()
            add_cores()
    outs.second(order[-1])
    outs.third(order[-2], False)
    outs.third(order[-1], True)
    for number, z in enumerate(order):
        outs.end(z, number == DEPTH - 1)
        tables.end(z, number == DEPTH - 1)
    for number in range(tall // 2):
        grad_down_store(number, True).wait_recv()
    rounds.finish()


def experts_round(rows, ups, gates, win, wout, experts):
    block, width = rows.shape
    plane = RING * block
    hidden = wout.shape[0]
    total = DEPTH * plane
    vmem = pl.BlockSpec(memory_space=pltpu.VMEM)
    return pl.pallas_call(
        experts_kernel,
        out_shape=(
            jax.ShapeDtypeStruct((block, width), single),
            jax.ShapeDtypeStruct((experts, block), single),
            jax.ShapeDtypeStruct((block, width), single),
            jax.ShapeDtypeStruct((width, hidden), narrow),
            jax.ShapeDtypeStruct((hidden // 2, width), narrow),
            jax.ShapeDtypeStruct((hidden // 2, width), narrow),
            jax.ShapeDtypeStruct((width, hidden), narrow),
            jax.ShapeDtypeStruct((width, hidden), narrow),
            jax.ShapeDtypeStruct((DEPTH, RING, block, width), narrow),
        ),
        in_specs=[HBM] * 5,
        out_specs=(vmem, vmem, vmem) + (HBM,) * 6,
        scratch_shapes=[
            pltpu.VMEM((width, 2 * hidden), narrow),
            pltpu.VMEM((hidden, width), narrow),
            pltpu.VMEM((total, 2 * hidden), narrow),
            pltpu.VMEM((total, hidden), narrow),
            pltpu.VMEM((RING, block, width), narrow),
            pltpu.VMEM((2, plane, width), narrow),
            pltpu.VMEM((2, plane, 128), single),
            pltpu.VMEM((plane, 128), single),
            pltpu.VMEM((2, DEPTH, RING, block, TILE), narrow),
            pltpu.VMEM((2, TILE, width), narrow),
            pltpu.SemaphoreType.DMA((11,)),
            pltpu.SemaphoreType.DMA((2,)),
        ]
        + GATHER_SEMS
        + sum_scratch(block, width, narrow, halves_of(block), made=True)
        + [pltpu.VMEM((DEPTH + 1, block, width), narrow)]
        + SUM_SEMS
        + sum_scratch(experts, block, single, halves_of(experts, False), made=True)
        + [
            pltpu.SemaphoreType.DMA((2, 2)),
            pltpu.SemaphoreType.DMA((2, 2)),
            pltpu.SemaphoreType.DMA((width // TILE, 2)),
        ]
        + [
            pltpu.SemaphoreType.DMA((2, 1)),
            pltpu.SemaphoreType.DMA((2, 1)),
            pltpu.SemaphoreType.DMA((hidden // TILE, 1)),
        ]
        + [pltpu.SemaphoreType.DMA((2, 2)), pltpu.SemaphoreType.DMA((2,))],
        compiler_params=pltpu.CompilerParams(
            collective_id=2, has_side_effects=True, vmem_limit_bytes=62 * 2**20
        ),
        name="experts",
    )(rows, ups, gates, win, wout)


def by_kernels():
    return lax.axis_size("dp") == DEPTH and lax.axis_size("expert") == 2 * RING


def bring_all(w_qkv, w_out, upstream, dense, gain_rows, expert_in, expert_out):
    width = upstream.shape[1]
    share = gain_rows.shape[1]
    if by_kernels():
        experts, rows = dense.shape[1], dense.shape[0]
        small = jnp.concatenate([dense.T, jnp.pad(gain_rows, ((0, 4), (0, rows - share)))], axis=0)
        wq, wo, up, all_small, weight_in, weight_down = first_gather(
            w_qkv, w_out, upstream, small, expert_in, expert_out
        )
        gains = all_small[:, :, :, experts : experts + 4, :share].transpose(3, 0, 1, 2, 4).reshape(4, -1)
        core = lax.rem(lax.axis_index("expert"), 2)
        every_gate = lax.dynamic_index_in_dim(all_small, core, axis=2, keepdims=False)[:, :, :experts]
        return (
            wq.reshape(-1, w_qkv.shape[1]),
            wo.reshape(-1, w_out.shape[1]),
            up.reshape(-1, width),
            every_gate,
            gains,
            weight_in,
            weight_down.reshape(-1, width),
        )
    everyone = ("dp", "expert")
    weight_in, weight_down = fetch_weights(expert_in, expert_out)
    return (
        lax.all_gather(w_qkv, everyone, axis=0, tiled=True),
        lax.all_gather(w_out, everyone, axis=0, tiled=True),
        gather_alike(upstream).reshape(-1, width),
        gather_alike(dense.T),
        lax.all_gather(gain_rows, everyone, axis=1, tiled=True),
        weight_in,
        weight_down,
    )


def experts_all(routed_in, up_rows, every_gate, weight_in, weight_down, held):
    depth = lax.axis_size("dp")
    owners = lax.axis_size("expert")
    chips = owners // 2
    experts = owners * held
    chip_experts = 2 * held
    rows, width = routed_in.shape
    chip = lax.axis_index("expert") // 2
    mine = lax.dynamic_slice_in_dim(every_gate, chip * chip_experts, chip_experts, axis=2)
    gate = mine.transpose(0, 1, 3, 2)
    if by_kernels():
        gate = jnp.pad(gate.reshape(DEPTH, -1, chip_experts), ((0, 0), (0, 0), (0, 128 - chip_experts)))
        ups = up_rows.reshape(DEPTH, -1, width)
        grad_routed, table, mixture, grad_in, grad_down, grad_down_other = experts_round(
            routed_in, ups, gate, weight_in, weight_down, experts
        )[:6]
        down = grad_down.astype(single) + grad_down_other.astype(single)
        return (mixture, grad_routed, table, (grad_in, down.reshape(held, -1, width)))
    mid_rows = gather_alike(routed_in).reshape(-1, width)
    out, mid, served, grad_in, grad_down = expert_rounds(
        mid_rows, up_rows, gate.reshape(-1, chip_experts), weight_in, weight_down
    )
    by_gate = served.reshape(depth, chips, rows, chip_experts).transpose(0, 1, 3, 2)
    spread = jnp.zeros((depth, chips, experts, rows), single)
    spread = lax.dynamic_update_slice_in_dim(spread, by_gate, chip * chip_experts, axis=2)
    return (
        scatter_alike(out.reshape(depth, chips, rows, width)).astype(single),
        scatter_alike(mid.reshape(depth, chips, rows, width)).astype(single),
        scatter_alike(spread),
        return_weights(grad_in, grad_down, held),
    )


def deliver_all(tokens, gain, grad_middle, pieces, normed, grad_qkv, weight_qkv, attended, branch, share_in, held):
    owners = lax.axis_size("dp") * lax.axis_size("expert")
    share = gain.shape[0] // owners
    if by_kernels():
        rows = jnp.stack([jnp.zeros_like(gain), *pieces] + [jnp.zeros_like(gain)] * (7 - len(pieces)))
        share_qkv, share_out, gains, grad_tokens, share_in = last_sum(
            normed, grad_qkv, attended, branch, share_in, weight_qkv, tokens, grad_middle, gain[None], rows, share, held
        )
        core = lax.rem(lax.axis_index("expert"), 2)
        gains = lax.dynamic_slice_in_dim(gains, core * share, share, axis=1)
        return (grad_tokens, gains, share_qkv, share_out, share_in.astype(single))
    everyone = ("dp", "expert")
    normal, factor = normalize(tokens.astype(single))
    grad_input, piece = rms_back(contract_last(grad_qkv, weight_qkv), normal, factor, gain)
    return (
        grad_middle + grad_input,
        lax.psum_scatter(jnp.stack([piece, *pieces]), everyone, scatter_dimension=1, tiled=True),
        *(
            lax.psum_scatter(
                contract_rows(left, right, narrow), everyone, scatter_dimension=0, tiled=True
            ).astype(single)
            for left, right in ((normed, grad_qkv), (attended, branch))
        ),
        share_in.astype(single),
    )


def local(
    tokens,
    lengths,
    expert_ids,
    gates,
    attn_gain,
    w_qkv,
    q_gain,
    k_gain,
    w_out,
    ffn_gain,
    expert_in,
    expert_out,
    out_grad,
):
    micro_count, seq_len, model_width = tokens.shape
    rows = micro_count * seq_len
    held = expert_in.shape[0]
    experts = lax.axis_size("expert") * held
    inputs = tokens.reshape(rows, model_width).astype(single)
    upstream = out_grad.reshape(rows, model_width)
    ids = expert_ids.reshape(rows, -1)
    gate_rows = gates.reshape(rows, -1)
    onehot = (ids[:, :, None] == jnp.arange(experts, dtype=jnp.int32)).astype(single)
    dense = jnp.sum(onehot * gate_rows[:, :, None], axis=1)
    gain_rows = jnp.stack([attn_gain, q_gain, k_gain, ffn_gain]).astype(single)
    weight_qkv, weight_out, up_rows, every_gate, gains, weight_in, weight_down = bring_all(
        w_qkv, w_out, upstream, dense, gain_rows, expert_in, expert_out
    )
    gain_attn, gain_query, gain_key, gain_ffn = gains[0], gains[1], gains[2], gains[3]

    normal_in, factor_in = normalize(inputs)
    normed_in = (normal_in * gain_attn).astype(narrow)
    projected = jnp.dot(normed_in, weight_qkv, preferred_element_type=single)
    normal_q, factor_q = normalize(projected[:, :model_width])
    normal_k, factor_k = normalize(projected[:, model_width : 2 * model_width])
    document, position = layout(lengths[:, 0], seq_len)
    cosine, sine = angles(position)
    query_rows = rotate(normal_q * gain_query, cosine, sine).astype(narrow).reshape(rows, -1, HEAD)
    key_rows = rotate(normal_k * gain_key, cosine, sine).astype(narrow).reshape(rows, -1, HEAD)
    value_rows = projected[:, 2 * model_width :].astype(narrow).reshape(rows, -1, HEAD)
    places = jnp.arange(rows, dtype=jnp.int32)
    allowed = (document[:, None] == document[None, :]) & (places[:, None] >= places[None, :])
    raw = jnp.einsum("qhd,khd->hqk", query_rows, key_rows, preferred_element_type=single)
    scores = jnp.where(allowed[None], raw * HEAD ** (-0.5), masked_score)
    highest = jnp.max(scores, axis=-1, keepdims=True)
    unnormed = jnp.exp(scores - highest)
    probs = unnormed / jnp.sum(unnormed, axis=-1, keepdims=True)
    attn_probs = probs.astype(narrow)
    attended = (
        jnp.einsum("hqk,khd->qhd", attn_probs, value_rows, preferred_element_type=single)
        .reshape(rows, model_width)
        .astype(narrow)
    )
    middle = inputs + jnp.dot(attended, weight_out, preferred_element_type=single)
    normal_mid, factor_mid = normalize(middle)
    routed_in = (normal_mid * gain_ffn).astype(narrow)

    mixture, grad_routed, gate_table, (share_in, share_down) = experts_all(
        routed_in, up_rows, every_gate, weight_in, weight_down, held
    )
    grad_gates = jnp.sum(onehot * gate_table.T[:, None, :], axis=2)
    results = (middle + mixture).astype(narrow)

    grad_mid, piece_ffn = rms_back(grad_routed, normal_mid, factor_mid, gain_ffn)
    grad_middle = upstream.astype(single) + grad_mid
    grad_branch = grad_middle.astype(narrow)
    grad_attended = contract_last(grad_branch, weight_out).astype(narrow).reshape(rows, -1, HEAD)
    grad_probs = jnp.einsum("qhd,khd->hqk", grad_attended, value_rows, preferred_element_type=single)
    inner = jnp.sum(grad_probs * probs, axis=-1, keepdims=True)
    grad_scores = (probs * (grad_probs - inner)).astype(narrow)
    grad_query = jnp.einsum(
        "hqk,khd->qhd", grad_scores, key_rows, preferred_element_type=single
    ) * HEAD ** (-0.5)
    grad_key = jnp.einsum(
        "hqk,qhd->khd", grad_scores, query_rows, preferred_element_type=single
    ) * HEAD ** (-0.5)
    grad_value = jnp.einsum("hqk,qhd->khd", attn_probs, grad_attended, preferred_element_type=single)
    grad_q_raw, piece_query = rms_back(
        rotate(grad_query.reshape(rows, model_width), cosine, -sine), normal_q, factor_q, gain_query
    )
    grad_k_raw, piece_key = rms_back(
        rotate(grad_key.reshape(rows, model_width), cosine, -sine), normal_k, factor_k, gain_key
    )
    grad_qkv = jnp.concatenate(
        [grad_q_raw, grad_k_raw, grad_value.reshape(rows, model_width)], axis=1
    ).astype(narrow)
    grad_tokens, gain_sums, grad_qkv_share, grad_out_share, share_in = deliver_all(
        tokens.reshape(rows, model_width),
        gain_attn,
        grad_middle,
        (piece_query, piece_key, piece_ffn),
        normed_in,
        grad_qkv,
        weight_qkv,
        attended,
        grad_branch,
        share_in,
        held,
    )
    shape = (micro_count, seq_len, model_width)
    return (
        results.reshape(shape),
        grad_tokens.reshape(shape),
        grad_gates.reshape(expert_ids.shape),
        gain_sums[0],
        grad_qkv_share,
        gain_sums[1],
        gain_sums[2],
        grad_out_share,
        gain_sums[3],
        share_in,
        share_down.astype(single),
    )


def solution(mesh):
    by_rows = P(None, ("dp", "expert"), None)
    flat = P(("dp", "expert"))
    split = P(("dp", "expert"), None)
    held = P("expert", "dp", None)
    return jax.shard_map(
        local,
        mesh=mesh,
        in_specs=(
            by_rows, by_rows, by_rows, by_rows, flat, split, flat, flat, split, flat, held, held, by_rows,
        ),
        out_specs=(by_rows, by_rows, by_rows, flat, split, flat, flat, split, flat, held, held),
        check_vma=False,
    )
```

```python
import jax
import jax.numpy as jnp
from jax import lax
from jax.experimental import pallas as pl
from jax.experimental.pallas import tpu as pltpu
from jax.sharding import PartitionSpec as P

HEAD = 128
epsilon = 1e-05
base_theta = 10000.0
masked_score = -1e30
single = jnp.float32
narrow = jnp.bfloat16


def normalize(values):
    factor = lax.rsqrt(jnp.mean(values * values, axis=-1, keepdims=True) + epsilon)
    return (values * factor, factor)


def rms_back(upstream, normal, factor, gain):
    weighted = upstream * gain
    inner = jnp.mean(weighted * normal, axis=-1, keepdims=True)
    return (factor * (weighted - normal * inner), jnp.sum(upstream * normal, axis=0))


def angles(position):
    half = HEAD // 2
    ladder = jnp.arange(half, dtype=single) * (2.0 / HEAD)
    frequency = jnp.exp(-jnp.log(base_theta) * ladder)
    angle = position.astype(single)[:, None] * frequency[None, :]
    return (jnp.cos(angle)[:, None, :], jnp.sin(angle)[:, None, :])


def rotate(field, cosine, sine):
    length = field.shape[0]
    heads = field.reshape(length, -1, HEAD)
    half = HEAD // 2
    first = heads[..., :half]
    second = heads[..., half:]
    turned = jnp.concatenate(
        [first * cosine - second * sine, second * cosine + first * sine], axis=-1
    )
    return turned.reshape(length, -1)


def layout(doc_lengths, length):
    packs, count = doc_lengths.shape
    upto = jnp.arange(count)[None, :] <= jnp.arange(count)[:, None]
    ends = jnp.sum(jnp.where(upto[None], doc_lengths[:, None, :], 0), axis=2)
    starts = ends - doc_lengths
    places = jnp.arange(length, dtype=jnp.int32)[None, :, None]
    document = jnp.sum((places >= ends[:, None, :]).astype(jnp.int32), axis=2)
    member = (places >= starts[:, None, :]) & (places < ends[:, None, :])
    first_place = jnp.sum(jnp.where(member, starts[:, None, :], 0), axis=2)
    document = document + (count + 1) * jnp.arange(packs, dtype=jnp.int32)[:, None]
    return (document.reshape(-1), (places[..., 0] - first_place).reshape(-1))


def contract_rows(left, right, kind=single):
    return lax.dot_general(left, right, (((0,), (0,)), ((), ())), preferred_element_type=kind)


def contract_last(left, right, kind=single):
    return lax.dot_general(left, right, (((1,), (1,)), ((), ())), preferred_element_type=kind)


def core_groups():
    return [[2 * chip + core for chip in range(lax.axis_size("expert") // 2)] for core in range(2)]


def chip_groups():
    return [[2 * chip, 2 * chip + 1] for chip in range(lax.axis_size("expert") // 2)]


def gather_alike(block):
    column = lax.all_gather(block, "dp", axis=0)
    return lax.all_gather(column, "expert", axis=1, axis_index_groups=core_groups())


def scatter_alike(blocks):
    column = lax.psum_scatter(
        blocks, "expert", scatter_dimension=1, axis_index_groups=core_groups()
    )
    return lax.psum_scatter(column, "dp", scatter_dimension=0)


def fetch_weights(expert_in, expert_out):
    depth = lax.axis_size("dp")
    held, rows, columns = expert_in.shape
    part = columns // (2 * depth)
    cut = expert_in.reshape(held, rows, 2, depth, part)
    turned = lax.all_to_all(cut, "dp", split_axis=3, concat_axis=1, tiled=True)
    both = lax.all_gather(turned[:, :, :, 0], "expert", axis=0, axis_index_groups=chip_groups())
    weight_in = both.transpose(2, 3, 0, 1, 4).reshape(depth * rows, 4 * held * part)
    weight_down = lax.all_gather(
        expert_out, "expert", axis=0, axis_index_groups=chip_groups()
    ).reshape(-1, expert_out.shape[2])
    return (weight_in, weight_down)


def return_weights(grad_in, grad_down, held):
    depth = lax.axis_size("dp")
    rows, columns = grad_in.shape
    part = columns // (4 * held)
    cut = grad_in.reshape(rows, 2, 2, held, part)
    own = lax.psum_scatter(cut, "expert", scatter_dimension=2, axis_index_groups=chip_groups())
    own = own.reshape(depth, rows // depth, 2, held, part)
    turned = lax.all_to_all(own, "dp", split_axis=0, concat_axis=0)
    share_in = turned.transpose(3, 1, 2, 0, 4).reshape(held, rows // depth, 2 * depth * part)
    down = grad_down.reshape(2, held, part, grad_down.shape[1])
    share_down = lax.psum_scatter(
        down, "expert", scatter_dimension=0, axis_index_groups=chip_groups()
    )
    return (share_in, share_down)


def expert_round(mid_rows, up_rows, gate, weight_in, weight_down):
    count = gate.shape[1]
    part = weight_down.shape[0] // count
    wide = jnp.broadcast_to(gate[:, :, None], gate.shape + (part,)).reshape(gate.shape[0], -1)
    gate_up = jnp.dot(mid_rows, weight_in, preferred_element_type=single)
    hidden_units = gate_up.shape[1] // 2
    gate_part = gate_up[:, :hidden_units]
    up_part = gate_up[:, hidden_units:]
    sigmoid = jax.nn.sigmoid(gate_part)
    activated = gate_part * sigmoid
    hidden = activated * up_part
    back = contract_last(up_rows, weight_down)
    scaled = (wide * hidden).astype(narrow)
    piece_out = jnp.dot(scaled, weight_down, preferred_element_type=narrow)
    piece_gates = jnp.sum((hidden * back).reshape(-1, count, part), axis=2)
    grad_hidden = wide * back
    grad_gate = grad_hidden * up_part * sigmoid * (1.0 + gate_part * (1.0 - sigmoid))
    grad_up = grad_hidden * activated
    grad_gate_up = jnp.concatenate([grad_gate, grad_up], axis=1).astype(narrow)
    piece_mid = contract_last(grad_gate_up, weight_in, narrow)
    return (piece_out, piece_mid, piece_gates, grad_gate_up, scaled)


def expert_rounds(mid_rows, up_rows, gate, weight_in, weight_down):
    total = mid_rows.shape[0]
    rounds = max(1, total // 2048)

    def one(sums, pieces):
        mid, up, weights = pieces
        piece_out, piece_mid, piece_gates, grad_gate_up, scaled = expert_round(
            mid, up, weights, weight_in, weight_down
        )
        grads = (contract_rows(mid, grad_gate_up), contract_rows(scaled, up))
        return (jax.tree.map(jnp.add, sums, grads), (piece_out, piece_mid, piece_gates))

    if rounds == 1:
        piece_out, piece_mid, piece_gates, grad_gate_up, scaled = expert_round(
            mid_rows, up_rows, gate, weight_in, weight_down
        )
        grads = (contract_rows(mid_rows, grad_gate_up, narrow), contract_rows(scaled, up_rows, narrow))
        return (piece_out, piece_mid, piece_gates) + grads
    start = (jnp.zeros(weight_in.shape, single), jnp.zeros(weight_down.shape, single))
    cut = jax.tree.map(lambda a: a.reshape(rounds, total // rounds, -1), (mid_rows, up_rows, gate))
    sums, made = lax.scan(one, start, cut)
    made = jax.tree.map(lambda a: a.reshape(total, -1), made)
    return made + (sums[0].astype(narrow), sums[1].astype(narrow))


MESH = pl.DeviceIdType.MESH
HBM = pl.BlockSpec(memory_space=pl.ANY)
DEPTH = 4
RING = 4


def ring_turn(number):
    high = lax.div(number, 2)
    return number + high * (1 - 2 * lax.rem(number, 2))


class Here:
    def __init__(self):
        number = lax.axis_index("expert")
        self.z = lax.axis_index("dp")
        self.core = lax.rem(number, 2)
        self.chip = lax.div(number, 2)
        self.q = ring_turn(self.chip)

    def chip_at(self, turn):
        return ring_turn(lax.rem(self.q + turn + RING, RING))

    def beside(self, turn):
        return (self.z, 2 * self.chip_at(turn) + self.core)

    def above(self, steps):
        return (lax.rem(self.z + steps + DEPTH, DEPTH), 2 * self.chip + self.core)

    def sibling(self):
        return (self.z, 2 * self.chip + 1 - self.core)

    def meet(self):
        barrier = pltpu.get_barrier_semaphore()
        others = [self.beside(1), self.beside(-1), self.sibling()]
        others += [self.above(steps) for steps in range(1, DEPTH)]
        for other in others:
            pl.semaphore_signal(barrier, inc=1, device_id=other, device_id_type=MESH)
        pl.semaphore_wait(barrier, len(others))


def remote(source, target, sent, arrived, device):
    return pltpu.make_async_remote_copy(
        src_ref=source,
        dst_ref=target,
        send_sem=sent,
        recv_sem=arrived,
        device_id=device,
        device_id_type=MESH,
    )


GATHER_SEMS = [
    pltpu.SemaphoreType.DMA((2, 2, DEPTH - 1)),
    pltpu.SemaphoreType.DMA((2, DEPTH, 2, 2)),
    pltpu.SemaphoreType.DMA((2, DEPTH)),
    pltpu.SemaphoreType.DMA((1,)),
]


class Gather:
    def __init__(self, here, source, whole, halves, shared, sems):
        self.here, self.source, self.whole, self.halves, self.shared = here, source, whole, halves, shared
        self.line, self.ring, self.pair, self.own = sems

    def block(self, z, turn):
        chip = self.here.chip_at(turn)
        return self.whole.at[z, chip, self.here.core] if self.shared else self.whole.at[z, chip]

    def keep(self):
        return pltpu.make_async_copy(self.source, self.block(self.here.z, 0), self.own.at[0])

    def along(self, step, way, first):
        z = self.here.z - step + 1 if way == 0 else self.here.z + step - 1
        block = self.block(z, 0)
        return remote(
            self.source if first else block,
            block,
            self.line.at[0, way, step - 1],
            self.line.at[1, way, step - 1],
            self.here.above(1 if way == 0 else -1),
        )

    def round(self, z, way, first=False):
        turn = 1 if way == 0 else -1
        block = self.block(z, 0)
        return remote(
            self.source if first else block,
            block,
            self.ring.at[0, z, way, 0],
            self.ring.at[1, z, way, 0],
            self.here.beside(turn),
        )

    def heard(self, z, way):
        block = self.block(z, -1 if way == 0 else 1)
        return remote(
            block, block, self.ring.at[0, z, way, 0], self.ring.at[1, z, way, 0], self.here.beside(1)
        )

    def onward(self, z, way, mine):
        if self.halves[way] is None:
            return None
        turn = (-1 if mine else -2) if way == 0 else (1 if mine else 2)
        block = self.block(z, turn).at[pl.ds(*self.halves[way])]
        return remote(
            block,
            block,
            self.ring.at[0, z, way, 1],
            self.ring.at[1, z, way, 1],
            self.here.beside(1 if way == 0 else -1),
        )

    def swap(self, z, mine):
        core = self.here.core if mine else 1 - self.here.core
        part = self.whole.at[z, :, core]
        return remote(part, part, self.pair.at[0, z], self.pair.at[1, z], self.here.sibling())


def start(copy):
    if copy is not None:
        copy.start()


def gather_third(item, z):
    for way in (0, 1):
        copy = item.onward(z, way, False)
        if copy is not None:
            copy.wait_recv()


class Rounds:
    def __init__(self, here, items, ring=True):
        self.here, self.items = here, items
        for item in items:
            item.keep().start()
            for way in (0, 1):
                self.depart(0, way, item)
            if ring:
                for way in (0, 1):
                    item.round(here.z, way, True).start()

    def depart(self, step, way, item):
        here = self.here
        ahead = here.z + 1 < DEPTH if way == 0 else here.z >= 1
        pl.when(ahead)(lambda: item.along(step + 1, way, step == 0).start())

    def places(self, step, body):
        here = self.here
        if step == 0:
            body(here.z, 0)
            return
        pl.when(here.z >= step)(lambda: body(here.z - step, 0))
        pl.when(here.z + step < DEPTH)(lambda: body(here.z + step, 1))

    def line(self, step, ring=True):
        def body(z, way):
            for item in self.items:
                block = item.block(z, 0)
                remote(
                    block, block, item.line.at[0, way, step - 1], item.line.at[1, way, step - 1], self.here.above(1)
                ).wait_recv()
                if step + 1 < DEPTH:
                    self.depart(step, way, item)
                if ring:
                    for side in (0, 1):
                        item.round(z, side).start()

        self.places(step, body)

    def ring(self, step):
        def body(z, way):
            for item in self.items:
                for side in (0, 1):
                    item.round(z, side, step == 0).start()

        self.places(step, body)

    def second(self, step):
        def body(z, way):
            for item in self.items:
                for side in (0, 1):
                    item.heard(z, side).wait_recv()
                    start(item.onward(z, side, True))

        self.places(step, body)

    def service(self, step, between=None):
        if step + 1 < DEPTH:
            self.line(step + 1)
        if between is not None:
            between()
        if step == 0:
            self.kept()
        self.second(step)

    def kept(self):
        for item in self.items:
            item.keep().wait()

    def third(self, step):
        def body(z, way):
            for item in self.items:
                gather_third(item, z)
                if item.shared:
                    item.swap(z, True).start()

        self.places(step, body)

    def finish(self):
        def settle(z, way):
            for item in self.items:
                for side in (0, 1):
                    item.round(z, side).wait_send()
                    copy = item.onward(z, side, True)
                    if copy is not None:
                        copy.wait_send()
                if item.shared:
                    item.swap(z, True).wait_send()
                    item.swap(z, False).wait_recv()

        for step in range(DEPTH):
            self.places(step, settle)
        here = self.here
        for item in self.items:
            for step in range(DEPTH - 1):
                for way in (0, 1):

                    def sent(z, side, step=step, way=way, item=item):
                        if step and side != way:
                            return
                        ahead = here.z + 1 < DEPTH if way == 0 else here.z >= 1
                        pl.when(ahead)(lambda: item.along(step + 1, way, step == 0).wait_send())

                    self.places(step, sent)


class Recut:
    def __init__(self, here, source_in, source_out, whole_in, whole_out, sems):
        self.here, self.source_in, self.source_out = here, source_in, source_out
        self.whole_in, self.whole_out = whole_in, whole_out
        self.cut, self.pair, self.down, self.own = sems
        self.held, self.rows, columns = source_in.shape
        self.hidden = columns // 2
        self.part = self.hidden // DEPTH

    def pieces(self, steps, arriving):
        here, copies = self.here, []
        mine = lax.rem(here.z + DEPTH - steps, DEPTH) if arriving else here.z
        away = lax.rem(here.z + steps, DEPTH)
        for side in range(2):
            for expert in range(self.held):
                columns = side * self.held * 2 * self.part + (here.core * self.held + expert) * self.part
                target = self.whole_in.at[
                    pl.ds(pl.multiple_of(mine * self.rows, 16), self.rows),
                    pl.ds(pl.multiple_of(columns, 128), self.part),
                ]
                source = self.source_in.at[
                    expert, :, pl.ds(pl.multiple_of(side * self.hidden + away * self.part, 128), self.part)
                ]
                spot = (steps, side * self.held + expert)
                if steps == 0:
                    copies.append(pltpu.make_async_copy(source, target, self.own.at[spot[1]]))
                else:
                    copies.append(
                        remote(
                            target if arriving else source,
                            target,
                            self.cut.at[(0,) + spot],
                            self.cut.at[(1,) + spot],
                            here.above(steps),
                        )
                    )
        return copies

    def across(self, steps, mine):
        here, copies = self.here, []
        core = here.core if mine else 1 - here.core
        row = lax.rem(here.z + DEPTH - steps, DEPTH)
        width = self.held * self.part
        for side in range(2):
            spot = self.whole_in.at[
                pl.ds(pl.multiple_of(row * self.rows, 16), self.rows),
                pl.ds(pl.multiple_of(side * 2 * width + core * width, 128), width),
            ]
            copies.append(
                remote(spot, spot, self.pair.at[0, steps, side], self.pair.at[1, steps, side], here.sibling())
            )
        return copies

    def lower(self, mine):
        here = self.here
        core = here.core if mine else 1 - here.core
        spot = self.whole_out.at[pl.ds(core * self.held, self.held)]
        return remote(
            self.source_out if mine else spot, spot, self.down.at[0], self.down.at[1], here.sibling()
        )

    def lower_own(self):
        return pltpu.make_async_copy(
            self.source_out, self.whole_out.at[pl.ds(self.here.core * self.held, self.held)], self.own.at[4]
        )

    def begin(self):
        for copy in self.pieces(0, False):
            copy.start()
        self.lower_own().start()
        self.lower(True).start()
        for copies in zip(*[self.pieces(steps, False) for steps in (2, 3, 1)]):
            for copy in copies:
                copy.start()

    def relay(self):
        for steps in range(DEPTH):
            for copy in self.pieces(steps, True):
                copy.wait() if steps == 0 else copy.wait_recv()
            for copy in self.across(steps, True):
                copy.start()

    def end(self):
        self.lower_own().wait()
        self.lower(True).wait_send()
        self.lower(False).wait_recv()
        for steps in range(DEPTH):
            if steps:
                for copy in self.pieces(steps, False):
                    copy.wait_send()
            for copy in self.across(steps, True):
                copy.wait_send()
            for copy in self.across(steps, False):
                copy.wait_recv()


RECUT_SEMS = [
    pltpu.SemaphoreType.DMA((2, DEPTH, 4)),
    pltpu.SemaphoreType.DMA((2, DEPTH, 2)),
    pltpu.SemaphoreType.DMA((2,)),
    pltpu.SemaphoreType.DMA((5,)),
]


def halves_of(rows, split=True):
    return ((0, rows // 2), (rows // 2, rows - rows // 2)) if split else ((0, rows), None)


PANEL = 512


def attention_forward(
    tokens, cosine, sine, allowed, wq, wo, gains, normed, raw, queries, keys, values, probs, attended, middle, routed,
    panel, panel_sems, between
):
    block, width = tokens.shape
    heads = width // HEAD
    wide = wq.shape[-1]
    high = 16
    per = width // PANEL

    def fetch(source, number):
        slot = lax.rem(number, 2)
        spot = pl.ds(pl.multiple_of(number * PANEL, PANEL), PANEL)
        return pltpu.make_async_copy(source.at[:, :, :, :, spot], panel.at[slot], panel_sems.at[slot])

    def slabs(body):
        def one(number, carry):
            body(pl.ds(pl.multiple_of(number * high, high), high))
            return carry

        lax.fori_loop(0, block // high, one, 0)

    def first(at):
        values = tokens[at].astype(single)
        factor = lax.rsqrt(jnp.mean(values * values, axis=-1, keepdims=True) + epsilon)
        normed[at] = (values * factor * gains[0:1]).astype(narrow)

    fetch(wq, 0).start()
    slabs(first)

    def through(source, left, total, finish):
        def one(number, carry):
            fetch(source, number).wait()
            pl.when(number + 1 < total)(lambda: fetch(source, number + 1).start())
            weights = panel[lax.rem(number, 2)].reshape(width, PANEL)
            finish(number, jnp.dot(left[...], weights, preferred_element_type=single))
            return carry

        lax.fori_loop(0, total, one, 0)

    def keep(number, made):
        side = lax.div(number, per)
        spot = pl.ds(pl.multiple_of(lax.rem(number, per) * PANEL, PANEL), PANEL)

        @pl.when(side < 2)
        def _():
            raw[side, :, spot] = made

        @pl.when(side == 2)
        def _():
            values[:, spot] = made.astype(narrow)

    through(wq, normed, wide // PANEL, keep)
    fetch(wo, 0).start()
    between(0)

    factors = [
        lax.rsqrt(jnp.mean(raw[side] * raw[side], axis=-1, keepdims=True) + epsilon) for side in range(2)
    ]
    turn_cos, turn_sin = cosine[...], sine[...]
    may = allowed[...] > 0.5
    group = 4

    def some_heads(number, carry):
        for inner in range(group):
            head = number * group + inner
            spot = pl.ds(pl.multiple_of(head * HEAD, HEAD), HEAD)
            turned = []
            for side, target in ((0, queries), (1, keys)):
                field = raw[side, :, spot] * factors[side] * gains[side + 1 : side + 2, spot]
                field = field * turn_cos + pltpu.roll(field, HEAD // 2, 1) * turn_sin
                target[:, spot] = field.astype(narrow)
                turned.append(field.astype(narrow))
            scores = jnp.where(may, contract_last(turned[0], turned[1]) * HEAD ** (-0.5), masked_score)
            highest = jnp.max(scores, axis=-1, keepdims=True)
            unnormed = jnp.exp(scores - highest)
            shares = unnormed / jnp.sum(unnormed, axis=-1, keepdims=True)
            probs[head] = shares
            mixed = jnp.dot(shares.astype(narrow), values[:, spot], preferred_element_type=single)
            attended[:, spot] = mixed.astype(narrow)
        return carry

    lax.fori_loop(0, heads // group, some_heads, 0)
    between(1)

    def add(number, made):
        spot = pl.ds(pl.multiple_of(number * PANEL, PANEL), PANEL)
        middle[:, spot] = tokens[:, spot].astype(single) + made

    through(wo, attended, per, add)

    def last(at):
        values = middle[at]
        factor = lax.rsqrt(jnp.mean(values * values, axis=-1, keepdims=True) + epsilon)
        routed[at] = (values * factor * gains[3:4]).astype(narrow)

    slabs(last)
    between(2)


def first_gather_kernel(
    wq, wo, up, small, ein, eout, tokens, cosine, sine, allowed,
    wq_all, wo_all, up_all, small_all, win, wout, gains, normed, raw, queries, keys, values, probs, attended, middle, routed,
    small_here, small_sem, panel, panel_sems, *sems
):
    here = Here()
    here.meet()
    items = [
        Gather(here, source, whole, halves, shared, sems[4 * number : 4 * number + 4])
        for number, (source, whole, halves, shared) in enumerate(
            (
                (small, small_all, halves_of(small.shape[0], False), True),
                (wq, wq_all, halves_of(wq.shape[0]), True),
                (wo, wo_all, halves_of(wo.shape[0]), True),
                (up, up_all, halves_of(up.shape[0]), False),
            )
        )
    ]
    recut = Recut(here, ein, eout, win, wout, sems[16:20])
    weights = Rounds(here, items[:3])
    rows = Rounds(here, items[3:], ring=False)
    weights.service(0, lambda: rows.line(1, ring=False))
    weights.service(1, lambda: rows.line(2, ring=False))
    recut.begin()
    weights.third(0)
    weights.service(2, lambda: rows.line(3, ring=False))
    weights.third(1)
    weights.service(3)
    rows.kept()
    for step in range(DEPTH):
        rows.ring(step)
    weights.third(2)
    weights.third(3)
    weights.finish()
    fetch = pltpu.make_async_copy(small_all, small_here, small_sem.at[0])
    fetch.start()
    fetch.wait()
    share = wq.shape[0]
    lanes = small.shape[1]
    lane = lax.broadcasted_iota(jnp.int32, (8, lanes), 1)
    skip = small.shape[0] - 8
    for z in range(DEPTH):
        for chip in range(RING):
            pair = [small_here[z, chip, core, skip : skip + 8] for core in (0, 1)]
            both = jnp.where(lane < share, pair[0], pltpu.roll(pair[1], share, 1))
            begin = (z * RING + chip) * 2 * share
            gains[:, begin : begin + 2 * share] = both

    def between(part):
        if part == 0:
            rows.second(0)
        elif part == 1:
            for step in range(1, DEPTH):
                rows.second(step)
        else:
            recut.relay()

    attention_forward(
        tokens, cosine, sine, allowed, wq_all, wo_all, gains, normed, raw, queries, keys, values, probs, attended,
        middle, routed, panel, panel_sems, between
    )
    for step in range(DEPTH):
        rows.third(step)
    rows.finish()
    recut.end()


def first_gather(wq, wo, up, small, ein, eout, tokens, cosine, sine, allowed):
    def whole(array, shared):
        lead = (DEPTH, RING, 2) if shared else (DEPTH, RING)
        return jax.ShapeDtypeStruct(lead + array.shape, array.dtype)

    held, rows, columns = ein.shape
    block, width = tokens.shape
    heads = width // HEAD
    vmem = pl.BlockSpec(memory_space=pltpu.VMEM)
    like = jax.ShapeDtypeStruct((block, width), narrow)
    return pl.pallas_call(
        first_gather_kernel,
        out_shape=(
            whole(wq, True),
            whole(wo, True),
            whole(up, False),
            whole(small, True),
            jax.ShapeDtypeStruct((DEPTH * rows, columns), ein.dtype),
            jax.ShapeDtypeStruct((2 * held,) + eout.shape[1:], eout.dtype),
            jax.ShapeDtypeStruct((8, width), single),
            like,
            jax.ShapeDtypeStruct((2, block, width), single),
            like,
            like,
            like,
            jax.ShapeDtypeStruct((heads, block, block), single),
            like,
            jax.ShapeDtypeStruct((block, width), single),
            like,
        ),
        in_specs=[HBM] * 6 + [vmem] * 4,
        out_specs=(HBM,) * 6 + (vmem,) * 10,
        scratch_shapes=[
            pltpu.VMEM((DEPTH, RING, 2) + small.shape, single),
            pltpu.SemaphoreType.DMA((1,)),
            pltpu.VMEM((2, DEPTH, RING, 2, wq.shape[0], PANEL), narrow),
            pltpu.SemaphoreType.DMA((2,)),
        ]
        + GATHER_SEMS * 4
        + RECUT_SEMS,
        compiler_params=pltpu.CompilerParams(
            collective_id=1, has_side_effects=True, vmem_limit_bytes=48 * 2**20
        ),
        name="bring",
    )(wq, wo, up, small, ein, eout, tokens, cosine, sine, allowed)

TILE = 256


def add_up(target, terms, rows, columns):
    high = 16 if rows % 16 == 0 else 8
    wide = min(columns, 1024)
    across = columns // wide

    def piece(number, carry):
        row = pl.multiple_of(lax.div(number, across) * high, high)
        column = pl.multiple_of(lax.rem(number, across) * wide, 128)
        spot = (pl.ds(row, high), pl.ds(column, wide))
        total = terms[0][spot].astype(single)
        for term in terms[1:]:
            total = total + term[spot].astype(single)
        target[spot] = total.astype(target.dtype)
        return carry

    lax.fori_loop(0, (rows // high) * across, piece, 0)


SUM_SEMS = [
    pltpu.SemaphoreType.DMA((2, DEPTH, 2)),
    pltpu.SemaphoreType.DMA((2, DEPTH, 2)),
    pltpu.SemaphoreType.DMA((2, 2, DEPTH)),
    pltpu.SemaphoreType.DMA((DEPTH, RING, 2)),
]


def sum_scratch(rows, columns, kind, halves, paired=False, made=False):
    high = max(size for _, size in filter(None, halves))
    kept = RING if paired or made else RING - 1
    scratch = [
        pltpu.VMEM((DEPTH, kept, rows, columns), kind),
        pltpu.VMEM((DEPTH, 2, high, columns), kind),
        pltpu.VMEM((DEPTH, 2, rows, columns), kind),
        pltpu.VMEM((DEPTH + 1, rows, columns), kind),
    ] + SUM_SEMS
    if paired:
        scratch += [pltpu.VMEM((DEPTH, RING, rows, columns), kind), pltpu.SemaphoreType.DMA((2, DEPTH, 2))]
    return scratch


class Sum:
    def __init__(self, here, sources, target, halves, paired, scratch):
        self.here, self.sources, self.halves, self.paired = here, sources, halves, paired
        self.target = target if isinstance(target, list) else [(target, 0, target.shape[0])]
        self.mine, self.half, self.full, self.column = scratch[:4]
        self.half_sem, self.full_sem, self.line_sem, self.load_sem = scratch[4:8]
        if paired:
            self.other, self.pair_sem = scratch[8:10]
        self.rows, self.columns = self.mine.shape[2:]

    def kept(self, z, turn):
        if self.sources is None:
            return self.mine.at[z, self.here.chip_at(turn)]
        return self.mine.at[z, turn if self.paired else {0: 0, 1: 1, 3: 2}[turn]]

    def raw(self, part, z, turn):
        chip = self.here.chip_at(turn)
        return part.at[z, chip, self.here.core] if self.paired else part.at[z, chip]

    def spots(self):
        at, spots = 0, []
        for part in self.sources or []:
            spots.append((part, pl.ds(at, part.shape[-1])))
            at += part.shape[-1]
        return spots

    def loads(self, z, turn):
        return [
            pltpu.make_async_copy(
                self.raw(part, z, turn), self.kept(z, turn).at[:, spot], self.load_sem.at[z, turn, number]
            )
            for number, (part, spot) in enumerate(self.spots())
        ]

    def swaps(self, z, mine):
        return [
            remote(
                part.at[z, :, 1 - self.here.core] if mine else self.other.at[z, :, :, spot],
                self.other.at[z, :, :, spot],
                self.pair_sem.at[0, z, number],
                self.pair_sem.at[1, z, number],
                self.here.sibling(),
            )
            for number, (part, spot) in enumerate(self.spots())
        ]

    def toss(self, z, way):
        if self.halves[way] is None:
            return None
        rows = pl.ds(*self.halves[way])
        loaded = self.sources is not None and not self.paired
        source = (self.raw(self.sources[0], z, 2) if loaded else self.kept(z, 2)).at[rows]
        return remote(
            source,
            self.half.at[z, way, pl.ds(0, self.halves[way][1])],
            self.half_sem.at[0, z, way],
            self.half_sem.at[1, z, way],
            self.here.beside(1 if way == 0 else -1),
        )

    def pass_on(self, z, way):
        return remote(
            self.kept(z, 1 if way == 0 else 3),
            self.full.at[z, way],
            self.full_sem.at[0, z, way],
            self.full_sem.at[1, z, way],
            self.here.beside(1 if way == 0 else -1),
        )

    def climb(self, z, way, up, slot=None):
        if slot is None:
            down_to_owner = way * (z == self.here.z - 1).astype(jnp.int32)
            slot = z + down_to_owner * (DEPTH - z)
        return remote(
            self.kept(z, 0),
            self.column.at[slot],
            self.line_sem.at[0, way, z],
            self.line_sem.at[1, way, z],
            self.here.above(2 * up - 1),
        )

    def begin(self, z):
        if self.paired:
            for copy in self.swaps(z, True):
                copy.start()
        for turn in (2, 1, 3, 0):
            if turn != 2 or self.paired:
                for copy in self.loads(z, turn):
                    copy.start()
        if not self.paired:
            for way in (0, 1):
                start(self.toss(z, way))

    def merge(self, z):
        if not self.paired:
            return
        for copy in self.swaps(z, False):
            copy.wait_recv()
        for turn in (2, 1, 3, 0):
            for copy in self.loads(z, turn):
                copy.wait()
            kept = self.kept(z, turn)
            add_up(kept, [kept, self.other.at[z, self.here.chip_at(turn)]], self.rows, self.columns)
            if turn == 2:
                for way in (0, 1):
                    start(self.toss(z, way))

    def second(self, z):
        for way, turn in ((0, 1), (1, 3)):
            if not self.paired:
                for copy in self.loads(z, turn):
                    copy.wait()
            copy = self.toss(z, way)
            if copy is not None:
                copy.wait_recv()
                begin, size = self.halves[way]
                rows = self.kept(z, turn).at[pl.ds(begin, size)]
                add_up(rows, [rows, self.half.at[z, way, pl.ds(0, size)]], size, self.columns)
        for way in (0, 1):
            self.pass_on(z, way).start()

    def third(self, z, last):
        here = self.here
        if not self.paired:
            for copy in self.loads(z, 0):
                copy.wait()
        for way in (0, 1):
            self.pass_on(z, way).wait_recv()
        kept = self.kept(z, 0)
        terms = [kept, self.full.at[z, 0], self.full.at[z, 1]]
        if last:
            self.arrive(z, terms)
            return
        up = (z > here.z).astype(jnp.int32)
        way = 1 - up
        follows = up * here.z + way * (DEPTH - 1 - here.z)

        @pl.when(follows > 0)
        def _():
            self.climb(z, way, up, z).wait_recv()
            add_up(kept, terms + [self.column.at[z]], self.rows, self.columns)

        @pl.when(follows == 0)
        def _():
            add_up(kept, terms, self.rows, self.columns)

        self.climb(z, way, up).start()

    def own_part(self, z):
        for way in (0, 1):
            self.pass_on(z, way).wait_recv()
        [(target, _, rows)] = self.target
        add_up(target, [self.kept(z, 0), self.full.at[z, 0], self.full.at[z, 1]], rows, self.columns)

    def own_rest(self, z):
        self.arrive(z, [self.target[0][0]])

    def arrive(self, z, terms):
        here = self.here
        below, above = self.column.at[z], self.column.at[DEPTH]

        def total(more):
            for target, row, rows in self.target:
                part = [term.at[pl.ds(row, rows)] for term in terms + more]
                add_up(target, part, rows, self.columns)

        @pl.when(here.z == 0)
        def _():
            self.climb(z, 1, 0, DEPTH).wait_recv()
            total([above])

        @pl.when(here.z == DEPTH - 1)
        def _():
            self.climb(z, 0, 0, z).wait_recv()
            total([below])

        @pl.when((here.z > 0) & (here.z < DEPTH - 1))
        def _():
            self.climb(z, 0, 0, z).wait_recv()
            self.climb(z, 1, 0, DEPTH).wait_recv()
            total([below, above])

    def end(self, z, last):
        if self.paired:
            for copy in self.swaps(z, True):
                copy.wait_send()
        for way in (0, 1):
            copy = self.toss(z, way)
            if copy is not None:
                copy.wait_send()
            self.pass_on(z, way).wait_send()
        if not last:
            up = (z > self.here.z).astype(jnp.int32)
            self.climb(z, 1 - up, up).wait_send()


def far_first(here, number):
    high = lax.div(here.z, 2)
    inner = lax.rem(lax.div(here.z + 1, 2), 2)
    low = (DEPTH - 1 - number) + inner * (0, -2, 1, 1)[number]
    return low + high * (DEPTH - 1 - 2 * low)


class Share:
    def __init__(self, here, source, target, sems):
        self.here, self.source, self.target, self.sems = here, source, target, sems
        self.held, self.rows, columns = target.shape
        self.part = columns // (2 * DEPTH)

    def pieces(self, steps, arriving):
        here = self.here
        origin = lax.rem(here.z + DEPTH - steps, DEPTH) if arriving else here.z
        away = lax.rem(here.z + steps, DEPTH)
        copies = []
        for number in range(2 * self.held):
            side, expert = divmod(number, self.held)
            column = (side * DEPTH + origin) * self.part
            target = self.target.at[expert, :, pl.ds(pl.multiple_of(column, 128), self.part)]
            source = self.source.at[
                pl.ds(pl.multiple_of(away * self.rows, 16), self.rows), pl.ds(number * self.part, self.part)
            ]
            if steps == 0:
                copies.append(pltpu.make_async_copy(source, target, self.sems.at[0, 0, number]))
            else:
                sems = (self.sems.at[0, steps, number], self.sems.at[1, steps, number])
                copies.append(remote(target if arriving else source, target, *sems, here.above(steps)))
        return copies

    def begin(self):
        for steps in range(DEPTH):
            for copy in self.pieces(steps, False):
                copy.start()

    def end(self):
        for steps in range(DEPTH):
            for copy in self.pieces(steps, False):
                copy.wait() if steps == 0 else copy.wait_send()
            if steps:
                for copy in self.pieces(steps, True):
                    copy.wait_recv()


def last_sum_kernel(
    normed,
    grad,
    attended,
    branch,
    gin_sum,
    weight,
    tokens,
    grad_middle,
    gain,
    pieces,
    q_sum,
    o_sum,
    gains,
    grad_tokens,
    share_in,
    left,
    left_out,
    right,
    sems,
    panel,
    panel_sems,
    back,
    piece,
    few_sum,
    few_other,
    pair_sems,
    share_sems,
    *scratch,
):
    here = Here()
    here.meet()
    block, width = normed.shape
    share = q_sum.shape[0]
    wide = grad.shape[1]
    sides = wide // width
    moved = [
        (normed, left, None),
        (grad, right, pl.ds(0, wide)),
        (attended, left_out, None),
        (branch, right, pl.ds(wide, width)),
    ]
    copies = []
    for number, (source, target, spot) in enumerate(moved):
        own, other = (target.at[core] if spot is None else target.at[core, :, spot] for core in (0, 1))
        copies.append(
            (
                pltpu.make_async_copy(source, own, sems.at[number]),
                remote(source, other, sems.at[4 + number], sems.at[8 + number], here.sibling()),
            )
        )
    for kept, sent in copies:
        sent.start()
        kept.start()
    back_share = Share(here, gin_sum, share_in, share_sems)
    back_share.begin()
    targets = [(q_sum.at[:, pl.ds(side * width, width)], side * share, share) for side in range(sides)]
    targets.append((o_sum, sides * share, share))
    big = Sum(here, None, targets, halves_of((sides + 1) * share), False, scratch[0:8])
    few = Sum(here, None, few_sum, halves_of(few_sum.shape[0], False), False, scratch[8:16])
    order = [far_first(here, number) for number in range(DEPTH)]

    def fetch_panel(number):
        slot = lax.rem(number, 2)
        rows = pl.ds(pl.multiple_of(number * TILE, TILE), TILE)
        return pltpu.make_async_copy(weight.at[rows], panel.at[slot], panel_sems.at[slot])

    panels = width // TILE
    fetch_panel(0).start()
    for kept, sent in copies:
        kept.wait()
        sent.wait_recv()
    step = 512
    each = width // step
    rows = RING * 2 * share

    def make(z):
        at = pl.ds(pl.multiple_of(z * rows, rows), rows)

        def one(number, source):
            spot = pl.ds(pl.multiple_of(number * step, step), step)
            turned = source[:, :, at].reshape(2 * block, rows)
            made = contract_rows(turned, right[:, :, spot].reshape(2 * block, step))
            made = made.reshape(RING, 2, share, step)
            mine = jnp.where(here.core == 0, made[:, 0], made[:, 1]).astype(narrow)
            row = pl.multiple_of(lax.div(number, each) * share, share)
            column = pl.multiple_of(lax.rem(number, each) * step, step)
            for chip in range(RING):
                big.mine[z, chip, pl.ds(row, share), pl.ds(column, step)] = mine[chip]

        def qkv(number, carry):
            one(number, left)
            return carry

        def out(number, carry):
            one(number, left_out)
            return carry

        lax.fori_loop(0, sides * each, qkv, 0)
        lax.fori_loop(sides * each, (sides + 1) * each, out, 0)

    def through(first, last):
        def body(number, carry):
            fetch_panel(number).wait()
            pl.when(number + 1 < panels)(lambda: fetch_panel(number + 1).start())
            spot = pl.ds(pl.multiple_of(number * TILE, TILE), TILE)
            back[:, spot] = contract_last(right[0, :, 0:wide], panel[lax.rem(number, 2)])
            return carry

        lax.fori_loop(first, last, body, 0)

    def norm_back():
        piece[...] = pieces[...]
        high = 16

        def body(number, carry):
            at = pl.ds(pl.multiple_of(number * high, high), high)
            values = tokens[at].astype(single)
            factor = lax.rsqrt(jnp.mean(values * values, axis=-1, keepdims=True) + epsilon)
            normal = values * factor
            upstream = back[at]
            weighted = upstream * gain[...]
            inner = jnp.mean(weighted * normal, axis=-1, keepdims=True)
            grad_tokens[at] = grad_middle[at] + factor * (weighted - normal * inner)
            piece[0:1] += jnp.sum(upstream * normal, axis=0, keepdims=True)
            return carry

        lax.fori_loop(0, block // high, body, 0)
        for z in range(DEPTH):
            for chip in range(RING):
                begin = (z * RING + chip) * 2 * share
                few.mine[z, chip] = piece[:, begin : begin + 2 * share]

    for number, z in enumerate(order):
        make(z)
        for way in (0, 1):
            start(big.toss(z, way))
        if number:
            big.second(order[number - 1])
        if number > 1:
            big.third(order[number - 2], False)
        if number < 2:
            through(number * panels // 2, (number + 1) * panels // 2)
        if number == 2:
            norm_back()
            for place in order:
                start(few.toss(place, 0))
    big.second(order[-1])
    for z in order:
        few.second(z)
    big.third(order[-2], False)
    for z in order[:-1]:
        few.third(z, False)
    big.third(order[-1], True)
    few.third(order[-1], True)
    swap = remote(few_sum, few_other, pair_sems.at[0], pair_sems.at[1], here.sibling())
    swap.start()
    swap.wait_recv()
    gains[...] = few_sum[...] + few_other[...]
    swap.wait_send()
    for number, z in enumerate(order):
        for item in (big, few):
            item.end(z, number == DEPTH - 1)
    for kept, sent in copies:
        sent.wait_send()
    back_share.end()


def last_sum(normed, grad, attended, branch, gin_sum, weight, tokens, grad_middle, gain, pieces, share, held):
    block, width = normed.shape
    wide = grad.shape[1]
    rows = (wide // width + 1) * share
    vmem = pl.BlockSpec(memory_space=pltpu.VMEM)
    few = (pieces.shape[0], 2 * share)
    return pl.pallas_call(
        last_sum_kernel,
        out_shape=(
            jax.ShapeDtypeStruct((share, wide), single),
            jax.ShapeDtypeStruct((share, width), single),
            jax.ShapeDtypeStruct(few, single),
            jax.ShapeDtypeStruct((block, width), single),
            jax.ShapeDtypeStruct((held, gin_sum.shape[0] // DEPTH, DEPTH * gin_sum.shape[1] // held), narrow),
        ),
        in_specs=[HBM] * 6 + [vmem] * 4,
        out_specs=(vmem, vmem, vmem, vmem, HBM),
        scratch_shapes=[
            pltpu.VMEM((2, block, width), narrow),
            pltpu.VMEM((2, block, width), narrow),
            pltpu.VMEM((2, block, wide + width), narrow),
            pltpu.SemaphoreType.DMA((12,)),
            pltpu.VMEM((2, TILE, wide), narrow),
            pltpu.SemaphoreType.DMA((2,)),
            pltpu.VMEM((block, width), single),
            pltpu.VMEM(pieces.shape, single),
            pltpu.VMEM(few, single),
            pltpu.VMEM(few, single),
            pltpu.SemaphoreType.DMA((2,)),
            pltpu.SemaphoreType.DMA((2, DEPTH, 2 * held)),
        ]
        + sum_scratch(rows, width, narrow, halves_of(rows), made=True)
        + sum_scratch(few[0], few[1], single, halves_of(few[0], False), made=True),
        compiler_params=pltpu.CompilerParams(
            collective_id=4, has_side_effects=True, vmem_limit_bytes=62 * 2**20
        ),
        name="deliver",
    )(normed, grad, attended, branch, gin_sum, weight, tokens, grad_middle, gain, pieces)

def near_first(here, number):
    high = lax.div(here.z, 2)
    inner = lax.rem(lax.div(here.z + 1, 2), 2)
    low = number + inner * (1, -1, 0, 0)[number]
    return low + high * (DEPTH - 1 - 2 * low)


class Tiles:
    def __init__(self, here, stage, count, sems, parts, targets):
        self.here, self.stage, self.count = here, stage, count
        self.kept, self.sent, self.came = sems
        self.parts, self.targets = parts, targets

    def copies(self, number, keep=True, give=True):
        slot = lax.rem(number, 2)
        own, other = self.targets
        made = []
        for piece, (mine, theirs, spot) in enumerate(self.parts(number, self.stage.at[slot])):
            if keep:
                made.append(pltpu.make_async_copy(mine, own.at[spot], self.kept.at[slot, piece]))
            if give:
                sems = (self.sent.at[slot, piece], self.came.at[number, piece])
                made.append(remote(theirs, other.at[spot], *sems, self.here.sibling()))
        return made

    def settle(self, number):
        for copy in self.copies(number, give=False):
            copy.wait()
        for copy in self.copies(number, keep=False):
            copy.wait_send()

    def run(self, first, last, make):
        def body(number, carry):
            pl.when(number >= 2)(lambda: self.settle(number - 2))
            make(number, self.stage.at[lax.rem(number, 2)])
            for copy in self.copies(number):
                copy.start()
            return carry

        lax.fori_loop(first, last, body, 0)
        if last == self.count:
            for number in (last - 2, last - 1):
                self.settle(number)

    def heard(self):
        for number in range(self.count):
            for copy in self.copies(number, keep=False):
                copy.wait_recv()


def experts_kernel(
    rows, ups, gates, win, wout, mid_sum, gate_sum, out_sum, gin_sum, gdown, gdown_other, gin, gin_other, rows_all, *scratch
):
    here = Here()
    here.meet()
    (
        w_in, w_out, grads, scaled, row_plane, up_plane, gate_plane, served, strip, stage, loads, strip_sems
    ) = scratch[:12]
    gather = Gather(here, rows, rows_all, halves_of(rows.shape[0]), False, scratch[12:16])
    mids = Sum(here, None, mid_sum, halves_of(rows.shape[0]), False, scratch[16:24])
    outs = Sum(here, None, out_sum, halves_of(rows.shape[0]), False, scratch[16:19] + scratch[24:29])
    tables = Sum(here, None, gate_sum, halves_of(gate_sum.shape[0], False), False, scratch[29:37])
    in_sems, down_sems = scratch[37:40], scratch[40:43]
    block, width = rows.shape
    plane = RING * block
    hidden = w_out.shape[0]
    chunk = hidden // 4
    column = lax.broadcasted_iota(jnp.int32, (plane, 128), 1)
    fetch_in = pltpu.make_async_copy(win, w_in, loads.at[0])
    fetch_out = pltpu.make_async_copy(wout, w_out, loads.at[1])
    fetch_in.start()
    fetch_out.start()

    def fetch_plane(number):
        z = near_first(here, number)
        return (
            pltpu.make_async_copy(ups.at[z], up_plane.at[number % 2], loads.at[2 + number % 2]),
            pltpu.make_async_copy(gates.at[z], gate_plane.at[number % 2], loads.at[4 + number % 2]),
        )

    def fetch_rows(number):
        return pltpu.make_async_copy(rows_all.at[near_first(here, number)], row_plane, loads.at[6])

    def hidden_units(number):
        z = near_first(here, number)
        fetch_rows(number).start()
        for copy in fetch_plane(number):
            copy.wait()
        if number == 0:
            fetch_in.wait()
            fetch_out.wait()
        fetch_rows(number).wait()
        served[...] = jnp.zeros_like(served)
        at = pl.ds(pl.multiple_of(z * plane, plane), plane)

        def one(expert, carry):
            mid = row_plane[...].reshape(plane, width)
            up_rows = up_plane[number % 2]
            spot = pl.ds(pl.multiple_of(expert * chunk, chunk), chunk)
            spot_up = pl.ds(pl.multiple_of(hidden + expert * chunk, chunk), chunk)
            gate = jnp.sum(jnp.where(column == expert, gate_plane[number % 2], 0.0), axis=1, keepdims=True)
            gate_part = jnp.dot(mid, w_in[:, spot], preferred_element_type=single)
            up_part = jnp.dot(mid, w_in[:, spot_up], preferred_element_type=single)
            back = contract_last(up_rows, w_out[spot])
            sigmoid = 1.0 / (1.0 + jnp.exp(-gate_part))
            activated = gate_part * sigmoid
            units = activated * up_part
            scaled[at, spot] = (gate * units).astype(narrow)
            total = jnp.sum(units * back, axis=1, keepdims=True)
            served[...] += jnp.where(column == here.chip * 4 + expert, total, 0.0)
            grad = gate * back
            grads[at, spot] = (grad * up_part * (sigmoid * (1.0 + gate_part * (1.0 - sigmoid)))).astype(narrow)
            grads[at, spot_up] = (grad * activated).astype(narrow)
            return carry

        lax.fori_loop(0, 4, one, 0)
        for chip in range(RING):
            turned = jnp.transpose(served[chip * block : (chip + 1) * block])
            tables.mine[z, chip] = turned[: tables.rows]

    def row_grads(z):
        at = pl.ds(pl.multiple_of(z * plane, plane), plane)

        def one(number, carry):
            spot = pl.ds(pl.multiple_of(number * TILE, TILE), TILE)
            made = contract_last(grads[at], w_in[spot]).astype(narrow)
            for chip in range(RING):
                mids.mine[z, chip, :, spot] = made[chip * block : (chip + 1) * block]
            return carry

        lax.fori_loop(0, width // TILE, one, 0)

    def products(z):
        at = pl.ds(pl.multiple_of(z * plane, plane), plane)

        def one(number, carry):
            spot = pl.ds(pl.multiple_of(number * TILE, TILE), TILE)
            made = jnp.dot(scaled[at], w_out[:, spot], preferred_element_type=single).astype(narrow)
            for chip in range(RING):
                outs.mine[z, chip, :, spot] = made[chip * block : (chip + 1) * block]
            return carry

        lax.fori_loop(0, width // TILE, one, 0)

    strips = width // TILE

    def fetch_strip(number):
        spot = pl.ds(pl.multiple_of(number * TILE, TILE), TILE)
        slot = lax.rem(number, 2)
        return pltpu.make_async_copy(rows_all.at[:, :, :, spot], strip.at[slot], strip_sems.at[slot])

    def columns_of(result, stage, step=512):
        for begin in range(0, width, step):
            stage[:, begin : begin + step] = result(begin, step).astype(narrow)

    def grad_in(number, stage):
        slot = lax.rem(number, 2)
        fetch_strip(number).wait()
        pl.when(number + 1 < strips)(lambda: fetch_strip(number + 1).start())
        left = strip[slot].reshape(DEPTH * plane, TILE)
        columns_of(lambda begin, step: contract_rows(left, grads[:, begin : begin + step]), stage)

    def grad_in_parts(number, stage):
        share = hidden // 2
        at = pl.ds(pl.multiple_of(number * TILE, TILE), TILE)
        for side in range(2):
            mine, theirs = (
                stage.at[:, pl.ds(pl.multiple_of(side * hidden + core * share, 128), share)]
                for core in (here.core, 1 - here.core)
            )
            yield mine, theirs, (at, pl.ds(side * share, share))

    def grad_down(number, stage):
        half = tall // 2
        core = here.core + (1 - lax.div(number, half)) * (1 - 2 * here.core)
        at = core * half + lax.rem(number, half)
        left = scaled[:, pl.ds(pl.multiple_of(at * TILE, TILE), TILE)]
        columns_of(lambda begin, step: contract_rows(left, w_in[:, begin : begin + step]), stage)

    tall = hidden // TILE
    tiles_in = Tiles(here, stage, strips, in_sems, grad_in_parts, (gin, gin_other))

    def grad_down_store(number, away):
        slot = lax.rem(number, 2)
        rest = lax.rem(number, tall // 2)
        spot = pl.ds(pl.multiple_of(rest * TILE, TILE), TILE)
        kept, sent, came = down_sems
        if away:
            return remote(stage.at[slot], gdown_other.at[spot], sent.at[slot, 0], came.at[rest, 0], here.sibling())
        return pltpu.make_async_copy(stage.at[slot], gdown.at[spot], kept.at[slot, 0])

    def grads_down(away):
        first = 0 if away else tall // 2

        def body(number, carry):
            grad_down(number, stage.at[lax.rem(number, 2)])
            grad_down_store(number, away).start()
            return carry

        lax.fori_loop(first, first + tall // 2, body, 0)
        for number in range(first, first + tall // 2):
            copy = grad_down_store(number, away)
            copy.wait_send() if away else copy.wait()

    def add_cores():
        half = hidden
        adds, puts = scratch[43], scratch[44]

        def fetch(number):
            slot = lax.rem(number, 2)
            at = pl.ds(pl.multiple_of(number * TILE, TILE), TILE)
            return [
                pltpu.make_async_copy(
                    source.at[at], stage.at[slot, :, pl.ds(side * half, half)], adds.at[slot, side]
                )
                for side, source in enumerate((gin, gin_other))
            ]

        def put(number):
            slot = lax.rem(number, 2)
            at = pl.ds(pl.multiple_of(number * TILE, TILE), TILE)
            return pltpu.make_async_copy(stage.at[slot, :, pl.ds(0, half)], gin_sum.at[at], puts.at[slot])

        def start_fetch(number):
            for copy in fetch(number):
                copy.start()

        def body(number, carry):
            for copy in fetch(number):
                copy.wait()
            pl.when(number >= 1)(lambda: put(number - 1).wait())
            pl.when(number + 1 < strips)(lambda: start_fetch(number + 1))
            slot = lax.rem(number, 2)
            own = stage.at[slot, :, pl.ds(0, half)]
            add_up(own, [own, stage.at[slot, :, pl.ds(half, half)]], TILE, half)
            put(number).start()
            return carry

        start_fetch(0)
        lax.fori_loop(0, strips, body, 0)
        put(strips - 1).wait()

    again = [
        pltpu.make_async_copy(ups.at[z], w_in.at[pl.ds(z * plane, plane)], loads.at[7 + z]) for z in range(DEPTH)
    ]

    def again_wait():
        for copy in again:
            copy.wait()

    order = [far_first(here, number) for number in range(DEPTH)]
    first = [mids, tables]
    steps = [(first, z, False) for z in [here.z] + order[:-1]]
    steps += [([outs], z, number == DEPTH - 1) for number, z in enumerate(order)]

    def begin(number):
        items, z, last = steps[number]
        if number < DEPTH:
            row_grads(z)
        else:
            mids.end(z, last)
            products(z)
        for item in items:
            for way in (0, 1):
                start(item.toss(z, way))

    def second(number):
        for item in steps[number][0]:
            item.second(steps[number][1])

    def third(number):
        items, z, last = steps[number]
        for item in items:
            item.own_part(z) if number == 0 else item.third(z, last)

    for copy in fetch_plane(0):
        copy.start()
    rounds = Rounds(here, [gather])
    rounds.service(0)
    for number in range(DEPTH):
        if number + 1 < DEPTH:
            rounds.service(number + 1)
        if number == DEPTH - 1:
            second(0)
        gather_third(gather, near_first(here, number))
        if number + 1 < DEPTH:
            for copy in fetch_plane(number + 1):
                copy.start()
        hidden_units(number)
        if number == 1:
            begin(0)
    fetch_strip(0).start()
    ends = [0] + [strips * (number + 1) // (DEPTH - 1) for number in range(DEPTH - 1)]
    for number in range(1, 2 * DEPTH):
        begin(number)
        if number > 1:
            second(number - 1)
            third(number - 2)
        if number == DEPTH - 1:
            for copy in again:
                copy.start()
        if number < DEPTH:
            tiles_in.run(ends[number - 1], ends[number], grad_in)
        elif number == DEPTH:
            again_wait()
            grads_down(True)
        elif number == DEPTH + 1:
            grads_down(False)
        elif number == DEPTH + 2:
            for item in first:
                item.own_rest(here.z)
            tiles_in.heard()
            add_cores()
    outs.second(order[-1])
    outs.third(order[-2], False)
    outs.third(order[-1], True)
    for number, z in enumerate(order):
        outs.end(z, number == DEPTH - 1)
        tables.end(z, number == DEPTH - 1)
    for number in range(tall // 2):
        grad_down_store(number, True).wait_recv()
    rounds.finish()


def experts_round(rows, ups, gates, win, wout, experts):
    block, width = rows.shape
    plane = RING * block
    hidden = wout.shape[0]
    total = DEPTH * plane
    vmem = pl.BlockSpec(memory_space=pltpu.VMEM)
    return pl.pallas_call(
        experts_kernel,
        out_shape=(
            jax.ShapeDtypeStruct((block, width), single),
            jax.ShapeDtypeStruct((experts, block), single),
            jax.ShapeDtypeStruct((block, width), single),
            jax.ShapeDtypeStruct((width, hidden), narrow),
            jax.ShapeDtypeStruct((hidden // 2, width), narrow),
            jax.ShapeDtypeStruct((hidden // 2, width), narrow),
            jax.ShapeDtypeStruct((width, hidden), narrow),
            jax.ShapeDtypeStruct((width, hidden), narrow),
            jax.ShapeDtypeStruct((DEPTH, RING, block, width), narrow),
        ),
        in_specs=[HBM] * 5,
        out_specs=(vmem, vmem, vmem) + (HBM,) * 6,
        scratch_shapes=[
            pltpu.VMEM((width, 2 * hidden), narrow),
            pltpu.VMEM((hidden, width), narrow),
            pltpu.VMEM((total, 2 * hidden), narrow),
            pltpu.VMEM((total, hidden), narrow),
            pltpu.VMEM((RING, block, width), narrow),
            pltpu.VMEM((2, plane, width), narrow),
            pltpu.VMEM((2, plane, 128), single),
            pltpu.VMEM((plane, 128), single),
            pltpu.VMEM((2, DEPTH, RING, block, TILE), narrow),
            pltpu.VMEM((2, TILE, width), narrow),
            pltpu.SemaphoreType.DMA((11,)),
            pltpu.SemaphoreType.DMA((2,)),
        ]
        + GATHER_SEMS
        + sum_scratch(block, width, narrow, halves_of(block), made=True)
        + [pltpu.VMEM((DEPTH + 1, block, width), narrow)]
        + SUM_SEMS
        + sum_scratch(experts, block, single, halves_of(experts, False), made=True)
        + [
            pltpu.SemaphoreType.DMA((2, 2)),
            pltpu.SemaphoreType.DMA((2, 2)),
            pltpu.SemaphoreType.DMA((width // TILE, 2)),
        ]
        + [
            pltpu.SemaphoreType.DMA((2, 1)),
            pltpu.SemaphoreType.DMA((2, 1)),
            pltpu.SemaphoreType.DMA((hidden // TILE, 1)),
        ]
        + [pltpu.SemaphoreType.DMA((2, 2)), pltpu.SemaphoreType.DMA((2,))],
        compiler_params=pltpu.CompilerParams(
            collective_id=2, has_side_effects=True, vmem_limit_bytes=62 * 2**20
        ),
        name="experts",
    )(rows, ups, gates, win, wout)


def by_kernels():
    return lax.axis_size("dp") == DEPTH and lax.axis_size("expert") == 2 * RING


def forward(tokens, gains, weight_qkv, weight_out, cosine, sine, allowed):
    rows, width = tokens.shape
    inputs = tokens.astype(single)
    normed_in = (normalize(inputs)[0] * gains[0]).astype(narrow)
    projected = jnp.dot(normed_in, weight_qkv, preferred_element_type=single)
    raw = jnp.stack([projected[:, :width], projected[:, width : 2 * width]])
    query_rows, key_rows = (
        rotate(normalize(raw[side])[0] * gains[side + 1], cosine, sine).astype(narrow) for side in range(2)
    )
    value_rows = projected[:, 2 * width :].astype(narrow)
    by_head = (rows, -1, HEAD)
    scores = jnp.einsum(
        "qhd,khd->hqk", query_rows.reshape(by_head), key_rows.reshape(by_head), preferred_element_type=single
    )
    scores = jnp.where(allowed[None], scores * HEAD ** (-0.5), masked_score)
    unnormed = jnp.exp(scores - jnp.max(scores, axis=-1, keepdims=True))
    probs = unnormed / jnp.sum(unnormed, axis=-1, keepdims=True)
    attended = jnp.einsum(
        "hqk,khd->qhd", probs.astype(narrow), value_rows.reshape(by_head), preferred_element_type=single
    )
    attended = attended.reshape(rows, width).astype(narrow)
    middle = inputs + jnp.dot(attended, weight_out, preferred_element_type=single)
    routed_in = (normalize(middle)[0] * gains[3]).astype(narrow)
    return (normed_in, raw, query_rows, key_rows, value_rows, probs, attended, middle, routed_in)


def bring_all(w_qkv, w_out, upstream, dense, gain_rows, expert_in, expert_out, tokens, cosine, sine, allowed):
    width = upstream.shape[1]
    share = gain_rows.shape[1]
    if by_kernels():
        experts, rows = dense.shape[1], dense.shape[0]
        small = jnp.concatenate([dense.T, jnp.pad(gain_rows, ((0, 4), (0, rows - share)))], axis=0)
        tables = (
            jnp.concatenate([cosine[:, 0], cosine[:, 0]], axis=1),
            jnp.concatenate([-sine[:, 0], sine[:, 0]], axis=1),
            allowed.astype(single),
        )
        wq, wo, up, all_small, weight_in, weight_down, gains, *made = first_gather(
            w_qkv, w_out, upstream, small, expert_in, expert_out, tokens, *tables
        )
        core = lax.rem(lax.axis_index("expert"), 2)
        every_gate = lax.dynamic_index_in_dim(all_small, core, axis=2, keepdims=False)[:, :, :experts]
        return (
            wq.reshape(-1, w_qkv.shape[1]),
            wo.reshape(-1, w_out.shape[1]),
            up.reshape(-1, width),
            every_gate,
            gains[:4],
            weight_in,
            weight_down.reshape(-1, width),
            made,
        )
    everyone = ("dp", "expert")
    weight_in, weight_down = fetch_weights(expert_in, expert_out)
    weight_qkv = lax.all_gather(w_qkv, everyone, axis=0, tiled=True)
    weight_out = lax.all_gather(w_out, everyone, axis=0, tiled=True)
    gains = lax.all_gather(gain_rows, everyone, axis=1, tiled=True)
    return (
        weight_qkv,
        weight_out,
        gather_alike(upstream).reshape(-1, width),
        gather_alike(dense.T),
        gains,
        weight_in,
        weight_down,
        forward(tokens, gains, weight_qkv, weight_out, cosine, sine, allowed),
    )


def experts_all(routed_in, up_rows, every_gate, weight_in, weight_down, held):
    depth = lax.axis_size("dp")
    owners = lax.axis_size("expert")
    chips = owners // 2
    experts = owners * held
    chip_experts = 2 * held
    rows, width = routed_in.shape
    chip = lax.axis_index("expert") // 2
    mine = lax.dynamic_slice_in_dim(every_gate, chip * chip_experts, chip_experts, axis=2)
    gate = mine.transpose(0, 1, 3, 2)
    if by_kernels():
        gate = jnp.pad(gate.reshape(DEPTH, -1, chip_experts), ((0, 0), (0, 0), (0, 128 - chip_experts)))
        ups = up_rows.reshape(DEPTH, -1, width)
        grad_routed, table, mixture, grad_in, grad_down, grad_down_other = experts_round(
            routed_in, ups, gate, weight_in, weight_down, experts
        )[:6]
        down = grad_down.astype(single) + grad_down_other.astype(single)
        return (mixture, grad_routed, table, (grad_in, down.reshape(held, -1, width)))
    mid_rows = gather_alike(routed_in).reshape(-1, width)
    out, mid, served, grad_in, grad_down = expert_rounds(
        mid_rows, up_rows, gate.reshape(-1, chip_experts), weight_in, weight_down
    )
    by_gate = served.reshape(depth, chips, rows, chip_experts).transpose(0, 1, 3, 2)
    spread = jnp.zeros((depth, chips, experts, rows), single)
    spread = lax.dynamic_update_slice_in_dim(spread, by_gate, chip * chip_experts, axis=2)
    return (
        scatter_alike(out.reshape(depth, chips, rows, width)).astype(single),
        scatter_alike(mid.reshape(depth, chips, rows, width)).astype(single),
        scatter_alike(spread),
        return_weights(grad_in, grad_down, held),
    )


def deliver_all(tokens, gain, grad_middle, pieces, normed, grad_qkv, weight_qkv, attended, branch, share_in, held):
    owners = lax.axis_size("dp") * lax.axis_size("expert")
    share = gain.shape[0] // owners
    if by_kernels():
        rows = jnp.stack([jnp.zeros_like(gain), *pieces] + [jnp.zeros_like(gain)] * (7 - len(pieces)))
        share_qkv, share_out, gains, grad_tokens, share_in = last_sum(
            normed, grad_qkv, attended, branch, share_in, weight_qkv, tokens, grad_middle, gain[None], rows, share, held
        )
        core = lax.rem(lax.axis_index("expert"), 2)
        gains = lax.dynamic_slice_in_dim(gains, core * share, share, axis=1)
        return (grad_tokens, gains, share_qkv, share_out, share_in.astype(single))
    everyone = ("dp", "expert")
    normal, factor = normalize(tokens.astype(single))
    grad_input, piece = rms_back(contract_last(grad_qkv, weight_qkv), normal, factor, gain)
    return (
        grad_middle + grad_input,
        lax.psum_scatter(jnp.stack([piece, *pieces]), everyone, scatter_dimension=1, tiled=True),
        *(
            lax.psum_scatter(
                contract_rows(left, right, narrow), everyone, scatter_dimension=0, tiled=True
            ).astype(single)
            for left, right in ((normed, grad_qkv), (attended, branch))
        ),
        share_in.astype(single),
    )


def local(
    tokens,
    lengths,
    expert_ids,
    gates,
    attn_gain,
    w_qkv,
    q_gain,
    k_gain,
    w_out,
    ffn_gain,
    expert_in,
    expert_out,
    out_grad,
):
    micro_count, seq_len, model_width = tokens.shape
    rows = micro_count * seq_len
    held = expert_in.shape[0]
    experts = lax.axis_size("expert") * held
    own = tokens.reshape(rows, model_width)
    upstream = out_grad.reshape(rows, model_width)
    ids = expert_ids.reshape(rows, -1)
    gate_rows = gates.reshape(rows, -1)
    onehot = (ids[:, :, None] == jnp.arange(experts, dtype=jnp.int32)).astype(single)
    dense = jnp.sum(onehot * gate_rows[:, :, None], axis=1)
    gain_rows = jnp.stack([attn_gain, q_gain, k_gain, ffn_gain]).astype(single)
    document, position = layout(lengths[:, 0], seq_len)
    cosine, sine = angles(position)
    places = jnp.arange(rows, dtype=jnp.int32)
    allowed = (document[:, None] == document[None, :]) & (places[:, None] >= places[None, :])
    weight_qkv, weight_out, up_rows, every_gate, gains, weight_in, weight_down, made = bring_all(
        w_qkv, w_out, upstream, dense, gain_rows, expert_in, expert_out, own, cosine, sine, allowed
    )
    gain_attn, gain_query, gain_key, gain_ffn = gains[0], gains[1], gains[2], gains[3]
    normed_in, raw, query_rows, key_rows, value_rows, probs, attended, middle, routed_in = made
    normal_q, factor_q = normalize(raw[0])
    normal_k, factor_k = normalize(raw[1])
    normal_mid, factor_mid = normalize(middle)
    query_rows, key_rows, value_rows = (
        field.reshape(rows, -1, HEAD) for field in (query_rows, key_rows, value_rows)
    )
    attn_probs = probs.astype(narrow)

    mixture, grad_routed, gate_table, (share_in, share_down) = experts_all(
        routed_in, up_rows, every_gate, weight_in, weight_down, held
    )
    grad_gates = jnp.sum(onehot * gate_table.T[:, None, :], axis=2)
    results = (middle + mixture).astype(narrow)

    grad_mid, piece_ffn = rms_back(grad_routed, normal_mid, factor_mid, gain_ffn)
    grad_middle = upstream.astype(single) + grad_mid
    grad_branch = grad_middle.astype(narrow)
    grad_attended = contract_last(grad_branch, weight_out).astype(narrow).reshape(rows, -1, HEAD)
    grad_probs = jnp.einsum("qhd,khd->hqk", grad_attended, value_rows, preferred_element_type=single)
    inner = jnp.sum(grad_probs * probs, axis=-1, keepdims=True)
    grad_scores = (probs * (grad_probs - inner)).astype(narrow)
    grad_query = jnp.einsum(
        "hqk,khd->qhd", grad_scores, key_rows, preferred_element_type=single
    ) * HEAD ** (-0.5)
    grad_key = jnp.einsum(
        "hqk,qhd->khd", grad_scores, query_rows, preferred_element_type=single
    ) * HEAD ** (-0.5)
    grad_value = jnp.einsum("hqk,qhd->khd", attn_probs, grad_attended, preferred_element_type=single)
    grad_q_raw, piece_query = rms_back(
        rotate(grad_query.reshape(rows, model_width), cosine, -sine), normal_q, factor_q, gain_query
    )
    grad_k_raw, piece_key = rms_back(
        rotate(grad_key.reshape(rows, model_width), cosine, -sine), normal_k, factor_k, gain_key
    )
    grad_qkv = jnp.concatenate(
        [grad_q_raw, grad_k_raw, grad_value.reshape(rows, model_width)], axis=1
    ).astype(narrow)
    grad_tokens, gain_sums, grad_qkv_share, grad_out_share, share_in = deliver_all(
        own,
        gain_attn,
        grad_middle,
        (piece_query, piece_key, piece_ffn),
        normed_in,
        grad_qkv,
        weight_qkv,
        attended,
        grad_branch,
        share_in,
        held,
    )
    shape = (micro_count, seq_len, model_width)
    return (
        results.reshape(shape),
        grad_tokens.reshape(shape),
        grad_gates.reshape(expert_ids.shape),
        gain_sums[0],
        grad_qkv_share,
        gain_sums[1],
        gain_sums[2],
        grad_out_share,
        gain_sums[3],
        share_in,
        share_down.astype(single),
    )


def solution(mesh):
    by_rows = P(None, ("dp", "expert"), None)
    flat = P(("dp", "expert"))
    split = P(("dp", "expert"), None)
    held = P("expert", "dp", None)
    return jax.shard_map(
        local,
        mesh=mesh,
        in_specs=(
            by_rows, by_rows, by_rows, by_rows, flat, split, flat, flat, split, flat, held, held, by_rows,
        ),
        out_specs=(by_rows, by_rows, by_rows, flat, split, flat, flat, split, flat, held, held),
        check_vma=False,
    )
```

```python
import jax
import jax.numpy as jnp
from jax import lax
from jax.experimental import pallas as pl
from jax.experimental.pallas import tpu as pltpu
from jax.sharding import PartitionSpec as P

HEAD = 128
epsilon = 1e-05
base_theta = 10000.0
masked_score = -1e30
single = jnp.float32
narrow = jnp.bfloat16


def normalize(values):
    factor = lax.rsqrt(jnp.mean(values * values, axis=-1, keepdims=True) + epsilon)
    return (values * factor, factor)


def rms_back(upstream, normal, factor, gain):
    weighted = upstream * gain
    inner = jnp.mean(weighted * normal, axis=-1, keepdims=True)
    return (factor * (weighted - normal * inner), jnp.sum(upstream * normal, axis=0))


def angles(position):
    half = HEAD // 2
    ladder = jnp.arange(half, dtype=single) * (2.0 / HEAD)
    frequency = jnp.exp(-jnp.log(base_theta) * ladder)
    angle = position.astype(single)[:, None] * frequency[None, :]
    return (jnp.cos(angle)[:, None, :], jnp.sin(angle)[:, None, :])


def rotate(field, cosine, sine):
    length = field.shape[0]
    heads = field.reshape(length, -1, HEAD)
    half = HEAD // 2
    first = heads[..., :half]
    second = heads[..., half:]
    turned = jnp.concatenate(
        [first * cosine - second * sine, second * cosine + first * sine], axis=-1
    )
    return turned.reshape(length, -1)


def layout(doc_lengths, length):
    packs, count = doc_lengths.shape
    upto = jnp.arange(count)[None, :] <= jnp.arange(count)[:, None]
    ends = jnp.sum(jnp.where(upto[None], doc_lengths[:, None, :], 0), axis=2)
    starts = ends - doc_lengths
    places = jnp.arange(length, dtype=jnp.int32)[None, :, None]
    document = jnp.sum((places >= ends[:, None, :]).astype(jnp.int32), axis=2)
    member = (places >= starts[:, None, :]) & (places < ends[:, None, :])
    first_place = jnp.sum(jnp.where(member, starts[:, None, :], 0), axis=2)
    document = document + (count + 1) * jnp.arange(packs, dtype=jnp.int32)[:, None]
    return (document.reshape(-1), (places[..., 0] - first_place).reshape(-1))


def contract_rows(left, right, kind=single):
    return lax.dot_general(left, right, (((0,), (0,)), ((), ())), preferred_element_type=kind)


def contract_last(left, right, kind=single):
    return lax.dot_general(left, right, (((1,), (1,)), ((), ())), preferred_element_type=kind)


def core_groups():
    return [[2 * chip + core for chip in range(lax.axis_size("expert") // 2)] for core in range(2)]


def chip_groups():
    return [[2 * chip, 2 * chip + 1] for chip in range(lax.axis_size("expert") // 2)]


def gather_alike(block):
    column = lax.all_gather(block, "dp", axis=0)
    return lax.all_gather(column, "expert", axis=1, axis_index_groups=core_groups())


def scatter_alike(blocks):
    column = lax.psum_scatter(
        blocks, "expert", scatter_dimension=1, axis_index_groups=core_groups()
    )
    return lax.psum_scatter(column, "dp", scatter_dimension=0)


def fetch_weights(expert_in, expert_out):
    depth = lax.axis_size("dp")
    held, rows, columns = expert_in.shape
    part = columns // (2 * depth)
    cut = expert_in.reshape(held, rows, 2, depth, part)
    turned = lax.all_to_all(cut, "dp", split_axis=3, concat_axis=1, tiled=True)
    both = lax.all_gather(turned[:, :, :, 0], "expert", axis=0, axis_index_groups=chip_groups())
    weight_in = both.transpose(2, 3, 0, 1, 4).reshape(depth * rows, 4 * held * part)
    weight_down = lax.all_gather(
        expert_out, "expert", axis=0, axis_index_groups=chip_groups()
    ).reshape(-1, expert_out.shape[2])
    return (weight_in, weight_down)


def return_weights(grad_in, grad_down, held):
    depth = lax.axis_size("dp")
    rows, columns = grad_in.shape
    part = columns // (4 * held)
    cut = grad_in.reshape(rows, 2, 2, held, part)
    own = lax.psum_scatter(cut, "expert", scatter_dimension=2, axis_index_groups=chip_groups())
    own = own.reshape(depth, rows // depth, 2, held, part)
    turned = lax.all_to_all(own, "dp", split_axis=0, concat_axis=0)
    share_in = turned.transpose(3, 1, 2, 0, 4).reshape(held, rows // depth, 2 * depth * part)
    down = grad_down.reshape(2, held, part, grad_down.shape[1])
    share_down = lax.psum_scatter(
        down, "expert", scatter_dimension=0, axis_index_groups=chip_groups()
    )
    return (share_in, share_down)


def expert_round(mid_rows, up_rows, gate, weight_in, weight_down):
    count = gate.shape[1]
    part = weight_down.shape[0] // count
    wide = jnp.broadcast_to(gate[:, :, None], gate.shape + (part,)).reshape(gate.shape[0], -1)
    gate_up = jnp.dot(mid_rows, weight_in, preferred_element_type=single)
    hidden_units = gate_up.shape[1] // 2
    gate_part = gate_up[:, :hidden_units]
    up_part = gate_up[:, hidden_units:]
    sigmoid = jax.nn.sigmoid(gate_part)
    activated = gate_part * sigmoid
    hidden = activated * up_part
    back = contract_last(up_rows, weight_down)
    scaled = (wide * hidden).astype(narrow)
    piece_out = jnp.dot(scaled, weight_down, preferred_element_type=narrow)
    piece_gates = jnp.sum((hidden * back).reshape(-1, count, part), axis=2)
    grad_hidden = wide * back
    grad_gate = grad_hidden * up_part * sigmoid * (1.0 + gate_part * (1.0 - sigmoid))
    grad_up = grad_hidden * activated
    grad_gate_up = jnp.concatenate([grad_gate, grad_up], axis=1).astype(narrow)
    piece_mid = contract_last(grad_gate_up, weight_in, narrow)
    return (piece_out, piece_mid, piece_gates, grad_gate_up, scaled)


def expert_rounds(mid_rows, up_rows, gate, weight_in, weight_down):
    total = mid_rows.shape[0]
    rounds = max(1, total // 2048)

    def one(sums, pieces):
        mid, up, weights = pieces
        piece_out, piece_mid, piece_gates, grad_gate_up, scaled = expert_round(
            mid, up, weights, weight_in, weight_down
        )
        grads = (contract_rows(mid, grad_gate_up), contract_rows(scaled, up))
        return (jax.tree.map(jnp.add, sums, grads), (piece_out, piece_mid, piece_gates))

    if rounds == 1:
        piece_out, piece_mid, piece_gates, grad_gate_up, scaled = expert_round(
            mid_rows, up_rows, gate, weight_in, weight_down
        )
        grads = (contract_rows(mid_rows, grad_gate_up, narrow), contract_rows(scaled, up_rows, narrow))
        return (piece_out, piece_mid, piece_gates) + grads
    start = (jnp.zeros(weight_in.shape, single), jnp.zeros(weight_down.shape, single))
    cut = jax.tree.map(lambda a: a.reshape(rounds, total // rounds, -1), (mid_rows, up_rows, gate))
    sums, made = lax.scan(one, start, cut)
    made = jax.tree.map(lambda a: a.reshape(total, -1), made)
    return made + (sums[0].astype(narrow), sums[1].astype(narrow))


MESH = pl.DeviceIdType.MESH
HBM = pl.BlockSpec(memory_space=pl.ANY)
DEPTH = 4
RING = 4


def ring_turn(number):
    high = lax.div(number, 2)
    return number + high * (1 - 2 * lax.rem(number, 2))


class Here:
    def __init__(self):
        number = lax.axis_index("expert")
        self.z = lax.axis_index("dp")
        self.core = lax.rem(number, 2)
        self.chip = lax.div(number, 2)
        self.q = ring_turn(self.chip)

    def chip_at(self, turn):
        return ring_turn(lax.rem(self.q + turn + RING, RING))

    def beside(self, turn):
        return (self.z, 2 * self.chip_at(turn) + self.core)

    def above(self, steps):
        return (lax.rem(self.z + steps + DEPTH, DEPTH), 2 * self.chip + self.core)

    def sibling(self):
        return (self.z, 2 * self.chip + 1 - self.core)

    def meet(self):
        barrier = pltpu.get_barrier_semaphore()
        others = [self.beside(1), self.beside(-1), self.sibling()]
        others += [self.above(steps) for steps in range(1, DEPTH)]
        for other in others:
            pl.semaphore_signal(barrier, inc=1, device_id=other, device_id_type=MESH)
        pl.semaphore_wait(barrier, len(others))


def remote(source, target, sent, arrived, device):
    return pltpu.make_async_remote_copy(
        src_ref=source,
        dst_ref=target,
        send_sem=sent,
        recv_sem=arrived,
        device_id=device,
        device_id_type=MESH,
    )


GATHER_SEMS = [
    pltpu.SemaphoreType.DMA((2, 2, DEPTH - 1)),
    pltpu.SemaphoreType.DMA((2, DEPTH, 2, 2)),
    pltpu.SemaphoreType.DMA((2, DEPTH)),
    pltpu.SemaphoreType.DMA((1,)),
]


class Gather:
    def __init__(self, here, source, whole, halves, shared, sems):
        self.here, self.source, self.whole, self.halves, self.shared = here, source, whole, halves, shared
        self.line, self.ring, self.pair, self.own = sems

    def block(self, z, turn):
        chip = self.here.chip_at(turn)
        return self.whole.at[z, chip, self.here.core] if self.shared else self.whole.at[z, chip]

    def keep(self):
        return pltpu.make_async_copy(self.source, self.block(self.here.z, 0), self.own.at[0])

    def along(self, step, way, first):
        z = self.here.z - step + 1 if way == 0 else self.here.z + step - 1
        block = self.block(z, 0)
        return remote(
            self.source if first else block,
            block,
            self.line.at[0, way, step - 1],
            self.line.at[1, way, step - 1],
            self.here.above(1 if way == 0 else -1),
        )

    def round(self, z, way, first=False):
        turn = 1 if way == 0 else -1
        block = self.block(z, 0)
        return remote(
            self.source if first else block,
            block,
            self.ring.at[0, z, way, 0],
            self.ring.at[1, z, way, 0],
            self.here.beside(turn),
        )

    def heard(self, z, way):
        block = self.block(z, -1 if way == 0 else 1)
        return remote(
            block, block, self.ring.at[0, z, way, 0], self.ring.at[1, z, way, 0], self.here.beside(1)
        )

    def onward(self, z, way, mine):
        if self.halves[way] is None:
            return None
        turn = (-1 if mine else -2) if way == 0 else (1 if mine else 2)
        block = self.block(z, turn).at[pl.ds(*self.halves[way])]
        return remote(
            block,
            block,
            self.ring.at[0, z, way, 1],
            self.ring.at[1, z, way, 1],
            self.here.beside(1 if way == 0 else -1),
        )

    def swap(self, z, mine):
        core = self.here.core if mine else 1 - self.here.core
        part = self.whole.at[z, :, core]
        return remote(part, part, self.pair.at[0, z], self.pair.at[1, z], self.here.sibling())


def start(copy):
    if copy is not None:
        copy.start()


def gather_third(item, z):
    for way in (0, 1):
        copy = item.onward(z, way, False)
        if copy is not None:
            copy.wait_recv()


class Rounds:
    def __init__(self, here, items, ring=True):
        self.here, self.items = here, items
        for item in items:
            item.keep().start()
            for way in (0, 1):
                self.depart(0, way, item)
            if ring:
                for way in (0, 1):
                    item.round(here.z, way, True).start()

    def depart(self, step, way, item):
        here = self.here
        ahead = here.z + 1 < DEPTH if way == 0 else here.z >= 1
        pl.when(ahead)(lambda: item.along(step + 1, way, step == 0).start())

    def places(self, step, body):
        here = self.here
        if step == 0:
            body(here.z, 0)
            return
        pl.when(here.z >= step)(lambda: body(here.z - step, 0))
        pl.when(here.z + step < DEPTH)(lambda: body(here.z + step, 1))

    def line(self, step, ring=True):
        def body(z, way):
            for item in self.items:
                block = item.block(z, 0)
                remote(
                    block, block, item.line.at[0, way, step - 1], item.line.at[1, way, step - 1], self.here.above(1)
                ).wait_recv()
                if step + 1 < DEPTH:
                    self.depart(step, way, item)
                if ring:
                    for side in (0, 1):
                        item.round(z, side).start()

        self.places(step, body)

    def ring(self, step):
        def body(z, way):
            for item in self.items:
                for side in (0, 1):
                    item.round(z, side, step == 0).start()

        self.places(step, body)

    def second(self, step):
        def body(z, way):
            for item in self.items:
                for side in (0, 1):
                    item.heard(z, side).wait_recv()
                    start(item.onward(z, side, True))

        self.places(step, body)

    def service(self, step, between=None):
        if step + 1 < DEPTH:
            self.line(step + 1)
        if between is not None:
            between()
        if step == 0:
            self.kept()
        self.second(step)

    def kept(self):
        for item in self.items:
            item.keep().wait()

    def third(self, step):
        def body(z, way):
            for item in self.items:
                gather_third(item, z)
                if item.shared:
                    item.swap(z, True).start()

        self.places(step, body)

    def finish(self):
        def settle(z, way):
            for item in self.items:
                for side in (0, 1):
                    item.round(z, side).wait_send()
                    copy = item.onward(z, side, True)
                    if copy is not None:
                        copy.wait_send()
                if item.shared:
                    item.swap(z, True).wait_send()
                    item.swap(z, False).wait_recv()

        for step in range(DEPTH):
            self.places(step, settle)
        here = self.here
        for item in self.items:
            for step in range(DEPTH - 1):
                for way in (0, 1):

                    def sent(z, side, step=step, way=way, item=item):
                        if step and side != way:
                            return
                        ahead = here.z + 1 < DEPTH if way == 0 else here.z >= 1
                        pl.when(ahead)(lambda: item.along(step + 1, way, step == 0).wait_send())

                    self.places(step, sent)


class Recut:
    def __init__(self, here, source_in, source_out, whole_in, whole_out, sems):
        self.here, self.source_in, self.source_out = here, source_in, source_out
        self.whole_in, self.whole_out = whole_in, whole_out
        self.cut, self.pair, self.down, self.own = sems
        self.held, self.rows, columns = source_in.shape
        self.hidden = columns // 2
        self.part = self.hidden // DEPTH

    def pieces(self, steps, arriving):
        here, copies = self.here, []
        mine = lax.rem(here.z + DEPTH - steps, DEPTH) if arriving else here.z
        away = lax.rem(here.z + steps, DEPTH)
        for side in range(2):
            for expert in range(self.held):
                columns = side * self.held * 2 * self.part + (here.core * self.held + expert) * self.part
                target = self.whole_in.at[
                    pl.ds(pl.multiple_of(mine * self.rows, 16), self.rows),
                    pl.ds(pl.multiple_of(columns, 128), self.part),
                ]
                source = self.source_in.at[
                    expert, :, pl.ds(pl.multiple_of(side * self.hidden + away * self.part, 128), self.part)
                ]
                spot = (steps, side * self.held + expert)
                if steps == 0:
                    copies.append(pltpu.make_async_copy(source, target, self.own.at[spot[1]]))
                else:
                    copies.append(
                        remote(
                            target if arriving else source,
                            target,
                            self.cut.at[(0,) + spot],
                            self.cut.at[(1,) + spot],
                            here.above(steps),
                        )
                    )
        return copies

    def across(self, steps, mine):
        here, copies = self.here, []
        core = here.core if mine else 1 - here.core
        row = lax.rem(here.z + DEPTH - steps, DEPTH)
        width = self.held * self.part
        for side in range(2):
            spot = self.whole_in.at[
                pl.ds(pl.multiple_of(row * self.rows, 16), self.rows),
                pl.ds(pl.multiple_of(side * 2 * width + core * width, 128), width),
            ]
            copies.append(
                remote(spot, spot, self.pair.at[0, steps, side], self.pair.at[1, steps, side], here.sibling())
            )
        return copies

    def lower(self, mine):
        here = self.here
        core = here.core if mine else 1 - here.core
        spot = self.whole_out.at[pl.ds(core * self.held, self.held)]
        return remote(
            self.source_out if mine else spot, spot, self.down.at[0], self.down.at[1], here.sibling()
        )

    def lower_own(self):
        return pltpu.make_async_copy(
            self.source_out, self.whole_out.at[pl.ds(self.here.core * self.held, self.held)], self.own.at[4]
        )

    def begin(self):
        for copy in self.pieces(0, False):
            copy.start()
        self.lower_own().start()
        self.lower(True).start()
        for copies in zip(*[self.pieces(steps, False) for steps in (2, 3, 1)]):
            for copy in copies:
                copy.start()

    def relay(self):
        for steps in range(DEPTH):
            for copy in self.pieces(steps, True):
                copy.wait() if steps == 0 else copy.wait_recv()
            for copy in self.across(steps, True):
                copy.start()

    def end(self):
        self.lower_own().wait()
        self.lower(True).wait_send()
        self.lower(False).wait_recv()
        for steps in range(DEPTH):
            if steps:
                for copy in self.pieces(steps, False):
                    copy.wait_send()
            for copy in self.across(steps, True):
                copy.wait_send()
            for copy in self.across(steps, False):
                copy.wait_recv()


RECUT_SEMS = [
    pltpu.SemaphoreType.DMA((2, DEPTH, 4)),
    pltpu.SemaphoreType.DMA((2, DEPTH, 2)),
    pltpu.SemaphoreType.DMA((2,)),
    pltpu.SemaphoreType.DMA((5,)),
]


def halves_of(rows, split=True):
    return ((0, rows // 2), (rows // 2, rows - rows // 2)) if split else ((0, rows), None)


PANEL = 512


def attention_forward(
    tokens, cosine, sine, allowed, wq, wo, gains, normed, raw, queries, keys, values, probs, attended, middle, routed,
    panel, panel_sems, between
):
    block, width = tokens.shape
    heads = width // HEAD
    wide = wq.shape[-1]
    high = 16
    per = width // PANEL

    def fetch(source, number):
        slot = lax.rem(number, 2)
        spot = pl.ds(pl.multiple_of(number * PANEL, PANEL), PANEL)
        return pltpu.make_async_copy(source.at[:, :, :, :, spot], panel.at[slot], panel_sems.at[slot])

    def slabs(body):
        def one(number, carry):
            body(pl.ds(pl.multiple_of(number * high, high), high))
            return carry

        lax.fori_loop(0, block // high, one, 0)

    def first(at):
        values = tokens[at].astype(single)
        factor = lax.rsqrt(jnp.mean(values * values, axis=-1, keepdims=True) + epsilon)
        normed[at] = (values * factor * gains[0:1]).astype(narrow)

    fetch(wq, 0).start()
    slabs(first)

    def through(source, left, total, finish):
        def one(number, carry):
            fetch(source, number).wait()
            pl.when(number + 1 < total)(lambda: fetch(source, number + 1).start())
            weights = panel[lax.rem(number, 2)].reshape(width, PANEL)
            finish(number, jnp.dot(left[...], weights, preferred_element_type=single))
            return carry

        lax.fori_loop(0, total, one, 0)

    def keep(number, made):
        side = lax.div(number, per)
        spot = pl.ds(pl.multiple_of(lax.rem(number, per) * PANEL, PANEL), PANEL)

        @pl.when(side < 2)
        def _():
            raw[side, :, spot] = made

        @pl.when(side == 2)
        def _():
            values[:, spot] = made.astype(narrow)

    through(wq, normed, wide // PANEL, keep)
    fetch(wo, 0).start()
    between(0)

    factors = [
        lax.rsqrt(jnp.mean(raw[side] * raw[side], axis=-1, keepdims=True) + epsilon) for side in range(2)
    ]
    turn_cos, turn_sin = cosine[...], sine[...]
    may = allowed[...] > 0.5
    group = 4

    def some_heads(number, carry):
        for inner in range(group):
            head = number * group + inner
            spot = pl.ds(pl.multiple_of(head * HEAD, HEAD), HEAD)
            turned = []
            for side, target in ((0, queries), (1, keys)):
                field = raw[side, :, spot] * factors[side] * gains[side + 1 : side + 2, spot]
                field = field * turn_cos + pltpu.roll(field, HEAD // 2, 1) * turn_sin
                target[:, spot] = field.astype(narrow)
                turned.append(field.astype(narrow))
            scores = jnp.where(may, contract_last(turned[0], turned[1]) * HEAD ** (-0.5), masked_score)
            highest = jnp.max(scores, axis=-1, keepdims=True)
            unnormed = jnp.exp(scores - highest)
            shares = unnormed / jnp.sum(unnormed, axis=-1, keepdims=True)
            probs[head] = shares
            mixed = jnp.dot(shares.astype(narrow), values[:, spot], preferred_element_type=single)
            attended[:, spot] = mixed.astype(narrow)
        return carry

    lax.fori_loop(0, heads // group, some_heads, 0)
    between(1)

    def add(number, made):
        spot = pl.ds(pl.multiple_of(number * PANEL, PANEL), PANEL)
        middle[:, spot] = tokens[:, spot].astype(single) + made

    through(wo, attended, per, add)

    def last(at):
        values = middle[at]
        factor = lax.rsqrt(jnp.mean(values * values, axis=-1, keepdims=True) + epsilon)
        routed[at] = (values * factor * gains[3:4]).astype(narrow)

    slabs(last)
    between(2)


def first_gather_kernel(
    wq, wo, up, small, ein, eout, tokens, cosine, sine, allowed,
    wq_all, wo_all, up_all, small_all, win, wout, gains, normed, raw, queries, keys, values, probs, attended, middle, routed,
    small_here, small_sem, panel, panel_sems, *sems
):
    here = Here()
    here.meet()
    items = [
        Gather(here, source, whole, halves, shared, sems[4 * number : 4 * number + 4])
        for number, (source, whole, halves, shared) in enumerate(
            (
                (small, small_all, halves_of(small.shape[0], False), True),
                (wq, wq_all, halves_of(wq.shape[0]), True),
                (wo, wo_all, halves_of(wo.shape[0]), True),
                (up, up_all, halves_of(up.shape[0]), False),
            )
        )
    ]
    recut = Recut(here, ein, eout, win, wout, sems[16:20])
    weights = Rounds(here, items[:3])
    rows = Rounds(here, items[3:], ring=False)
    weights.service(0, lambda: rows.line(1, ring=False))
    weights.service(1, lambda: rows.line(2, ring=False))
    recut.begin()
    weights.third(0)
    weights.service(2, lambda: rows.line(3, ring=False))
    weights.third(1)
    weights.service(3)
    rows.kept()
    for step in range(DEPTH):
        rows.ring(step)
    weights.third(2)
    weights.third(3)
    weights.finish()
    fetch = pltpu.make_async_copy(small_all, small_here, small_sem.at[0])
    fetch.start()
    fetch.wait()
    share = wq.shape[0]
    lanes = small.shape[1]
    lane = lax.broadcasted_iota(jnp.int32, (8, lanes), 1)
    skip = small.shape[0] - 8
    for z in range(DEPTH):
        for chip in range(RING):
            pair = [small_here[z, chip, core, skip : skip + 8] for core in (0, 1)]
            both = jnp.where(lane < share, pair[0], pltpu.roll(pair[1], share, 1))
            begin = (z * RING + chip) * 2 * share
            gains[:, begin : begin + 2 * share] = both

    def between(part):
        if part == 0:
            rows.second(0)
        elif part == 1:
            for step in range(1, DEPTH):
                rows.second(step)
        else:
            recut.relay()

    attention_forward(
        tokens, cosine, sine, allowed, wq_all, wo_all, gains, normed, raw, queries, keys, values, probs, attended,
        middle, routed, panel, panel_sems, between
    )
    for step in range(DEPTH):
        rows.third(step)
    rows.finish()
    recut.end()


def first_gather(wq, wo, up, small, ein, eout, tokens, cosine, sine, allowed):
    def whole(array, shared):
        lead = (DEPTH, RING, 2) if shared else (DEPTH, RING)
        return jax.ShapeDtypeStruct(lead + array.shape, array.dtype)

    held, rows, columns = ein.shape
    block, width = tokens.shape
    heads = width // HEAD
    vmem = pl.BlockSpec(memory_space=pltpu.VMEM)
    like = jax.ShapeDtypeStruct((block, width), narrow)
    return pl.pallas_call(
        first_gather_kernel,
        out_shape=(
            whole(wq, True),
            whole(wo, True),
            whole(up, False),
            whole(small, True),
            jax.ShapeDtypeStruct((DEPTH * rows, columns), ein.dtype),
            jax.ShapeDtypeStruct((2 * held,) + eout.shape[1:], eout.dtype),
            jax.ShapeDtypeStruct((8, width), single),
            like,
            jax.ShapeDtypeStruct((2, block, width), single),
            like,
            like,
            like,
            jax.ShapeDtypeStruct((heads, block, block), single),
            like,
            jax.ShapeDtypeStruct((block, width), single),
            like,
        ),
        in_specs=[HBM] * 6 + [vmem] * 4,
        out_specs=(HBM,) * 6 + (vmem,) * 10,
        scratch_shapes=[
            pltpu.VMEM((DEPTH, RING, 2) + small.shape, single),
            pltpu.SemaphoreType.DMA((1,)),
            pltpu.VMEM((2, DEPTH, RING, 2, wq.shape[0], PANEL), narrow),
            pltpu.SemaphoreType.DMA((2,)),
        ]
        + GATHER_SEMS * 4
        + RECUT_SEMS,
        compiler_params=pltpu.CompilerParams(
            collective_id=1, has_side_effects=True, vmem_limit_bytes=48 * 2**20
        ),
        name="bring",
    )(wq, wo, up, small, ein, eout, tokens, cosine, sine, allowed)

TILE = 256


def add_up(target, terms, rows, columns):
    high = 16 if rows % 16 == 0 else 8
    wide = min(columns, 1024)
    across = columns // wide

    def piece(number, carry):
        row = pl.multiple_of(lax.div(number, across) * high, high)
        column = pl.multiple_of(lax.rem(number, across) * wide, 128)
        spot = (pl.ds(row, high), pl.ds(column, wide))
        total = terms[0][spot].astype(single)
        for term in terms[1:]:
            total = total + term[spot].astype(single)
        target[spot] = total.astype(target.dtype)
        return carry

    lax.fori_loop(0, (rows // high) * across, piece, 0)


SUM_SEMS = [
    pltpu.SemaphoreType.DMA((2, DEPTH, 2)),
    pltpu.SemaphoreType.DMA((2, DEPTH, 2)),
    pltpu.SemaphoreType.DMA((2, 2, DEPTH)),
    pltpu.SemaphoreType.DMA((DEPTH, RING, 2)),
]


def sum_scratch(rows, columns, kind, halves, paired=False, made=False):
    high = max(size for _, size in filter(None, halves))
    kept = RING if paired or made else RING - 1
    scratch = [
        pltpu.VMEM((DEPTH, kept, rows, columns), kind),
        pltpu.VMEM((DEPTH, 2, high, columns), kind),
        pltpu.VMEM((DEPTH, 2, rows, columns), kind),
        pltpu.VMEM((DEPTH + 1, rows, columns), kind),
    ] + SUM_SEMS
    if paired:
        scratch += [pltpu.VMEM((DEPTH, RING, rows, columns), kind), pltpu.SemaphoreType.DMA((2, DEPTH, 2))]
    return scratch


class Sum:
    def __init__(self, here, sources, target, halves, paired, scratch):
        self.here, self.sources, self.halves, self.paired = here, sources, halves, paired
        self.target = target if isinstance(target, list) else [(target, 0, target.shape[0])]
        self.mine, self.half, self.full, self.column = scratch[:4]
        self.half_sem, self.full_sem, self.line_sem, self.load_sem = scratch[4:8]
        if paired:
            self.other, self.pair_sem = scratch[8:10]
        self.rows, self.columns = self.mine.shape[2:]

    def kept(self, z, turn):
        if self.sources is None:
            return self.mine.at[z, self.here.chip_at(turn)]
        return self.mine.at[z, turn if self.paired else {0: 0, 1: 1, 3: 2}[turn]]

    def raw(self, part, z, turn):
        chip = self.here.chip_at(turn)
        return part.at[z, chip, self.here.core] if self.paired else part.at[z, chip]

    def spots(self):
        at, spots = 0, []
        for part in self.sources or []:
            spots.append((part, pl.ds(at, part.shape[-1])))
            at += part.shape[-1]
        return spots

    def loads(self, z, turn):
        return [
            pltpu.make_async_copy(
                self.raw(part, z, turn), self.kept(z, turn).at[:, spot], self.load_sem.at[z, turn, number]
            )
            for number, (part, spot) in enumerate(self.spots())
        ]

    def swaps(self, z, mine):
        return [
            remote(
                part.at[z, :, 1 - self.here.core] if mine else self.other.at[z, :, :, spot],
                self.other.at[z, :, :, spot],
                self.pair_sem.at[0, z, number],
                self.pair_sem.at[1, z, number],
                self.here.sibling(),
            )
            for number, (part, spot) in enumerate(self.spots())
        ]

    def toss(self, z, way):
        if self.halves[way] is None:
            return None
        rows = pl.ds(*self.halves[way])
        loaded = self.sources is not None and not self.paired
        source = (self.raw(self.sources[0], z, 2) if loaded else self.kept(z, 2)).at[rows]
        return remote(
            source,
            self.half.at[z, way, pl.ds(0, self.halves[way][1])],
            self.half_sem.at[0, z, way],
            self.half_sem.at[1, z, way],
            self.here.beside(1 if way == 0 else -1),
        )

    def pass_on(self, z, way):
        return remote(
            self.kept(z, 1 if way == 0 else 3),
            self.full.at[z, way],
            self.full_sem.at[0, z, way],
            self.full_sem.at[1, z, way],
            self.here.beside(1 if way == 0 else -1),
        )

    def climb(self, z, way, up, slot=None):
        if slot is None:
            down_to_owner = way * (z == self.here.z - 1).astype(jnp.int32)
            slot = z + down_to_owner * (DEPTH - z)
        return remote(
            self.kept(z, 0),
            self.column.at[slot],
            self.line_sem.at[0, way, z],
            self.line_sem.at[1, way, z],
            self.here.above(2 * up - 1),
        )

    def begin(self, z):
        if self.paired:
            for copy in self.swaps(z, True):
                copy.start()
        for turn in (2, 1, 3, 0):
            if turn != 2 or self.paired:
                for copy in self.loads(z, turn):
                    copy.start()
        if not self.paired:
            for way in (0, 1):
                start(self.toss(z, way))

    def merge(self, z):
        if not self.paired:
            return
        for copy in self.swaps(z, False):
            copy.wait_recv()
        for turn in (2, 1, 3, 0):
            for copy in self.loads(z, turn):
                copy.wait()
            kept = self.kept(z, turn)
            add_up(kept, [kept, self.other.at[z, self.here.chip_at(turn)]], self.rows, self.columns)
            if turn == 2:
                for way in (0, 1):
                    start(self.toss(z, way))

    def second(self, z):
        for way, turn in ((0, 1), (1, 3)):
            if not self.paired:
                for copy in self.loads(z, turn):
                    copy.wait()
            copy = self.toss(z, way)
            if copy is not None:
                copy.wait_recv()
                begin, size = self.halves[way]
                rows = self.kept(z, turn).at[pl.ds(begin, size)]
                add_up(rows, [rows, self.half.at[z, way, pl.ds(0, size)]], size, self.columns)
        for way in (0, 1):
            self.pass_on(z, way).start()

    def third(self, z, last):
        here = self.here
        if not self.paired:
            for copy in self.loads(z, 0):
                copy.wait()
        for way in (0, 1):
            self.pass_on(z, way).wait_recv()
        kept = self.kept(z, 0)
        terms = [kept, self.full.at[z, 0], self.full.at[z, 1]]
        if last:
            self.arrive(z, terms)
            return
        up = (z > here.z).astype(jnp.int32)
        way = 1 - up
        follows = up * here.z + way * (DEPTH - 1 - here.z)

        @pl.when(follows > 0)
        def _():
            self.climb(z, way, up, z).wait_recv()
            add_up(kept, terms + [self.column.at[z]], self.rows, self.columns)

        @pl.when(follows == 0)
        def _():
            add_up(kept, terms, self.rows, self.columns)

        self.climb(z, way, up).start()

    def own_part(self, z):
        for way in (0, 1):
            self.pass_on(z, way).wait_recv()
        [(target, _, rows)] = self.target
        add_up(target, [self.kept(z, 0), self.full.at[z, 0], self.full.at[z, 1]], rows, self.columns)

    def own_rest(self, z):
        self.arrive(z, [self.target[0][0]])

    def arrive(self, z, terms):
        here = self.here
        below, above = self.column.at[z], self.column.at[DEPTH]

        def total(more):
            for target, row, rows in self.target:
                part = [term.at[pl.ds(row, rows)] for term in terms + more]
                add_up(target, part, rows, self.columns)

        @pl.when(here.z == 0)
        def _():
            self.climb(z, 1, 0, DEPTH).wait_recv()
            total([above])

        @pl.when(here.z == DEPTH - 1)
        def _():
            self.climb(z, 0, 0, z).wait_recv()
            total([below])

        @pl.when((here.z > 0) & (here.z < DEPTH - 1))
        def _():
            self.climb(z, 0, 0, z).wait_recv()
            self.climb(z, 1, 0, DEPTH).wait_recv()
            total([below, above])

    def end(self, z, last):
        if self.paired:
            for copy in self.swaps(z, True):
                copy.wait_send()
        for way in (0, 1):
            copy = self.toss(z, way)
            if copy is not None:
                copy.wait_send()
            self.pass_on(z, way).wait_send()
        if not last:
            up = (z > self.here.z).astype(jnp.int32)
            self.climb(z, 1 - up, up).wait_send()


def far_first(here, number):
    high = lax.div(here.z, 2)
    inner = lax.rem(lax.div(here.z + 1, 2), 2)
    low = (DEPTH - 1 - number) + inner * (0, -2, 1, 1)[number]
    return low + high * (DEPTH - 1 - 2 * low)


class Share:
    def __init__(self, here, source, target, side, sems):
        self.here, self.source, self.target, self.side, self.sems = here, source, target, side, sems
        self.held, self.rows, columns = target.shape
        self.part = columns // (2 * DEPTH)

    def pieces(self, steps, arriving):
        here = self.here
        origin = lax.rem(here.z + DEPTH - steps, DEPTH) if arriving else here.z
        away = lax.rem(here.z + steps, DEPTH)
        copies = []
        for expert in range(self.held):
            column = (self.side * DEPTH + origin) * self.part
            target = self.target.at[expert, :, pl.ds(pl.multiple_of(column, 128), self.part)]
            source = self.source.at[
                pl.ds(pl.multiple_of(away * self.rows, 16), self.rows),
                pl.ds((self.side * self.held + expert) * self.part, self.part),
            ]
            if steps == 0:
                copies.append(pltpu.make_async_copy(source, target, self.sems.at[0, 0, expert]))
            else:
                sems = (self.sems.at[0, steps, expert], self.sems.at[1, steps, expert])
                copies.append(remote(target if arriving else source, target, *sems, here.above(steps)))
        return copies

    def begin(self):
        for copies in zip(*[self.pieces(steps, False) for steps in (2, 3, 1, 0)]):
            for copy in copies:
                copy.start()

    def end(self):
        for steps in range(DEPTH):
            for copy in self.pieces(steps, False):
                copy.wait() if steps == 0 else copy.wait_send()
            if steps:
                for copy in self.pieces(steps, True):
                    copy.wait_recv()


STRIP = 128


def last_sum_kernel(
    normed,
    attended,
    gin_sum,
    weight,
    weight_out,
    tokens,
    routed,
    upstream,
    middle,
    raw,
    queries,
    keys,
    values,
    probs,
    cosine,
    sine,
    gains,
    q_sum,
    o_sum,
    gain_sums,
    grad_tokens,
    share_in,
    *scratch,
):
    here = Here()
    here.meet()
    block, width = tokens.shape
    share = q_sum.shape[0]
    wide = q_sum.shape[1]
    sides = wide // width
    heads = width // HEAD
    (
        left, left_out, right, panel, x, routed_v, upstream_v, middle_v, raw_v, queries_v, keys_v, values_v, probs_v,
        grad_middle, grad_heads, turned, piece, few_sum, few_other, sems, panel_sems, pair_sems, share_sems
    ) = scratch[:23]
    big = Sum(
        here,
        None,
        [(q_sum.at[:, pl.ds(side * width, width)], side * share, share) for side in range(sides)],
        halves_of(sides * share),
        False,
        scratch[23:31],
    )
    outer = Sum(here, None, o_sum, halves_of(share), False, scratch[31:39])
    few = Sum(here, None, few_sum, halves_of(few_sum.shape[0], False), False, scratch[39:47])
    order = [far_first(here, number) for number in range(DEPTH)]
    loads = [
        pltpu.make_async_copy(source, target, sems.at[number])
        for number, (source, target) in enumerate(
            (
                (middle, middle_v),
                (routed, routed_v),
                (upstream, upstream_v),
                (attended, left_out.at[0]),
                (values, values_v),
                (probs, probs_v),
                (queries, queries_v),
                (keys, keys_v),
                (raw, raw_v),
                (normed, left.at[0]),
                (tokens, x),
            )
        )
    ]

    def fetch(source, number, columns):
        slot = lax.rem(number, 2)
        rows = pl.ds(pl.multiple_of(number * STRIP, STRIP), STRIP)
        return pltpu.make_async_copy(source.at[rows], panel.at[slot, :, pl.ds(0, columns)], panel_sems.at[slot])

    for copy in loads:
        copy.start()
    fetch(weight_out, 0, width).start()
    shares_in = [Share(here, gin_sum, share_in, side, share_sems.at[side]) for side in range(2)]
    for share_side in shares_in:
        share_side.begin()

    def swap(number, source, target):
        base = 16 + 2 * number
        return remote(source, target, sems.at[base], sems.at[base + 1], here.sibling())

    side_out = pl.ds(wide, width)
    side_qkv = pl.ds(0, wide)
    swaps = [
        swap(0, left_out.at[0], left_out.at[1]),
        swap(1, right.at[0, :, side_out], right.at[1, :, side_out]),
        swap(2, left.at[0], left.at[1]),
        swap(3, right.at[0, :, side_qkv], right.at[1, :, side_qkv]),
    ]
    high = 16
    panels = width // STRIP

    def slabs(body):
        def one(number, carry):
            body(pl.ds(pl.multiple_of(number * high, high), high))
            return carry

        lax.fori_loop(0, block // high, one, 0)

    def norm(values):
        factor = lax.rsqrt(jnp.mean(values * values, axis=-1, keepdims=True) + epsilon)
        return values * factor, factor

    def norm_grad(up, values, row):
        normal, factor = norm(values)
        weighted = up * gains[row : row + 1]
        inner = jnp.mean(weighted * normal, axis=-1, keepdims=True)
        piece[row : row + 1] += jnp.sum(up * normal, axis=0, keepdims=True)
        return factor * (weighted - normal * inner)

    def first(at):
        grad = upstream_v[at].astype(single) + norm_grad(routed_v[at], middle_v[at], 3)
        grad_middle[at] = grad
        right[0, at, side_out] = grad.astype(narrow)

    piece[...] = jnp.zeros_like(piece)
    for number in range(4):
        loads[number].wait()
    swaps[0].start()
    slabs(first)
    swaps[1].start()

    def through(source, columns, left_rows, finish, begin=0, end=panels):
        def one(number, carry):
            fetch(source, number, columns).wait()
            pl.when(number + 1 < panels)(lambda: fetch(source, number + 1, columns).start())
            rows = panel[lax.rem(number, 2), :, 0:columns]
            finish(pl.ds(pl.multiple_of(number * STRIP, STRIP), STRIP), contract_last(left_rows, rows))
            return carry

        lax.fori_loop(begin, end, one, 0)

    def keep_heads(spot, made):
        grad_heads[:, spot] = made.astype(narrow)

    through(weight_out, width, right[0, :, side_out], keep_heads)
    fetch(weight, 0, wide).start()

    step = 512
    each = width // step
    rows = RING * 2 * share

    def make(z, item, source, first_chunk, last_chunk):
        at = pl.ds(pl.multiple_of(z * rows, rows), rows)

        def one(number, carry):
            spot = pl.ds(pl.multiple_of(number * step, step), step)
            left_rows = source[:, :, at].reshape(2 * block, rows)
            made = contract_rows(left_rows, right[:, :, spot].reshape(2 * block, step))
            made = made.reshape(RING, 2, share, step)
            mine = jnp.where(here.core == 0, made[:, 0], made[:, 1]).astype(narrow)
            row = pl.multiple_of(lax.div(number - first_chunk, each) * share, share)
            column = pl.multiple_of(lax.rem(number, each) * step, step)
            for chip in range(RING):
                item.mine[z, chip, pl.ds(row, share), pl.ds(column, step)] = mine[chip]
            return carry

        lax.fori_loop(first_chunk, last_chunk, one, 0)

    swaps[0].wait_recv()
    swaps[1].wait_recv()
    for z in order:
        make(z, outer, left_out, sides * each, (sides + 1) * each)
        for way in (0, 1):
            start(outer.toss(z, way))
    for number in range(4, len(loads)):
        loads[number].wait()
    swaps[2].start()
    turn_cos, turn_sin = cosine[...], sine[...]
    group = 4

    def some_heads(number, carry):
        for inner in range(group):
            head = number * group + inner
            spot = pl.ds(pl.multiple_of(head * HEAD, HEAD), HEAD)
            grad = grad_heads[:, spot]
            shares = probs_v[head]
            grad_shares = contract_last(grad, values_v[:, spot])
            along = jnp.sum(grad_shares * shares, axis=-1, keepdims=True)
            scores = (shares * (grad_shares - along)).astype(narrow)
            made = (
                jnp.dot(scores, keys_v[:, spot], preferred_element_type=single),
                contract_rows(scores, queries_v[:, spot]),
            )
            for side, field in enumerate(made):
                field = field * HEAD ** (-0.5)
                turned[side, :, spot] = field * turn_cos - pltpu.roll(field, HEAD // 2, 1) * turn_sin
            spot_v = pl.ds(pl.multiple_of(2 * width + head * HEAD, HEAD), HEAD)
            right[0, :, spot_v] = contract_rows(shares.astype(narrow), grad).astype(narrow)
        return carry

    lax.fori_loop(0, heads // group, some_heads, 0)

    def second(at):
        for side in range(2):
            grad = norm_grad(turned[side, at], raw_v[side, at], side + 1)
            right[0, at, side * width : (side + 1) * width] = grad.astype(narrow)

    for z in order[:2]:
        outer.second(z)
    slabs(second)
    swaps[3].start()
    for z in order[2:]:
        outer.second(z)
    swaps[2].wait_recv()
    swaps[3].wait_recv()

    def keep_back(spot, made):
        routed_v[:, spot] = made

    def third(at):
        grad_tokens[at] = grad_middle[at] + norm_grad(routed_v[at], x[at].astype(single), 0)

    for number, z in enumerate(order):
        make(z, big, left, 0, sides * each)
        for way in (0, 1):
            start(big.toss(z, way))
        if number:
            big.second(order[number - 1])
        outer.third(z, number == DEPTH - 1)
        if number > 1:
            big.third(order[number - 2], False)
        cut = panels // DEPTH
        through(weight, wide, right[0, :, side_qkv], keep_back, number * cut, (number + 1) * cut)
        if number == DEPTH - 1:
            slabs(third)
            for plane in range(DEPTH):
                for chip in range(RING):
                    begin = (plane * RING + chip) * 2 * share
                    few.mine[plane, chip] = piece[:, begin : begin + 2 * share]
            for place in order:
                start(few.toss(place, 0))
    big.second(order[-1])
    for z in order:
        few.second(z)
    big.third(order[-2], False)
    for z in order[:-1]:
        few.third(z, False)
    big.third(order[-1], True)
    few.third(order[-1], True)
    pair = remote(few_sum, few_other, pair_sems.at[0], pair_sems.at[1], here.sibling())
    pair.start()
    pair.wait_recv()
    gain_sums[...] = few_sum[...] + few_other[...]
    pair.wait_send()
    for number, z in enumerate(order):
        for item in (big, outer, few):
            item.end(z, number == DEPTH - 1)
    for copy in swaps:
        copy.wait_send()
    for share_side in shares_in:
        share_side.end()


def last_sum(
    normed, attended, gin_sum, weight, weight_out, tokens, routed, upstream, middle, raw, queries, keys, values, probs,
    cosine, sine, gains, share, held
):
    block, width = normed.shape
    wide = weight.shape[1]
    sides = wide // width
    vmem = pl.BlockSpec(memory_space=pltpu.VMEM)
    few = (gains.shape[0], 2 * share)
    like = pltpu.VMEM((block, width), narrow)
    like_single = pltpu.VMEM((block, width), single)
    return pl.pallas_call(
        last_sum_kernel,
        out_shape=(
            jax.ShapeDtypeStruct((share, wide), single),
            jax.ShapeDtypeStruct((share, width), single),
            jax.ShapeDtypeStruct(few, single),
            jax.ShapeDtypeStruct((block, width), single),
            jax.ShapeDtypeStruct((held, gin_sum.shape[0] // DEPTH, DEPTH * gin_sum.shape[1] // held), narrow),
        ),
        in_specs=[HBM] * 14 + [vmem] * 3,
        out_specs=(vmem, vmem, vmem, vmem, HBM),
        scratch_shapes=[
            pltpu.VMEM((2, block, width), narrow),
            pltpu.VMEM((2, block, width), narrow),
            pltpu.VMEM((2, block, wide + width), narrow),
            pltpu.VMEM((2, STRIP, wide), narrow),
            like,
            like_single,
            like,
            like_single,
            pltpu.VMEM(raw.shape, single),
            like,
            like,
            like,
            pltpu.VMEM(probs.shape, single),
            like_single,
            like,
            pltpu.VMEM((2, block, width), single),
            pltpu.VMEM(gains.shape, single),
            pltpu.VMEM(few, single),
            pltpu.VMEM(few, single),
            pltpu.SemaphoreType.DMA((24,)),
            pltpu.SemaphoreType.DMA((2,)),
            pltpu.SemaphoreType.DMA((2,)),
            pltpu.SemaphoreType.DMA((2, 2, DEPTH, held)),
        ]
        + sum_scratch(sides * share, width, narrow, halves_of(sides * share), made=True)
        + sum_scratch(share, width, narrow, halves_of(share), made=True)
        + sum_scratch(few[0], few[1], single, halves_of(few[0], False), made=True),
        compiler_params=pltpu.CompilerParams(
            collective_id=4, has_side_effects=True, vmem_limit_bytes=62 * 2**20
        ),
        name="deliver",
    )(
        normed, attended, gin_sum, weight, weight_out, tokens, routed, upstream, middle, raw, queries, keys, values, probs,
        cosine, sine, gains
    )

def near_first(here, number):
    high = lax.div(here.z, 2)
    inner = lax.rem(lax.div(here.z + 1, 2), 2)
    low = number + inner * (1, -1, 0, 0)[number]
    return low + high * (DEPTH - 1 - 2 * low)


class Tiles:
    def __init__(self, here, stage, count, sems, parts, targets):
        self.here, self.stage, self.count = here, stage, count
        self.kept, self.sent, self.came = sems
        self.parts, self.targets = parts, targets

    def copies(self, number, keep=True, give=True):
        slot = lax.rem(number, 2)
        own, other = self.targets
        made = []
        for piece, (mine, theirs, spot) in enumerate(self.parts(number, self.stage.at[slot])):
            if keep:
                made.append(pltpu.make_async_copy(mine, own.at[spot], self.kept.at[slot, piece]))
            if give:
                sems = (self.sent.at[slot, piece], self.came.at[number, piece])
                made.append(remote(theirs, other.at[spot], *sems, self.here.sibling()))
        return made

    def settle(self, number):
        for copy in self.copies(number, give=False):
            copy.wait()
        for copy in self.copies(number, keep=False):
            copy.wait_send()

    def run(self, first, last, make):
        def body(number, carry):
            pl.when(number >= 2)(lambda: self.settle(number - 2))
            make(number, self.stage.at[lax.rem(number, 2)])
            for copy in self.copies(number):
                copy.start()
            return carry

        lax.fori_loop(first, last, body, 0)
        if last == self.count:
            for number in (last - 2, last - 1):
                self.settle(number)

    def heard(self):
        for number in range(self.count):
            for copy in self.copies(number, keep=False):
                copy.wait_recv()


def experts_kernel(
    rows, ups, gates, win, wout, mid_sum, gate_sum, out_sum, gin_sum, gdown, gdown_other, gin, gin_other, rows_all, *scratch
):
    here = Here()
    here.meet()
    (
        w_in, w_out, grads, scaled, row_plane, up_plane, gate_plane, served, strip, stage, loads, strip_sems
    ) = scratch[:12]
    gather = Gather(here, rows, rows_all, halves_of(rows.shape[0]), False, scratch[12:16])
    mids = Sum(here, None, mid_sum, halves_of(rows.shape[0]), False, scratch[16:24])
    outs = Sum(here, None, out_sum, halves_of(rows.shape[0]), False, scratch[16:19] + scratch[24:29])
    tables = Sum(here, None, gate_sum, halves_of(gate_sum.shape[0], False), False, scratch[29:37])
    in_sems, down_sems = scratch[37:40], scratch[40:43]
    block, width = rows.shape
    plane = RING * block
    hidden = w_out.shape[0]
    chunk = hidden // 4
    column = lax.broadcasted_iota(jnp.int32, (plane, 128), 1)
    fetch_in = pltpu.make_async_copy(win, w_in, loads.at[0])
    fetch_out = pltpu.make_async_copy(wout, w_out, loads.at[1])
    fetch_in.start()
    fetch_out.start()

    def fetch_plane(number):
        z = near_first(here, number)
        return (
            pltpu.make_async_copy(ups.at[z], up_plane.at[number % 2], loads.at[2 + number % 2]),
            pltpu.make_async_copy(gates.at[z], gate_plane.at[number % 2], loads.at[4 + number % 2]),
        )

    def fetch_rows(number):
        return pltpu.make_async_copy(rows_all.at[near_first(here, number)], row_plane, loads.at[6])

    def hidden_units(number):
        z = near_first(here, number)
        fetch_rows(number).start()
        for copy in fetch_plane(number):
            copy.wait()
        if number == 0:
            fetch_in.wait()
            fetch_out.wait()
        fetch_rows(number).wait()
        served[...] = jnp.zeros_like(served)
        at = pl.ds(pl.multiple_of(z * plane, plane), plane)

        def one(expert, carry):
            mid = row_plane[...].reshape(plane, width)
            up_rows = up_plane[number % 2]
            spot = pl.ds(pl.multiple_of(expert * chunk, chunk), chunk)
            spot_up = pl.ds(pl.multiple_of(hidden + expert * chunk, chunk), chunk)
            gate = jnp.sum(jnp.where(column == expert, gate_plane[number % 2], 0.0), axis=1, keepdims=True)
            gate_part = jnp.dot(mid, w_in[:, spot], preferred_element_type=single)
            up_part = jnp.dot(mid, w_in[:, spot_up], preferred_element_type=single)
            back = contract_last(up_rows, w_out[spot])
            sigmoid = 1.0 / (1.0 + jnp.exp(-gate_part))
            activated = gate_part * sigmoid
            units = activated * up_part
            scaled[at, spot] = (gate * units).astype(narrow)
            total = jnp.sum(units * back, axis=1, keepdims=True)
            served[...] += jnp.where(column == here.chip * 4 + expert, total, 0.0)
            grad = gate * back
            grads[at, spot] = (grad * up_part * (sigmoid * (1.0 + gate_part * (1.0 - sigmoid)))).astype(narrow)
            grads[at, spot_up] = (grad * activated).astype(narrow)
            return carry

        lax.fori_loop(0, 4, one, 0)
        for chip in range(RING):
            turned = jnp.transpose(served[chip * block : (chip + 1) * block])
            tables.mine[z, chip] = turned[: tables.rows]

    def row_grads(z):
        at = pl.ds(pl.multiple_of(z * plane, plane), plane)

        def one(number, carry):
            spot = pl.ds(pl.multiple_of(number * TILE, TILE), TILE)
            made = contract_last(grads[at], w_in[spot]).astype(narrow)
            for chip in range(RING):
                mids.mine[z, chip, :, spot] = made[chip * block : (chip + 1) * block]
            return carry

        lax.fori_loop(0, width // TILE, one, 0)

    def products(z):
        at = pl.ds(pl.multiple_of(z * plane, plane), plane)

        def one(number, carry):
            spot = pl.ds(pl.multiple_of(number * TILE, TILE), TILE)
            made = jnp.dot(scaled[at], w_out[:, spot], preferred_element_type=single).astype(narrow)
            for chip in range(RING):
                outs.mine[z, chip, :, spot] = made[chip * block : (chip + 1) * block]
            return carry

        lax.fori_loop(0, width // TILE, one, 0)

    strips = width // TILE

    def fetch_strip(number):
        spot = pl.ds(pl.multiple_of(number * TILE, TILE), TILE)
        slot = lax.rem(number, 2)
        return pltpu.make_async_copy(rows_all.at[:, :, :, spot], strip.at[slot], strip_sems.at[slot])

    def columns_of(result, stage, step=512):
        for begin in range(0, width, step):
            stage[:, begin : begin + step] = result(begin, step).astype(narrow)

    def grad_in(number, stage):
        slot = lax.rem(number, 2)
        fetch_strip(number).wait()
        pl.when(number + 1 < strips)(lambda: fetch_strip(number + 1).start())
        left = strip[slot].reshape(DEPTH * plane, TILE)
        columns_of(lambda begin, step: contract_rows(left, grads[:, begin : begin + step]), stage)

    def grad_in_parts(number, stage):
        share = hidden // 2
        at = pl.ds(pl.multiple_of(number * TILE, TILE), TILE)
        for side in range(2):
            mine, theirs = (
                stage.at[:, pl.ds(pl.multiple_of(side * hidden + core * share, 128), share)]
                for core in (here.core, 1 - here.core)
            )
            yield mine, theirs, (at, pl.ds(side * share, share))

    def grad_down(number, stage):
        half = tall // 2
        core = here.core + (1 - lax.div(number, half)) * (1 - 2 * here.core)
        at = core * half + lax.rem(number, half)
        left = scaled[:, pl.ds(pl.multiple_of(at * TILE, TILE), TILE)]
        columns_of(lambda begin, step: contract_rows(left, w_in[:, begin : begin + step]), stage)

    tall = hidden // TILE
    tiles_in = Tiles(here, stage, strips, in_sems, grad_in_parts, (gin, gin_other))

    def grad_down_store(number, away):
        slot = lax.rem(number, 2)
        rest = lax.rem(number, tall // 2)
        spot = pl.ds(pl.multiple_of(rest * TILE, TILE), TILE)
        kept, sent, came = down_sems
        if away:
            return remote(stage.at[slot], gdown_other.at[spot], sent.at[slot, 0], came.at[rest, 0], here.sibling())
        return pltpu.make_async_copy(stage.at[slot], gdown.at[spot], kept.at[slot, 0])

    def grads_down(away):
        first = 0 if away else tall // 2

        def body(number, carry):
            grad_down(number, stage.at[lax.rem(number, 2)])
            grad_down_store(number, away).start()
            return carry

        lax.fori_loop(first, first + tall // 2, body, 0)
        for number in range(first, first + tall // 2):
            copy = grad_down_store(number, away)
            copy.wait_send() if away else copy.wait()

    def add_cores():
        half = hidden
        adds, puts = scratch[43], scratch[44]

        def fetch(number):
            slot = lax.rem(number, 2)
            at = pl.ds(pl.multiple_of(number * TILE, TILE), TILE)
            return [
                pltpu.make_async_copy(
                    source.at[at], stage.at[slot, :, pl.ds(side * half, half)], adds.at[slot, side]
                )
                for side, source in enumerate((gin, gin_other))
            ]

        def put(number):
            slot = lax.rem(number, 2)
            at = pl.ds(pl.multiple_of(number * TILE, TILE), TILE)
            return pltpu.make_async_copy(stage.at[slot, :, pl.ds(0, half)], gin_sum.at[at], puts.at[slot])

        def start_fetch(number):
            for copy in fetch(number):
                copy.start()

        def body(number, carry):
            for copy in fetch(number):
                copy.wait()
            pl.when(number >= 1)(lambda: put(number - 1).wait())
            pl.when(number + 1 < strips)(lambda: start_fetch(number + 1))
            slot = lax.rem(number, 2)
            own = stage.at[slot, :, pl.ds(0, half)]
            add_up(own, [own, stage.at[slot, :, pl.ds(half, half)]], TILE, half)
            put(number).start()
            return carry

        start_fetch(0)
        lax.fori_loop(0, strips, body, 0)
        put(strips - 1).wait()

    again = [
        pltpu.make_async_copy(ups.at[z], w_in.at[pl.ds(z * plane, plane)], loads.at[7 + z]) for z in range(DEPTH)
    ]

    def again_wait():
        for copy in again:
            copy.wait()

    order = [far_first(here, number) for number in range(DEPTH)]
    first = [mids, tables]
    steps = [(first, z, False) for z in [here.z] + order[:-1]]
    steps += [([outs], z, number == DEPTH - 1) for number, z in enumerate(order)]

    def begin(number):
        items, z, last = steps[number]
        if number < DEPTH:
            row_grads(z)
        else:
            mids.end(z, last)
            products(z)
        for item in items:
            for way in (0, 1):
                start(item.toss(z, way))

    def second(number):
        for item in steps[number][0]:
            item.second(steps[number][1])

    def third(number):
        items, z, last = steps[number]
        for item in items:
            item.own_part(z) if number == 0 else item.third(z, last)

    for copy in fetch_plane(0):
        copy.start()
    rounds = Rounds(here, [gather])
    rounds.service(0)
    for number in range(DEPTH):
        if number + 1 < DEPTH:
            rounds.service(number + 1)
        if number == DEPTH - 1:
            second(0)
        gather_third(gather, near_first(here, number))
        if number + 1 < DEPTH:
            for copy in fetch_plane(number + 1):
                copy.start()
        hidden_units(number)
        if number == 1:
            begin(0)
    fetch_strip(0).start()
    ends = [0] + [strips * (number + 1) // (DEPTH - 1) for number in range(DEPTH - 1)]
    for number in range(1, 2 * DEPTH):
        begin(number)
        if number > 1:
            second(number - 1)
            third(number - 2)
        if number == DEPTH - 1:
            for copy in again:
                copy.start()
        if number < DEPTH:
            tiles_in.run(ends[number - 1], ends[number], grad_in)
        elif number == DEPTH:
            again_wait()
            grads_down(True)
        elif number == DEPTH + 1:
            grads_down(False)
        elif number == DEPTH + 2:
            for item in first:
                item.own_rest(here.z)
            tiles_in.heard()
            add_cores()
    outs.second(order[-1])
    outs.third(order[-2], False)
    outs.third(order[-1], True)
    for number, z in enumerate(order):
        outs.end(z, number == DEPTH - 1)
        tables.end(z, number == DEPTH - 1)
    for number in range(tall // 2):
        grad_down_store(number, True).wait_recv()
    rounds.finish()


def experts_round(rows, ups, gates, win, wout, experts):
    block, width = rows.shape
    plane = RING * block
    hidden = wout.shape[0]
    total = DEPTH * plane
    vmem = pl.BlockSpec(memory_space=pltpu.VMEM)
    return pl.pallas_call(
        experts_kernel,
        out_shape=(
            jax.ShapeDtypeStruct((block, width), single),
            jax.ShapeDtypeStruct((experts, block), single),
            jax.ShapeDtypeStruct((block, width), single),
            jax.ShapeDtypeStruct((width, hidden), narrow),
            jax.ShapeDtypeStruct((hidden // 2, width), narrow),
            jax.ShapeDtypeStruct((hidden // 2, width), narrow),
            jax.ShapeDtypeStruct((width, hidden), narrow),
            jax.ShapeDtypeStruct((width, hidden), narrow),
            jax.ShapeDtypeStruct((DEPTH, RING, block, width), narrow),
        ),
        in_specs=[HBM] * 5,
        out_specs=(vmem, vmem, vmem) + (HBM,) * 6,
        scratch_shapes=[
            pltpu.VMEM((width, 2 * hidden), narrow),
            pltpu.VMEM((hidden, width), narrow),
            pltpu.VMEM((total, 2 * hidden), narrow),
            pltpu.VMEM((total, hidden), narrow),
            pltpu.VMEM((RING, block, width), narrow),
            pltpu.VMEM((2, plane, width), narrow),
            pltpu.VMEM((2, plane, 128), single),
            pltpu.VMEM((plane, 128), single),
            pltpu.VMEM((2, DEPTH, RING, block, TILE), narrow),
            pltpu.VMEM((2, TILE, width), narrow),
            pltpu.SemaphoreType.DMA((11,)),
            pltpu.SemaphoreType.DMA((2,)),
        ]
        + GATHER_SEMS
        + sum_scratch(block, width, narrow, halves_of(block), made=True)
        + [pltpu.VMEM((DEPTH + 1, block, width), narrow)]
        + SUM_SEMS
        + sum_scratch(experts, block, single, halves_of(experts, False), made=True)
        + [
            pltpu.SemaphoreType.DMA((2, 2)),
            pltpu.SemaphoreType.DMA((2, 2)),
            pltpu.SemaphoreType.DMA((width // TILE, 2)),
        ]
        + [
            pltpu.SemaphoreType.DMA((2, 1)),
            pltpu.SemaphoreType.DMA((2, 1)),
            pltpu.SemaphoreType.DMA((hidden // TILE, 1)),
        ]
        + [pltpu.SemaphoreType.DMA((2, 2)), pltpu.SemaphoreType.DMA((2,))],
        compiler_params=pltpu.CompilerParams(
            collective_id=2, has_side_effects=True, vmem_limit_bytes=62 * 2**20
        ),
        name="experts",
    )(rows, ups, gates, win, wout)


def by_kernels():
    return lax.axis_size("dp") == DEPTH and lax.axis_size("expert") == 2 * RING


def forward(tokens, gains, weight_qkv, weight_out, cosine, sine, allowed):
    rows, width = tokens.shape
    inputs = tokens.astype(single)
    normed_in = (normalize(inputs)[0] * gains[0]).astype(narrow)
    projected = jnp.dot(normed_in, weight_qkv, preferred_element_type=single)
    raw = jnp.stack([projected[:, :width], projected[:, width : 2 * width]])
    query_rows, key_rows = (
        rotate(normalize(raw[side])[0] * gains[side + 1], cosine, sine).astype(narrow) for side in range(2)
    )
    value_rows = projected[:, 2 * width :].astype(narrow)
    by_head = (rows, -1, HEAD)
    scores = jnp.einsum(
        "qhd,khd->hqk", query_rows.reshape(by_head), key_rows.reshape(by_head), preferred_element_type=single
    )
    scores = jnp.where(allowed[None], scores * HEAD ** (-0.5), masked_score)
    unnormed = jnp.exp(scores - jnp.max(scores, axis=-1, keepdims=True))
    probs = unnormed / jnp.sum(unnormed, axis=-1, keepdims=True)
    attended = jnp.einsum(
        "hqk,khd->qhd", probs.astype(narrow), value_rows.reshape(by_head), preferred_element_type=single
    )
    attended = attended.reshape(rows, width).astype(narrow)
    middle = inputs + jnp.dot(attended, weight_out, preferred_element_type=single)
    routed_in = (normalize(middle)[0] * gains[3]).astype(narrow)
    return (normed_in, raw, query_rows, key_rows, value_rows, probs, attended, middle, routed_in)


def wide_tables(cosine, sine):
    return (
        jnp.concatenate([cosine[:, 0], cosine[:, 0]], axis=1),
        jnp.concatenate([-sine[:, 0], sine[:, 0]], axis=1),
    )


def bring_all(w_qkv, w_out, upstream, dense, gain_rows, expert_in, expert_out, tokens, cosine, sine, allowed):
    width = upstream.shape[1]
    share = gain_rows.shape[1]
    if by_kernels():
        experts, rows = dense.shape[1], dense.shape[0]
        small = jnp.concatenate([dense.T, jnp.pad(gain_rows, ((0, 4), (0, rows - share)))], axis=0)
        tables = (*wide_tables(cosine, sine), allowed.astype(single))
        wq, wo, up, all_small, weight_in, weight_down, gains, *made = first_gather(
            w_qkv, w_out, upstream, small, expert_in, expert_out, tokens, *tables
        )
        core = lax.rem(lax.axis_index("expert"), 2)
        every_gate = lax.dynamic_index_in_dim(all_small, core, axis=2, keepdims=False)[:, :, :experts]
        return (
            wq.reshape(-1, w_qkv.shape[1]),
            wo.reshape(-1, w_out.shape[1]),
            up.reshape(-1, width),
            every_gate,
            gains,
            weight_in,
            weight_down.reshape(-1, width),
            made,
        )
    everyone = ("dp", "expert")
    weight_in, weight_down = fetch_weights(expert_in, expert_out)
    weight_qkv = lax.all_gather(w_qkv, everyone, axis=0, tiled=True)
    weight_out = lax.all_gather(w_out, everyone, axis=0, tiled=True)
    gains = lax.all_gather(gain_rows, everyone, axis=1, tiled=True)
    return (
        weight_qkv,
        weight_out,
        gather_alike(upstream).reshape(-1, width),
        gather_alike(dense.T),
        gains,
        weight_in,
        weight_down,
        forward(tokens, gains, weight_qkv, weight_out, cosine, sine, allowed),
    )


def experts_all(routed_in, up_rows, every_gate, weight_in, weight_down, held):
    depth = lax.axis_size("dp")
    owners = lax.axis_size("expert")
    chips = owners // 2
    experts = owners * held
    chip_experts = 2 * held
    rows, width = routed_in.shape
    chip = lax.axis_index("expert") // 2
    mine = lax.dynamic_slice_in_dim(every_gate, chip * chip_experts, chip_experts, axis=2)
    gate = mine.transpose(0, 1, 3, 2)
    if by_kernels():
        gate = jnp.pad(gate.reshape(DEPTH, -1, chip_experts), ((0, 0), (0, 0), (0, 128 - chip_experts)))
        ups = up_rows.reshape(DEPTH, -1, width)
        grad_routed, table, mixture, grad_in, grad_down, grad_down_other = experts_round(
            routed_in, ups, gate, weight_in, weight_down, experts
        )[:6]
        down = grad_down.astype(single) + grad_down_other.astype(single)
        return (mixture, grad_routed, table, (grad_in, down.reshape(held, -1, width)))
    mid_rows = gather_alike(routed_in).reshape(-1, width)
    out, mid, served, grad_in, grad_down = expert_rounds(
        mid_rows, up_rows, gate.reshape(-1, chip_experts), weight_in, weight_down
    )
    by_gate = served.reshape(depth, chips, rows, chip_experts).transpose(0, 1, 3, 2)
    spread = jnp.zeros((depth, chips, experts, rows), single)
    spread = lax.dynamic_update_slice_in_dim(spread, by_gate, chip * chip_experts, axis=2)
    return (
        scatter_alike(out.reshape(depth, chips, rows, width)).astype(single),
        scatter_alike(mid.reshape(depth, chips, rows, width)).astype(single),
        scatter_alike(spread),
        return_weights(grad_in, grad_down, held),
    )


def backward(
    tokens, gains, grad_routed, upstream, normed, raw, queries, keys, values, probs, attended, middle, weight_qkv, weight_out,
    cosine, sine
):
    rows, width = tokens.shape
    by_head = (rows, -1, HEAD)
    grad_mid, piece_ffn = rms_back(grad_routed, *normalize(middle), gains[3])
    grad_middle = upstream.astype(single) + grad_mid
    branch = grad_middle.astype(narrow)
    grad_heads = contract_last(branch, weight_out).astype(narrow).reshape(by_head)
    grad_probs = jnp.einsum("qhd,khd->hqk", grad_heads, values.reshape(by_head), preferred_element_type=single)
    inner = jnp.sum(grad_probs * probs, axis=-1, keepdims=True)
    grad_scores = (probs * (grad_probs - inner)).astype(narrow)
    grads = (
        jnp.einsum("hqk,khd->qhd", grad_scores, keys.reshape(by_head), preferred_element_type=single),
        jnp.einsum("hqk,qhd->khd", grad_scores, queries.reshape(by_head), preferred_element_type=single),
    )
    grad_value = jnp.einsum("hqk,qhd->khd", probs.astype(narrow), grad_heads, preferred_element_type=single)
    (grad_q, piece_query), (grad_k, piece_key) = (
        rms_back(
            rotate(grads[side].reshape(rows, width) * HEAD ** (-0.5), cosine, -sine),
            *normalize(raw[side]),
            gains[side + 1],
        )
        for side in range(2)
    )
    grad_qkv = jnp.concatenate([grad_q, grad_k, grad_value.reshape(rows, width)], axis=1).astype(narrow)
    grad_input, piece_attn = rms_back(
        contract_last(grad_qkv, weight_qkv), *normalize(tokens.astype(single)), gains[0]
    )
    pieces = jnp.stack([piece_attn, piece_query, piece_key, piece_ffn])
    return (grad_middle + grad_input, pieces, (normed, grad_qkv), (attended, branch))


def deliver_all(tokens, gains, grad_routed, upstream, made, weight_qkv, weight_out, cosine, sine, share_in, held):
    normed, raw, queries, keys, values, probs, attended, middle, _ = made
    owners = lax.axis_size("dp") * lax.axis_size("expert")
    share = gains.shape[1] // owners
    if by_kernels():
        share_qkv, share_out, gain_sums, grad_tokens, share_in = last_sum(
            normed, attended, share_in, weight_qkv, weight_out, tokens, grad_routed, upstream, middle, raw, queries, keys,
            values, probs, *wide_tables(cosine, sine), gains, share, held
        )
        core = lax.rem(lax.axis_index("expert"), 2)
        gain_sums = lax.dynamic_slice_in_dim(gain_sums, core * share, share, axis=1)
        return (grad_tokens, gain_sums, share_qkv, share_out, share_in.astype(single))
    everyone = ("dp", "expert")
    grad_tokens, pieces, *pairs = backward(
        tokens, gains, grad_routed, upstream, normed, raw, queries, keys, values, probs, attended, middle, weight_qkv,
        weight_out, cosine, sine
    )
    return (
        grad_tokens,
        lax.psum_scatter(pieces, everyone, scatter_dimension=1, tiled=True),
        *(
            lax.psum_scatter(
                contract_rows(left, right, narrow), everyone, scatter_dimension=0, tiled=True
            ).astype(single)
            for left, right in pairs
        ),
        share_in.astype(single),
    )


def local(
    tokens,
    lengths,
    expert_ids,
    gates,
    attn_gain,
    w_qkv,
    q_gain,
    k_gain,
    w_out,
    ffn_gain,
    expert_in,
    expert_out,
    out_grad,
):
    micro_count, seq_len, model_width = tokens.shape
    rows = micro_count * seq_len
    held = expert_in.shape[0]
    experts = lax.axis_size("expert") * held
    own = tokens.reshape(rows, model_width)
    upstream = out_grad.reshape(rows, model_width)
    ids = expert_ids.reshape(rows, -1)
    gate_rows = gates.reshape(rows, -1)
    onehot = (ids[:, :, None] == jnp.arange(experts, dtype=jnp.int32)).astype(single)
    dense = jnp.sum(onehot * gate_rows[:, :, None], axis=1)
    gain_rows = jnp.stack([attn_gain, q_gain, k_gain, ffn_gain]).astype(single)
    document, position = layout(lengths[:, 0], seq_len)
    cosine, sine = angles(position)
    places = jnp.arange(rows, dtype=jnp.int32)
    allowed = (document[:, None] == document[None, :]) & (places[:, None] >= places[None, :])
    weight_qkv, weight_out, up_rows, every_gate, gains, weight_in, weight_down, made = bring_all(
        w_qkv, w_out, upstream, dense, gain_rows, expert_in, expert_out, own, cosine, sine, allowed
    )
    middle, routed_in = made[-2:]

    mixture, grad_routed, gate_table, (share_in, share_down) = experts_all(
        routed_in, up_rows, every_gate, weight_in, weight_down, held
    )
    grad_gates = jnp.sum(onehot * gate_table.T[:, None, :], axis=2)
    results = (middle + mixture).astype(narrow)

    grad_tokens, gain_sums, grad_qkv_share, grad_out_share, share_in = deliver_all(
        own, gains, grad_routed, upstream, made, weight_qkv, weight_out, cosine, sine, share_in, held
    )
    shape = (micro_count, seq_len, model_width)
    return (
        results.reshape(shape),
        grad_tokens.reshape(shape),
        grad_gates.reshape(expert_ids.shape),
        gain_sums[0],
        grad_qkv_share,
        gain_sums[1],
        gain_sums[2],
        grad_out_share,
        gain_sums[3],
        share_in,
        share_down.astype(single),
    )


def solution(mesh):
    by_rows = P(None, ("dp", "expert"), None)
    flat = P(("dp", "expert"))
    split = P(("dp", "expert"), None)
    held = P("expert", "dp", None)
    return jax.shard_map(
        local,
        mesh=mesh,
        in_specs=(
            by_rows, by_rows, by_rows, by_rows, flat, split, flat, flat, split, flat, held, held, by_rows,
        ),
        out_specs=(by_rows, by_rows, by_rows, flat, split, flat, flat, split, flat, held, held),
        check_vma=False,
    )
```

```python
import jax
import jax.numpy as jnp
from jax import lax
from jax.experimental import pallas as pl
from jax.experimental.pallas import tpu as pltpu
from jax.sharding import PartitionSpec as P

HEAD = 128
epsilon = 1e-05
base_theta = 10000.0
masked_score = -1e30
single = jnp.float32
narrow = jnp.bfloat16


def normalize(values):
    factor = lax.rsqrt(jnp.mean(values * values, axis=-1, keepdims=True) + epsilon)
    return (values * factor, factor)


def rms_back(upstream, normal, factor, gain):
    weighted = upstream * gain
    inner = jnp.mean(weighted * normal, axis=-1, keepdims=True)
    return (factor * (weighted - normal * inner), jnp.sum(upstream * normal, axis=0))


def angles(position):
    half = HEAD // 2
    ladder = jnp.arange(half, dtype=single) * (2.0 / HEAD)
    frequency = jnp.exp(-jnp.log(base_theta) * ladder)
    angle = position.astype(single)[:, None] * frequency[None, :]
    return (jnp.cos(angle)[:, None, :], jnp.sin(angle)[:, None, :])


def rotate(field, cosine, sine):
    length = field.shape[0]
    heads = field.reshape(length, -1, HEAD)
    half = HEAD // 2
    first = heads[..., :half]
    second = heads[..., half:]
    turned = jnp.concatenate(
        [first * cosine - second * sine, second * cosine + first * sine], axis=-1
    )
    return turned.reshape(length, -1)


def layout(doc_lengths, length):
    packs, count = doc_lengths.shape
    upto = jnp.arange(count)[None, :] <= jnp.arange(count)[:, None]
    ends = jnp.sum(jnp.where(upto[None], doc_lengths[:, None, :], 0), axis=2)
    starts = ends - doc_lengths
    places = jnp.arange(length, dtype=jnp.int32)[None, :, None]
    document = jnp.sum((places >= ends[:, None, :]).astype(jnp.int32), axis=2)
    member = (places >= starts[:, None, :]) & (places < ends[:, None, :])
    first_place = jnp.sum(jnp.where(member, starts[:, None, :], 0), axis=2)
    document = document + (count + 1) * jnp.arange(packs, dtype=jnp.int32)[:, None]
    return (document.reshape(-1), (places[..., 0] - first_place).reshape(-1))


def contract_rows(left, right, kind=single):
    return lax.dot_general(left, right, (((0,), (0,)), ((), ())), preferred_element_type=kind)


def contract_last(left, right, kind=single):
    return lax.dot_general(left, right, (((1,), (1,)), ((), ())), preferred_element_type=kind)


def core_groups():
    return [[2 * chip + core for chip in range(lax.axis_size("expert") // 2)] for core in range(2)]


def chip_groups():
    return [[2 * chip, 2 * chip + 1] for chip in range(lax.axis_size("expert") // 2)]


def gather_alike(block):
    column = lax.all_gather(block, "dp", axis=0)
    return lax.all_gather(column, "expert", axis=1, axis_index_groups=core_groups())


def scatter_alike(blocks):
    column = lax.psum_scatter(
        blocks, "expert", scatter_dimension=1, axis_index_groups=core_groups()
    )
    return lax.psum_scatter(column, "dp", scatter_dimension=0)


def fetch_weights(expert_in, expert_out):
    depth = lax.axis_size("dp")
    held, rows, columns = expert_in.shape
    part = columns // (2 * depth)
    cut = expert_in.reshape(held, rows, 2, depth, part)
    turned = lax.all_to_all(cut, "dp", split_axis=3, concat_axis=1, tiled=True)
    both = lax.all_gather(turned[:, :, :, 0], "expert", axis=0, axis_index_groups=chip_groups())
    weight_in = both.transpose(2, 3, 0, 1, 4).reshape(depth * rows, 4 * held * part)
    weight_down = lax.all_gather(
        expert_out, "expert", axis=0, axis_index_groups=chip_groups()
    ).reshape(-1, expert_out.shape[2])
    return (weight_in, weight_down)


def return_weights(grad_in, grad_down, held):
    depth = lax.axis_size("dp")
    rows, columns = grad_in.shape
    part = columns // (4 * held)
    cut = grad_in.reshape(rows, 2, 2, held, part)
    own = lax.psum_scatter(cut, "expert", scatter_dimension=2, axis_index_groups=chip_groups())
    own = own.reshape(depth, rows // depth, 2, held, part)
    turned = lax.all_to_all(own, "dp", split_axis=0, concat_axis=0)
    share_in = turned.transpose(3, 1, 2, 0, 4).reshape(held, rows // depth, 2 * depth * part)
    down = grad_down.reshape(2, held, part, grad_down.shape[1])
    share_down = lax.psum_scatter(
        down, "expert", scatter_dimension=0, axis_index_groups=chip_groups()
    )
    return (share_in, share_down)


def expert_round(mid_rows, up_rows, gate, weight_in, weight_down):
    count = gate.shape[1]
    part = weight_down.shape[0] // count
    wide = jnp.broadcast_to(gate[:, :, None], gate.shape + (part,)).reshape(gate.shape[0], -1)
    gate_up = jnp.dot(mid_rows, weight_in, preferred_element_type=single)
    hidden_units = gate_up.shape[1] // 2
    gate_part = gate_up[:, :hidden_units]
    up_part = gate_up[:, hidden_units:]
    sigmoid = jax.nn.sigmoid(gate_part)
    activated = gate_part * sigmoid
    hidden = activated * up_part
    back = contract_last(up_rows, weight_down)
    scaled = (wide * hidden).astype(narrow)
    piece_out = jnp.dot(scaled, weight_down, preferred_element_type=narrow)
    piece_gates = jnp.sum((hidden * back).reshape(-1, count, part), axis=2)
    grad_hidden = wide * back
    grad_gate = grad_hidden * up_part * sigmoid * (1.0 + gate_part * (1.0 - sigmoid))
    grad_up = grad_hidden * activated
    grad_gate_up = jnp.concatenate([grad_gate, grad_up], axis=1).astype(narrow)
    piece_mid = contract_last(grad_gate_up, weight_in, narrow)
    return (piece_out, piece_mid, piece_gates, grad_gate_up, scaled)


def expert_rounds(mid_rows, up_rows, gate, weight_in, weight_down):
    total = mid_rows.shape[0]
    rounds = max(1, total // 2048)

    def one(sums, pieces):
        mid, up, weights = pieces
        piece_out, piece_mid, piece_gates, grad_gate_up, scaled = expert_round(
            mid, up, weights, weight_in, weight_down
        )
        grads = (contract_rows(mid, grad_gate_up), contract_rows(scaled, up))
        return (jax.tree.map(jnp.add, sums, grads), (piece_out, piece_mid, piece_gates))

    if rounds == 1:
        piece_out, piece_mid, piece_gates, grad_gate_up, scaled = expert_round(
            mid_rows, up_rows, gate, weight_in, weight_down
        )
        grads = (contract_rows(mid_rows, grad_gate_up, narrow), contract_rows(scaled, up_rows, narrow))
        return (piece_out, piece_mid, piece_gates) + grads
    start = (jnp.zeros(weight_in.shape, single), jnp.zeros(weight_down.shape, single))
    cut = jax.tree.map(lambda a: a.reshape(rounds, total // rounds, -1), (mid_rows, up_rows, gate))
    sums, made = lax.scan(one, start, cut)
    made = jax.tree.map(lambda a: a.reshape(total, -1), made)
    return made + (sums[0].astype(narrow), sums[1].astype(narrow))


MESH = pl.DeviceIdType.MESH
HBM = pl.BlockSpec(memory_space=pl.ANY)
DEPTH = 4
RING = 4


def ring_turn(number):
    high = lax.div(number, 2)
    return number + high * (1 - 2 * lax.rem(number, 2))


class Here:
    def __init__(self):
        number = lax.axis_index("expert")
        self.z = lax.axis_index("dp")
        self.core = lax.rem(number, 2)
        self.chip = lax.div(number, 2)
        self.q = ring_turn(self.chip)

    def chip_at(self, turn):
        return ring_turn(lax.rem(self.q + turn + RING, RING))

    def beside(self, turn):
        return (self.z, 2 * self.chip_at(turn) + self.core)

    def above(self, steps):
        return (lax.rem(self.z + steps + DEPTH, DEPTH), 2 * self.chip + self.core)

    def sibling(self):
        return (self.z, 2 * self.chip + 1 - self.core)

    def meet(self):
        barrier = pltpu.get_barrier_semaphore()
        others = [self.beside(1), self.beside(-1), self.sibling()]
        others += [self.above(steps) for steps in range(1, DEPTH)]
        for other in others:
            pl.semaphore_signal(barrier, inc=1, device_id=other, device_id_type=MESH)
        pl.semaphore_wait(barrier, len(others))


def remote(source, target, sent, arrived, device):
    return pltpu.make_async_remote_copy(
        src_ref=source,
        dst_ref=target,
        send_sem=sent,
        recv_sem=arrived,
        device_id=device,
        device_id_type=MESH,
    )


GATHER_SEMS = [
    pltpu.SemaphoreType.DMA((2, 2, DEPTH - 1)),
    pltpu.SemaphoreType.DMA((2, DEPTH, 2, 2)),
    pltpu.SemaphoreType.DMA((2, DEPTH)),
    pltpu.SemaphoreType.DMA((1,)),
]


class Gather:
    def __init__(self, here, source, whole, halves, shared, sems):
        self.here, self.source, self.whole, self.halves, self.shared = here, source, whole, halves, shared
        self.line, self.ring, self.pair, self.own = sems

    def block(self, z, turn):
        chip = self.here.chip_at(turn)
        return self.whole.at[z, chip, self.here.core] if self.shared else self.whole.at[z, chip]

    def keep(self):
        return pltpu.make_async_copy(self.source, self.block(self.here.z, 0), self.own.at[0])

    def along(self, step, way, first):
        z = self.here.z - step + 1 if way == 0 else self.here.z + step - 1
        block = self.block(z, 0)
        return remote(
            self.source if first else block,
            block,
            self.line.at[0, way, step - 1],
            self.line.at[1, way, step - 1],
            self.here.above(1 if way == 0 else -1),
        )

    def round(self, z, way, first=False):
        turn = 1 if way == 0 else -1
        block = self.block(z, 0)
        return remote(
            self.source if first else block,
            block,
            self.ring.at[0, z, way, 0],
            self.ring.at[1, z, way, 0],
            self.here.beside(turn),
        )

    def heard(self, z, way):
        block = self.block(z, -1 if way == 0 else 1)
        return remote(
            block, block, self.ring.at[0, z, way, 0], self.ring.at[1, z, way, 0], self.here.beside(1)
        )

    def onward(self, z, way, mine):
        if self.halves[way] is None:
            return None
        turn = (-1 if mine else -2) if way == 0 else (1 if mine else 2)
        block = self.block(z, turn).at[pl.ds(*self.halves[way])]
        return remote(
            block,
            block,
            self.ring.at[0, z, way, 1],
            self.ring.at[1, z, way, 1],
            self.here.beside(1 if way == 0 else -1),
        )

    def swap(self, z, mine):
        core = self.here.core if mine else 1 - self.here.core
        part = self.whole.at[z, :, core]
        return remote(part, part, self.pair.at[0, z], self.pair.at[1, z], self.here.sibling())


def start(copy):
    if copy is not None:
        copy.start()


def gather_third(item, z):
    for way in (0, 1):
        copy = item.onward(z, way, False)
        if copy is not None:
            copy.wait_recv()


class Rounds:
    def __init__(self, here, items, ring=True):
        self.here, self.items = here, items
        for item in items:
            item.keep().start()
            for way in (0, 1):
                self.depart(0, way, item)
            if ring:
                for way in (0, 1):
                    item.round(here.z, way, True).start()

    def depart(self, step, way, item):
        here = self.here
        ahead = here.z + 1 < DEPTH if way == 0 else here.z >= 1
        pl.when(ahead)(lambda: item.along(step + 1, way, step == 0).start())

    def places(self, step, body):
        here = self.here
        if step == 0:
            body(here.z, 0)
            return
        pl.when(here.z >= step)(lambda: body(here.z - step, 0))
        pl.when(here.z + step < DEPTH)(lambda: body(here.z + step, 1))

    def line(self, step, ring=True):
        def body(z, way):
            for item in self.items:
                block = item.block(z, 0)
                remote(
                    block, block, item.line.at[0, way, step - 1], item.line.at[1, way, step - 1], self.here.above(1)
                ).wait_recv()
                if step + 1 < DEPTH:
                    self.depart(step, way, item)
                if ring:
                    for side in (0, 1):
                        item.round(z, side).start()

        self.places(step, body)

    def ring(self, step):
        def body(z, way):
            for item in self.items:
                for side in (0, 1):
                    item.round(z, side, step == 0).start()

        self.places(step, body)

    def second(self, step):
        def body(z, way):
            for item in self.items:
                for side in (0, 1):
                    item.heard(z, side).wait_recv()
                    start(item.onward(z, side, True))

        self.places(step, body)

    def service(self, step, between=None):
        if step + 1 < DEPTH:
            self.line(step + 1)
        if between is not None:
            between()
        if step == 0:
            self.kept()
        self.second(step)

    def kept(self):
        for item in self.items:
            item.keep().wait()

    def third(self, step):
        def body(z, way):
            for item in self.items:
                gather_third(item, z)
                if item.shared:
                    item.swap(z, True).start()

        self.places(step, body)

    def finish(self):
        def settle(z, way):
            for item in self.items:
                for side in (0, 1):
                    item.round(z, side).wait_send()
                    copy = item.onward(z, side, True)
                    if copy is not None:
                        copy.wait_send()
                if item.shared:
                    item.swap(z, True).wait_send()
                    item.swap(z, False).wait_recv()

        for step in range(DEPTH):
            self.places(step, settle)
        here = self.here
        for item in self.items:
            for step in range(DEPTH - 1):
                for way in (0, 1):

                    def sent(z, side, step=step, way=way, item=item):
                        if step and side != way:
                            return
                        ahead = here.z + 1 < DEPTH if way == 0 else here.z >= 1
                        pl.when(ahead)(lambda: item.along(step + 1, way, step == 0).wait_send())

                    self.places(step, sent)


class Recut:
    def __init__(self, here, source_in, source_out, whole_in, whole_out, sems):
        self.here, self.source_in, self.source_out = here, source_in, source_out
        self.whole_in, self.whole_out = whole_in, whole_out
        self.cut, self.pair, self.down, self.own = sems
        self.held, self.rows, columns = source_in.shape
        self.hidden = columns // 2
        self.part = self.hidden // DEPTH

    def pieces(self, steps, arriving):
        here, copies = self.here, []
        mine = lax.rem(here.z + DEPTH - steps, DEPTH) if arriving else here.z
        away = lax.rem(here.z + steps, DEPTH)
        for side in range(2):
            for expert in range(self.held):
                columns = side * self.held * 2 * self.part + (here.core * self.held + expert) * self.part
                target = self.whole_in.at[
                    pl.ds(pl.multiple_of(mine * self.rows, 16), self.rows),
                    pl.ds(pl.multiple_of(columns, 128), self.part),
                ]
                source = self.source_in.at[
                    expert, :, pl.ds(pl.multiple_of(side * self.hidden + away * self.part, 128), self.part)
                ]
                spot = (steps, side * self.held + expert)
                if steps == 0:
                    copies.append(pltpu.make_async_copy(source, target, self.own.at[spot[1]]))
                else:
                    copies.append(
                        remote(
                            target if arriving else source,
                            target,
                            self.cut.at[(0,) + spot],
                            self.cut.at[(1,) + spot],
                            here.above(steps),
                        )
                    )
        return copies

    def across(self, steps, mine):
        here, copies = self.here, []
        core = here.core if mine else 1 - here.core
        row = lax.rem(here.z + DEPTH - steps, DEPTH)
        width = self.held * self.part
        for side in range(2):
            spot = self.whole_in.at[
                pl.ds(pl.multiple_of(row * self.rows, 16), self.rows),
                pl.ds(pl.multiple_of(side * 2 * width + core * width, 128), width),
            ]
            copies.append(
                remote(spot, spot, self.pair.at[0, steps, side], self.pair.at[1, steps, side], here.sibling())
            )
        return copies

    def lower(self, mine):
        here = self.here
        core = here.core if mine else 1 - here.core
        spot = self.whole_out.at[pl.ds(core * self.held, self.held)]
        return remote(
            self.source_out if mine else spot, spot, self.down.at[0], self.down.at[1], here.sibling()
        )

    def lower_own(self):
        return pltpu.make_async_copy(
            self.source_out, self.whole_out.at[pl.ds(self.here.core * self.held, self.held)], self.own.at[4]
        )

    def begin(self):
        for copy in self.pieces(0, False):
            copy.start()
        self.lower_own().start()
        self.lower(True).start()
        for copies in zip(*[self.pieces(steps, False) for steps in (2, 3, 1)]):
            for copy in copies:
                copy.start()

    def relay(self):
        for steps in range(DEPTH):
            for copy in self.pieces(steps, True):
                copy.wait() if steps == 0 else copy.wait_recv()
            for copy in self.across(steps, True):
                copy.start()

    def end(self):
        self.lower_own().wait()
        self.lower(True).wait_send()
        self.lower(False).wait_recv()
        for steps in range(DEPTH):
            if steps:
                for copy in self.pieces(steps, False):
                    copy.wait_send()
            for copy in self.across(steps, True):
                copy.wait_send()
            for copy in self.across(steps, False):
                copy.wait_recv()


RECUT_SEMS = [
    pltpu.SemaphoreType.DMA((2, DEPTH, 4)),
    pltpu.SemaphoreType.DMA((2, DEPTH, 2)),
    pltpu.SemaphoreType.DMA((2,)),
    pltpu.SemaphoreType.DMA((5,)),
]


def halves_of(rows, split=True):
    return ((0, rows // 2), (rows // 2, rows - rows // 2)) if split else ((0, rows), None)


PANEL = 512


def attention_forward(
    tokens, cosine, sine, allowed, wq, wo, gains, normed, raw, queries, keys, values, probs, attended, middle, routed,
    panel, panel_sems, between
):
    block, width = tokens.shape
    heads = width // HEAD
    wide = wq.shape[-1]
    high = 16
    per = width // PANEL

    def fetch(source, number):
        slot = lax.rem(number, 2)
        spot = pl.ds(pl.multiple_of(number * PANEL, PANEL), PANEL)
        return pltpu.make_async_copy(source.at[:, :, :, :, spot], panel.at[slot], panel_sems.at[slot])

    def slabs(body):
        def one(number, carry):
            body(pl.ds(pl.multiple_of(number * high, high), high))
            return carry

        lax.fori_loop(0, block // high, one, 0)

    def first(at):
        values = tokens[at].astype(single)
        factor = lax.rsqrt(jnp.mean(values * values, axis=-1, keepdims=True) + epsilon)
        normed[at] = (values * factor * gains[0:1]).astype(narrow)

    fetch(wq, 0).start()
    slabs(first)

    def through(source, left, total, finish):
        def one(number, carry):
            fetch(source, number).wait()
            pl.when(number + 1 < total)(lambda: fetch(source, number + 1).start())
            weights = panel[lax.rem(number, 2)].reshape(width, PANEL)
            finish(number, jnp.dot(left[...], weights, preferred_element_type=single))
            return carry

        lax.fori_loop(0, total, one, 0)

    def keep(number, made):
        side = lax.div(number, per)
        spot = pl.ds(pl.multiple_of(lax.rem(number, per) * PANEL, PANEL), PANEL)

        @pl.when(side < 2)
        def _():
            raw[side, :, spot] = made

        @pl.when(side == 2)
        def _():
            values[:, spot] = made.astype(narrow)

    through(wq, normed, wide // PANEL, keep)
    fetch(wo, 0).start()
    between(0)

    factors = [
        lax.rsqrt(jnp.mean(raw[side] * raw[side], axis=-1, keepdims=True) + epsilon) for side in range(2)
    ]
    turn_cos, turn_sin = cosine[...], sine[...]
    may = allowed[...] > 0.5
    group = 4

    def some_heads(number, carry):
        for inner in range(group):
            head = number * group + inner
            spot = pl.ds(pl.multiple_of(head * HEAD, HEAD), HEAD)
            turned = []
            for side, target in ((0, queries), (1, keys)):
                field = raw[side, :, spot] * factors[side] * gains[side + 1 : side + 2, spot]
                field = field * turn_cos + pltpu.roll(field, HEAD // 2, 1) * turn_sin
                target[:, spot] = field.astype(narrow)
                turned.append(field.astype(narrow))
            scores = jnp.where(may, contract_last(turned[0], turned[1]) * HEAD ** (-0.5), masked_score)
            highest = jnp.max(scores, axis=-1, keepdims=True)
            unnormed = jnp.exp(scores - highest)
            shares = unnormed / jnp.sum(unnormed, axis=-1, keepdims=True)
            probs[head] = shares
            mixed = jnp.dot(shares.astype(narrow), values[:, spot], preferred_element_type=single)
            attended[:, spot] = mixed.astype(narrow)
        return carry

    lax.fori_loop(0, heads // group, some_heads, 0)
    between(1)

    def add(number, made):
        spot = pl.ds(pl.multiple_of(number * PANEL, PANEL), PANEL)
        middle[:, spot] = tokens[:, spot].astype(single) + made

    through(wo, attended, per, add)

    def last(at):
        values = middle[at]
        factor = lax.rsqrt(jnp.mean(values * values, axis=-1, keepdims=True) + epsilon)
        routed[at] = (values * factor * gains[3:4]).astype(narrow)

    slabs(last)
    between(2)


def first_gather_kernel(
    wq, wo, up, small, ein, eout, tokens, cosine, sine, allowed,
    wq_all, wo_all, up_all, small_all, win, wout, *rest
):
    made, (tokens_v, small_here, small_sem, panel, panel_sems, put_sems), sems = rest[:10], rest[20:26], rest[26:]
    results = rest[10:20]
    gains, normed, raw, queries, keys, values, probs, attended, middle, routed = results
    here = Here()
    here.meet()
    fetch_tokens = pltpu.make_async_copy(tokens, tokens_v, small_sem.at[1])
    fetch_tokens.start()
    puts = [
        pltpu.make_async_copy(source, target, put_sems.at[number])
        for number, (source, target) in enumerate(zip(results, made))
    ]
    items = [
        Gather(here, source, whole, halves, shared, sems[4 * number : 4 * number + 4])
        for number, (source, whole, halves, shared) in enumerate(
            (
                (small, small_all, halves_of(small.shape[0], False), True),
                (wq, wq_all, halves_of(wq.shape[0]), True),
                (wo, wo_all, halves_of(wo.shape[0]), True),
                (up, up_all, halves_of(up.shape[0]), False),
            )
        )
    ]
    recut = Recut(here, ein, eout, win, wout, sems[16:20])
    weights = Rounds(here, items[:3])
    rows = Rounds(here, items[3:], ring=False)
    weights.service(0, lambda: rows.line(1, ring=False))
    weights.service(1, lambda: rows.line(2, ring=False))
    recut.begin()
    weights.third(0)
    weights.service(2, lambda: rows.line(3, ring=False))
    weights.third(1)
    weights.service(3)
    rows.kept()
    for step in range(DEPTH):
        rows.ring(step)
    weights.third(2)
    weights.third(3)
    weights.finish()
    fetch = pltpu.make_async_copy(small_all, small_here, small_sem.at[0])
    fetch.start()
    fetch.wait()
    fetch_tokens.wait()
    share = wq.shape[0]
    lanes = small.shape[1]
    lane = lax.broadcasted_iota(jnp.int32, (8, lanes), 1)
    skip = small.shape[0] - 8
    for z in range(DEPTH):
        for chip in range(RING):
            pair = [small_here[z, chip, core, skip : skip + 8] for core in (0, 1)]
            both = jnp.where(lane < share, pair[0], pltpu.roll(pair[1], share, 1))
            begin = (z * RING + chip) * 2 * share
            gains[:, begin : begin + 2 * share] = both

    def between(part):
        if part == 0:
            rows.second(0)
        elif part == 1:
            for step in range(1, DEPTH):
                rows.second(step)
        else:
            for copy in puts:
                copy.start()
            recut.relay()

    attention_forward(
        tokens_v, cosine, sine, allowed, wq_all, wo_all, gains, normed, raw, queries, keys, values, probs, attended,
        middle, routed, panel, panel_sems, between
    )
    for step in range(DEPTH):
        rows.third(step)
    rows.finish()
    recut.end()
    for copy in puts:
        copy.wait()


def first_gather(wq, wo, up, small, ein, eout, tokens, cosine, sine, allowed):
    def whole(array, shared):
        lead = (DEPTH, RING, 2) if shared else (DEPTH, RING)
        return jax.ShapeDtypeStruct(lead + array.shape, array.dtype)

    held, rows, columns = ein.shape
    block, width = tokens.shape
    heads = width // HEAD
    vmem = pl.BlockSpec(memory_space=pltpu.VMEM)
    like = ((block, width), narrow)
    made = (
        ((8, width), single),
        like,
        ((2, block, width), single),
        like,
        like,
        like,
        ((heads, block, block), single),
        like,
        ((block, width), single),
        like,
    )
    return pl.pallas_call(
        first_gather_kernel,
        out_shape=(
            whole(wq, True),
            whole(wo, True),
            whole(up, False),
            whole(small, True),
            jax.ShapeDtypeStruct((DEPTH * rows, columns), ein.dtype),
            jax.ShapeDtypeStruct((2 * held,) + eout.shape[1:], eout.dtype),
            *(jax.ShapeDtypeStruct(*one) for one in made),
        ),
        in_specs=[HBM] * 7 + [vmem] * 3,
        out_specs=(HBM,) * 16,
        scratch_shapes=[pltpu.VMEM(*one) for one in made]
        + [
            pltpu.VMEM((block, width), tokens.dtype),
            pltpu.VMEM((DEPTH, RING, 2) + small.shape, single),
            pltpu.SemaphoreType.DMA((2,)),
            pltpu.VMEM((2, DEPTH, RING, 2, wq.shape[0], PANEL), narrow),
            pltpu.SemaphoreType.DMA((2,)),
            pltpu.SemaphoreType.DMA((len(made),)),
        ]
        + GATHER_SEMS * 4
        + RECUT_SEMS,
        compiler_params=pltpu.CompilerParams(
            collective_id=1, has_side_effects=True, vmem_limit_bytes=62 * 2**20
        ),
        name="bring",
    )(wq, wo, up, small, ein, eout, tokens, cosine, sine, allowed)

TILE = 256


def add_up(target, terms, rows, columns):
    high = 16 if rows % 16 == 0 else 8
    wide = min(columns, 1024)
    across = columns // wide

    def piece(number, carry):
        row = pl.multiple_of(lax.div(number, across) * high, high)
        column = pl.multiple_of(lax.rem(number, across) * wide, 128)
        spot = (pl.ds(row, high), pl.ds(column, wide))
        total = terms[0][spot].astype(single)
        for term in terms[1:]:
            total = total + term[spot].astype(single)
        target[spot] = total.astype(target.dtype)
        return carry

    lax.fori_loop(0, (rows // high) * across, piece, 0)


SUM_SEMS = [
    pltpu.SemaphoreType.DMA((2, DEPTH, 2)),
    pltpu.SemaphoreType.DMA((2, DEPTH, 2)),
    pltpu.SemaphoreType.DMA((2, 2, DEPTH)),
    pltpu.SemaphoreType.DMA((DEPTH, RING, 2)),
]


def sum_scratch(rows, columns, kind, halves, paired=False, made=False):
    high = max(size for _, size in filter(None, halves))
    kept = RING if paired or made else RING - 1
    scratch = [
        pltpu.VMEM((DEPTH, kept, rows, columns), kind),
        pltpu.VMEM((DEPTH, 2, high, columns), kind),
        pltpu.VMEM((DEPTH, 2, rows, columns), kind),
        pltpu.VMEM((DEPTH + 1, rows, columns), kind),
    ] + SUM_SEMS
    if paired:
        scratch += [pltpu.VMEM((DEPTH, RING, rows, columns), kind), pltpu.SemaphoreType.DMA((2, DEPTH, 2))]
    return scratch


class Sum:
    def __init__(self, here, sources, target, halves, paired, scratch):
        self.here, self.sources, self.halves, self.paired = here, sources, halves, paired
        self.target = target if isinstance(target, list) else [(target, 0, target.shape[0])]
        self.extra = []
        self.mine, self.half, self.full, self.column = scratch[:4]
        self.half_sem, self.full_sem, self.line_sem, self.load_sem = scratch[4:8]
        if paired:
            self.other, self.pair_sem = scratch[8:10]
        self.rows, self.columns = self.mine.shape[2:]

    def kept(self, z, turn):
        if self.sources is None:
            return self.mine.at[z, self.here.chip_at(turn)]
        return self.mine.at[z, turn if self.paired else {0: 0, 1: 1, 3: 2}[turn]]

    def raw(self, part, z, turn):
        chip = self.here.chip_at(turn)
        return part.at[z, chip, self.here.core] if self.paired else part.at[z, chip]

    def spots(self):
        at, spots = 0, []
        for part in self.sources or []:
            spots.append((part, pl.ds(at, part.shape[-1])))
            at += part.shape[-1]
        return spots

    def loads(self, z, turn):
        return [
            pltpu.make_async_copy(
                self.raw(part, z, turn), self.kept(z, turn).at[:, spot], self.load_sem.at[z, turn, number]
            )
            for number, (part, spot) in enumerate(self.spots())
        ]

    def swaps(self, z, mine):
        return [
            remote(
                part.at[z, :, 1 - self.here.core] if mine else self.other.at[z, :, :, spot],
                self.other.at[z, :, :, spot],
                self.pair_sem.at[0, z, number],
                self.pair_sem.at[1, z, number],
                self.here.sibling(),
            )
            for number, (part, spot) in enumerate(self.spots())
        ]

    def toss(self, z, way):
        if self.halves[way] is None:
            return None
        rows = pl.ds(*self.halves[way])
        loaded = self.sources is not None and not self.paired
        source = (self.raw(self.sources[0], z, 2) if loaded else self.kept(z, 2)).at[rows]
        return remote(
            source,
            self.half.at[z, way, pl.ds(0, self.halves[way][1])],
            self.half_sem.at[0, z, way],
            self.half_sem.at[1, z, way],
            self.here.beside(1 if way == 0 else -1),
        )

    def pass_on(self, z, way):
        return remote(
            self.kept(z, 1 if way == 0 else 3),
            self.full.at[z, way],
            self.full_sem.at[0, z, way],
            self.full_sem.at[1, z, way],
            self.here.beside(1 if way == 0 else -1),
        )

    def climb(self, z, way, up, slot=None):
        if slot is None:
            down_to_owner = way * (z == self.here.z - 1).astype(jnp.int32)
            slot = z + down_to_owner * (DEPTH - z)
        return remote(
            self.kept(z, 0),
            self.column.at[slot],
            self.line_sem.at[0, way, z],
            self.line_sem.at[1, way, z],
            self.here.above(2 * up - 1),
        )

    def begin(self, z):
        if self.paired:
            for copy in self.swaps(z, True):
                copy.start()
        for turn in (2, 1, 3, 0):
            if turn != 2 or self.paired:
                for copy in self.loads(z, turn):
                    copy.start()
        if not self.paired:
            for way in (0, 1):
                start(self.toss(z, way))

    def merge(self, z):
        if not self.paired:
            return
        for copy in self.swaps(z, False):
            copy.wait_recv()
        for turn in (2, 1, 3, 0):
            for copy in self.loads(z, turn):
                copy.wait()
            kept = self.kept(z, turn)
            add_up(kept, [kept, self.other.at[z, self.here.chip_at(turn)]], self.rows, self.columns)
            if turn == 2:
                for way in (0, 1):
                    start(self.toss(z, way))

    def second(self, z):
        for way, turn in ((0, 1), (1, 3)):
            if not self.paired:
                for copy in self.loads(z, turn):
                    copy.wait()
            copy = self.toss(z, way)
            if copy is not None:
                copy.wait_recv()
                begin, size = self.halves[way]
                rows = self.kept(z, turn).at[pl.ds(begin, size)]
                add_up(rows, [rows, self.half.at[z, way, pl.ds(0, size)]], size, self.columns)
        for way in (0, 1):
            self.pass_on(z, way).start()

    def third(self, z, last):
        here = self.here
        if not self.paired:
            for copy in self.loads(z, 0):
                copy.wait()
        for way in (0, 1):
            self.pass_on(z, way).wait_recv()
        kept = self.kept(z, 0)
        terms = [kept, self.full.at[z, 0], self.full.at[z, 1]]
        if last:
            self.arrive(z, terms)
            return
        up = (z > here.z).astype(jnp.int32)
        way = 1 - up
        follows = up * here.z + way * (DEPTH - 1 - here.z)

        @pl.when(follows > 0)
        def _():
            self.climb(z, way, up, z).wait_recv()
            add_up(kept, terms + [self.column.at[z]], self.rows, self.columns)

        @pl.when(follows == 0)
        def _():
            add_up(kept, terms, self.rows, self.columns)

        self.climb(z, way, up).start()

    def own_part(self, z):
        for way in (0, 1):
            self.pass_on(z, way).wait_recv()
        [(target, _, rows)] = self.target
        add_up(target, [self.kept(z, 0), self.full.at[z, 0], self.full.at[z, 1]], rows, self.columns)

    def own_rest(self, z):
        self.arrive(z, [self.target[0][0]])

    def arrive(self, z, terms):
        here = self.here
        below, above = self.column.at[z], self.column.at[DEPTH]

        def total(more):
            for target, row, rows in self.target:
                part = [term.at[pl.ds(row, rows)] for term in terms + more + self.extra]
                add_up(target, part, rows, self.columns)

        @pl.when(here.z == 0)
        def _():
            self.climb(z, 1, 0, DEPTH).wait_recv()
            total([above])

        @pl.when(here.z == DEPTH - 1)
        def _():
            self.climb(z, 0, 0, z).wait_recv()
            total([below])

        @pl.when((here.z > 0) & (here.z < DEPTH - 1))
        def _():
            self.climb(z, 0, 0, z).wait_recv()
            self.climb(z, 1, 0, DEPTH).wait_recv()
            total([below, above])

    def end(self, z, last):
        if self.paired:
            for copy in self.swaps(z, True):
                copy.wait_send()
        for way in (0, 1):
            copy = self.toss(z, way)
            if copy is not None:
                copy.wait_send()
            self.pass_on(z, way).wait_send()
        if not last:
            up = (z > self.here.z).astype(jnp.int32)
            self.climb(z, 1 - up, up).wait_send()


def far_first(here, number):
    high = lax.div(here.z, 2)
    inner = lax.rem(lax.div(here.z + 1, 2), 2)
    low = (DEPTH - 1 - number) + inner * (0, -2, 1, 1)[number]
    return low + high * (DEPTH - 1 - 2 * low)


class Share:
    def __init__(self, here, source, target, side, sems):
        self.here, self.source, self.target, self.side, self.sems = here, source, target, side, sems
        self.held, self.rows, columns = target.shape
        self.part = columns // (2 * DEPTH)

    def pieces(self, steps, arriving):
        here = self.here
        origin = lax.rem(here.z + DEPTH - steps, DEPTH) if arriving else here.z
        away = lax.rem(here.z + steps, DEPTH)
        copies = []
        for expert in range(self.held):
            column = (self.side * DEPTH + origin) * self.part
            target = self.target.at[expert, :, pl.ds(pl.multiple_of(column, 128), self.part)]
            source = self.source.at[
                pl.ds(pl.multiple_of(away * self.rows, 16), self.rows),
                pl.ds((self.side * self.held + expert) * self.part, self.part),
            ]
            if steps == 0:
                copies.append(pltpu.make_async_copy(source, target, self.sems.at[0, 0, expert]))
            else:
                sems = (self.sems.at[0, steps, expert], self.sems.at[1, steps, expert])
                copies.append(remote(target if arriving else source, target, *sems, here.above(steps)))
        return copies

    def begin(self):
        for copies in zip(*[self.pieces(steps, False) for steps in (2, 3, 1, 0)]):
            for copy in copies:
                copy.start()

    def end(self):
        for steps in range(DEPTH):
            for copy in self.pieces(steps, False):
                copy.wait() if steps == 0 else copy.wait_send()
            if steps:
                for copy in self.pieces(steps, True):
                    copy.wait_recv()


STRIP = 128


def last_sum_kernel(
    normed,
    attended,
    gin_sum,
    weight,
    weight_out,
    tokens,
    routed,
    upstream,
    middle,
    raw,
    queries,
    keys,
    values,
    probs,
    cosine,
    sine,
    gains,
    q_sum,
    o_sum,
    gain_sums,
    grad_tokens,
    share_in,
    *scratch,
):
    here = Here()
    here.meet()
    block, width = tokens.shape
    share = q_sum.shape[0]
    wide = q_sum.shape[1]
    sides = wide // width
    heads = width // HEAD
    (
        left, left_out, right, panel, x, routed_v, upstream_v, middle_v, raw_v, queries_v, keys_v, values_v, probs_v,
        grad_middle, grad_heads, turned, piece, few_sum, few_other, sems, panel_sems, pair_sems, share_sems
    ) = scratch[:23]
    big = Sum(
        here,
        None,
        [(q_sum.at[:, pl.ds(side * width, width)], side * share, share) for side in range(sides)],
        halves_of(sides * share),
        False,
        scratch[23:31],
    )
    outer = Sum(here, None, o_sum, halves_of(share), False, scratch[31:39])
    few = Sum(here, None, few_sum, halves_of(few_sum.shape[0], False), False, scratch[39:47])
    order = [far_first(here, number) for number in range(DEPTH)]
    loads = [
        pltpu.make_async_copy(source, target, sems.at[number])
        for number, (source, target) in enumerate(
            (
                (middle, middle_v),
                (routed, routed_v),
                (upstream, upstream_v),
                (attended, left_out.at[0]),
                (values, values_v),
                (probs, probs_v),
                (queries, queries_v),
                (keys, keys_v),
                (raw, raw_v),
                (normed, left.at[0]),
                (tokens, x),
            )
        )
    ]

    def fetch(source, number, columns):
        slot = lax.rem(number, 2)
        rows = pl.ds(pl.multiple_of(number * STRIP, STRIP), STRIP)
        return pltpu.make_async_copy(source.at[rows], panel.at[slot, :, pl.ds(0, columns)], panel_sems.at[slot])

    for copy in loads:
        copy.start()
    fetch(weight_out, 0, width).start()
    shares_in = [Share(here, gin_sum, share_in, side, share_sems.at[side]) for side in range(2)]
    for share_side in shares_in:
        share_side.begin()

    def swap(number, source, target):
        base = 16 + 2 * number
        return remote(source, target, sems.at[base], sems.at[base + 1], here.sibling())

    side_out = pl.ds(wide, width)
    side_qkv = pl.ds(0, wide)
    swaps = [
        swap(0, left_out.at[0], left_out.at[1]),
        swap(1, right.at[0, :, side_out], right.at[1, :, side_out]),
        swap(2, left.at[0], left.at[1]),
        swap(3, right.at[0, :, side_qkv], right.at[1, :, side_qkv]),
    ]
    high = 16
    panels = width // STRIP

    def slabs(body):
        def one(number, carry):
            body(pl.ds(pl.multiple_of(number * high, high), high))
            return carry

        lax.fori_loop(0, block // high, one, 0)

    def norm(values):
        factor = lax.rsqrt(jnp.mean(values * values, axis=-1, keepdims=True) + epsilon)
        return values * factor, factor

    def norm_grad(up, values, row):
        normal, factor = norm(values)
        weighted = up * gains[row : row + 1]
        inner = jnp.mean(weighted * normal, axis=-1, keepdims=True)
        piece[row : row + 1] += jnp.sum(up * normal, axis=0, keepdims=True)
        return factor * (weighted - normal * inner)

    def first(at):
        grad = upstream_v[at].astype(single) + norm_grad(routed_v[at], middle_v[at], 3)
        grad_middle[at] = grad
        right[0, at, side_out] = grad.astype(narrow)

    piece[...] = jnp.zeros_like(piece)
    for number in range(4):
        loads[number].wait()
    swaps[0].start()
    slabs(first)
    swaps[1].start()

    def through(source, columns, left_rows, finish, begin=0, end=panels):
        def one(number, carry):
            fetch(source, number, columns).wait()
            pl.when(number + 1 < panels)(lambda: fetch(source, number + 1, columns).start())
            rows = panel[lax.rem(number, 2), :, 0:columns]
            finish(pl.ds(pl.multiple_of(number * STRIP, STRIP), STRIP), contract_last(left_rows, rows))
            return carry

        lax.fori_loop(begin, end, one, 0)

    def keep_heads(spot, made):
        grad_heads[:, spot] = made.astype(narrow)

    step = 512
    each = width // step
    rows = RING * 2 * share

    def make(z, item, source, first_chunk, last_chunk):
        at = pl.ds(pl.multiple_of(z * rows, rows), rows)

        def one(number, carry):
            spot = pl.ds(pl.multiple_of(number * step, step), step)
            left_rows = source[:, :, at].reshape(2 * block, rows)
            made = contract_rows(left_rows, right[:, :, spot].reshape(2 * block, step))
            made = made.reshape(RING, 2, share, step)
            mine = jnp.where(here.core == 0, made[:, 0], made[:, 1]).astype(narrow)
            row = pl.multiple_of(lax.div(number - first_chunk, each) * share, share)
            column = pl.multiple_of(lax.rem(number, each) * step, step)
            for chip in range(RING):
                item.mine[z, chip, pl.ds(row, share), pl.ds(column, step)] = mine[chip]
            return carry

        lax.fori_loop(first_chunk, last_chunk, one, 0)

    swaps[0].wait_recv()
    swaps[1].wait_recv()
    for z in order:
        make(z, outer, left_out, sides * each, (sides + 1) * each)
        for way in (0, 1):
            start(outer.toss(z, way))
    through(weight_out, width, right[0, :, side_out], keep_heads)
    fetch(weight, 0, wide).start()
    for number in range(4, len(loads)):
        loads[number].wait()
    swaps[2].start()
    turn_cos, turn_sin = cosine[...], sine[...]
    group = 4

    def some_heads(number, carry):
        for inner in range(group):
            head = number * group + inner
            spot = pl.ds(pl.multiple_of(head * HEAD, HEAD), HEAD)
            grad = grad_heads[:, spot]
            shares = probs_v[head]
            grad_shares = contract_last(grad, values_v[:, spot])
            along = jnp.sum(grad_shares * shares, axis=-1, keepdims=True)
            scores = (shares * (grad_shares - along)).astype(narrow)
            made = (
                jnp.dot(scores, keys_v[:, spot], preferred_element_type=single),
                contract_rows(scores, queries_v[:, spot]),
            )
            for side, field in enumerate(made):
                field = field * HEAD ** (-0.5)
                turned[side, :, spot] = field * turn_cos - pltpu.roll(field, HEAD // 2, 1) * turn_sin
            spot_v = pl.ds(pl.multiple_of(2 * width + head * HEAD, HEAD), HEAD)
            right[0, :, spot_v] = contract_rows(shares.astype(narrow), grad).astype(narrow)
        return carry

    lax.fori_loop(0, heads // group, some_heads, 0)

    def second(at):
        for side in range(2):
            grad = norm_grad(turned[side, at], raw_v[side, at], side + 1)
            right[0, at, side * width : (side + 1) * width] = grad.astype(narrow)

    for z in order[:2]:
        outer.second(z)
    slabs(second)
    swaps[3].start()
    for z in order[2:]:
        outer.second(z)
    swaps[2].wait_recv()
    swaps[3].wait_recv()

    def keep_back(spot, made):
        routed_v[:, spot] = made

    def third(at):
        grad_tokens[at] = grad_middle[at] + norm_grad(routed_v[at], x[at].astype(single), 0)

    for number, z in enumerate(order):
        make(z, big, left, 0, sides * each)
        for way in (0, 1):
            start(big.toss(z, way))
        if number:
            big.second(order[number - 1])
        outer.third(z, number == DEPTH - 1)
        if number > 1:
            big.third(order[number - 2], False)
        cut = panels // DEPTH
        through(weight, wide, right[0, :, side_qkv], keep_back, number * cut, (number + 1) * cut)
        if number == DEPTH - 1:
            slabs(third)
            for plane in range(DEPTH):
                for chip in range(RING):
                    begin = (plane * RING + chip) * 2 * share
                    few.mine[plane, chip] = piece[:, begin : begin + 2 * share]
            for place in order:
                start(few.toss(place, 0))
    big.second(order[-1])
    for z in order:
        few.second(z)
    big.third(order[-2], False)
    for z in order[:-1]:
        few.third(z, False)
    big.third(order[-1], True)
    few.third(order[-1], True)
    pair = remote(few_sum, few_other, pair_sems.at[0], pair_sems.at[1], here.sibling())
    pair.start()
    pair.wait_recv()
    gain_sums[...] = few_sum[...] + few_other[...]
    pair.wait_send()
    for number, z in enumerate(order):
        for item in (big, outer, few):
            item.end(z, number == DEPTH - 1)
    for copy in swaps:
        copy.wait_send()
    for share_side in shares_in:
        share_side.end()


def last_sum(
    normed, attended, gin_sum, weight, weight_out, tokens, routed, upstream, middle, raw, queries, keys, values, probs,
    cosine, sine, gains, share, held
):
    block, width = normed.shape
    wide = weight.shape[1]
    sides = wide // width
    vmem = pl.BlockSpec(memory_space=pltpu.VMEM)
    few = (gains.shape[0], 2 * share)
    like = pltpu.VMEM((block, width), narrow)
    like_single = pltpu.VMEM((block, width), single)
    return pl.pallas_call(
        last_sum_kernel,
        out_shape=(
            jax.ShapeDtypeStruct((share, wide), single),
            jax.ShapeDtypeStruct((share, width), single),
            jax.ShapeDtypeStruct(few, single),
            jax.ShapeDtypeStruct((block, width), single),
            jax.ShapeDtypeStruct((held, gin_sum.shape[0] // DEPTH, DEPTH * gin_sum.shape[1] // held), narrow),
        ),
        in_specs=[HBM] * 14 + [vmem] * 3,
        out_specs=(vmem, vmem, vmem, vmem, HBM),
        scratch_shapes=[
            pltpu.VMEM((2, block, width), narrow),
            pltpu.VMEM((2, block, width), narrow),
            pltpu.VMEM((2, block, wide + width), narrow),
            pltpu.VMEM((2, STRIP, wide), narrow),
            like,
            like_single,
            like,
            like_single,
            pltpu.VMEM(raw.shape, single),
            like,
            like,
            like,
            pltpu.VMEM(probs.shape, single),
            like_single,
            like,
            pltpu.VMEM((2, block, width), single),
            pltpu.VMEM(gains.shape, single),
            pltpu.VMEM(few, single),
            pltpu.VMEM(few, single),
            pltpu.SemaphoreType.DMA((24,)),
            pltpu.SemaphoreType.DMA((2,)),
            pltpu.SemaphoreType.DMA((2,)),
            pltpu.SemaphoreType.DMA((2, 2, DEPTH, held)),
        ]
        + sum_scratch(sides * share, width, narrow, halves_of(sides * share), made=True)
        + sum_scratch(share, width, narrow, halves_of(share), made=True)
        + sum_scratch(few[0], few[1], single, halves_of(few[0], False), made=True),
        compiler_params=pltpu.CompilerParams(
            collective_id=4, has_side_effects=True, vmem_limit_bytes=62 * 2**20
        ),
        name="deliver",
    )(
        normed, attended, gin_sum, weight, weight_out, tokens, routed, upstream, middle, raw, queries, keys, values, probs,
        cosine, sine, gains
    )

def near_first(here, number):
    high = lax.div(here.z, 2)
    inner = lax.rem(lax.div(here.z + 1, 2), 2)
    low = number + inner * (1, -1, 0, 0)[number]
    return low + high * (DEPTH - 1 - 2 * low)


class Tiles:
    def __init__(self, here, stage, count, sems, parts, targets):
        self.here, self.stage, self.count = here, stage, count
        self.kept, self.sent, self.came = sems
        self.parts, self.targets = parts, targets

    def copies(self, number, keep=True, give=True):
        slot = lax.rem(number, 2)
        own, other = self.targets
        made = []
        for piece, (mine, theirs, spot) in enumerate(self.parts(number, self.stage.at[slot])):
            if keep:
                made.append(pltpu.make_async_copy(mine, own.at[spot], self.kept.at[slot, piece]))
            if give:
                sems = (self.sent.at[slot, piece], self.came.at[number, piece])
                made.append(remote(theirs, other.at[spot], *sems, self.here.sibling()))
        return made

    def settle(self, number):
        for copy in self.copies(number, give=False):
            copy.wait()
        for copy in self.copies(number, keep=False):
            copy.wait_send()

    def run(self, first, last, make):
        def body(number, carry):
            pl.when(number >= 2)(lambda: self.settle(number - 2))
            make(number, self.stage.at[lax.rem(number, 2)])
            for copy in self.copies(number):
                copy.start()
            return carry

        lax.fori_loop(first, last, body, 0)
        if last == self.count:
            for number in (last - 2, last - 1):
                self.settle(number)

    def heard(self):
        for number in range(self.count):
            for copy in self.copies(number, keep=False):
                copy.wait_recv()


def experts_kernel(
    rows, ups, gates, win, wout, middle, mid_sum, gate_sum, out_sum, gin_sum, gdown, gdown_other, gin, gin_other, rows_all, *scratch
):
    here = Here()
    here.meet()
    (
        w_in, w_out, grads, scaled, row_plane, up_plane, gate_plane, served, strip, stage, loads, strip_sems
    ) = scratch[:12]
    gather = Gather(here, rows, rows_all, halves_of(rows.shape[0]), False, scratch[12:16])
    mids = Sum(here, None, mid_sum, halves_of(rows.shape[0]), False, scratch[16:24])
    outs = Sum(here, None, out_sum, halves_of(rows.shape[0]), False, scratch[16:19] + scratch[24:29])
    fetch_middle = pltpu.make_async_copy(middle, scratch[45], scratch[46].at[0])
    fetch_middle.start()
    outs.extra = [scratch[45]]
    tables = Sum(here, None, gate_sum, halves_of(gate_sum.shape[0], False), False, scratch[29:37])
    in_sems, down_sems = scratch[37:40], scratch[40:43]
    block, width = rows.shape
    plane = RING * block
    hidden = w_out.shape[0]
    chunk = hidden // 4
    column = lax.broadcasted_iota(jnp.int32, (plane, 128), 1)
    fetch_in = pltpu.make_async_copy(win, w_in, loads.at[0])
    fetch_out = pltpu.make_async_copy(wout, w_out, loads.at[1])
    fetch_in.start()
    fetch_out.start()

    def fetch_plane(number):
        z = near_first(here, number)
        return (
            pltpu.make_async_copy(ups.at[z], up_plane.at[number % 2], loads.at[2 + number % 2]),
            pltpu.make_async_copy(gates.at[z], gate_plane.at[number % 2], loads.at[4 + number % 2]),
        )

    def fetch_rows(number):
        return pltpu.make_async_copy(rows_all.at[near_first(here, number)], row_plane, loads.at[6])

    def hidden_units(number):
        z = near_first(here, number)
        fetch_rows(number).start()
        for copy in fetch_plane(number):
            copy.wait()
        if number == 0:
            fetch_in.wait()
            fetch_out.wait()
        fetch_rows(number).wait()
        served[...] = jnp.zeros_like(served)
        at = pl.ds(pl.multiple_of(z * plane, plane), plane)

        def one(expert, carry):
            mid = row_plane[...].reshape(plane, width)
            up_rows = up_plane[number % 2]
            spot = pl.ds(pl.multiple_of(expert * chunk, chunk), chunk)
            spot_up = pl.ds(pl.multiple_of(hidden + expert * chunk, chunk), chunk)
            gate = jnp.sum(jnp.where(column == expert, gate_plane[number % 2], 0.0), axis=1, keepdims=True)
            gate_part = jnp.dot(mid, w_in[:, spot], preferred_element_type=single)
            up_part = jnp.dot(mid, w_in[:, spot_up], preferred_element_type=single)
            back = contract_last(up_rows, w_out[spot])
            sigmoid = 1.0 / (1.0 + jnp.exp(-gate_part))
            activated = gate_part * sigmoid
            units = activated * up_part
            scaled[at, spot] = (gate * units).astype(narrow)
            total = jnp.sum(units * back, axis=1, keepdims=True)
            served[...] += jnp.where(column == here.chip * 4 + expert, total, 0.0)
            grad = gate * back
            grads[at, spot] = (grad * up_part * (sigmoid * (1.0 + gate_part * (1.0 - sigmoid)))).astype(narrow)
            grads[at, spot_up] = (grad * activated).astype(narrow)
            return carry

        lax.fori_loop(0, 4, one, 0)
        for chip in range(RING):
            turned = jnp.transpose(served[chip * block : (chip + 1) * block])
            tables.mine[z, chip] = turned[: tables.rows]

    def row_grads(z):
        at = pl.ds(pl.multiple_of(z * plane, plane), plane)

        def one(number, carry):
            spot = pl.ds(pl.multiple_of(number * TILE, TILE), TILE)
            made = contract_last(grads[at], w_in[spot]).astype(narrow)
            for chip in range(RING):
                mids.mine[z, chip, :, spot] = made[chip * block : (chip + 1) * block]
            return carry

        lax.fori_loop(0, width // TILE, one, 0)

    def products(z):
        at = pl.ds(pl.multiple_of(z * plane, plane), plane)

        def one(number, carry):
            spot = pl.ds(pl.multiple_of(number * TILE, TILE), TILE)
            made = jnp.dot(scaled[at], w_out[:, spot], preferred_element_type=single).astype(narrow)
            for chip in range(RING):
                outs.mine[z, chip, :, spot] = made[chip * block : (chip + 1) * block]
            return carry

        lax.fori_loop(0, width // TILE, one, 0)

    strips = width // TILE

    def fetch_strip(number):
        spot = pl.ds(pl.multiple_of(number * TILE, TILE), TILE)
        slot = lax.rem(number, 2)
        return pltpu.make_async_copy(rows_all.at[:, :, :, spot], strip.at[slot], strip_sems.at[slot])

    def columns_of(result, stage, step=512):
        for begin in range(0, width, step):
            stage[:, begin : begin + step] = result(begin, step).astype(narrow)

    def grad_in(number, stage):
        slot = lax.rem(number, 2)
        fetch_strip(number).wait()
        pl.when(number + 1 < strips)(lambda: fetch_strip(number + 1).start())
        left = strip[slot].reshape(DEPTH * plane, TILE)
        columns_of(lambda begin, step: contract_rows(left, grads[:, begin : begin + step]), stage)

    def grad_in_parts(number, stage):
        share = hidden // 2
        at = pl.ds(pl.multiple_of(number * TILE, TILE), TILE)
        for side in range(2):
            mine, theirs = (
                stage.at[:, pl.ds(pl.multiple_of(side * hidden + core * share, 128), share)]
                for core in (here.core, 1 - here.core)
            )
            yield mine, theirs, (at, pl.ds(side * share, share))

    def grad_down(number, stage):
        half = tall // 2
        core = here.core + (1 - lax.div(number, half)) * (1 - 2 * here.core)
        at = core * half + lax.rem(number, half)
        left = scaled[:, pl.ds(pl.multiple_of(at * TILE, TILE), TILE)]
        columns_of(lambda begin, step: contract_rows(left, w_in[:, begin : begin + step]), stage)

    tall = hidden // TILE
    tiles_in = Tiles(here, stage, strips, in_sems, grad_in_parts, (gin, gin_other))

    def grad_down_store(number, away):
        slot = lax.rem(number, 2)
        rest = lax.rem(number, tall // 2)
        spot = pl.ds(pl.multiple_of(rest * TILE, TILE), TILE)
        kept, sent, came = down_sems
        if away:
            return remote(stage.at[slot], gdown_other.at[spot], sent.at[slot, 0], came.at[rest, 0], here.sibling())
        return pltpu.make_async_copy(stage.at[slot], gdown.at[spot], kept.at[slot, 0])

    def grads_down(away):
        first = 0 if away else tall // 2

        def body(number, carry):
            grad_down(number, stage.at[lax.rem(number, 2)])
            grad_down_store(number, away).start()
            return carry

        lax.fori_loop(first, first + tall // 2, body, 0)
        for number in range(first, first + tall // 2):
            copy = grad_down_store(number, away)
            copy.wait_send() if away else copy.wait()

    def add_cores():
        half = hidden
        adds, puts = scratch[43], scratch[44]

        def fetch(number):
            slot = lax.rem(number, 2)
            at = pl.ds(pl.multiple_of(number * TILE, TILE), TILE)
            return [
                pltpu.make_async_copy(
                    source.at[at], stage.at[slot, :, pl.ds(side * half, half)], adds.at[slot, side]
                )
                for side, source in enumerate((gin, gin_other))
            ]

        def put(number):
            slot = lax.rem(number, 2)
            at = pl.ds(pl.multiple_of(number * TILE, TILE), TILE)
            return pltpu.make_async_copy(stage.at[slot, :, pl.ds(0, half)], gin_sum.at[at], puts.at[slot])

        def start_fetch(number):
            for copy in fetch(number):
                copy.start()

        def body(number, carry):
            for copy in fetch(number):
                copy.wait()
            pl.when(number >= 1)(lambda: put(number - 1).wait())
            pl.when(number + 1 < strips)(lambda: start_fetch(number + 1))
            slot = lax.rem(number, 2)
            own = stage.at[slot, :, pl.ds(0, half)]
            add_up(own, [own, stage.at[slot, :, pl.ds(half, half)]], TILE, half)
            put(number).start()
            return carry

        start_fetch(0)
        lax.fori_loop(0, strips, body, 0)
        put(strips - 1).wait()

    again = [
        pltpu.make_async_copy(ups.at[z], w_in.at[pl.ds(z * plane, plane)], loads.at[7 + z]) for z in range(DEPTH)
    ]

    def again_wait():
        for copy in again:
            copy.wait()

    order = [far_first(here, number) for number in range(DEPTH)]
    first = [mids, tables]
    steps = [(first, z, False) for z in [here.z] + order[:-1]]
    steps += [([outs], z, number == DEPTH - 1) for number, z in enumerate(order)]

    def begin(number):
        items, z, last = steps[number]
        if number < DEPTH:
            row_grads(z)
        else:
            mids.end(z, last)
            products(z)
        for item in items:
            for way in (0, 1):
                start(item.toss(z, way))

    def second(number):
        for item in steps[number][0]:
            item.second(steps[number][1])

    def third(number):
        items, z, last = steps[number]
        for item in items:
            item.own_part(z) if number == 0 else item.third(z, last)

    for copy in fetch_plane(0):
        copy.start()
    rounds = Rounds(here, [gather])
    rounds.service(0)
    for number in range(DEPTH):
        if number + 1 < DEPTH:
            rounds.service(number + 1)
        if number == DEPTH - 1:
            second(0)
        gather_third(gather, near_first(here, number))
        if number + 1 < DEPTH:
            for copy in fetch_plane(number + 1):
                copy.start()
        hidden_units(number)
        if number == 1:
            begin(0)
    fetch_strip(0).start()
    ends = [0] + [strips * (number + 1) // (DEPTH - 1) for number in range(DEPTH - 1)]
    for number in range(1, 2 * DEPTH):
        begin(number)
        if number > 1:
            second(number - 1)
            third(number - 2)
        if number == DEPTH - 1:
            for copy in again:
                copy.start()
        if number < DEPTH:
            tiles_in.run(ends[number - 1], ends[number], grad_in)
        elif number == DEPTH:
            again_wait()
            grads_down(True)
        elif number == DEPTH + 1:
            grads_down(False)
        elif number == DEPTH + 2:
            for item in first:
                item.own_rest(here.z)
            tiles_in.heard()
            add_cores()
    outs.second(order[-1])
    outs.third(order[-2], False)
    fetch_middle.wait()
    outs.third(order[-1], True)
    for number, z in enumerate(order):
        outs.end(z, number == DEPTH - 1)
        tables.end(z, number == DEPTH - 1)
    for number in range(tall // 2):
        grad_down_store(number, True).wait_recv()
    rounds.finish()


def experts_round(rows, ups, gates, win, wout, middle, experts):
    block, width = rows.shape
    plane = RING * block
    hidden = wout.shape[0]
    total = DEPTH * plane
    vmem = pl.BlockSpec(memory_space=pltpu.VMEM)
    return pl.pallas_call(
        experts_kernel,
        out_shape=(
            jax.ShapeDtypeStruct((block, width), single),
            jax.ShapeDtypeStruct((experts, block), single),
            jax.ShapeDtypeStruct((block, width), narrow),
            jax.ShapeDtypeStruct((width, hidden), narrow),
            jax.ShapeDtypeStruct((hidden // 2, width), narrow),
            jax.ShapeDtypeStruct((hidden // 2, width), narrow),
            jax.ShapeDtypeStruct((width, hidden), narrow),
            jax.ShapeDtypeStruct((width, hidden), narrow),
            jax.ShapeDtypeStruct((DEPTH, RING, block, width), narrow),
        ),
        in_specs=[HBM] * 6,
        out_specs=(vmem, vmem, vmem) + (HBM,) * 6,
        scratch_shapes=[
            pltpu.VMEM((width, 2 * hidden), narrow),
            pltpu.VMEM((hidden, width), narrow),
            pltpu.VMEM((total, 2 * hidden), narrow),
            pltpu.VMEM((total, hidden), narrow),
            pltpu.VMEM((RING, block, width), narrow),
            pltpu.VMEM((2, plane, width), narrow),
            pltpu.VMEM((2, plane, 128), single),
            pltpu.VMEM((plane, 128), single),
            pltpu.VMEM((2, DEPTH, RING, block, TILE), narrow),
            pltpu.VMEM((2, TILE, width), narrow),
            pltpu.SemaphoreType.DMA((11,)),
            pltpu.SemaphoreType.DMA((2,)),
        ]
        + GATHER_SEMS
        + sum_scratch(block, width, narrow, halves_of(block), made=True)
        + [pltpu.VMEM((DEPTH + 1, block, width), narrow)]
        + SUM_SEMS
        + sum_scratch(experts, block, single, halves_of(experts, False), made=True)
        + [
            pltpu.SemaphoreType.DMA((2, 2)),
            pltpu.SemaphoreType.DMA((2, 2)),
            pltpu.SemaphoreType.DMA((width // TILE, 2)),
        ]
        + [
            pltpu.SemaphoreType.DMA((2, 1)),
            pltpu.SemaphoreType.DMA((2, 1)),
            pltpu.SemaphoreType.DMA((hidden // TILE, 1)),
        ]
        + [pltpu.SemaphoreType.DMA((2, 2)), pltpu.SemaphoreType.DMA((2,))]
        + [pltpu.VMEM((block, width), single), pltpu.SemaphoreType.DMA((1,))],
        compiler_params=pltpu.CompilerParams(
            collective_id=2, has_side_effects=True, vmem_limit_bytes=62 * 2**20
        ),
        name="experts",
    )(rows, ups, gates, win, wout, middle)


def by_kernels():
    return lax.axis_size("dp") == DEPTH and lax.axis_size("expert") == 2 * RING


def forward(tokens, gains, weight_qkv, weight_out, cosine, sine, allowed):
    rows, width = tokens.shape
    inputs = tokens.astype(single)
    normed_in = (normalize(inputs)[0] * gains[0]).astype(narrow)
    projected = jnp.dot(normed_in, weight_qkv, preferred_element_type=single)
    raw = jnp.stack([projected[:, :width], projected[:, width : 2 * width]])
    query_rows, key_rows = (
        rotate(normalize(raw[side])[0] * gains[side + 1], cosine, sine).astype(narrow) for side in range(2)
    )
    value_rows = projected[:, 2 * width :].astype(narrow)
    by_head = (rows, -1, HEAD)
    scores = jnp.einsum(
        "qhd,khd->hqk", query_rows.reshape(by_head), key_rows.reshape(by_head), preferred_element_type=single
    )
    scores = jnp.where(allowed[None], scores * HEAD ** (-0.5), masked_score)
    unnormed = jnp.exp(scores - jnp.max(scores, axis=-1, keepdims=True))
    probs = unnormed / jnp.sum(unnormed, axis=-1, keepdims=True)
    attended = jnp.einsum(
        "hqk,khd->qhd", probs.astype(narrow), value_rows.reshape(by_head), preferred_element_type=single
    )
    attended = attended.reshape(rows, width).astype(narrow)
    middle = inputs + jnp.dot(attended, weight_out, preferred_element_type=single)
    routed_in = (normalize(middle)[0] * gains[3]).astype(narrow)
    return (normed_in, raw, query_rows, key_rows, value_rows, probs, attended, middle, routed_in)


def wide_tables(cosine, sine):
    return (
        jnp.concatenate([cosine[:, 0], cosine[:, 0]], axis=1),
        jnp.concatenate([-sine[:, 0], sine[:, 0]], axis=1),
    )


def bring_all(w_qkv, w_out, upstream, dense, gain_rows, expert_in, expert_out, tokens, cosine, sine, allowed):
    width = upstream.shape[1]
    share = gain_rows.shape[1]
    if by_kernels():
        experts, rows = dense.shape[1], dense.shape[0]
        small = jnp.concatenate([dense.T, jnp.pad(gain_rows, ((0, 4), (0, rows - share)))], axis=0)
        tables = (*wide_tables(cosine, sine), allowed.astype(single))
        wq, wo, up, all_small, weight_in, weight_down, gains, *made = first_gather(
            w_qkv, w_out, upstream, small, expert_in, expert_out, tokens, *tables
        )
        core = lax.rem(lax.axis_index("expert"), 2)
        every_gate = lax.dynamic_index_in_dim(all_small, core, axis=2, keepdims=False)[:, :, :experts]
        return (
            wq.reshape(-1, w_qkv.shape[1]),
            wo.reshape(-1, w_out.shape[1]),
            up.reshape(-1, width),
            every_gate,
            gains,
            weight_in,
            weight_down.reshape(-1, width),
            made,
        )
    everyone = ("dp", "expert")
    weight_in, weight_down = fetch_weights(expert_in, expert_out)
    weight_qkv = lax.all_gather(w_qkv, everyone, axis=0, tiled=True)
    weight_out = lax.all_gather(w_out, everyone, axis=0, tiled=True)
    gains = lax.all_gather(gain_rows, everyone, axis=1, tiled=True)
    return (
        weight_qkv,
        weight_out,
        gather_alike(upstream).reshape(-1, width),
        gather_alike(dense.T),
        gains,
        weight_in,
        weight_down,
        forward(tokens, gains, weight_qkv, weight_out, cosine, sine, allowed),
    )


def experts_all(middle, routed_in, up_rows, every_gate, weight_in, weight_down, held):
    depth = lax.axis_size("dp")
    owners = lax.axis_size("expert")
    chips = owners // 2
    experts = owners * held
    chip_experts = 2 * held
    rows, width = routed_in.shape
    chip = lax.axis_index("expert") // 2
    mine = lax.dynamic_slice_in_dim(every_gate, chip * chip_experts, chip_experts, axis=2)
    gate = mine.transpose(0, 1, 3, 2)
    if by_kernels():
        gate = jnp.pad(gate.reshape(DEPTH, -1, chip_experts), ((0, 0), (0, 0), (0, 128 - chip_experts)))
        ups = up_rows.reshape(DEPTH, -1, width)
        grad_routed, table, results, grad_in, grad_down, grad_down_other = experts_round(
            routed_in, ups, gate, weight_in, weight_down, middle, experts
        )[:6]
        down = grad_down.astype(single) + grad_down_other.astype(single)
        return (results, grad_routed, table, (grad_in, down.reshape(held, -1, width)))
    mid_rows = gather_alike(routed_in).reshape(-1, width)
    out, mid, served, grad_in, grad_down = expert_rounds(
        mid_rows, up_rows, gate.reshape(-1, chip_experts), weight_in, weight_down
    )
    by_gate = served.reshape(depth, chips, rows, chip_experts).transpose(0, 1, 3, 2)
    spread = jnp.zeros((depth, chips, experts, rows), single)
    spread = lax.dynamic_update_slice_in_dim(spread, by_gate, chip * chip_experts, axis=2)
    mixture = scatter_alike(out.reshape(depth, chips, rows, width)).astype(single)
    return (
        (middle + mixture).astype(narrow),
        scatter_alike(mid.reshape(depth, chips, rows, width)).astype(single),
        scatter_alike(spread),
        return_weights(grad_in, grad_down, held),
    )


def backward(
    tokens, gains, grad_routed, upstream, normed, raw, queries, keys, values, probs, attended, middle, weight_qkv, weight_out,
    cosine, sine
):
    rows, width = tokens.shape
    by_head = (rows, -1, HEAD)
    grad_mid, piece_ffn = rms_back(grad_routed, *normalize(middle), gains[3])
    grad_middle = upstream.astype(single) + grad_mid
    branch = grad_middle.astype(narrow)
    grad_heads = contract_last(branch, weight_out).astype(narrow).reshape(by_head)
    grad_probs = jnp.einsum("qhd,khd->hqk", grad_heads, values.reshape(by_head), preferred_element_type=single)
    inner = jnp.sum(grad_probs * probs, axis=-1, keepdims=True)
    grad_scores = (probs * (grad_probs - inner)).astype(narrow)
    grads = (
        jnp.einsum("hqk,khd->qhd", grad_scores, keys.reshape(by_head), preferred_element_type=single),
        jnp.einsum("hqk,qhd->khd", grad_scores, queries.reshape(by_head), preferred_element_type=single),
    )
    grad_value = jnp.einsum("hqk,qhd->khd", probs.astype(narrow), grad_heads, preferred_element_type=single)
    (grad_q, piece_query), (grad_k, piece_key) = (
        rms_back(
            rotate(grads[side].reshape(rows, width) * HEAD ** (-0.5), cosine, -sine),
            *normalize(raw[side]),
            gains[side + 1],
        )
        for side in range(2)
    )
    grad_qkv = jnp.concatenate([grad_q, grad_k, grad_value.reshape(rows, width)], axis=1).astype(narrow)
    grad_input, piece_attn = rms_back(
        contract_last(grad_qkv, weight_qkv), *normalize(tokens.astype(single)), gains[0]
    )
    pieces = jnp.stack([piece_attn, piece_query, piece_key, piece_ffn])
    return (grad_middle + grad_input, pieces, (normed, grad_qkv), (attended, branch))


def deliver_all(tokens, gains, grad_routed, upstream, made, weight_qkv, weight_out, cosine, sine, share_in, held):
    normed, raw, queries, keys, values, probs, attended, middle, _ = made
    owners = lax.axis_size("dp") * lax.axis_size("expert")
    share = gains.shape[1] // owners
    if by_kernels():
        share_qkv, share_out, gain_sums, grad_tokens, share_in = last_sum(
            normed, attended, share_in, weight_qkv, weight_out, tokens, grad_routed, upstream, middle, raw, queries, keys,
            values, probs, *wide_tables(cosine, sine), gains, share, held
        )
        core = lax.rem(lax.axis_index("expert"), 2)
        gain_sums = lax.dynamic_slice_in_dim(gain_sums, core * share, share, axis=1)
        return (grad_tokens, gain_sums, share_qkv, share_out, share_in.astype(single))
    everyone = ("dp", "expert")
    grad_tokens, pieces, *pairs = backward(
        tokens, gains, grad_routed, upstream, normed, raw, queries, keys, values, probs, attended, middle, weight_qkv,
        weight_out, cosine, sine
    )
    return (
        grad_tokens,
        lax.psum_scatter(pieces, everyone, scatter_dimension=1, tiled=True),
        *(
            lax.psum_scatter(
                contract_rows(left, right, narrow), everyone, scatter_dimension=0, tiled=True
            ).astype(single)
            for left, right in pairs
        ),
        share_in.astype(single),
    )


def local(
    tokens,
    lengths,
    expert_ids,
    gates,
    attn_gain,
    w_qkv,
    q_gain,
    k_gain,
    w_out,
    ffn_gain,
    expert_in,
    expert_out,
    out_grad,
):
    micro_count, seq_len, model_width = tokens.shape
    rows = micro_count * seq_len
    held = expert_in.shape[0]
    experts = lax.axis_size("expert") * held
    own = tokens.reshape(rows, model_width)
    upstream = out_grad.reshape(rows, model_width)
    ids = expert_ids.reshape(rows, -1)
    gate_rows = gates.reshape(rows, -1)
    onehot = (ids[:, :, None] == jnp.arange(experts, dtype=jnp.int32)).astype(single)
    dense = jnp.sum(onehot * gate_rows[:, :, None], axis=1)
    gain_rows = jnp.stack([attn_gain, q_gain, k_gain, ffn_gain]).astype(single)
    document, position = layout(lengths[:, 0], seq_len)
    cosine, sine = angles(position)
    places = jnp.arange(rows, dtype=jnp.int32)
    allowed = (document[:, None] == document[None, :]) & (places[:, None] >= places[None, :])
    weight_qkv, weight_out, up_rows, every_gate, gains, weight_in, weight_down, made = bring_all(
        w_qkv, w_out, upstream, dense, gain_rows, expert_in, expert_out, own, cosine, sine, allowed
    )
    middle, routed_in = made[-2:]

    results, grad_routed, gate_table, (share_in, share_down) = experts_all(
        middle, routed_in, up_rows, every_gate, weight_in, weight_down, held
    )
    grad_gates = jnp.sum(onehot * gate_table.T[:, None, :], axis=2)

    grad_tokens, gain_sums, grad_qkv_share, grad_out_share, share_in = deliver_all(
        own, gains, grad_routed, upstream, made, weight_qkv, weight_out, cosine, sine, share_in, held
    )
    shape = (micro_count, seq_len, model_width)
    return (
        results.reshape(shape),
        grad_tokens.reshape(shape),
        grad_gates.reshape(expert_ids.shape),
        gain_sums[0],
        grad_qkv_share,
        gain_sums[1],
        gain_sums[2],
        grad_out_share,
        gain_sums[3],
        share_in,
        share_down.astype(single),
    )


def solution(mesh):
    by_rows = P(None, ("dp", "expert"), None)
    flat = P(("dp", "expert"))
    split = P(("dp", "expert"), None)
    held = P("expert", "dp", None)
    return jax.shard_map(
        local,
        mesh=mesh,
        in_specs=(
            by_rows, by_rows, by_rows, by_rows, flat, split, flat, flat, split, flat, held, held, by_rows,
        ),
        out_specs=(by_rows, by_rows, by_rows, flat, split, flat, flat, split, flat, held, held),
        check_vma=False,
    )
```

```python
import jax
import jax.numpy as jnp
from jax import lax
from jax.experimental import pallas as pl
from jax.experimental.pallas import tpu as pltpu
from jax.sharding import PartitionSpec as P

HEAD = 128
epsilon = 1e-05
base_theta = 10000.0
masked_score = -1e30
single = jnp.float32
narrow = jnp.bfloat16


def normalize(values):
    factor = lax.rsqrt(jnp.mean(values * values, axis=-1, keepdims=True) + epsilon)
    return (values * factor, factor)


def rms_back(upstream, normal, factor, gain):
    weighted = upstream * gain
    inner = jnp.mean(weighted * normal, axis=-1, keepdims=True)
    return (factor * (weighted - normal * inner), jnp.sum(upstream * normal, axis=0))


def angles(position):
    half = HEAD // 2
    ladder = jnp.arange(half, dtype=single) * (2.0 / HEAD)
    frequency = jnp.exp(-jnp.log(base_theta) * ladder)
    angle = position.astype(single)[:, None] * frequency[None, :]
    return (jnp.cos(angle)[:, None, :], jnp.sin(angle)[:, None, :])


def rotate(field, cosine, sine):
    length = field.shape[0]
    heads = field.reshape(length, -1, HEAD)
    half = HEAD // 2
    first = heads[..., :half]
    second = heads[..., half:]
    turned = jnp.concatenate(
        [first * cosine - second * sine, second * cosine + first * sine], axis=-1
    )
    return turned.reshape(length, -1)


def layout(doc_lengths, length):
    packs, count = doc_lengths.shape
    upto = jnp.arange(count)[None, :] <= jnp.arange(count)[:, None]
    ends = jnp.sum(jnp.where(upto[None], doc_lengths[:, None, :], 0), axis=2)
    starts = ends - doc_lengths
    places = jnp.arange(length, dtype=jnp.int32)[None, :, None]
    document = jnp.sum((places >= ends[:, None, :]).astype(jnp.int32), axis=2)
    member = (places >= starts[:, None, :]) & (places < ends[:, None, :])
    first_place = jnp.sum(jnp.where(member, starts[:, None, :], 0), axis=2)
    document = document + (count + 1) * jnp.arange(packs, dtype=jnp.int32)[:, None]
    return (document.reshape(-1), (places[..., 0] - first_place).reshape(-1))


def contract_rows(left, right, kind=single):
    return lax.dot_general(left, right, (((0,), (0,)), ((), ())), preferred_element_type=kind)


def contract_last(left, right, kind=single):
    return lax.dot_general(left, right, (((1,), (1,)), ((), ())), preferred_element_type=kind)


def core_groups():
    return [[2 * chip + core for chip in range(lax.axis_size("expert") // 2)] for core in range(2)]


def chip_groups():
    return [[2 * chip, 2 * chip + 1] for chip in range(lax.axis_size("expert") // 2)]


def gather_alike(block):
    column = lax.all_gather(block, "dp", axis=0)
    return lax.all_gather(column, "expert", axis=1, axis_index_groups=core_groups())


def scatter_alike(blocks):
    column = lax.psum_scatter(
        blocks, "expert", scatter_dimension=1, axis_index_groups=core_groups()
    )
    return lax.psum_scatter(column, "dp", scatter_dimension=0)


def fetch_weights(expert_in, expert_out):
    depth = lax.axis_size("dp")
    held, rows, columns = expert_in.shape
    part = columns // (2 * depth)
    cut = expert_in.reshape(held, rows, 2, depth, part)
    turned = lax.all_to_all(cut, "dp", split_axis=3, concat_axis=1, tiled=True)
    both = lax.all_gather(turned[:, :, :, 0], "expert", axis=0, axis_index_groups=chip_groups())
    weight_in = both.transpose(2, 3, 0, 1, 4).reshape(depth * rows, 4 * held * part)
    weight_down = lax.all_gather(
        expert_out, "expert", axis=0, axis_index_groups=chip_groups()
    ).reshape(-1, expert_out.shape[2])
    return (weight_in, weight_down)


def return_weights(grad_in, grad_down, held):
    depth = lax.axis_size("dp")
    rows, columns = grad_in.shape
    part = columns // (4 * held)
    cut = grad_in.reshape(rows, 2, 2, held, part)
    own = lax.psum_scatter(cut, "expert", scatter_dimension=2, axis_index_groups=chip_groups())
    own = own.reshape(depth, rows // depth, 2, held, part)
    turned = lax.all_to_all(own, "dp", split_axis=0, concat_axis=0)
    share_in = turned.transpose(3, 1, 2, 0, 4).reshape(held, rows // depth, 2 * depth * part)
    down = grad_down.reshape(2, held, part, grad_down.shape[1])
    share_down = lax.psum_scatter(
        down, "expert", scatter_dimension=0, axis_index_groups=chip_groups()
    )
    return (share_in, share_down)


def expert_round(mid_rows, up_rows, gate, weight_in, weight_down):
    count = gate.shape[1]
    part = weight_down.shape[0] // count
    wide = jnp.broadcast_to(gate[:, :, None], gate.shape + (part,)).reshape(gate.shape[0], -1)
    gate_up = jnp.dot(mid_rows, weight_in, preferred_element_type=single)
    hidden_units = gate_up.shape[1] // 2
    gate_part = gate_up[:, :hidden_units]
    up_part = gate_up[:, hidden_units:]
    sigmoid = jax.nn.sigmoid(gate_part)
    activated = gate_part * sigmoid
    hidden = activated * up_part
    back = contract_last(up_rows, weight_down)
    scaled = (wide * hidden).astype(narrow)
    piece_out = jnp.dot(scaled, weight_down, preferred_element_type=narrow)
    piece_gates = jnp.sum((hidden * back).reshape(-1, count, part), axis=2)
    grad_hidden = wide * back
    grad_gate = grad_hidden * up_part * sigmoid * (1.0 + gate_part * (1.0 - sigmoid))
    grad_up = grad_hidden * activated
    grad_gate_up = jnp.concatenate([grad_gate, grad_up], axis=1).astype(narrow)
    piece_mid = contract_last(grad_gate_up, weight_in, narrow)
    return (piece_out, piece_mid, piece_gates, grad_gate_up, scaled)


def expert_rounds(mid_rows, up_rows, gate, weight_in, weight_down):
    total = mid_rows.shape[0]
    rounds = max(1, total // 2048)

    def one(sums, pieces):
        mid, up, weights = pieces
        piece_out, piece_mid, piece_gates, grad_gate_up, scaled = expert_round(
            mid, up, weights, weight_in, weight_down
        )
        grads = (contract_rows(mid, grad_gate_up), contract_rows(scaled, up))
        return (jax.tree.map(jnp.add, sums, grads), (piece_out, piece_mid, piece_gates))

    if rounds == 1:
        piece_out, piece_mid, piece_gates, grad_gate_up, scaled = expert_round(
            mid_rows, up_rows, gate, weight_in, weight_down
        )
        grads = (contract_rows(mid_rows, grad_gate_up, narrow), contract_rows(scaled, up_rows, narrow))
        return (piece_out, piece_mid, piece_gates) + grads
    start = (jnp.zeros(weight_in.shape, single), jnp.zeros(weight_down.shape, single))
    cut = jax.tree.map(lambda a: a.reshape(rounds, total // rounds, -1), (mid_rows, up_rows, gate))
    sums, made = lax.scan(one, start, cut)
    made = jax.tree.map(lambda a: a.reshape(total, -1), made)
    return made + (sums[0].astype(narrow), sums[1].astype(narrow))


MESH = pl.DeviceIdType.MESH
HBM = pl.BlockSpec(memory_space=pl.ANY)
DEPTH = 4
RING = 4


def ring_turn(number):
    high = lax.div(number, 2)
    return number + high * (1 - 2 * lax.rem(number, 2))


class Here:
    def __init__(self):
        number = lax.axis_index("expert")
        self.z = lax.axis_index("dp")
        self.core = lax.rem(number, 2)
        self.chip = lax.div(number, 2)
        self.q = ring_turn(self.chip)

    def chip_at(self, turn):
        return ring_turn(lax.rem(self.q + turn + RING, RING))

    def beside(self, turn):
        return (self.z, 2 * self.chip_at(turn) + self.core)

    def above(self, steps):
        return (lax.rem(self.z + steps + DEPTH, DEPTH), 2 * self.chip + self.core)

    def sibling(self):
        return (self.z, 2 * self.chip + 1 - self.core)

    def meet(self):
        barrier = pltpu.get_barrier_semaphore()
        others = [self.beside(1), self.beside(-1), self.sibling()]
        others += [self.above(steps) for steps in range(1, DEPTH)]
        for other in others:
            pl.semaphore_signal(barrier, inc=1, device_id=other, device_id_type=MESH)
        pl.semaphore_wait(barrier, len(others))


def remote(source, target, sent, arrived, device):
    return pltpu.make_async_remote_copy(
        src_ref=source,
        dst_ref=target,
        send_sem=sent,
        recv_sem=arrived,
        device_id=device,
        device_id_type=MESH,
    )


GATHER_SEMS = [
    pltpu.SemaphoreType.DMA((2, 2, DEPTH - 1)),
    pltpu.SemaphoreType.DMA((2, DEPTH, 2, 2)),
    pltpu.SemaphoreType.DMA((2, DEPTH)),
    pltpu.SemaphoreType.DMA((1,)),
]


class Gather:
    def __init__(self, here, source, whole, halves, shared, sems):
        self.here, self.source, self.whole, self.halves, self.shared = here, source, whole, halves, shared
        self.line, self.ring, self.pair, self.own = sems

    def block(self, z, turn):
        chip = self.here.chip_at(turn)
        return self.whole.at[z, chip, self.here.core] if self.shared else self.whole.at[z, chip]

    def keep(self):
        return pltpu.make_async_copy(self.source, self.block(self.here.z, 0), self.own.at[0])

    def along(self, step, way, first):
        z = self.here.z - step + 1 if way == 0 else self.here.z + step - 1
        block = self.block(z, 0)
        return remote(
            self.source if first else block,
            block,
            self.line.at[0, way, step - 1],
            self.line.at[1, way, step - 1],
            self.here.above(1 if way == 0 else -1),
        )

    def round(self, z, way, first=False):
        turn = 1 if way == 0 else -1
        block = self.block(z, 0)
        return remote(
            self.source if first else block,
            block,
            self.ring.at[0, z, way, 0],
            self.ring.at[1, z, way, 0],
            self.here.beside(turn),
        )

    def heard(self, z, way):
        block = self.block(z, -1 if way == 0 else 1)
        return remote(
            block, block, self.ring.at[0, z, way, 0], self.ring.at[1, z, way, 0], self.here.beside(1)
        )

    def onward(self, z, way, mine):
        if self.halves[way] is None:
            return None
        turn = (-1 if mine else -2) if way == 0 else (1 if mine else 2)
        block = self.block(z, turn).at[pl.ds(*self.halves[way])]
        return remote(
            block,
            block,
            self.ring.at[0, z, way, 1],
            self.ring.at[1, z, way, 1],
            self.here.beside(1 if way == 0 else -1),
        )

    def swap(self, z, mine):
        core = self.here.core if mine else 1 - self.here.core
        part = self.whole.at[z, :, core]
        return remote(part, part, self.pair.at[0, z], self.pair.at[1, z], self.here.sibling())


def start(copy):
    if copy is not None:
        copy.start()


def gather_third(item, z):
    for way in (0, 1):
        copy = item.onward(z, way, False)
        if copy is not None:
            copy.wait_recv()


class Rounds:
    def __init__(self, here, items, ring=True):
        self.here, self.items = here, items
        for item in items:
            item.keep().start()
            for way in (0, 1):
                self.depart(0, way, item)
            if ring:
                for way in (0, 1):
                    item.round(here.z, way, True).start()

    def depart(self, step, way, item):
        here = self.here
        ahead = here.z + 1 < DEPTH if way == 0 else here.z >= 1
        pl.when(ahead)(lambda: item.along(step + 1, way, step == 0).start())

    def places(self, step, body):
        here = self.here
        if step == 0:
            body(here.z, 0)
            return
        pl.when(here.z >= step)(lambda: body(here.z - step, 0))
        pl.when(here.z + step < DEPTH)(lambda: body(here.z + step, 1))

    def line(self, step, ring=True):
        def body(z, way):
            for item in self.items:
                block = item.block(z, 0)
                remote(
                    block, block, item.line.at[0, way, step - 1], item.line.at[1, way, step - 1], self.here.above(1)
                ).wait_recv()
                if step + 1 < DEPTH:
                    self.depart(step, way, item)
                if ring:
                    for side in (0, 1):
                        item.round(z, side).start()

        self.places(step, body)

    def ring(self, step):
        def body(z, way):
            for item in self.items:
                for side in (0, 1):
                    item.round(z, side, step == 0).start()

        self.places(step, body)

    def second(self, step):
        def body(z, way):
            for item in self.items:
                for side in (0, 1):
                    item.heard(z, side).wait_recv()
                    start(item.onward(z, side, True))

        self.places(step, body)

    def service(self, step, between=None):
        if step + 1 < DEPTH:
            self.line(step + 1)
        if between is not None:
            between()
        if step == 0:
            self.kept()
        self.second(step)

    def kept(self):
        for item in self.items:
            item.keep().wait()

    def third(self, step):
        def body(z, way):
            for item in self.items:
                gather_third(item, z)
                if item.shared:
                    item.swap(z, True).start()

        self.places(step, body)

    def finish(self):
        def settle(z, way):
            for item in self.items:
                for side in (0, 1):
                    item.round(z, side).wait_send()
                    copy = item.onward(z, side, True)
                    if copy is not None:
                        copy.wait_send()
                if item.shared:
                    item.swap(z, True).wait_send()
                    item.swap(z, False).wait_recv()

        for step in range(DEPTH):
            self.places(step, settle)
        here = self.here
        for item in self.items:
            for step in range(DEPTH - 1):
                for way in (0, 1):

                    def sent(z, side, step=step, way=way, item=item):
                        if step and side != way:
                            return
                        ahead = here.z + 1 < DEPTH if way == 0 else here.z >= 1
                        pl.when(ahead)(lambda: item.along(step + 1, way, step == 0).wait_send())

                    self.places(step, sent)


def inner_first(here, count, begin):
    for group in (range(1, DEPTH - 1), (0, DEPTH - 1)):
        for number in range(count):
            for target in group:

                @pl.when(here.z != target)
                def _(target=target, number=number):
                    begin(lax.rem(target - here.z + DEPTH, DEPTH), number)


class Recut:
    def __init__(self, here, source_in, source_out, whole_in, whole_out, sems):
        self.here, self.source_in, self.source_out = here, source_in, source_out
        self.whole_in, self.whole_out = whole_in, whole_out
        self.cut, self.pair, self.down, self.own = sems
        self.held, self.rows, columns = source_in.shape
        self.hidden = columns // 2
        self.part = self.hidden // DEPTH

    def pieces(self, steps, arriving, only=None):
        here, copies = self.here, []
        mine = lax.rem(here.z + DEPTH - steps, DEPTH) if arriving else here.z
        away = lax.rem(here.z + steps, DEPTH)
        for side in range(2):
            for expert in range(self.held):
                if only not in (None, side * self.held + expert):
                    continue
                columns = side * self.held * 2 * self.part + (here.core * self.held + expert) * self.part
                target = self.whole_in.at[
                    pl.ds(pl.multiple_of(mine * self.rows, 16), self.rows),
                    pl.ds(pl.multiple_of(columns, 128), self.part),
                ]
                source = self.source_in.at[
                    expert, :, pl.ds(pl.multiple_of(side * self.hidden + away * self.part, 128), self.part)
                ]
                spot = (steps, side * self.held + expert)
                if isinstance(steps, int) and steps == 0:
                    copies.append(pltpu.make_async_copy(source, target, self.own.at[spot[1]]))
                else:
                    copies.append(
                        remote(
                            target if arriving else source,
                            target,
                            self.cut.at[(0,) + spot],
                            self.cut.at[(1,) + spot],
                            here.above(steps),
                        )
                    )
        return copies

    def across(self, steps, mine):
        here, copies = self.here, []
        core = here.core if mine else 1 - here.core
        row = lax.rem(here.z + DEPTH - steps, DEPTH)
        width = self.held * self.part
        for side in range(2):
            spot = self.whole_in.at[
                pl.ds(pl.multiple_of(row * self.rows, 16), self.rows),
                pl.ds(pl.multiple_of(side * 2 * width + core * width, 128), width),
            ]
            copies.append(
                remote(spot, spot, self.pair.at[0, steps, side], self.pair.at[1, steps, side], here.sibling())
            )
        return copies

    def lower(self, mine):
        here = self.here
        core = here.core if mine else 1 - here.core
        spot = self.whole_out.at[pl.ds(core * self.held, self.held)]
        return remote(
            self.source_out if mine else spot, spot, self.down.at[0], self.down.at[1], here.sibling()
        )

    def lower_own(self):
        return pltpu.make_async_copy(
            self.source_out, self.whole_out.at[pl.ds(self.here.core * self.held, self.held)], self.own.at[4]
        )

    def begin(self):
        for copy in self.pieces(0, False):
            copy.start()
        self.lower_own().start()
        self.lower(True).start()
        inner_first(self.here, 2 * self.held, lambda steps, number: self.pieces(steps, False, number)[0].start())

    def relay(self):
        for steps in range(DEPTH):
            for copy in self.pieces(steps, True):
                copy.wait() if steps == 0 else copy.wait_recv()
            for copy in self.across(steps, True):
                copy.start()

    def end(self):
        self.lower_own().wait()
        self.lower(True).wait_send()
        self.lower(False).wait_recv()
        for steps in range(DEPTH):
            if steps:
                for copy in self.pieces(steps, False):
                    copy.wait_send()
            for copy in self.across(steps, True):
                copy.wait_send()
            for copy in self.across(steps, False):
                copy.wait_recv()


RECUT_SEMS = [
    pltpu.SemaphoreType.DMA((2, DEPTH, 4)),
    pltpu.SemaphoreType.DMA((2, DEPTH, 2)),
    pltpu.SemaphoreType.DMA((2,)),
    pltpu.SemaphoreType.DMA((5,)),
]


def halves_of(rows, split=True):
    return ((0, rows // 2), (rows // 2, rows - rows // 2)) if split else ((0, rows), None)


PANEL = 512


def attention_forward(
    tokens, cosine, sine, allowed, wq, wo, gains, normed, raw, queries, keys, values, probs, attended, middle, routed,
    panel, panel_sems, between
):
    block, width = tokens.shape
    heads = width // HEAD
    wide = wq.shape[-1]
    high = 16
    per = width // PANEL

    def fetch(source, number):
        slot = lax.rem(number, 2)
        spot = pl.ds(pl.multiple_of(number * PANEL, PANEL), PANEL)
        return pltpu.make_async_copy(source.at[:, :, :, :, spot], panel.at[slot], panel_sems.at[slot])

    def slabs(body):
        def one(number, carry):
            body(pl.ds(pl.multiple_of(number * high, high), high))
            return carry

        lax.fori_loop(0, block // high, one, 0)

    def first(at):
        values = tokens[at].astype(single)
        factor = lax.rsqrt(jnp.mean(values * values, axis=-1, keepdims=True) + epsilon)
        normed[at] = (values * factor * gains[0:1]).astype(narrow)

    fetch(wq, 0).start()
    slabs(first)

    def through(source, left, total, finish):
        def one(number, carry):
            fetch(source, number).wait()
            pl.when(number + 1 < total)(lambda: fetch(source, number + 1).start())
            weights = panel[lax.rem(number, 2)].reshape(width, PANEL)
            finish(number, jnp.dot(left[...], weights, preferred_element_type=single))
            return carry

        lax.fori_loop(0, total, one, 0)

    def keep(number, made):
        side = lax.div(number, per)
        spot = pl.ds(pl.multiple_of(lax.rem(number, per) * PANEL, PANEL), PANEL)

        @pl.when(side < 2)
        def _():
            raw[side, :, spot] = made

        @pl.when(side == 2)
        def _():
            values[:, spot] = made.astype(narrow)

    through(wq, normed, wide // PANEL, keep)
    fetch(wo, 0).start()
    between(0)

    factors = [
        lax.rsqrt(jnp.mean(raw[side] * raw[side], axis=-1, keepdims=True) + epsilon) for side in range(2)
    ]
    turn_cos, turn_sin = cosine[...], sine[...]
    may = allowed[...] > 0.5
    group = 4

    def some_heads(number, carry):
        for inner in range(group):
            head = number * group + inner
            spot = pl.ds(pl.multiple_of(head * HEAD, HEAD), HEAD)
            turned = []
            for side, target in ((0, queries), (1, keys)):
                field = raw[side, :, spot] * factors[side] * gains[side + 1 : side + 2, spot]
                field = field * turn_cos + pltpu.roll(field, HEAD // 2, 1) * turn_sin
                target[:, spot] = field.astype(narrow)
                turned.append(field.astype(narrow))
            scores = jnp.where(may, contract_last(turned[0], turned[1]) * HEAD ** (-0.5), masked_score)
            highest = jnp.max(scores, axis=-1, keepdims=True)
            unnormed = jnp.exp(scores - highest)
            shares = unnormed / jnp.sum(unnormed, axis=-1, keepdims=True)
            probs[head] = shares
            mixed = jnp.dot(shares.astype(narrow), values[:, spot], preferred_element_type=single)
            attended[:, spot] = mixed.astype(narrow)
        return carry

    lax.fori_loop(0, heads // group, some_heads, 0)
    between(1)

    def add(number, made):
        spot = pl.ds(pl.multiple_of(number * PANEL, PANEL), PANEL)
        middle[:, spot] = tokens[:, spot].astype(single) + made

    through(wo, attended, per, add)

    def last(at):
        values = middle[at]
        factor = lax.rsqrt(jnp.mean(values * values, axis=-1, keepdims=True) + epsilon)
        routed[at] = (values * factor * gains[3:4]).astype(narrow)

    slabs(last)
    between(2)


def first_gather_kernel(
    wq, wo, up, small, ein, eout, tokens, cosine, sine, allowed,
    wq_all, wo_all, up_all, small_all, win, wout, *rest
):
    made, (tokens_v, small_here, small_sem, panel, panel_sems, put_sems), sems = rest[:10], rest[20:26], rest[26:]
    results = rest[10:20]
    gains, normed, raw, queries, keys, values, probs, attended, middle, routed = results
    here = Here()
    here.meet()
    fetch_tokens = pltpu.make_async_copy(tokens, tokens_v, small_sem.at[1])
    fetch_tokens.start()
    puts = [
        pltpu.make_async_copy(source, target, put_sems.at[number])
        for number, (source, target) in enumerate(zip(results, made))
    ]
    items = [
        Gather(here, source, whole, halves, shared, sems[4 * number : 4 * number + 4])
        for number, (source, whole, halves, shared) in enumerate(
            (
                (small, small_all, halves_of(small.shape[0], False), True),
                (wq, wq_all, halves_of(wq.shape[0]), True),
                (wo, wo_all, halves_of(wo.shape[0]), True),
                (up, up_all, halves_of(up.shape[0]), False),
            )
        )
    ]
    recut = Recut(here, ein, eout, win, wout, sems[16:20])
    weights = Rounds(here, items[:3])
    rows = Rounds(here, items[3:], ring=False)
    weights.service(0, lambda: rows.line(1, ring=False))
    weights.service(1, lambda: rows.line(2, ring=False))
    recut.begin()
    weights.third(0)
    weights.service(2, lambda: rows.line(3, ring=False))
    weights.third(1)
    weights.service(3)
    rows.kept()
    for step in range(DEPTH):
        rows.ring(step)
    weights.third(2)
    weights.third(3)
    weights.finish()
    fetch = pltpu.make_async_copy(small_all, small_here, small_sem.at[0])
    fetch.start()
    fetch.wait()
    fetch_tokens.wait()
    share = wq.shape[0]
    lanes = small.shape[1]
    lane = lax.broadcasted_iota(jnp.int32, (8, lanes), 1)
    skip = small.shape[0] - 8
    for z in range(DEPTH):
        for chip in range(RING):
            pair = [small_here[z, chip, core, skip : skip + 8] for core in (0, 1)]
            both = jnp.where(lane < share, pair[0], pltpu.roll(pair[1], share, 1))
            begin = (z * RING + chip) * 2 * share
            gains[:, begin : begin + 2 * share] = both

    def between(part):
        if part == 0:
            rows.second(0)
        elif part == 1:
            for step in range(1, DEPTH):
                rows.second(step)
        else:
            for copy in puts:
                copy.start()
            recut.relay()

    attention_forward(
        tokens_v, cosine, sine, allowed, wq_all, wo_all, gains, normed, raw, queries, keys, values, probs, attended,
        middle, routed, panel, panel_sems, between
    )
    for step in range(DEPTH):
        rows.third(step)
    rows.finish()
    recut.end()
    for copy in puts:
        copy.wait()


def first_gather(wq, wo, up, small, ein, eout, tokens, cosine, sine, allowed):
    def whole(array, shared):
        lead = (DEPTH, RING, 2) if shared else (DEPTH, RING)
        return jax.ShapeDtypeStruct(lead + array.shape, array.dtype)

    held, rows, columns = ein.shape
    block, width = tokens.shape
    heads = width // HEAD
    vmem = pl.BlockSpec(memory_space=pltpu.VMEM)
    like = ((block, width), narrow)
    made = (
        ((8, width), single),
        like,
        ((2, block, width), single),
        like,
        like,
        like,
        ((heads, block, block), single),
        like,
        ((block, width), single),
        like,
    )
    return pl.pallas_call(
        first_gather_kernel,
        out_shape=(
            whole(wq, True),
            whole(wo, True),
            whole(up, False),
            whole(small, True),
            jax.ShapeDtypeStruct((DEPTH * rows, columns), ein.dtype),
            jax.ShapeDtypeStruct((2 * held,) + eout.shape[1:], eout.dtype),
            *(jax.ShapeDtypeStruct(*one) for one in made),
        ),
        in_specs=[HBM] * 7 + [vmem] * 3,
        out_specs=(HBM,) * 16,
        scratch_shapes=[pltpu.VMEM(*one) for one in made]
        + [
            pltpu.VMEM((block, width), tokens.dtype),
            pltpu.VMEM((DEPTH, RING, 2) + small.shape, single),
            pltpu.SemaphoreType.DMA((2,)),
            pltpu.VMEM((2, DEPTH, RING, 2, wq.shape[0], PANEL), narrow),
            pltpu.SemaphoreType.DMA((2,)),
            pltpu.SemaphoreType.DMA((len(made),)),
        ]
        + GATHER_SEMS * 4
        + RECUT_SEMS,
        compiler_params=pltpu.CompilerParams(
            collective_id=1, has_side_effects=True, vmem_limit_bytes=62 * 2**20
        ),
        name="bring",
    )(wq, wo, up, small, ein, eout, tokens, cosine, sine, allowed)

TILE = 256


def add_up(target, terms, rows, columns):
    high = 16 if rows % 16 == 0 else 8
    wide = min(columns, 1024)
    across = columns // wide

    def piece(number, carry):
        row = pl.multiple_of(lax.div(number, across) * high, high)
        column = pl.multiple_of(lax.rem(number, across) * wide, 128)
        spot = (pl.ds(row, high), pl.ds(column, wide))
        total = terms[0][spot].astype(single)
        for term in terms[1:]:
            total = total + term[spot].astype(single)
        target[spot] = total.astype(target.dtype)
        return carry

    lax.fori_loop(0, (rows // high) * across, piece, 0)


SUM_SEMS = [
    pltpu.SemaphoreType.DMA((2, DEPTH, 2)),
    pltpu.SemaphoreType.DMA((2, DEPTH, 2)),
    pltpu.SemaphoreType.DMA((2, 2, DEPTH)),
    pltpu.SemaphoreType.DMA((DEPTH, RING, 2)),
]


def sum_scratch(rows, columns, kind, halves, paired=False, made=False):
    high = max(size for _, size in filter(None, halves))
    kept = RING if paired or made else RING - 1
    scratch = [
        pltpu.VMEM((DEPTH, kept, rows, columns), kind),
        pltpu.VMEM((DEPTH, 2, high, columns), kind),
        pltpu.VMEM((DEPTH, 2, rows, columns), kind),
        pltpu.VMEM((DEPTH + 1, rows, columns), kind),
    ] + SUM_SEMS
    if paired:
        scratch += [pltpu.VMEM((DEPTH, RING, rows, columns), kind), pltpu.SemaphoreType.DMA((2, DEPTH, 2))]
    return scratch


class Sum:
    def __init__(self, here, sources, target, halves, paired, scratch):
        self.here, self.sources, self.halves, self.paired = here, sources, halves, paired
        self.target = target if isinstance(target, list) else [(target, 0, target.shape[0])]
        self.extra = []
        self.mine, self.half, self.full, self.column = scratch[:4]
        self.half_sem, self.full_sem, self.line_sem, self.load_sem = scratch[4:8]
        if paired:
            self.other, self.pair_sem = scratch[8:10]
        self.rows, self.columns = self.mine.shape[2:]

    def kept(self, z, turn):
        if self.sources is None:
            return self.mine.at[z, self.here.chip_at(turn)]
        return self.mine.at[z, turn if self.paired else {0: 0, 1: 1, 3: 2}[turn]]

    def raw(self, part, z, turn):
        chip = self.here.chip_at(turn)
        return part.at[z, chip, self.here.core] if self.paired else part.at[z, chip]

    def spots(self):
        at, spots = 0, []
        for part in self.sources or []:
            spots.append((part, pl.ds(at, part.shape[-1])))
            at += part.shape[-1]
        return spots

    def loads(self, z, turn):
        return [
            pltpu.make_async_copy(
                self.raw(part, z, turn), self.kept(z, turn).at[:, spot], self.load_sem.at[z, turn, number]
            )
            for number, (part, spot) in enumerate(self.spots())
        ]

    def swaps(self, z, mine):
        return [
            remote(
                part.at[z, :, 1 - self.here.core] if mine else self.other.at[z, :, :, spot],
                self.other.at[z, :, :, spot],
                self.pair_sem.at[0, z, number],
                self.pair_sem.at[1, z, number],
                self.here.sibling(),
            )
            for number, (part, spot) in enumerate(self.spots())
        ]

    def toss(self, z, way):
        if self.halves[way] is None:
            return None
        rows = pl.ds(*self.halves[way])
        loaded = self.sources is not None and not self.paired
        source = (self.raw(self.sources[0], z, 2) if loaded else self.kept(z, 2)).at[rows]
        return remote(
            source,
            self.half.at[z, way, pl.ds(0, self.halves[way][1])],
            self.half_sem.at[0, z, way],
            self.half_sem.at[1, z, way],
            self.here.beside(1 if way == 0 else -1),
        )

    def pass_on(self, z, way):
        return remote(
            self.kept(z, 1 if way == 0 else 3),
            self.full.at[z, way],
            self.full_sem.at[0, z, way],
            self.full_sem.at[1, z, way],
            self.here.beside(1 if way == 0 else -1),
        )

    def climb(self, z, way, up, slot=None):
        if slot is None:
            down_to_owner = way * (z == self.here.z - 1).astype(jnp.int32)
            slot = z + down_to_owner * (DEPTH - z)
        return remote(
            self.kept(z, 0),
            self.column.at[slot],
            self.line_sem.at[0, way, z],
            self.line_sem.at[1, way, z],
            self.here.above(2 * up - 1),
        )

    def begin(self, z):
        if self.paired:
            for copy in self.swaps(z, True):
                copy.start()
        for turn in (2, 1, 3, 0):
            if turn != 2 or self.paired:
                for copy in self.loads(z, turn):
                    copy.start()
        if not self.paired:
            for way in (0, 1):
                start(self.toss(z, way))

    def merge(self, z):
        if not self.paired:
            return
        for copy in self.swaps(z, False):
            copy.wait_recv()
        for turn in (2, 1, 3, 0):
            for copy in self.loads(z, turn):
                copy.wait()
            kept = self.kept(z, turn)
            add_up(kept, [kept, self.other.at[z, self.here.chip_at(turn)]], self.rows, self.columns)
            if turn == 2:
                for way in (0, 1):
                    start(self.toss(z, way))

    def second(self, z):
        for way, turn in ((0, 1), (1, 3)):
            if not self.paired:
                for copy in self.loads(z, turn):
                    copy.wait()
            copy = self.toss(z, way)
            if copy is not None:
                copy.wait_recv()
                begin, size = self.halves[way]
                rows = self.kept(z, turn).at[pl.ds(begin, size)]
                add_up(rows, [rows, self.half.at[z, way, pl.ds(0, size)]], size, self.columns)
        for way in (0, 1):
            self.pass_on(z, way).start()

    def third(self, z, last):
        here = self.here
        if not self.paired:
            for copy in self.loads(z, 0):
                copy.wait()
        for way in (0, 1):
            self.pass_on(z, way).wait_recv()
        kept = self.kept(z, 0)
        terms = [kept, self.full.at[z, 0], self.full.at[z, 1]]
        if last:
            self.arrive(z, terms)
            return
        up = (z > here.z).astype(jnp.int32)
        way = 1 - up
        follows = up * here.z + way * (DEPTH - 1 - here.z)

        @pl.when(follows > 0)
        def _():
            self.climb(z, way, up, z).wait_recv()
            add_up(kept, terms + [self.column.at[z]], self.rows, self.columns)

        @pl.when(follows == 0)
        def _():
            add_up(kept, terms, self.rows, self.columns)

        self.climb(z, way, up).start()

    def own_part(self, z):
        for way in (0, 1):
            self.pass_on(z, way).wait_recv()
        [(target, _, rows)] = self.target
        add_up(target, [self.kept(z, 0), self.full.at[z, 0], self.full.at[z, 1]], rows, self.columns)

    def own_rest(self, z):
        self.arrive(z, [self.target[0][0]])

    def arrive(self, z, terms):
        here = self.here
        below, above = self.column.at[z], self.column.at[DEPTH]

        def total(more):
            for target, row, rows in self.target:
                part = [term.at[pl.ds(row, rows)] for term in terms + more + self.extra]
                add_up(target, part, rows, self.columns)

        @pl.when(here.z == 0)
        def _():
            self.climb(z, 1, 0, DEPTH).wait_recv()
            total([above])

        @pl.when(here.z == DEPTH - 1)
        def _():
            self.climb(z, 0, 0, z).wait_recv()
            total([below])

        @pl.when((here.z > 0) & (here.z < DEPTH - 1))
        def _():
            self.climb(z, 0, 0, z).wait_recv()
            self.climb(z, 1, 0, DEPTH).wait_recv()
            total([below, above])

    def end(self, z, last):
        if self.paired:
            for copy in self.swaps(z, True):
                copy.wait_send()
        for way in (0, 1):
            copy = self.toss(z, way)
            if copy is not None:
                copy.wait_send()
            self.pass_on(z, way).wait_send()
        if not last:
            up = (z > self.here.z).astype(jnp.int32)
            self.climb(z, 1 - up, up).wait_send()


def far_first(here, number):
    high = lax.div(here.z, 2)
    inner = lax.rem(lax.div(here.z + 1, 2), 2)
    low = (DEPTH - 1 - number) + inner * (0, -2, 1, 1)[number]
    return low + high * (DEPTH - 1 - 2 * low)


class Share:
    def __init__(self, here, source, target, side, sems):
        self.here, self.source, self.target, self.side, self.sems = here, source, target, side, sems
        self.held, self.rows, columns = target.shape
        self.part = columns // (2 * DEPTH)

    def pieces(self, steps, arriving, only=None):
        here = self.here
        origin = lax.rem(here.z + DEPTH - steps, DEPTH) if arriving else here.z
        away = lax.rem(here.z + steps, DEPTH)
        copies = []
        for expert in range(self.held):
            if only not in (None, expert):
                continue
            column = (self.side * DEPTH + origin) * self.part
            target = self.target.at[expert, :, pl.ds(pl.multiple_of(column, 128), self.part)]
            source = self.source.at[
                pl.ds(pl.multiple_of(away * self.rows, 16), self.rows),
                pl.ds((self.side * self.held + expert) * self.part, self.part),
            ]
            if isinstance(steps, int) and steps == 0:
                copies.append(pltpu.make_async_copy(source, target, self.sems.at[0, 0, expert]))
            else:
                sems = (self.sems.at[0, steps, expert], self.sems.at[1, steps, expert])
                copies.append(remote(target if arriving else source, target, *sems, here.above(steps)))
        return copies

    def begin(self):
        for copy in self.pieces(0, False):
            copy.start()
        inner_first(self.here, self.held, lambda steps, number: self.pieces(steps, False, number)[0].start())

    def end(self):
        for steps in range(DEPTH):
            for copy in self.pieces(steps, False):
                copy.wait() if steps == 0 else copy.wait_send()
            if steps:
                for copy in self.pieces(steps, True):
                    copy.wait_recv()


STRIP = 128


def last_sum_kernel(
    normed,
    attended,
    gin_sum,
    weight,
    weight_out,
    tokens,
    routed,
    upstream,
    middle,
    raw,
    queries,
    keys,
    values,
    probs,
    cosine,
    sine,
    gains,
    q_sum,
    o_sum,
    gain_sums,
    grad_tokens,
    share_in,
    *scratch,
):
    here = Here()
    here.meet()
    block, width = tokens.shape
    share = q_sum.shape[0]
    wide = q_sum.shape[1]
    sides = wide // width
    heads = width // HEAD
    (
        left, left_out, right, panel, x, routed_v, upstream_v, middle_v, raw_v, queries_v, keys_v, values_v, probs_v,
        grad_middle, grad_heads, turned, piece, few_sum, few_other, sems, panel_sems, pair_sems, share_sems
    ) = scratch[:23]
    big = Sum(
        here,
        None,
        [(q_sum.at[:, pl.ds(side * width, width)], side * share, share) for side in range(sides)],
        halves_of(sides * share),
        False,
        scratch[23:31],
    )
    outer = Sum(here, None, o_sum, halves_of(share), False, scratch[31:39])
    few = Sum(here, None, few_sum, halves_of(few_sum.shape[0], False), False, scratch[39:47])
    order = [far_first(here, number) for number in range(DEPTH)]
    loads = [
        pltpu.make_async_copy(source, target, sems.at[number])
        for number, (source, target) in enumerate(
            (
                (middle, middle_v),
                (routed, routed_v),
                (upstream, upstream_v),
                (attended, left_out.at[0]),
                (values, values_v),
                (probs, probs_v),
                (queries, queries_v),
                (keys, keys_v),
                (raw, raw_v),
                (normed, left.at[0]),
                (tokens, x),
            )
        )
    ]

    def fetch(source, number, columns):
        slot = lax.rem(number, 2)
        rows = pl.ds(pl.multiple_of(number * STRIP, STRIP), STRIP)
        return pltpu.make_async_copy(source.at[rows], panel.at[slot, :, pl.ds(0, columns)], panel_sems.at[slot])

    for copy in loads:
        copy.start()
    fetch(weight_out, 0, width).start()
    shares_in = [Share(here, gin_sum, share_in, side, share_sems.at[side]) for side in range(2)]
    for share_side in shares_in:
        share_side.begin()

    def swap(number, source, target):
        base = 16 + 2 * number
        return remote(source, target, sems.at[base], sems.at[base + 1], here.sibling())

    side_out = pl.ds(wide, width)
    side_qkv = pl.ds(0, wide)
    swaps = [
        swap(0, left_out.at[0], left_out.at[1]),
        swap(1, right.at[0, :, side_out], right.at[1, :, side_out]),
        swap(2, left.at[0], left.at[1]),
        swap(3, right.at[0, :, side_qkv], right.at[1, :, side_qkv]),
    ]
    high = 16
    panels = width // STRIP

    def slabs(body):
        def one(number, carry):
            body(pl.ds(pl.multiple_of(number * high, high), high))
            return carry

        lax.fori_loop(0, block // high, one, 0)

    def norm(values):
        factor = lax.rsqrt(jnp.mean(values * values, axis=-1, keepdims=True) + epsilon)
        return values * factor, factor

    def norm_grad(up, values, row):
        normal, factor = norm(values)
        weighted = up * gains[row : row + 1]
        inner = jnp.mean(weighted * normal, axis=-1, keepdims=True)
        piece[row : row + 1] += jnp.sum(up * normal, axis=0, keepdims=True)
        return factor * (weighted - normal * inner)

    def first(at):
        grad = upstream_v[at].astype(single) + norm_grad(routed_v[at], middle_v[at], 3)
        grad_middle[at] = grad
        right[0, at, side_out] = grad.astype(narrow)

    piece[...] = jnp.zeros_like(piece)
    for number in range(4):
        loads[number].wait()
    swaps[0].start()
    slabs(first)
    swaps[1].start()

    def through(source, columns, left_rows, finish, begin=0, end=panels):
        def one(number, carry):
            fetch(source, number, columns).wait()
            pl.when(number + 1 < panels)(lambda: fetch(source, number + 1, columns).start())
            rows = panel[lax.rem(number, 2), :, 0:columns]
            finish(pl.ds(pl.multiple_of(number * STRIP, STRIP), STRIP), contract_last(left_rows, rows))
            return carry

        lax.fori_loop(begin, end, one, 0)

    def keep_heads(spot, made):
        grad_heads[:, spot] = made.astype(narrow)

    step = 512
    each = width // step
    rows = RING * 2 * share

    def make(z, item, source, first_chunk, last_chunk):
        at = pl.ds(pl.multiple_of(z * rows, rows), rows)

        def one(number, carry):
            spot = pl.ds(pl.multiple_of(number * step, step), step)
            left_rows = source[:, :, at].reshape(2 * block, rows)
            made = contract_rows(left_rows, right[:, :, spot].reshape(2 * block, step))
            made = made.reshape(RING, 2, share, step)
            mine = jnp.where(here.core == 0, made[:, 0], made[:, 1]).astype(narrow)
            row = pl.multiple_of(lax.div(number - first_chunk, each) * share, share)
            column = pl.multiple_of(lax.rem(number, each) * step, step)
            for chip in range(RING):
                item.mine[z, chip, pl.ds(row, share), pl.ds(column, step)] = mine[chip]
            return carry

        lax.fori_loop(first_chunk, last_chunk, one, 0)

    swaps[0].wait_recv()
    swaps[1].wait_recv()
    for z in order:
        make(z, outer, left_out, sides * each, (sides + 1) * each)
        for way in (0, 1):
            start(outer.toss(z, way))
    through(weight_out, width, right[0, :, side_out], keep_heads)
    fetch(weight, 0, wide).start()
    for number in range(4, len(loads)):
        loads[number].wait()
    swaps[2].start()
    turn_cos, turn_sin = cosine[...], sine[...]
    group = 4

    def some_heads(number, carry):
        for inner in range(group):
            head = number * group + inner
            spot = pl.ds(pl.multiple_of(head * HEAD, HEAD), HEAD)
            grad = grad_heads[:, spot]
            shares = probs_v[head]
            grad_shares = contract_last(grad, values_v[:, spot])
            along = jnp.sum(grad_shares * shares, axis=-1, keepdims=True)
            scores = (shares * (grad_shares - along)).astype(narrow)
            made = (
                jnp.dot(scores, keys_v[:, spot], preferred_element_type=single),
                contract_rows(scores, queries_v[:, spot]),
            )
            for side, field in enumerate(made):
                field = field * HEAD ** (-0.5)
                turned[side, :, spot] = field * turn_cos - pltpu.roll(field, HEAD // 2, 1) * turn_sin
            spot_v = pl.ds(pl.multiple_of(2 * width + head * HEAD, HEAD), HEAD)
            right[0, :, spot_v] = contract_rows(shares.astype(narrow), grad).astype(narrow)
        return carry

    lax.fori_loop(0, heads // group, some_heads, 0)

    def second(at):
        for side in range(2):
            grad = norm_grad(turned[side, at], raw_v[side, at], side + 1)
            right[0, at, side * width : (side + 1) * width] = grad.astype(narrow)

    for z in order[:2]:
        outer.second(z)
    slabs(second)
    swaps[3].start()
    for z in order[2:]:
        outer.second(z)
    swaps[2].wait_recv()
    swaps[3].wait_recv()

    def keep_back(spot, made):
        routed_v[:, spot] = made

    def third(at):
        grad_tokens[at] = grad_middle[at] + norm_grad(routed_v[at], x[at].astype(single), 0)

    for number, z in enumerate(order):
        make(z, big, left, 0, sides * each)
        for way in (0, 1):
            start(big.toss(z, way))
        if number:
            big.second(order[number - 1])
        outer.third(z, number == DEPTH - 1)
        if number > 1:
            big.third(order[number - 2], False)
        cut = panels // DEPTH
        through(weight, wide, right[0, :, side_qkv], keep_back, number * cut, (number + 1) * cut)
        if number == DEPTH - 1:
            slabs(third)
            for plane in range(DEPTH):
                for chip in range(RING):
                    begin = (plane * RING + chip) * 2 * share
                    few.mine[plane, chip] = piece[:, begin : begin + 2 * share]
            for place in order:
                start(few.toss(place, 0))
    big.second(order[-1])
    for z in order:
        few.second(z)
    big.third(order[-2], False)
    for z in order[:-1]:
        few.third(z, False)
    big.third(order[-1], True)
    few.third(order[-1], True)
    pair = remote(few_sum, few_other, pair_sems.at[0], pair_sems.at[1], here.sibling())
    pair.start()
    pair.wait_recv()
    gain_sums[...] = few_sum[...] + few_other[...]
    pair.wait_send()
    for number, z in enumerate(order):
        for item in (big, outer, few):
            item.end(z, number == DEPTH - 1)
    for copy in swaps:
        copy.wait_send()
    for share_side in shares_in:
        share_side.end()


def last_sum(
    normed, attended, gin_sum, weight, weight_out, tokens, routed, upstream, middle, raw, queries, keys, values, probs,
    cosine, sine, gains, share, held
):
    block, width = normed.shape
    wide = weight.shape[1]
    sides = wide // width
    vmem = pl.BlockSpec(memory_space=pltpu.VMEM)
    few = (gains.shape[0], 2 * share)
    like = pltpu.VMEM((block, width), narrow)
    like_single = pltpu.VMEM((block, width), single)
    return pl.pallas_call(
        last_sum_kernel,
        out_shape=(
            jax.ShapeDtypeStruct((share, wide), single),
            jax.ShapeDtypeStruct((share, width), single),
            jax.ShapeDtypeStruct(few, single),
            jax.ShapeDtypeStruct((block, width), single),
            jax.ShapeDtypeStruct((held, gin_sum.shape[0] // DEPTH, DEPTH * gin_sum.shape[1] // held), narrow),
        ),
        in_specs=[HBM] * 14 + [vmem] * 3,
        out_specs=(vmem, vmem, vmem, vmem, HBM),
        scratch_shapes=[
            pltpu.VMEM((2, block, width), narrow),
            pltpu.VMEM((2, block, width), narrow),
            pltpu.VMEM((2, block, wide + width), narrow),
            pltpu.VMEM((2, STRIP, wide), narrow),
            like,
            like_single,
            like,
            like_single,
            pltpu.VMEM(raw.shape, single),
            like,
            like,
            like,
            pltpu.VMEM(probs.shape, single),
            like_single,
            like,
            pltpu.VMEM((2, block, width), single),
            pltpu.VMEM(gains.shape, single),
            pltpu.VMEM(few, single),
            pltpu.VMEM(few, single),
            pltpu.SemaphoreType.DMA((24,)),
            pltpu.SemaphoreType.DMA((2,)),
            pltpu.SemaphoreType.DMA((2,)),
            pltpu.SemaphoreType.DMA((2, 2, DEPTH, held)),
        ]
        + sum_scratch(sides * share, width, narrow, halves_of(sides * share), made=True)
        + sum_scratch(share, width, narrow, halves_of(share), made=True)
        + sum_scratch(few[0], few[1], single, halves_of(few[0], False), made=True),
        compiler_params=pltpu.CompilerParams(
            collective_id=4, has_side_effects=True, vmem_limit_bytes=62 * 2**20
        ),
        name="deliver",
    )(
        normed, attended, gin_sum, weight, weight_out, tokens, routed, upstream, middle, raw, queries, keys, values, probs,
        cosine, sine, gains
    )

def near_first(here, number):
    high = lax.div(here.z, 2)
    inner = lax.rem(lax.div(here.z + 1, 2), 2)
    low = number + inner * (1, -1, 0, 0)[number]
    return low + high * (DEPTH - 1 - 2 * low)


class Tiles:
    def __init__(self, here, stage, count, sems, parts, targets):
        self.here, self.stage, self.count = here, stage, count
        self.kept, self.sent, self.came = sems
        self.parts, self.targets = parts, targets

    def copies(self, number, keep=True, give=True):
        slot = lax.rem(number, 2)
        own, other = self.targets
        made = []
        for piece, (mine, theirs, spot) in enumerate(self.parts(number, self.stage.at[slot])):
            if keep:
                made.append(pltpu.make_async_copy(mine, own.at[spot], self.kept.at[slot, piece]))
            if give:
                sems = (self.sent.at[slot, piece], self.came.at[number, piece])
                made.append(remote(theirs, other.at[spot], *sems, self.here.sibling()))
        return made

    def settle(self, number):
        for copy in self.copies(number, give=False):
            copy.wait()
        for copy in self.copies(number, keep=False):
            copy.wait_send()

    def run(self, first, last, make):
        def body(number, carry):
            pl.when(number >= 2)(lambda: self.settle(number - 2))
            make(number, self.stage.at[lax.rem(number, 2)])
            for copy in self.copies(number):
                copy.start()
            return carry

        lax.fori_loop(first, last, body, 0)
        if last == self.count:
            for number in (last - 2, last - 1):
                self.settle(number)

    def heard(self):
        for number in range(self.count):
            for copy in self.copies(number, keep=False):
                copy.wait_recv()


def experts_kernel(
    rows, ups, gates, win, wout, middle, mid_sum, gate_sum, out_sum, gin_sum, gdown, gdown_other, gin, gin_other, rows_all, *scratch
):
    here = Here()
    here.meet()
    (
        w_in, w_out, grads, scaled, row_plane, up_plane, gate_plane, served, strip, stage, loads, strip_sems
    ) = scratch[:12]
    gather = Gather(here, rows, rows_all, halves_of(rows.shape[0]), False, scratch[12:16])
    mids = Sum(here, None, mid_sum, halves_of(rows.shape[0]), False, scratch[16:24])
    outs = Sum(here, None, out_sum, halves_of(rows.shape[0]), False, scratch[16:19] + scratch[24:29])
    fetch_middle = pltpu.make_async_copy(middle, scratch[45], scratch[46].at[0])
    fetch_middle.start()
    outs.extra = [scratch[45]]
    tables = Sum(here, None, gate_sum, halves_of(gate_sum.shape[0], False), False, scratch[29:37])
    in_sems, down_sems = scratch[37:40], scratch[40:43]
    block, width = rows.shape
    plane = RING * block
    hidden = w_out.shape[0]
    chunk = hidden // 4
    column = lax.broadcasted_iota(jnp.int32, (plane, 128), 1)
    fetch_in = pltpu.make_async_copy(win, w_in, loads.at[0])
    fetch_out = pltpu.make_async_copy(wout, w_out, loads.at[1])
    fetch_in.start()
    fetch_out.start()

    def fetch_plane(number):
        z = near_first(here, number)
        return (
            pltpu.make_async_copy(ups.at[z], up_plane.at[number % 2], loads.at[2 + number % 2]),
            pltpu.make_async_copy(gates.at[z], gate_plane.at[number % 2], loads.at[4 + number % 2]),
        )

    def fetch_rows(number):
        return pltpu.make_async_copy(rows_all.at[near_first(here, number)], row_plane, loads.at[6])

    def hidden_units(number):
        z = near_first(here, number)
        fetch_rows(number).start()
        for copy in fetch_plane(number):
            copy.wait()
        if number == 0:
            fetch_in.wait()
            fetch_out.wait()
        fetch_rows(number).wait()
        served[...] = jnp.zeros_like(served)
        at = pl.ds(pl.multiple_of(z * plane, plane), plane)

        def one(expert, carry):
            mid = row_plane[...].reshape(plane, width)
            up_rows = up_plane[number % 2]
            spot = pl.ds(pl.multiple_of(expert * chunk, chunk), chunk)
            spot_up = pl.ds(pl.multiple_of(hidden + expert * chunk, chunk), chunk)
            gate = jnp.sum(jnp.where(column == expert, gate_plane[number % 2], 0.0), axis=1, keepdims=True)
            gate_part = jnp.dot(mid, w_in[:, spot], preferred_element_type=single)
            up_part = jnp.dot(mid, w_in[:, spot_up], preferred_element_type=single)
            back = contract_last(up_rows, w_out[spot])
            sigmoid = 1.0 / (1.0 + jnp.exp(-gate_part))
            activated = gate_part * sigmoid
            units = activated * up_part
            scaled[at, spot] = (gate * units).astype(narrow)
            total = jnp.sum(units * back, axis=1, keepdims=True)
            served[...] += jnp.where(column == here.chip * 4 + expert, total, 0.0)
            grad = gate * back
            grads[at, spot] = (grad * up_part * (sigmoid * (1.0 + gate_part * (1.0 - sigmoid)))).astype(narrow)
            grads[at, spot_up] = (grad * activated).astype(narrow)
            return carry

        lax.fori_loop(0, 4, one, 0)
        for chip in range(RING):
            turned = jnp.transpose(served[chip * block : (chip + 1) * block])
            tables.mine[z, chip] = turned[: tables.rows]

    def row_grads(z):
        at = pl.ds(pl.multiple_of(z * plane, plane), plane)

        def one(number, carry):
            spot = pl.ds(pl.multiple_of(number * TILE, TILE), TILE)
            made = contract_last(grads[at], w_in[spot]).astype(narrow)
            for chip in range(RING):
                mids.mine[z, chip, :, spot] = made[chip * block : (chip + 1) * block]
            return carry

        lax.fori_loop(0, width // TILE, one, 0)

    def products(z):
        at = pl.ds(pl.multiple_of(z * plane, plane), plane)

        def one(number, carry):
            spot = pl.ds(pl.multiple_of(number * TILE, TILE), TILE)
            made = jnp.dot(scaled[at], w_out[:, spot], preferred_element_type=single).astype(narrow)
            for chip in range(RING):
                outs.mine[z, chip, :, spot] = made[chip * block : (chip + 1) * block]
            return carry

        lax.fori_loop(0, width // TILE, one, 0)

    strips = width // TILE

    def fetch_strip(number):
        spot = pl.ds(pl.multiple_of(number * TILE, TILE), TILE)
        slot = lax.rem(number, 2)
        return pltpu.make_async_copy(rows_all.at[:, :, :, spot], strip.at[slot], strip_sems.at[slot])

    def columns_of(result, stage, step=512):
        for begin in range(0, width, step):
            stage[:, begin : begin + step] = result(begin, step).astype(narrow)

    def grad_in(number, stage):
        slot = lax.rem(number, 2)
        fetch_strip(number).wait()
        pl.when(number + 1 < strips)(lambda: fetch_strip(number + 1).start())
        left = strip[slot].reshape(DEPTH * plane, TILE)
        columns_of(lambda begin, step: contract_rows(left, grads[:, begin : begin + step]), stage)

    def grad_in_parts(number, stage):
        share = hidden // 2
        at = pl.ds(pl.multiple_of(number * TILE, TILE), TILE)
        for side in range(2):
            mine, theirs = (
                stage.at[:, pl.ds(pl.multiple_of(side * hidden + core * share, 128), share)]
                for core in (here.core, 1 - here.core)
            )
            yield mine, theirs, (at, pl.ds(side * share, share))

    def grad_down(number, stage):
        half = tall // 2
        core = here.core + (1 - lax.div(number, half)) * (1 - 2 * here.core)
        at = core * half + lax.rem(number, half)
        left = scaled[:, pl.ds(pl.multiple_of(at * TILE, TILE), TILE)]
        columns_of(lambda begin, step: contract_rows(left, w_in[:, begin : begin + step]), stage)

    tall = hidden // TILE
    tiles_in = Tiles(here, stage, strips, in_sems, grad_in_parts, (gin, gin_other))

    def grad_down_store(number, away):
        slot = lax.rem(number, 2)
        rest = lax.rem(number, tall // 2)
        spot = pl.ds(pl.multiple_of(rest * TILE, TILE), TILE)
        kept, sent, came = down_sems
        if away:
            return remote(stage.at[slot], gdown_other.at[spot], sent.at[slot, 0], came.at[rest, 0], here.sibling())
        return pltpu.make_async_copy(stage.at[slot], gdown.at[spot], kept.at[slot, 0])

    def grads_down(away):
        first = 0 if away else tall // 2

        def body(number, carry):
            grad_down(number, stage.at[lax.rem(number, 2)])
            grad_down_store(number, away).start()
            return carry

        lax.fori_loop(first, first + tall // 2, body, 0)
        for number in range(first, first + tall // 2):
            copy = grad_down_store(number, away)
            copy.wait_send() if away else copy.wait()

    def add_cores():
        half = hidden
        adds, puts = scratch[43], scratch[44]

        def fetch(number):
            slot = lax.rem(number, 2)
            at = pl.ds(pl.multiple_of(number * TILE, TILE), TILE)
            return [
                pltpu.make_async_copy(
                    source.at[at], stage.at[slot, :, pl.ds(side * half, half)], adds.at[slot, side]
                )
                for side, source in enumerate((gin, gin_other))
            ]

        def put(number):
            slot = lax.rem(number, 2)
            at = pl.ds(pl.multiple_of(number * TILE, TILE), TILE)
            return pltpu.make_async_copy(stage.at[slot, :, pl.ds(0, half)], gin_sum.at[at], puts.at[slot])

        def start_fetch(number):
            for copy in fetch(number):
                copy.start()

        def body(number, carry):
            for copy in fetch(number):
                copy.wait()
            pl.when(number >= 1)(lambda: put(number - 1).wait())
            pl.when(number + 1 < strips)(lambda: start_fetch(number + 1))
            slot = lax.rem(number, 2)
            own = stage.at[slot, :, pl.ds(0, half)]
            add_up(own, [own, stage.at[slot, :, pl.ds(half, half)]], TILE, half)
            put(number).start()
            return carry

        start_fetch(0)
        lax.fori_loop(0, strips, body, 0)
        put(strips - 1).wait()

    again = [
        pltpu.make_async_copy(ups.at[z], w_in.at[pl.ds(z * plane, plane)], loads.at[7 + z]) for z in range(DEPTH)
    ]

    def again_wait():
        for copy in again:
            copy.wait()

    order = [far_first(here, number) for number in range(DEPTH)]
    first = [mids, tables]
    steps = [(first, z, False) for z in [here.z] + order[:-1]]
    steps += [([outs], z, number == DEPTH - 1) for number, z in enumerate(order)]

    def begin(number):
        items, z, last = steps[number]
        if number < DEPTH:
            row_grads(z)
        else:
            mids.end(z, last)
            products(z)
        for item in items:
            for way in (0, 1):
                start(item.toss(z, way))

    def second(number):
        for item in steps[number][0]:
            item.second(steps[number][1])

    def third(number):
        items, z, last = steps[number]
        for item in items:
            item.own_part(z) if number == 0 else item.third(z, last)

    for copy in fetch_plane(0):
        copy.start()
    rounds = Rounds(here, [gather])
    rounds.service(0)
    for number in range(DEPTH):
        if number + 1 < DEPTH:
            rounds.service(number + 1)
        if number == DEPTH - 1:
            second(0)
        gather_third(gather, near_first(here, number))
        if number + 1 < DEPTH:
            for copy in fetch_plane(number + 1):
                copy.start()
        hidden_units(number)
        if number == 1:
            begin(0)
    fetch_strip(0).start()
    ends = [0] + [strips * (number + 1) // (DEPTH - 1) for number in range(DEPTH - 1)]
    for number in range(1, 2 * DEPTH):
        begin(number)
        if number > 1:
            second(number - 1)
            third(number - 2)
        if number == DEPTH - 1:
            for copy in again:
                copy.start()
        if number < DEPTH:
            tiles_in.run(ends[number - 1], ends[number], grad_in)
        elif number == DEPTH:
            again_wait()
            grads_down(True)
        elif number == DEPTH + 1:
            grads_down(False)
        elif number == DEPTH + 2:
            for item in first:
                item.own_rest(here.z)
            tiles_in.heard()
            add_cores()
    outs.second(order[-1])
    outs.third(order[-2], False)
    fetch_middle.wait()
    outs.third(order[-1], True)
    for number, z in enumerate(order):
        outs.end(z, number == DEPTH - 1)
        tables.end(z, number == DEPTH - 1)
    for number in range(tall // 2):
        grad_down_store(number, True).wait_recv()
    rounds.finish()


def experts_round(rows, ups, gates, win, wout, middle, experts):
    block, width = rows.shape
    plane = RING * block
    hidden = wout.shape[0]
    total = DEPTH * plane
    vmem = pl.BlockSpec(memory_space=pltpu.VMEM)
    return pl.pallas_call(
        experts_kernel,
        out_shape=(
            jax.ShapeDtypeStruct((block, width), single),
            jax.ShapeDtypeStruct((experts, block), single),
            jax.ShapeDtypeStruct((block, width), narrow),
            jax.ShapeDtypeStruct((width, hidden), narrow),
            jax.ShapeDtypeStruct((hidden // 2, width), narrow),
            jax.ShapeDtypeStruct((hidden // 2, width), narrow),
            jax.ShapeDtypeStruct((width, hidden), narrow),
            jax.ShapeDtypeStruct((width, hidden), narrow),
            jax.ShapeDtypeStruct((DEPTH, RING, block, width), narrow),
        ),
        in_specs=[HBM] * 6,
        out_specs=(vmem, vmem, vmem) + (HBM,) * 6,
        scratch_shapes=[
            pltpu.VMEM((width, 2 * hidden), narrow),
            pltpu.VMEM((hidden, width), narrow),
            pltpu.VMEM((total, 2 * hidden), narrow),
            pltpu.VMEM((total, hidden), narrow),
            pltpu.VMEM((RING, block, width), narrow),
            pltpu.VMEM((2, plane, width), narrow),
            pltpu.VMEM((2, plane, 128), single),
            pltpu.VMEM((plane, 128), single),
            pltpu.VMEM((2, DEPTH, RING, block, TILE), narrow),
            pltpu.VMEM((2, TILE, width), narrow),
            pltpu.SemaphoreType.DMA((11,)),
            pltpu.SemaphoreType.DMA((2,)),
        ]
        + GATHER_SEMS
        + sum_scratch(block, width, narrow, halves_of(block), made=True)
        + [pltpu.VMEM((DEPTH + 1, block, width), narrow)]
        + SUM_SEMS
        + sum_scratch(experts, block, single, halves_of(experts, False), made=True)
        + [
            pltpu.SemaphoreType.DMA((2, 2)),
            pltpu.SemaphoreType.DMA((2, 2)),
            pltpu.SemaphoreType.DMA((width // TILE, 2)),
        ]
        + [
            pltpu.SemaphoreType.DMA((2, 1)),
            pltpu.SemaphoreType.DMA((2, 1)),
            pltpu.SemaphoreType.DMA((hidden // TILE, 1)),
        ]
        + [pltpu.SemaphoreType.DMA((2, 2)), pltpu.SemaphoreType.DMA((2,))]
        + [pltpu.VMEM((block, width), single), pltpu.SemaphoreType.DMA((1,))],
        compiler_params=pltpu.CompilerParams(
            collective_id=2, has_side_effects=True, vmem_limit_bytes=62 * 2**20
        ),
        name="experts",
    )(rows, ups, gates, win, wout, middle)


def by_kernels():
    return lax.axis_size("dp") == DEPTH and lax.axis_size("expert") == 2 * RING


def forward(tokens, gains, weight_qkv, weight_out, cosine, sine, allowed):
    rows, width = tokens.shape
    inputs = tokens.astype(single)
    normed_in = (normalize(inputs)[0] * gains[0]).astype(narrow)
    projected = jnp.dot(normed_in, weight_qkv, preferred_element_type=single)
    raw = jnp.stack([projected[:, :width], projected[:, width : 2 * width]])
    query_rows, key_rows = (
        rotate(normalize(raw[side])[0] * gains[side + 1], cosine, sine).astype(narrow) for side in range(2)
    )
    value_rows = projected[:, 2 * width :].astype(narrow)
    by_head = (rows, -1, HEAD)
    scores = jnp.einsum(
        "qhd,khd->hqk", query_rows.reshape(by_head), key_rows.reshape(by_head), preferred_element_type=single
    )
    scores = jnp.where(allowed[None], scores * HEAD ** (-0.5), masked_score)
    unnormed = jnp.exp(scores - jnp.max(scores, axis=-1, keepdims=True))
    probs = unnormed / jnp.sum(unnormed, axis=-1, keepdims=True)
    attended = jnp.einsum(
        "hqk,khd->qhd", probs.astype(narrow), value_rows.reshape(by_head), preferred_element_type=single
    )
    attended = attended.reshape(rows, width).astype(narrow)
    middle = inputs + jnp.dot(attended, weight_out, preferred_element_type=single)
    routed_in = (normalize(middle)[0] * gains[3]).astype(narrow)
    return (normed_in, raw, query_rows, key_rows, value_rows, probs, attended, middle, routed_in)


def wide_tables(cosine, sine):
    return (
        jnp.concatenate([cosine[:, 0], cosine[:, 0]], axis=1),
        jnp.concatenate([-sine[:, 0], sine[:, 0]], axis=1),
    )


def bring_all(w_qkv, w_out, upstream, dense, gain_rows, expert_in, expert_out, tokens, cosine, sine, allowed):
    width = upstream.shape[1]
    share = gain_rows.shape[1]
    if by_kernels():
        experts, rows = dense.shape[1], dense.shape[0]
        small = jnp.concatenate([dense.T, jnp.pad(gain_rows, ((0, 4), (0, rows - share)))], axis=0)
        tables = (*wide_tables(cosine, sine), allowed.astype(single))
        wq, wo, up, all_small, weight_in, weight_down, gains, *made = first_gather(
            w_qkv, w_out, upstream, small, expert_in, expert_out, tokens, *tables
        )
        core = lax.rem(lax.axis_index("expert"), 2)
        every_gate = lax.dynamic_index_in_dim(all_small, core, axis=2, keepdims=False)[:, :, :experts]
        return (
            wq.reshape(-1, w_qkv.shape[1]),
            wo.reshape(-1, w_out.shape[1]),
            up.reshape(-1, width),
            every_gate,
            gains,
            weight_in,
            weight_down.reshape(-1, width),
            made,
        )
    everyone = ("dp", "expert")
    weight_in, weight_down = fetch_weights(expert_in, expert_out)
    weight_qkv = lax.all_gather(w_qkv, everyone, axis=0, tiled=True)
    weight_out = lax.all_gather(w_out, everyone, axis=0, tiled=True)
    gains = lax.all_gather(gain_rows, everyone, axis=1, tiled=True)
    return (
        weight_qkv,
        weight_out,
        gather_alike(upstream).reshape(-1, width),
        gather_alike(dense.T),
        gains,
        weight_in,
        weight_down,
        forward(tokens, gains, weight_qkv, weight_out, cosine, sine, allowed),
    )


def experts_all(middle, routed_in, up_rows, every_gate, weight_in, weight_down, held):
    depth = lax.axis_size("dp")
    owners = lax.axis_size("expert")
    chips = owners // 2
    experts = owners * held
    chip_experts = 2 * held
    rows, width = routed_in.shape
    chip = lax.axis_index("expert") // 2
    mine = lax.dynamic_slice_in_dim(every_gate, chip * chip_experts, chip_experts, axis=2)
    gate = mine.transpose(0, 1, 3, 2)
    if by_kernels():
        gate = jnp.pad(gate.reshape(DEPTH, -1, chip_experts), ((0, 0), (0, 0), (0, 128 - chip_experts)))
        ups = up_rows.reshape(DEPTH, -1, width)
        grad_routed, table, results, grad_in, grad_down, grad_down_other = experts_round(
            routed_in, ups, gate, weight_in, weight_down, middle, experts
        )[:6]
        down = grad_down.astype(single) + grad_down_other.astype(single)
        return (results, grad_routed, table, (grad_in, down.reshape(held, -1, width)))
    mid_rows = gather_alike(routed_in).reshape(-1, width)
    out, mid, served, grad_in, grad_down = expert_rounds(
        mid_rows, up_rows, gate.reshape(-1, chip_experts), weight_in, weight_down
    )
    by_gate = served.reshape(depth, chips, rows, chip_experts).transpose(0, 1, 3, 2)
    spread = jnp.zeros((depth, chips, experts, rows), single)
    spread = lax.dynamic_update_slice_in_dim(spread, by_gate, chip * chip_experts, axis=2)
    mixture = scatter_alike(out.reshape(depth, chips, rows, width)).astype(single)
    return (
        (middle + mixture).astype(narrow),
        scatter_alike(mid.reshape(depth, chips, rows, width)).astype(single),
        scatter_alike(spread),
        return_weights(grad_in, grad_down, held),
    )


def backward(
    tokens, gains, grad_routed, upstream, normed, raw, queries, keys, values, probs, attended, middle, weight_qkv, weight_out,
    cosine, sine
):
    rows, width = tokens.shape
    by_head = (rows, -1, HEAD)
    grad_mid, piece_ffn = rms_back(grad_routed, *normalize(middle), gains[3])
    grad_middle = upstream.astype(single) + grad_mid
    branch = grad_middle.astype(narrow)
    grad_heads = contract_last(branch, weight_out).astype(narrow).reshape(by_head)
    grad_probs = jnp.einsum("qhd,khd->hqk", grad_heads, values.reshape(by_head), preferred_element_type=single)
    inner = jnp.sum(grad_probs * probs, axis=-1, keepdims=True)
    grad_scores = (probs * (grad_probs - inner)).astype(narrow)
    grads = (
        jnp.einsum("hqk,khd->qhd", grad_scores, keys.reshape(by_head), preferred_element_type=single),
        jnp.einsum("hqk,qhd->khd", grad_scores, queries.reshape(by_head), preferred_element_type=single),
    )
    grad_value = jnp.einsum("hqk,qhd->khd", probs.astype(narrow), grad_heads, preferred_element_type=single)
    (grad_q, piece_query), (grad_k, piece_key) = (
        rms_back(
            rotate(grads[side].reshape(rows, width) * HEAD ** (-0.5), cosine, -sine),
            *normalize(raw[side]),
            gains[side + 1],
        )
        for side in range(2)
    )
    grad_qkv = jnp.concatenate([grad_q, grad_k, grad_value.reshape(rows, width)], axis=1).astype(narrow)
    grad_input, piece_attn = rms_back(
        contract_last(grad_qkv, weight_qkv), *normalize(tokens.astype(single)), gains[0]
    )
    pieces = jnp.stack([piece_attn, piece_query, piece_key, piece_ffn])
    return (grad_middle + grad_input, pieces, (normed, grad_qkv), (attended, branch))


def deliver_all(tokens, gains, grad_routed, upstream, made, weight_qkv, weight_out, cosine, sine, share_in, held):
    normed, raw, queries, keys, values, probs, attended, middle, _ = made
    owners = lax.axis_size("dp") * lax.axis_size("expert")
    share = gains.shape[1] // owners
    if by_kernels():
        share_qkv, share_out, gain_sums, grad_tokens, share_in = last_sum(
            normed, attended, share_in, weight_qkv, weight_out, tokens, grad_routed, upstream, middle, raw, queries, keys,
            values, probs, *wide_tables(cosine, sine), gains, share, held
        )
        core = lax.rem(lax.axis_index("expert"), 2)
        gain_sums = lax.dynamic_slice_in_dim(gain_sums, core * share, share, axis=1)
        return (grad_tokens, gain_sums, share_qkv, share_out, share_in.astype(single))
    everyone = ("dp", "expert")
    grad_tokens, pieces, *pairs = backward(
        tokens, gains, grad_routed, upstream, normed, raw, queries, keys, values, probs, attended, middle, weight_qkv,
        weight_out, cosine, sine
    )
    return (
        grad_tokens,
        lax.psum_scatter(pieces, everyone, scatter_dimension=1, tiled=True),
        *(
            lax.psum_scatter(
                contract_rows(left, right, narrow), everyone, scatter_dimension=0, tiled=True
            ).astype(single)
            for left, right in pairs
        ),
        share_in.astype(single),
    )


def local(
    tokens,
    lengths,
    expert_ids,
    gates,
    attn_gain,
    w_qkv,
    q_gain,
    k_gain,
    w_out,
    ffn_gain,
    expert_in,
    expert_out,
    out_grad,
):
    micro_count, seq_len, model_width = tokens.shape
    rows = micro_count * seq_len
    held = expert_in.shape[0]
    experts = lax.axis_size("expert") * held
    own = tokens.reshape(rows, model_width)
    upstream = out_grad.reshape(rows, model_width)
    ids = expert_ids.reshape(rows, -1)
    gate_rows = gates.reshape(rows, -1)
    onehot = (ids[:, :, None] == jnp.arange(experts, dtype=jnp.int32)).astype(single)
    dense = jnp.sum(onehot * gate_rows[:, :, None], axis=1)
    gain_rows = jnp.stack([attn_gain, q_gain, k_gain, ffn_gain]).astype(single)
    document, position = layout(lengths[:, 0], seq_len)
    cosine, sine = angles(position)
    places = jnp.arange(rows, dtype=jnp.int32)
    allowed = (document[:, None] == document[None, :]) & (places[:, None] >= places[None, :])
    weight_qkv, weight_out, up_rows, every_gate, gains, weight_in, weight_down, made = bring_all(
        w_qkv, w_out, upstream, dense, gain_rows, expert_in, expert_out, own, cosine, sine, allowed
    )
    middle, routed_in = made[-2:]

    results, grad_routed, gate_table, (share_in, share_down) = experts_all(
        middle, routed_in, up_rows, every_gate, weight_in, weight_down, held
    )
    grad_gates = jnp.sum(onehot * gate_table.T[:, None, :], axis=2)

    grad_tokens, gain_sums, grad_qkv_share, grad_out_share, share_in = deliver_all(
        own, gains, grad_routed, upstream, made, weight_qkv, weight_out, cosine, sine, share_in, held
    )
    shape = (micro_count, seq_len, model_width)
    return (
        results.reshape(shape),
        grad_tokens.reshape(shape),
        grad_gates.reshape(expert_ids.shape),
        gain_sums[0],
        grad_qkv_share,
        gain_sums[1],
        gain_sums[2],
        grad_out_share,
        gain_sums[3],
        share_in,
        share_down.astype(single),
    )


def solution(mesh):
    by_rows = P(None, ("dp", "expert"), None)
    flat = P(("dp", "expert"))
    split = P(("dp", "expert"), None)
    held = P("expert", "dp", None)
    return jax.shard_map(
        local,
        mesh=mesh,
        in_specs=(
            by_rows, by_rows, by_rows, by_rows, flat, split, flat, flat, split, flat, held, held, by_rows,
        ),
        out_specs=(by_rows, by_rows, by_rows, flat, split, flat, flat, split, flat, held, held),
        check_vma=False,
    )
```

```python
import jax
import jax.numpy as jnp
from jax import lax
from jax.experimental import pallas as pl
from jax.experimental.pallas import tpu as pltpu
from jax.sharding import PartitionSpec as P

HEAD = 128
epsilon = 1e-05
base_theta = 10000.0
masked_score = -1e30
single = jnp.float32
narrow = jnp.bfloat16


def normalize(values):
    factor = lax.rsqrt(jnp.mean(values * values, axis=-1, keepdims=True) + epsilon)
    return (values * factor, factor)


def rms_back(upstream, normal, factor, gain):
    weighted = upstream * gain
    inner = jnp.mean(weighted * normal, axis=-1, keepdims=True)
    return (factor * (weighted - normal * inner), jnp.sum(upstream * normal, axis=0))


def angles(position):
    half = HEAD // 2
    ladder = jnp.arange(half, dtype=single) * (2.0 / HEAD)
    frequency = jnp.exp(-jnp.log(base_theta) * ladder)
    angle = position.astype(single)[:, None] * frequency[None, :]
    return (jnp.cos(angle)[:, None, :], jnp.sin(angle)[:, None, :])


def rotate(field, cosine, sine):
    length = field.shape[0]
    heads = field.reshape(length, -1, HEAD)
    half = HEAD // 2
    first = heads[..., :half]
    second = heads[..., half:]
    turned = jnp.concatenate(
        [first * cosine - second * sine, second * cosine + first * sine], axis=-1
    )
    return turned.reshape(length, -1)


def layout(doc_lengths, length):
    packs, count = doc_lengths.shape
    upto = jnp.arange(count)[None, :] <= jnp.arange(count)[:, None]
    ends = jnp.sum(jnp.where(upto[None], doc_lengths[:, None, :], 0), axis=2)
    starts = ends - doc_lengths
    places = jnp.arange(length, dtype=jnp.int32)[None, :, None]
    document = jnp.sum((places >= ends[:, None, :]).astype(jnp.int32), axis=2)
    member = (places >= starts[:, None, :]) & (places < ends[:, None, :])
    first_place = jnp.sum(jnp.where(member, starts[:, None, :], 0), axis=2)
    document = document + (count + 1) * jnp.arange(packs, dtype=jnp.int32)[:, None]
    return (document.reshape(-1), (places[..., 0] - first_place).reshape(-1))


def contract_rows(left, right, kind=single):
    return lax.dot_general(left, right, (((0,), (0,)), ((), ())), preferred_element_type=kind)


def contract_last(left, right, kind=single):
    return lax.dot_general(left, right, (((1,), (1,)), ((), ())), preferred_element_type=kind)


def core_groups():
    return [[2 * chip + core for chip in range(lax.axis_size("expert") // 2)] for core in range(2)]


def chip_groups():
    return [[2 * chip, 2 * chip + 1] for chip in range(lax.axis_size("expert") // 2)]


def gather_alike(block):
    column = lax.all_gather(block, "dp", axis=0)
    return lax.all_gather(column, "expert", axis=1, axis_index_groups=core_groups())


def scatter_alike(blocks):
    column = lax.psum_scatter(
        blocks, "expert", scatter_dimension=1, axis_index_groups=core_groups()
    )
    return lax.psum_scatter(column, "dp", scatter_dimension=0)


def fetch_weights(expert_in, expert_out):
    depth = lax.axis_size("dp")
    held, rows, columns = expert_in.shape
    part = columns // (2 * depth)
    cut = expert_in.reshape(held, rows, 2, depth, part)
    turned = lax.all_to_all(cut, "dp", split_axis=3, concat_axis=1, tiled=True)
    both = lax.all_gather(turned[:, :, :, 0], "expert", axis=0, axis_index_groups=chip_groups())
    weight_in = both.transpose(2, 3, 0, 1, 4).reshape(depth * rows, 4 * held * part)
    weight_down = lax.all_gather(
        expert_out, "expert", axis=0, axis_index_groups=chip_groups()
    ).reshape(-1, expert_out.shape[2])
    return (weight_in, weight_down)


def return_weights(grad_in, grad_down, held):
    depth = lax.axis_size("dp")
    rows, columns = grad_in.shape
    part = columns // (4 * held)
    cut = grad_in.reshape(rows, 2, 2, held, part)
    own = lax.psum_scatter(cut, "expert", scatter_dimension=2, axis_index_groups=chip_groups())
    own = own.reshape(depth, rows // depth, 2, held, part)
    turned = lax.all_to_all(own, "dp", split_axis=0, concat_axis=0)
    share_in = turned.transpose(3, 1, 2, 0, 4).reshape(held, rows // depth, 2 * depth * part)
    down = grad_down.reshape(2, held, part, grad_down.shape[1])
    share_down = lax.psum_scatter(
        down, "expert", scatter_dimension=0, axis_index_groups=chip_groups()
    )
    return (share_in, share_down)


def expert_round(mid_rows, up_rows, gate, weight_in, weight_down):
    count = gate.shape[1]
    part = weight_down.shape[0] // count
    wide = jnp.broadcast_to(gate[:, :, None], gate.shape + (part,)).reshape(gate.shape[0], -1)
    gate_up = jnp.dot(mid_rows, weight_in, preferred_element_type=single)
    hidden_units = gate_up.shape[1] // 2
    gate_part = gate_up[:, :hidden_units]
    up_part = gate_up[:, hidden_units:]
    sigmoid = jax.nn.sigmoid(gate_part)
    activated = gate_part * sigmoid
    hidden = activated * up_part
    back = contract_last(up_rows, weight_down)
    scaled = (wide * hidden).astype(narrow)
    piece_out = jnp.dot(scaled, weight_down, preferred_element_type=narrow)
    piece_gates = jnp.sum((hidden * back).reshape(-1, count, part), axis=2)
    grad_hidden = wide * back
    grad_gate = grad_hidden * up_part * sigmoid * (1.0 + gate_part * (1.0 - sigmoid))
    grad_up = grad_hidden * activated
    grad_gate_up = jnp.concatenate([grad_gate, grad_up], axis=1).astype(narrow)
    piece_mid = contract_last(grad_gate_up, weight_in, narrow)
    return (piece_out, piece_mid, piece_gates, grad_gate_up, scaled)


def expert_rounds(mid_rows, up_rows, gate, weight_in, weight_down):
    total = mid_rows.shape[0]
    rounds = max(1, total // 2048)

    def one(sums, pieces):
        mid, up, weights = pieces
        piece_out, piece_mid, piece_gates, grad_gate_up, scaled = expert_round(
            mid, up, weights, weight_in, weight_down
        )
        grads = (contract_rows(mid, grad_gate_up), contract_rows(scaled, up))
        return (jax.tree.map(jnp.add, sums, grads), (piece_out, piece_mid, piece_gates))

    if rounds == 1:
        piece_out, piece_mid, piece_gates, grad_gate_up, scaled = expert_round(
            mid_rows, up_rows, gate, weight_in, weight_down
        )
        grads = (contract_rows(mid_rows, grad_gate_up, narrow), contract_rows(scaled, up_rows, narrow))
        return (piece_out, piece_mid, piece_gates) + grads
    start = (jnp.zeros(weight_in.shape, single), jnp.zeros(weight_down.shape, single))
    cut = jax.tree.map(lambda a: a.reshape(rounds, total // rounds, -1), (mid_rows, up_rows, gate))
    sums, made = lax.scan(one, start, cut)
    made = jax.tree.map(lambda a: a.reshape(total, -1), made)
    return made + (sums[0].astype(narrow), sums[1].astype(narrow))


MESH = pl.DeviceIdType.MESH
HBM = pl.BlockSpec(memory_space=pl.ANY)
DEPTH = 4
RING = 4


def ring_turn(number):
    high = lax.div(number, 2)
    return number + high * (1 - 2 * lax.rem(number, 2))


class Here:
    def __init__(self):
        number = lax.axis_index("expert")
        self.z = lax.axis_index("dp")
        self.core = lax.rem(number, 2)
        self.chip = lax.div(number, 2)
        self.q = ring_turn(self.chip)

    def chip_at(self, turn):
        return ring_turn(lax.rem(self.q + turn + RING, RING))

    def beside(self, turn):
        return (self.z, 2 * self.chip_at(turn) + self.core)

    def above(self, steps):
        return (lax.rem(self.z + steps + DEPTH, DEPTH), 2 * self.chip + self.core)

    def sibling(self):
        return (self.z, 2 * self.chip + 1 - self.core)

    def meet(self):
        barrier = pltpu.get_barrier_semaphore()
        others = [self.beside(1), self.beside(-1), self.sibling()]
        others += [self.above(steps) for steps in range(1, DEPTH)]
        for other in others:
            pl.semaphore_signal(barrier, inc=1, device_id=other, device_id_type=MESH)
        pl.semaphore_wait(barrier, len(others))


def remote(source, target, sent, arrived, device):
    return pltpu.make_async_remote_copy(
        src_ref=source,
        dst_ref=target,
        send_sem=sent,
        recv_sem=arrived,
        device_id=device,
        device_id_type=MESH,
    )


GATHER_SEMS = [
    pltpu.SemaphoreType.DMA((2, 2, DEPTH - 1)),
    pltpu.SemaphoreType.DMA((2, DEPTH, 2, 2)),
    pltpu.SemaphoreType.DMA((2, DEPTH)),
    pltpu.SemaphoreType.DMA((1,)),
]


class Gather:
    def __init__(self, here, source, whole, halves, shared, sems):
        self.here, self.source, self.whole, self.halves, self.shared = here, source, whole, halves, shared
        self.line, self.ring, self.pair, self.own = sems

    def block(self, z, turn):
        chip = self.here.chip_at(turn)
        return self.whole.at[z, chip, self.here.core] if self.shared else self.whole.at[z, chip]

    def keep(self):
        return pltpu.make_async_copy(self.source, self.block(self.here.z, 0), self.own.at[0])

    def along(self, step, way, first):
        z = self.here.z - step + 1 if way == 0 else self.here.z + step - 1
        block = self.block(z, 0)
        return remote(
            self.source if first else block,
            block,
            self.line.at[0, way, step - 1],
            self.line.at[1, way, step - 1],
            self.here.above(1 if way == 0 else -1),
        )

    def round(self, z, way, first=False):
        turn = 1 if way == 0 else -1
        block = self.block(z, 0)
        return remote(
            self.source if first else block,
            block,
            self.ring.at[0, z, way, 0],
            self.ring.at[1, z, way, 0],
            self.here.beside(turn),
        )

    def heard(self, z, way):
        block = self.block(z, -1 if way == 0 else 1)
        return remote(
            block, block, self.ring.at[0, z, way, 0], self.ring.at[1, z, way, 0], self.here.beside(1)
        )

    def onward(self, z, way, mine):
        if self.halves[way] is None:
            return None
        turn = (-1 if mine else -2) if way == 0 else (1 if mine else 2)
        block = self.block(z, turn).at[pl.ds(*self.halves[way])]
        return remote(
            block,
            block,
            self.ring.at[0, z, way, 1],
            self.ring.at[1, z, way, 1],
            self.here.beside(1 if way == 0 else -1),
        )

    def swap(self, z, mine):
        core = self.here.core if mine else 1 - self.here.core
        part = self.whole.at[z, :, core]
        return remote(part, part, self.pair.at[0, z], self.pair.at[1, z], self.here.sibling())


def start(copy):
    if copy is not None:
        copy.start()


def gather_third(item, z):
    for way in (0, 1):
        copy = item.onward(z, way, False)
        if copy is not None:
            copy.wait_recv()


class Rounds:
    def __init__(self, here, items, ring=True):
        self.here, self.items = here, items
        for item in items:
            item.keep().start()
            for way in (0, 1):
                self.depart(0, way, item)
            if ring:
                for way in (0, 1):
                    item.round(here.z, way, True).start()

    def depart(self, step, way, item):
        here = self.here
        ahead = here.z + 1 < DEPTH if way == 0 else here.z >= 1
        pl.when(ahead)(lambda: item.along(step + 1, way, step == 0).start())

    def places(self, step, body):
        here = self.here
        if step == 0:
            body(here.z, 0)
            return
        pl.when(here.z >= step)(lambda: body(here.z - step, 0))
        pl.when(here.z + step < DEPTH)(lambda: body(here.z + step, 1))

    def line(self, step, ring=True):
        def body(z, way):
            for item in self.items:
                block = item.block(z, 0)
                remote(
                    block, block, item.line.at[0, way, step - 1], item.line.at[1, way, step - 1], self.here.above(1)
                ).wait_recv()
                if step + 1 < DEPTH:
                    self.depart(step, way, item)
                if ring:
                    for side in (0, 1):
                        item.round(z, side).start()

        self.places(step, body)

    def ring(self, step):
        def body(z, way):
            for item in self.items:
                for side in (0, 1):
                    item.round(z, side, step == 0).start()

        self.places(step, body)

    def second(self, step):
        def body(z, way):
            for item in self.items:
                for side in (0, 1):
                    item.heard(z, side).wait_recv()
                    start(item.onward(z, side, True))

        self.places(step, body)

    def service(self, step, between=None):
        if step + 1 < DEPTH:
            self.line(step + 1)
        if between is not None:
            between()
        if step == 0:
            self.kept()
        self.second(step)

    def kept(self):
        for item in self.items:
            item.keep().wait()

    def third(self, step):
        def body(z, way):
            for item in self.items:
                gather_third(item, z)
                if item.shared:
                    item.swap(z, True).start()

        self.places(step, body)

    def finish(self):
        def settle(z, way):
            for item in self.items:
                for side in (0, 1):
                    item.round(z, side).wait_send()
                    copy = item.onward(z, side, True)
                    if copy is not None:
                        copy.wait_send()
                if item.shared:
                    item.swap(z, True).wait_send()
                    item.swap(z, False).wait_recv()

        for step in range(DEPTH):
            self.places(step, settle)
        here = self.here
        for item in self.items:
            for step in range(DEPTH - 1):
                for way in (0, 1):

                    def sent(z, side, step=step, way=way, item=item):
                        if step and side != way:
                            return
                        ahead = here.z + 1 < DEPTH if way == 0 else here.z >= 1
                        pl.when(ahead)(lambda: item.along(step + 1, way, step == 0).wait_send())

                    self.places(step, sent)


def inner_first(here, count, begin):
    for group in (range(1, DEPTH - 1), (0, DEPTH - 1)):
        for number in range(count):
            for target in group:

                @pl.when(here.z != target)
                def _(target=target, number=number):
                    begin(lax.rem(target - here.z + DEPTH, DEPTH), number)


class Recut:
    def __init__(self, here, source_in, source_out, whole_in, whole_out, sems):
        self.here, self.source_in, self.source_out = here, source_in, source_out
        self.whole_in, self.whole_out = whole_in, whole_out
        self.cut, self.pair, self.down, self.own = sems
        self.held, self.rows, columns = source_in.shape
        self.hidden = columns // 2
        self.part = self.hidden // DEPTH

    def pieces(self, steps, arriving, only=None):
        here, copies = self.here, []
        mine = lax.rem(here.z + DEPTH - steps, DEPTH) if arriving else here.z
        away = lax.rem(here.z + steps, DEPTH)
        for side in range(2):
            for expert in range(self.held):
                if only not in (None, side * self.held + expert):
                    continue
                columns = side * self.held * 2 * self.part + (here.core * self.held + expert) * self.part
                target = self.whole_in.at[
                    pl.ds(pl.multiple_of(mine * self.rows, 16), self.rows),
                    pl.ds(pl.multiple_of(columns, 128), self.part),
                ]
                source = self.source_in.at[
                    expert, :, pl.ds(pl.multiple_of(side * self.hidden + away * self.part, 128), self.part)
                ]
                spot = (steps, side * self.held + expert)
                if isinstance(steps, int) and steps == 0:
                    copies.append(pltpu.make_async_copy(source, target, self.own.at[spot[1]]))
                else:
                    copies.append(
                        remote(
                            target if arriving else source,
                            target,
                            self.cut.at[(0,) + spot],
                            self.cut.at[(1,) + spot],
                            here.above(steps),
                        )
                    )
        return copies

    def across(self, steps, mine):
        here, copies = self.here, []
        core = here.core if mine else 1 - here.core
        row = lax.rem(here.z + DEPTH - steps, DEPTH)
        width = self.held * self.part
        for side in range(2):
            spot = self.whole_in.at[
                pl.ds(pl.multiple_of(row * self.rows, 16), self.rows),
                pl.ds(pl.multiple_of(side * 2 * width + core * width, 128), width),
            ]
            copies.append(
                remote(spot, spot, self.pair.at[0, steps, side], self.pair.at[1, steps, side], here.sibling())
            )
        return copies

    def lower(self, mine):
        here = self.here
        core = here.core if mine else 1 - here.core
        spot = self.whole_out.at[pl.ds(core * self.held, self.held)]
        return remote(
            self.source_out if mine else spot, spot, self.down.at[0], self.down.at[1], here.sibling()
        )

    def lower_own(self):
        return pltpu.make_async_copy(
            self.source_out, self.whole_out.at[pl.ds(self.here.core * self.held, self.held)], self.own.at[4]
        )

    def begin(self):
        for copy in self.pieces(0, False):
            copy.start()
        self.lower_own().start()
        self.lower(True).start()
        inner_first(self.here, 2 * self.held, lambda steps, number: self.pieces(steps, False, number)[0].start())

    def relay(self):
        for steps in range(DEPTH):
            for copy in self.pieces(steps, True):
                copy.wait() if steps == 0 else copy.wait_recv()
            for copy in self.across(steps, True):
                copy.start()

    def end(self):
        self.lower_own().wait()
        self.lower(True).wait_send()
        self.lower(False).wait_recv()
        for steps in range(DEPTH):
            if steps:
                for copy in self.pieces(steps, False):
                    copy.wait_send()
            for copy in self.across(steps, True):
                copy.wait_send()
            for copy in self.across(steps, False):
                copy.wait_recv()


RECUT_SEMS = [
    pltpu.SemaphoreType.DMA((2, DEPTH, 4)),
    pltpu.SemaphoreType.DMA((2, DEPTH, 2)),
    pltpu.SemaphoreType.DMA((2,)),
    pltpu.SemaphoreType.DMA((5,)),
]


def halves_of(rows, split=True):
    return ((0, rows // 2), (rows // 2, rows - rows // 2)) if split else ((0, rows), None)


PANEL = 512


def attention_forward(
    tokens, cosine, sine, allowed, wq, wo, gains, normed, raw, queries, keys, values, probs, attended, middle, routed,
    panel, panel_sems, between
):
    block, width = tokens.shape
    heads = width // HEAD
    wide = wq.shape[-1]
    high = 16
    per = width // PANEL

    def fetch(source, number):
        slot = lax.rem(number, 2)
        spot = pl.ds(pl.multiple_of(number * PANEL, PANEL), PANEL)
        return pltpu.make_async_copy(source.at[:, :, :, :, spot], panel.at[slot], panel_sems.at[slot])

    def slabs(body):
        def one(number, carry):
            body(pl.ds(pl.multiple_of(number * high, high), high))
            return carry

        lax.fori_loop(0, block // high, one, 0)

    def first(at):
        values = tokens[at].astype(single)
        factor = lax.rsqrt(jnp.mean(values * values, axis=-1, keepdims=True) + epsilon)
        normed[at] = (values * factor * gains[0:1]).astype(narrow)

    fetch(wq, 0).start()
    slabs(first)

    def through(source, left, total, finish):
        def one(number, carry):
            fetch(source, number).wait()
            pl.when(number + 1 < total)(lambda: fetch(source, number + 1).start())
            weights = panel[lax.rem(number, 2)].reshape(width, PANEL)
            finish(number, jnp.dot(left[...], weights, preferred_element_type=single))
            return carry

        lax.fori_loop(0, total, one, 0)

    def keep(number, made):
        side = lax.div(number, per)
        spot = pl.ds(pl.multiple_of(lax.rem(number, per) * PANEL, PANEL), PANEL)

        @pl.when(side < 2)
        def _():
            raw[side, :, spot] = made

        @pl.when(side == 2)
        def _():
            values[:, spot] = made.astype(narrow)

    through(wq, normed, wide // PANEL, keep)
    fetch(wo, 0).start()
    between(0)

    factors = [
        lax.rsqrt(jnp.mean(raw[side] * raw[side], axis=-1, keepdims=True) + epsilon) for side in range(2)
    ]
    turn_cos, turn_sin = cosine[...], sine[...]
    may = allowed[...] > 0.5
    group = 4

    def some_heads(number, carry):
        for inner in range(group):
            head = number * group + inner
            spot = pl.ds(pl.multiple_of(head * HEAD, HEAD), HEAD)
            turned = []
            for side, target in ((0, queries), (1, keys)):
                field = raw[side, :, spot] * factors[side] * gains[side + 1 : side + 2, spot]
                field = field * turn_cos + pltpu.roll(field, HEAD // 2, 1) * turn_sin
                target[:, spot] = field.astype(narrow)
                turned.append(field.astype(narrow))
            scores = jnp.where(may, contract_last(turned[0], turned[1]) * HEAD ** (-0.5), masked_score)
            highest = jnp.max(scores, axis=-1, keepdims=True)
            unnormed = jnp.exp(scores - highest)
            shares = unnormed / jnp.sum(unnormed, axis=-1, keepdims=True)
            probs[head] = shares
            mixed = jnp.dot(shares.astype(narrow), values[:, spot], preferred_element_type=single)
            attended[:, spot] = mixed.astype(narrow)
        return carry

    lax.fori_loop(0, heads // group, some_heads, 0)
    between(1)

    def add(number, made):
        spot = pl.ds(pl.multiple_of(number * PANEL, PANEL), PANEL)
        middle[:, spot] = tokens[:, spot].astype(single) + made

    through(wo, attended, per, add)

    def last(at):
        values = middle[at]
        factor = lax.rsqrt(jnp.mean(values * values, axis=-1, keepdims=True) + epsilon)
        routed[at] = (values * factor * gains[3:4]).astype(narrow)

    slabs(last)
    between(2)


def first_gather_kernel(
    wq, wo, up, small, ein, eout, tokens, cosine, sine, allowed,
    wq_all, wo_all, up_all, small_all, win, wout, *rest
):
    made, (tokens_v, small_here, small_sem, panel, panel_sems, put_sems), sems = rest[:10], rest[20:26], rest[26:]
    results = rest[10:20]
    gains, normed, raw, queries, keys, values, probs, attended, middle, routed = results
    here = Here()
    here.meet()
    fetch_tokens = pltpu.make_async_copy(tokens, tokens_v, small_sem.at[1])
    fetch_tokens.start()
    puts = [
        pltpu.make_async_copy(source, target, put_sems.at[number])
        for number, (source, target) in enumerate(zip(results, made))
    ]
    items = [
        Gather(here, source, whole, halves, shared, sems[4 * number : 4 * number + 4])
        for number, (source, whole, halves, shared) in enumerate(
            (
                (small, small_all, halves_of(small.shape[0], False), True),
                (wq, wq_all, halves_of(wq.shape[0]), True),
                (wo, wo_all, halves_of(wo.shape[0]), True),
                (up, up_all, halves_of(up.shape[0]), False),
            )
        )
    ]
    recut = Recut(here, ein, eout, win, wout, sems[16:20])
    weights = Rounds(here, items[:3])
    rows = Rounds(here, items[3:], ring=False)
    weights.service(0, lambda: rows.line(1, ring=False))
    weights.service(1, lambda: rows.line(2, ring=False))
    recut.begin()
    weights.third(0)
    weights.service(2, lambda: rows.line(3, ring=False))
    weights.third(1)
    weights.service(3)
    rows.kept()
    for step in range(DEPTH):
        rows.ring(step)
    weights.third(2)
    weights.third(3)
    weights.finish()
    fetch = pltpu.make_async_copy(small_all, small_here, small_sem.at[0])
    fetch.start()
    fetch.wait()
    fetch_tokens.wait()
    share = wq.shape[0]
    lanes = small.shape[1]
    lane = lax.broadcasted_iota(jnp.int32, (8, lanes), 1)
    skip = small.shape[0] - 8
    for z in range(DEPTH):
        for chip in range(RING):
            pair = [small_here[z, chip, core, skip : skip + 8] for core in (0, 1)]
            both = jnp.where(lane < share, pair[0], pltpu.roll(pair[1], share, 1))
            begin = (z * RING + chip) * 2 * share
            gains[:, begin : begin + 2 * share] = both

    def between(part):
        if part == 0:
            rows.second(0)
        elif part == 1:
            for step in range(1, DEPTH):
                rows.second(step)
        else:
            for copy in puts:
                copy.start()
            recut.relay()

    attention_forward(
        tokens_v, cosine, sine, allowed, wq_all, wo_all, gains, normed, raw, queries, keys, values, probs, attended,
        middle, routed, panel, panel_sems, between
    )
    for step in range(DEPTH):
        rows.third(step)
    rows.finish()
    recut.end()
    for copy in puts:
        copy.wait()


def first_gather(wq, wo, up, small, ein, eout, tokens, cosine, sine, allowed):
    def whole(array, shared):
        lead = (DEPTH, RING, 2) if shared else (DEPTH, RING)
        return jax.ShapeDtypeStruct(lead + array.shape, array.dtype)

    held, rows, columns = ein.shape
    block, width = tokens.shape
    heads = width // HEAD
    vmem = pl.BlockSpec(memory_space=pltpu.VMEM)
    like = ((block, width), narrow)
    made = (
        ((8, width), single),
        like,
        ((2, block, width), single),
        like,
        like,
        like,
        ((heads, block, block), single),
        like,
        ((block, width), single),
        like,
    )
    return pl.pallas_call(
        first_gather_kernel,
        out_shape=(
            whole(wq, True),
            whole(wo, True),
            whole(up, False),
            whole(small, True),
            jax.ShapeDtypeStruct((DEPTH * rows, columns), ein.dtype),
            jax.ShapeDtypeStruct((2 * held,) + eout.shape[1:], eout.dtype),
            *(jax.ShapeDtypeStruct(*one) for one in made),
        ),
        in_specs=[HBM] * 7 + [vmem] * 3,
        out_specs=(HBM,) * 16,
        scratch_shapes=[pltpu.VMEM(*one) for one in made]
        + [
            pltpu.VMEM((block, width), tokens.dtype),
            pltpu.VMEM((DEPTH, RING, 2) + small.shape, single),
            pltpu.SemaphoreType.DMA((2,)),
            pltpu.VMEM((2, DEPTH, RING, 2, wq.shape[0], PANEL), narrow),
            pltpu.SemaphoreType.DMA((2,)),
            pltpu.SemaphoreType.DMA((len(made),)),
        ]
        + GATHER_SEMS * 4
        + RECUT_SEMS,
        compiler_params=pltpu.CompilerParams(
            collective_id=1, has_side_effects=True, vmem_limit_bytes=62 * 2**20
        ),
        name="bring",
    )(wq, wo, up, small, ein, eout, tokens, cosine, sine, allowed)

TILE = 256


def add_up(target, terms, rows, columns):
    high = 16 if rows % 16 == 0 else 8
    wide = min(columns, 1024)
    across = columns // wide

    def piece(number, carry):
        row = pl.multiple_of(lax.div(number, across) * high, high)
        column = pl.multiple_of(lax.rem(number, across) * wide, 128)
        spot = (pl.ds(row, high), pl.ds(column, wide))
        total = terms[0][spot].astype(single)
        for term in terms[1:]:
            total = total + term[spot].astype(single)
        target[spot] = total.astype(target.dtype)
        return carry

    lax.fori_loop(0, (rows // high) * across, piece, 0)


SUM_SEMS = [
    pltpu.SemaphoreType.DMA((2, DEPTH, 2)),
    pltpu.SemaphoreType.DMA((2, DEPTH, 2)),
    pltpu.SemaphoreType.DMA((2, 2, DEPTH)),
    pltpu.SemaphoreType.DMA((DEPTH, RING, 2)),
]


def sum_scratch(rows, columns, kind, halves, paired=False, made=False):
    high = max(size for _, size in filter(None, halves))
    kept = RING if paired or made else RING - 1
    scratch = [
        pltpu.VMEM((DEPTH, kept, rows, columns), kind),
        pltpu.VMEM((DEPTH, 2, high, columns), kind),
        pltpu.VMEM((DEPTH, 2, rows, columns), kind),
        pltpu.VMEM((DEPTH + 1, rows, columns), kind),
    ] + SUM_SEMS
    if paired:
        scratch += [pltpu.VMEM((DEPTH, RING, rows, columns), kind), pltpu.SemaphoreType.DMA((2, DEPTH, 2))]
    return scratch


class Sum:
    def __init__(self, here, sources, target, halves, paired, scratch):
        self.here, self.sources, self.halves, self.paired = here, sources, halves, paired
        self.target = target if isinstance(target, list) else [(target, 0, target.shape[0])]
        self.extra = []
        self.mine, self.half, self.full, self.column = scratch[:4]
        self.half_sem, self.full_sem, self.line_sem, self.load_sem = scratch[4:8]
        if paired:
            self.other, self.pair_sem = scratch[8:10]
        self.rows, self.columns = self.mine.shape[2:]

    def kept(self, z, turn):
        if self.sources is None:
            return self.mine.at[z, self.here.chip_at(turn)]
        return self.mine.at[z, turn if self.paired else {0: 0, 1: 1, 3: 2}[turn]]

    def raw(self, part, z, turn):
        chip = self.here.chip_at(turn)
        return part.at[z, chip, self.here.core] if self.paired else part.at[z, chip]

    def spots(self):
        at, spots = 0, []
        for part in self.sources or []:
            spots.append((part, pl.ds(at, part.shape[-1])))
            at += part.shape[-1]
        return spots

    def loads(self, z, turn):
        return [
            pltpu.make_async_copy(
                self.raw(part, z, turn), self.kept(z, turn).at[:, spot], self.load_sem.at[z, turn, number]
            )
            for number, (part, spot) in enumerate(self.spots())
        ]

    def swaps(self, z, mine):
        return [
            remote(
                part.at[z, :, 1 - self.here.core] if mine else self.other.at[z, :, :, spot],
                self.other.at[z, :, :, spot],
                self.pair_sem.at[0, z, number],
                self.pair_sem.at[1, z, number],
                self.here.sibling(),
            )
            for number, (part, spot) in enumerate(self.spots())
        ]

    def toss(self, z, way):
        if self.halves[way] is None:
            return None
        rows = pl.ds(*self.halves[way])
        loaded = self.sources is not None and not self.paired
        source = (self.raw(self.sources[0], z, 2) if loaded else self.kept(z, 2)).at[rows]
        return remote(
            source,
            self.half.at[z, way, pl.ds(0, self.halves[way][1])],
            self.half_sem.at[0, z, way],
            self.half_sem.at[1, z, way],
            self.here.beside(1 if way == 0 else -1),
        )

    def pass_on(self, z, way):
        return remote(
            self.kept(z, 1 if way == 0 else 3),
            self.full.at[z, way],
            self.full_sem.at[0, z, way],
            self.full_sem.at[1, z, way],
            self.here.beside(1 if way == 0 else -1),
        )

    def climb(self, z, way, up, slot=None):
        if slot is None:
            down_to_owner = way * (z == self.here.z - 1).astype(jnp.int32)
            slot = z + down_to_owner * (DEPTH - z)
        return remote(
            self.kept(z, 0),
            self.column.at[slot],
            self.line_sem.at[0, way, z],
            self.line_sem.at[1, way, z],
            self.here.above(2 * up - 1),
        )

    def begin(self, z):
        if self.paired:
            for copy in self.swaps(z, True):
                copy.start()
        for turn in (2, 1, 3, 0):
            if turn != 2 or self.paired:
                for copy in self.loads(z, turn):
                    copy.start()
        if not self.paired:
            for way in (0, 1):
                start(self.toss(z, way))

    def merge(self, z):
        if not self.paired:
            return
        for copy in self.swaps(z, False):
            copy.wait_recv()
        for turn in (2, 1, 3, 0):
            for copy in self.loads(z, turn):
                copy.wait()
            kept = self.kept(z, turn)
            add_up(kept, [kept, self.other.at[z, self.here.chip_at(turn)]], self.rows, self.columns)
            if turn == 2:
                for way in (0, 1):
                    start(self.toss(z, way))

    def second(self, z):
        for way, turn in ((0, 1), (1, 3)):
            if not self.paired:
                for copy in self.loads(z, turn):
                    copy.wait()
            copy = self.toss(z, way)
            if copy is not None:
                copy.wait_recv()
                begin, size = self.halves[way]
                rows = self.kept(z, turn).at[pl.ds(begin, size)]
                add_up(rows, [rows, self.half.at[z, way, pl.ds(0, size)]], size, self.columns)
        for way in (0, 1):
            self.pass_on(z, way).start()

    def third(self, z, last):
        here = self.here
        if not self.paired:
            for copy in self.loads(z, 0):
                copy.wait()
        for way in (0, 1):
            self.pass_on(z, way).wait_recv()
        kept = self.kept(z, 0)
        terms = [kept, self.full.at[z, 0], self.full.at[z, 1]]
        if last:
            self.arrive(z, terms)
            return
        up = (z > here.z).astype(jnp.int32)
        way = 1 - up
        follows = up * here.z + way * (DEPTH - 1 - here.z)

        @pl.when(follows > 0)
        def _():
            self.climb(z, way, up, z).wait_recv()
            add_up(kept, terms + [self.column.at[z]], self.rows, self.columns)

        @pl.when(follows == 0)
        def _():
            add_up(kept, terms, self.rows, self.columns)

        self.climb(z, way, up).start()

    def own_part(self, z):
        for way in (0, 1):
            self.pass_on(z, way).wait_recv()
        [(target, _, rows)] = self.target
        add_up(target, [self.kept(z, 0), self.full.at[z, 0], self.full.at[z, 1]], rows, self.columns)

    def own_rest(self, z):
        self.arrive(z, [self.target[0][0]])

    def arrive(self, z, terms):
        here = self.here
        below, above = self.column.at[z], self.column.at[DEPTH]

        def total(more):
            for target, row, rows in self.target:
                part = [term.at[pl.ds(row, rows)] for term in terms + more + self.extra]
                add_up(target, part, rows, self.columns)

        @pl.when(here.z == 0)
        def _():
            self.climb(z, 1, 0, DEPTH).wait_recv()
            total([above])

        @pl.when(here.z == DEPTH - 1)
        def _():
            self.climb(z, 0, 0, z).wait_recv()
            total([below])

        @pl.when((here.z > 0) & (here.z < DEPTH - 1))
        def _():
            self.climb(z, 0, 0, z).wait_recv()
            self.climb(z, 1, 0, DEPTH).wait_recv()
            total([below, above])

    def end(self, z, last):
        if self.paired:
            for copy in self.swaps(z, True):
                copy.wait_send()
        for way in (0, 1):
            copy = self.toss(z, way)
            if copy is not None:
                copy.wait_send()
            self.pass_on(z, way).wait_send()
        if not last:
            up = (z > self.here.z).astype(jnp.int32)
            self.climb(z, 1 - up, up).wait_send()


def far_first(here, number):
    high = lax.div(here.z, 2)
    inner = lax.rem(lax.div(here.z + 1, 2), 2)
    low = (DEPTH - 1 - number) + inner * (0, -2, 1, 1)[number]
    return low + high * (DEPTH - 1 - 2 * low)


class Share:
    def __init__(self, here, source, target, side, sems):
        self.here, self.source, self.target, self.side, self.sems = here, source, target, side, sems
        self.held, self.rows, columns = target.shape
        self.part = columns // (2 * DEPTH)

    def pieces(self, steps, arriving, only=None):
        here = self.here
        origin = lax.rem(here.z + DEPTH - steps, DEPTH) if arriving else here.z
        away = lax.rem(here.z + steps, DEPTH)
        copies = []
        for expert in range(self.held):
            if only not in (None, expert):
                continue
            column = (self.side * DEPTH + origin) * self.part
            target = self.target.at[expert, :, pl.ds(pl.multiple_of(column, 128), self.part)]
            source = self.source.at[
                pl.ds(pl.multiple_of(away * self.rows, 16), self.rows),
                pl.ds((self.side * self.held + expert) * self.part, self.part),
            ]
            if isinstance(steps, int) and steps == 0:
                copies.append(pltpu.make_async_copy(source, target, self.sems.at[0, 0, expert]))
            else:
                sems = (self.sems.at[0, steps, expert], self.sems.at[1, steps, expert])
                copies.append(remote(target if arriving else source, target, *sems, here.above(steps)))
        return copies

    def begin(self):
        for copy in self.pieces(0, False):
            copy.start()
        inner_first(self.here, self.held, lambda steps, number: self.pieces(steps, False, number)[0].start())

    def end(self):
        for steps in range(DEPTH):
            for copy in self.pieces(steps, False):
                copy.wait() if steps == 0 else copy.wait_send()
            if steps:
                for copy in self.pieces(steps, True):
                    copy.wait_recv()


STRIP = 128


def last_sum_kernel(
    normed,
    attended,
    gin_sum,
    weight,
    weight_out,
    tokens,
    routed,
    upstream,
    middle,
    raw,
    queries,
    keys,
    values,
    probs,
    cosine,
    sine,
    gains,
    q_sum,
    o_sum,
    gain_sums,
    grad_tokens,
    share_in,
    *scratch,
):
    here = Here()
    here.meet()
    block, width = tokens.shape
    share = q_sum.shape[0]
    wide = q_sum.shape[1]
    sides = wide // width
    heads = width // HEAD
    (
        left, left_out, right, panel, x, routed_v, upstream_v, middle_v, raw_v, queries_v, keys_v, values_v, probs_v,
        grad_middle, grad_heads, turned, piece, few_sum, few_other, sems, panel_sems, pair_sems, share_sems
    ) = scratch[:23]
    big = Sum(
        here,
        None,
        [(q_sum.at[:, pl.ds(side * width, width)], side * share, share) for side in range(sides)],
        halves_of(sides * share),
        False,
        scratch[23:31],
    )
    outer = Sum(here, None, o_sum, halves_of(share), False, scratch[31:39])
    few = Sum(here, None, few_sum, halves_of(few_sum.shape[0], False), False, scratch[39:47])
    order = [far_first(here, number) for number in range(DEPTH)]
    loads = [
        pltpu.make_async_copy(source, target, sems.at[number])
        for number, (source, target) in enumerate(
            (
                (middle, middle_v),
                (routed, routed_v),
                (upstream, upstream_v),
                (attended, left_out.at[0]),
                (values, values_v),
                (probs, probs_v),
                (queries, queries_v),
                (keys, keys_v),
                (raw, raw_v),
                (normed, left.at[0]),
                (tokens, x),
            )
        )
    ]

    def fetch(source, number, columns):
        slot = lax.rem(number, 2)
        rows = pl.ds(pl.multiple_of(number * STRIP, STRIP), STRIP)
        return pltpu.make_async_copy(source.at[rows], panel.at[slot, :, pl.ds(0, columns)], panel_sems.at[slot])

    for copy in loads:
        copy.start()
    fetch(weight_out, 0, width).start()
    shares_in = [Share(here, gin_sum, share_in, side, share_sems.at[side]) for side in range(2)]
    for share_side in shares_in:
        share_side.begin()

    def swap(number, source, target):
        base = 16 + 2 * number
        return remote(source, target, sems.at[base], sems.at[base + 1], here.sibling())

    side_out = pl.ds(wide, width)
    side_qkv = pl.ds(0, wide)
    swaps = [
        swap(0, left_out.at[0], left_out.at[1]),
        swap(1, right.at[0, :, side_out], right.at[1, :, side_out]),
        swap(2, left.at[0], left.at[1]),
        swap(3, right.at[0, :, side_qkv], right.at[1, :, side_qkv]),
    ]
    high = 16
    panels = width // STRIP

    def slabs(body):
        def one(number, carry):
            body(pl.ds(pl.multiple_of(number * high, high), high))
            return carry

        lax.fori_loop(0, block // high, one, 0)

    def norm(values):
        factor = lax.rsqrt(jnp.mean(values * values, axis=-1, keepdims=True) + epsilon)
        return values * factor, factor

    def norm_grad(up, values, row):
        normal, factor = norm(values)
        weighted = up * gains[row : row + 1]
        inner = jnp.mean(weighted * normal, axis=-1, keepdims=True)
        piece[row : row + 1] += jnp.sum(up * normal, axis=0, keepdims=True)
        return factor * (weighted - normal * inner)

    def first(at):
        grad = upstream_v[at].astype(single) + norm_grad(routed_v[at], middle_v[at], 3)
        grad_middle[at] = grad
        right[0, at, side_out] = grad.astype(narrow)

    piece[...] = jnp.zeros_like(piece)
    for number in range(4):
        loads[number].wait()
    swaps[0].start()
    slabs(first)
    swaps[1].start()

    def through(source, columns, left_rows, finish, begin=0, end=panels):
        def one(number, carry):
            fetch(source, number, columns).wait()
            pl.when(number + 1 < panels)(lambda: fetch(source, number + 1, columns).start())
            rows = panel[lax.rem(number, 2), :, 0:columns]
            finish(pl.ds(pl.multiple_of(number * STRIP, STRIP), STRIP), contract_last(left_rows, rows))
            return carry

        lax.fori_loop(begin, end, one, 0)

    def keep_heads(spot, made):
        grad_heads[:, spot] = made.astype(narrow)

    step = 512
    each = width // step
    rows = RING * 2 * share

    def make(z, item, source, first_chunk, last_chunk):
        at = pl.ds(pl.multiple_of(z * rows, rows), rows)

        def one(number, carry):
            spot = pl.ds(pl.multiple_of(number * step, step), step)
            left_rows = source[:, :, at].reshape(2 * block, rows)
            made = contract_rows(left_rows, right[:, :, spot].reshape(2 * block, step))
            made = made.reshape(RING, 2, share, step)
            mine = jnp.where(here.core == 0, made[:, 0], made[:, 1]).astype(narrow)
            row = pl.multiple_of(lax.div(number - first_chunk, each) * share, share)
            column = pl.multiple_of(lax.rem(number, each) * step, step)
            for chip in range(RING):
                item.mine[z, chip, pl.ds(row, share), pl.ds(column, step)] = mine[chip]
            return carry

        lax.fori_loop(first_chunk, last_chunk, one, 0)

    swaps[0].wait_recv()
    swaps[1].wait_recv()
    for z in order:
        make(z, outer, left_out, sides * each, (sides + 1) * each)
        for way in (0, 1):
            start(outer.toss(z, way))
    through(weight_out, width, right[0, :, side_out], keep_heads)
    fetch(weight, 0, wide).start()
    for z in order:
        outer.second(z)
    for number in range(4, len(loads)):
        loads[number].wait()
    swaps[2].start()
    turn_cos, turn_sin = cosine[...], sine[...]
    group = 4

    def some_heads(number, carry):
        for inner in range(group):
            head = number * group + inner
            spot = pl.ds(pl.multiple_of(head * HEAD, HEAD), HEAD)
            grad = grad_heads[:, spot]
            shares = probs_v[head]
            grad_shares = contract_last(grad, values_v[:, spot])
            along = jnp.sum(grad_shares * shares, axis=-1, keepdims=True)
            scores = (shares * (grad_shares - along)).astype(narrow)
            made = (
                jnp.dot(scores, keys_v[:, spot], preferred_element_type=single),
                contract_rows(scores, queries_v[:, spot]),
            )
            for side, field in enumerate(made):
                field = field * HEAD ** (-0.5)
                turned[side, :, spot] = field * turn_cos - pltpu.roll(field, HEAD // 2, 1) * turn_sin
            spot_v = pl.ds(pl.multiple_of(2 * width + head * HEAD, HEAD), HEAD)
            right[0, :, spot_v] = contract_rows(shares.astype(narrow), grad).astype(narrow)
        return carry

    lax.fori_loop(0, heads // group, some_heads, 0)

    def second(at):
        for side in range(2):
            grad = norm_grad(turned[side, at], raw_v[side, at], side + 1)
            right[0, at, side * width : (side + 1) * width] = grad.astype(narrow)

    slabs(second)
    swaps[3].start()
    swaps[2].wait_recv()
    swaps[3].wait_recv()

    def keep_back(spot, made):
        routed_v[:, spot] = made

    def third(at):
        grad_tokens[at] = grad_middle[at] + norm_grad(routed_v[at], x[at].astype(single), 0)

    for number, z in enumerate(order):
        make(z, big, left, 0, sides * each)
        for way in (0, 1):
            start(big.toss(z, way))
        if number:
            big.second(order[number - 1])
        outer.third(z, number == DEPTH - 1)
        if number > 1:
            big.third(order[number - 2], False)
        cut = panels // DEPTH
        through(weight, wide, right[0, :, side_qkv], keep_back, number * cut, (number + 1) * cut)
        if number == DEPTH - 1:
            slabs(third)
            for plane in range(DEPTH):
                for chip in range(RING):
                    begin = (plane * RING + chip) * 2 * share
                    few.mine[plane, chip] = piece[:, begin : begin + 2 * share]
            for place in order:
                start(few.toss(place, 0))
    big.second(order[-1])
    for z in order:
        few.second(z)
    big.third(order[-2], False)
    for z in order[:-1]:
        few.third(z, False)
    big.third(order[-1], True)
    few.third(order[-1], True)
    pair = remote(few_sum, few_other, pair_sems.at[0], pair_sems.at[1], here.sibling())
    pair.start()
    pair.wait_recv()
    gain_sums[...] = few_sum[...] + few_other[...]
    pair.wait_send()
    for number, z in enumerate(order):
        for item in (big, outer, few):
            item.end(z, number == DEPTH - 1)
    for copy in swaps:
        copy.wait_send()
    for share_side in shares_in:
        share_side.end()


def last_sum(
    normed, attended, gin_sum, weight, weight_out, tokens, routed, upstream, middle, raw, queries, keys, values, probs,
    cosine, sine, gains, share, held
):
    block, width = normed.shape
    wide = weight.shape[1]
    sides = wide // width
    vmem = pl.BlockSpec(memory_space=pltpu.VMEM)
    few = (gains.shape[0], 2 * share)
    like = pltpu.VMEM((block, width), narrow)
    like_single = pltpu.VMEM((block, width), single)
    return pl.pallas_call(
        last_sum_kernel,
        out_shape=(
            jax.ShapeDtypeStruct((share, wide), single),
            jax.ShapeDtypeStruct((share, width), single),
            jax.ShapeDtypeStruct(few, single),
            jax.ShapeDtypeStruct((block, width), single),
            jax.ShapeDtypeStruct((held, gin_sum.shape[0] // DEPTH, DEPTH * gin_sum.shape[1] // held), narrow),
        ),
        in_specs=[HBM] * 14 + [vmem] * 3,
        out_specs=(vmem, vmem, vmem, vmem, HBM),
        scratch_shapes=[
            pltpu.VMEM((2, block, width), narrow),
            pltpu.VMEM((2, block, width), narrow),
            pltpu.VMEM((2, block, wide + width), narrow),
            pltpu.VMEM((2, STRIP, wide), narrow),
            like,
            like_single,
            like,
            like_single,
            pltpu.VMEM(raw.shape, single),
            like,
            like,
            like,
            pltpu.VMEM(probs.shape, single),
            like_single,
            like,
            pltpu.VMEM((2, block, width), single),
            pltpu.VMEM(gains.shape, single),
            pltpu.VMEM(few, single),
            pltpu.VMEM(few, single),
            pltpu.SemaphoreType.DMA((24,)),
            pltpu.SemaphoreType.DMA((2,)),
            pltpu.SemaphoreType.DMA((2,)),
            pltpu.SemaphoreType.DMA((2, 2, DEPTH, held)),
        ]
        + sum_scratch(sides * share, width, narrow, halves_of(sides * share), made=True)
        + sum_scratch(share, width, narrow, halves_of(share), made=True)
        + sum_scratch(few[0], few[1], single, halves_of(few[0], False), made=True),
        compiler_params=pltpu.CompilerParams(
            collective_id=4, has_side_effects=True, vmem_limit_bytes=62 * 2**20
        ),
        name="deliver",
    )(
        normed, attended, gin_sum, weight, weight_out, tokens, routed, upstream, middle, raw, queries, keys, values, probs,
        cosine, sine, gains
    )

def near_first(here, number):
    high = lax.div(here.z, 2)
    inner = lax.rem(lax.div(here.z + 1, 2), 2)
    low = number + inner * (1, -1, 0, 0)[number]
    return low + high * (DEPTH - 1 - 2 * low)


class Tiles:
    def __init__(self, here, stage, count, sems, parts, targets):
        self.here, self.stage, self.count = here, stage, count
        self.kept, self.sent, self.came = sems
        self.parts, self.targets = parts, targets

    def copies(self, number, keep=True, give=True):
        slot = lax.rem(number, 2)
        own, other = self.targets
        made = []
        for piece, (mine, theirs, spot) in enumerate(self.parts(number, self.stage.at[slot])):
            if keep:
                made.append(pltpu.make_async_copy(mine, own.at[spot], self.kept.at[slot, piece]))
            if give:
                sems = (self.sent.at[slot, piece], self.came.at[number, piece])
                made.append(remote(theirs, other.at[spot], *sems, self.here.sibling()))
        return made

    def settle(self, number):
        for copy in self.copies(number, give=False):
            copy.wait()
        for copy in self.copies(number, keep=False):
            copy.wait_send()

    def run(self, first, last, make):
        def body(number, carry):
            pl.when(number >= 2)(lambda: self.settle(number - 2))
            make(number, self.stage.at[lax.rem(number, 2)])
            for copy in self.copies(number):
                copy.start()
            return carry

        lax.fori_loop(first, last, body, 0)
        if last == self.count:
            for number in (last - 2, last - 1):
                self.settle(number)

    def heard(self):
        for number in range(self.count):
            for copy in self.copies(number, keep=False):
                copy.wait_recv()


def experts_kernel(
    rows, ups, gates, win, wout, middle, mid_sum, gate_sum, out_sum, gin_sum, gdown, gdown_other, gin, gin_other, rows_all, *scratch
):
    here = Here()
    here.meet()
    (
        w_in, w_out, grads, scaled, row_plane, up_plane, gate_plane, served, strip, stage, loads, strip_sems
    ) = scratch[:12]
    gather = Gather(here, rows, rows_all, halves_of(rows.shape[0]), False, scratch[12:16])
    mids = Sum(here, None, mid_sum, halves_of(rows.shape[0]), False, scratch[16:24])
    outs = Sum(here, None, out_sum, halves_of(rows.shape[0]), False, scratch[16:19] + scratch[24:29])
    fetch_middle = pltpu.make_async_copy(middle, scratch[45], scratch[46].at[0])
    fetch_middle.start()
    outs.extra = [scratch[45]]
    tables = Sum(here, None, gate_sum, halves_of(gate_sum.shape[0], False), False, scratch[29:37])
    in_sems, down_sems = scratch[37:40], scratch[40:43]
    block, width = rows.shape
    plane = RING * block
    hidden = w_out.shape[0]
    chunk = hidden // 4
    column = lax.broadcasted_iota(jnp.int32, (plane, 128), 1)
    fetch_in = pltpu.make_async_copy(win, w_in, loads.at[0])
    fetch_out = pltpu.make_async_copy(wout, w_out, loads.at[1])
    fetch_in.start()
    fetch_out.start()

    def fetch_plane(number):
        z = near_first(here, number)
        return (
            pltpu.make_async_copy(ups.at[z], up_plane.at[number % 2], loads.at[2 + number % 2]),
            pltpu.make_async_copy(gates.at[z], gate_plane.at[number % 2], loads.at[4 + number % 2]),
        )

    def fetch_rows(number):
        return pltpu.make_async_copy(rows_all.at[near_first(here, number)], row_plane, loads.at[6])

    def hidden_units(number):
        z = near_first(here, number)
        fetch_rows(number).start()
        for copy in fetch_plane(number):
            copy.wait()
        if number == 0:
            fetch_in.wait()
            fetch_out.wait()
        fetch_rows(number).wait()
        served[...] = jnp.zeros_like(served)
        at = pl.ds(pl.multiple_of(z * plane, plane), plane)

        def one(expert, carry):
            mid = row_plane[...].reshape(plane, width)
            up_rows = up_plane[number % 2]
            spot = pl.ds(pl.multiple_of(expert * chunk, chunk), chunk)
            spot_up = pl.ds(pl.multiple_of(hidden + expert * chunk, chunk), chunk)
            gate = jnp.sum(jnp.where(column == expert, gate_plane[number % 2], 0.0), axis=1, keepdims=True)
            gate_part = jnp.dot(mid, w_in[:, spot], preferred_element_type=single)
            up_part = jnp.dot(mid, w_in[:, spot_up], preferred_element_type=single)
            back = contract_last(up_rows, w_out[spot])
            sigmoid = 1.0 / (1.0 + jnp.exp(-gate_part))
            activated = gate_part * sigmoid
            units = activated * up_part
            scaled[at, spot] = (gate * units).astype(narrow)
            total = jnp.sum(units * back, axis=1, keepdims=True)
            served[...] += jnp.where(column == here.chip * 4 + expert, total, 0.0)
            grad = gate * back
            grads[at, spot] = (grad * up_part * (sigmoid * (1.0 + gate_part * (1.0 - sigmoid)))).astype(narrow)
            grads[at, spot_up] = (grad * activated).astype(narrow)
            return carry

        lax.fori_loop(0, 4, one, 0)
        for chip in range(RING):
            turned = jnp.transpose(served[chip * block : (chip + 1) * block])
            tables.mine[z, chip] = turned[: tables.rows]

    def row_grads(z):
        at = pl.ds(pl.multiple_of(z * plane, plane), plane)

        def one(number, carry):
            spot = pl.ds(pl.multiple_of(number * TILE, TILE), TILE)
            made = contract_last(grads[at], w_in[spot]).astype(narrow)
            for chip in range(RING):
                mids.mine[z, chip, :, spot] = made[chip * block : (chip + 1) * block]
            return carry

        lax.fori_loop(0, width // TILE, one, 0)

    def products(z):
        at = pl.ds(pl.multiple_of(z * plane, plane), plane)

        def one(number, carry):
            spot = pl.ds(pl.multiple_of(number * TILE, TILE), TILE)
            made = jnp.dot(scaled[at], w_out[:, spot], preferred_element_type=single).astype(narrow)
            for chip in range(RING):
                outs.mine[z, chip, :, spot] = made[chip * block : (chip + 1) * block]
            return carry

        lax.fori_loop(0, width // TILE, one, 0)

    strips = width // TILE

    def fetch_strip(number):
        spot = pl.ds(pl.multiple_of(number * TILE, TILE), TILE)
        slot = lax.rem(number, 2)
        return pltpu.make_async_copy(rows_all.at[:, :, :, spot], strip.at[slot], strip_sems.at[slot])

    def columns_of(result, stage, step=512):
        for begin in range(0, width, step):
            stage[:, begin : begin + step] = result(begin, step).astype(narrow)

    def grad_in(number, stage):
        slot = lax.rem(number, 2)
        fetch_strip(number).wait()
        pl.when(number + 1 < strips)(lambda: fetch_strip(number + 1).start())
        left = strip[slot].reshape(DEPTH * plane, TILE)
        columns_of(lambda begin, step: contract_rows(left, grads[:, begin : begin + step]), stage)

    def grad_in_parts(number, stage):
        share = hidden // 2
        at = pl.ds(pl.multiple_of(number * TILE, TILE), TILE)
        for side in range(2):
            mine, theirs = (
                stage.at[:, pl.ds(pl.multiple_of(side * hidden + core * share, 128), share)]
                for core in (here.core, 1 - here.core)
            )
            yield mine, theirs, (at, pl.ds(side * share, share))

    def grad_down(number, stage):
        half = tall // 2
        core = here.core + (1 - lax.div(number, half)) * (1 - 2 * here.core)
        at = core * half + lax.rem(number, half)
        left = scaled[:, pl.ds(pl.multiple_of(at * TILE, TILE), TILE)]
        columns_of(lambda begin, step: contract_rows(left, w_in[:, begin : begin + step]), stage)

    tall = hidden // TILE
    tiles_in = Tiles(here, stage, strips, in_sems, grad_in_parts, (gin, gin_other))

    def grad_down_store(number, away):
        slot = lax.rem(number, 2)
        rest = lax.rem(number, tall // 2)
        spot = pl.ds(pl.multiple_of(rest * TILE, TILE), TILE)
        kept, sent, came = down_sems
        if away:
            return remote(stage.at[slot], gdown_other.at[spot], sent.at[slot, 0], came.at[rest, 0], here.sibling())
        return pltpu.make_async_copy(stage.at[slot], gdown.at[spot], kept.at[slot, 0])

    def grads_down(away):
        first = 0 if away else tall // 2

        def body(number, carry):
            grad_down(number, stage.at[lax.rem(number, 2)])
            grad_down_store(number, away).start()
            return carry

        lax.fori_loop(first, first + tall // 2, body, 0)
        for number in range(first, first + tall // 2):
            copy = grad_down_store(number, away)
            copy.wait_send() if away else copy.wait()

    def add_cores():
        half = hidden
        adds, puts = scratch[43], scratch[44]

        def fetch(number):
            slot = lax.rem(number, 2)
            at = pl.ds(pl.multiple_of(number * TILE, TILE), TILE)
            return [
                pltpu.make_async_copy(
                    source.at[at], stage.at[slot, :, pl.ds(side * half, half)], adds.at[slot, side]
                )
                for side, source in enumerate((gin, gin_other))
            ]

        def put(number):
            slot = lax.rem(number, 2)
            at = pl.ds(pl.multiple_of(number * TILE, TILE), TILE)
            return pltpu.make_async_copy(stage.at[slot, :, pl.ds(0, half)], gin_sum.at[at], puts.at[slot])

        def start_fetch(number):
            for copy in fetch(number):
                copy.start()

        def body(number, carry):
            for copy in fetch(number):
                copy.wait()
            pl.when(number >= 1)(lambda: put(number - 1).wait())
            pl.when(number + 1 < strips)(lambda: start_fetch(number + 1))
            slot = lax.rem(number, 2)
            own = stage.at[slot, :, pl.ds(0, half)]
            add_up(own, [own, stage.at[slot, :, pl.ds(half, half)]], TILE, half)
            put(number).start()
            return carry

        start_fetch(0)
        lax.fori_loop(0, strips, body, 0)
        put(strips - 1).wait()

    again = [
        pltpu.make_async_copy(ups.at[z], w_in.at[pl.ds(z * plane, plane)], loads.at[7 + z]) for z in range(DEPTH)
    ]

    def again_wait():
        for copy in again:
            copy.wait()

    order = [far_first(here, number) for number in range(DEPTH)]
    first = [mids, tables]
    steps = [(first, z, False) for z in [here.z] + order[:-1]]
    steps += [([outs], z, number == DEPTH - 1) for number, z in enumerate(order)]

    def begin(number):
        items, z, last = steps[number]
        if number < DEPTH:
            row_grads(z)
        else:
            mids.end(z, last)
            products(z)
        for item in items:
            for way in (0, 1):
                start(item.toss(z, way))

    def second(number):
        for item in steps[number][0]:
            item.second(steps[number][1])

    def third(number):
        items, z, last = steps[number]
        for item in items:
            item.own_part(z) if number == 0 else item.third(z, last)

    for copy in fetch_plane(0):
        copy.start()
    rounds = Rounds(here, [gather])
    rounds.service(0)
    for number in range(DEPTH):
        if number + 1 < DEPTH:
            rounds.service(number + 1)
        if number == DEPTH - 1:
            second(0)
        gather_third(gather, near_first(here, number))
        if number + 1 < DEPTH:
            for copy in fetch_plane(number + 1):
                copy.start()
        hidden_units(number)
        if number == 1:
            begin(0)
    fetch_strip(0).start()
    ends = [0] + [strips * (number + 1) // (DEPTH - 1) for number in range(DEPTH - 1)]
    for number in range(1, 2 * DEPTH):
        begin(number)
        if number > 1:
            second(number - 1)
            third(number - 2)
        if number == DEPTH - 1:
            for copy in again:
                copy.start()
        if number < DEPTH:
            tiles_in.run(ends[number - 1], ends[number], grad_in)
        elif number == DEPTH:
            again_wait()
            grads_down(True)
        elif number == DEPTH + 1:
            grads_down(False)
        elif number == DEPTH + 2:
            for item in first:
                item.own_rest(here.z)
            tiles_in.heard()
            add_cores()
    outs.second(order[-1])
    outs.third(order[-2], False)
    fetch_middle.wait()
    outs.third(order[-1], True)
    for number, z in enumerate(order):
        outs.end(z, number == DEPTH - 1)
        tables.end(z, number == DEPTH - 1)
    for number in range(tall // 2):
        grad_down_store(number, True).wait_recv()
    rounds.finish()


def experts_round(rows, ups, gates, win, wout, middle, experts):
    block, width = rows.shape
    plane = RING * block
    hidden = wout.shape[0]
    total = DEPTH * plane
    vmem = pl.BlockSpec(memory_space=pltpu.VMEM)
    return pl.pallas_call(
        experts_kernel,
        out_shape=(
            jax.ShapeDtypeStruct((block, width), single),
            jax.ShapeDtypeStruct((experts, block), single),
            jax.ShapeDtypeStruct((block, width), narrow),
            jax.ShapeDtypeStruct((width, hidden), narrow),
            jax.ShapeDtypeStruct((hidden // 2, width), narrow),
            jax.ShapeDtypeStruct((hidden // 2, width), narrow),
            jax.ShapeDtypeStruct((width, hidden), narrow),
            jax.ShapeDtypeStruct((width, hidden), narrow),
            jax.ShapeDtypeStruct((DEPTH, RING, block, width), narrow),
        ),
        in_specs=[HBM] * 6,
        out_specs=(vmem, vmem, vmem) + (HBM,) * 6,
        scratch_shapes=[
            pltpu.VMEM((width, 2 * hidden), narrow),
            pltpu.VMEM((hidden, width), narrow),
            pltpu.VMEM((total, 2 * hidden), narrow),
            pltpu.VMEM((total, hidden), narrow),
            pltpu.VMEM((RING, block, width), narrow),
            pltpu.VMEM((2, plane, width), narrow),
            pltpu.VMEM((2, plane, 128), single),
            pltpu.VMEM((plane, 128), single),
            pltpu.VMEM((2, DEPTH, RING, block, TILE), narrow),
            pltpu.VMEM((2, TILE, width), narrow),
            pltpu.SemaphoreType.DMA((11,)),
            pltpu.SemaphoreType.DMA((2,)),
        ]
        + GATHER_SEMS
        + sum_scratch(block, width, narrow, halves_of(block), made=True)
        + [pltpu.VMEM((DEPTH + 1, block, width), narrow)]
        + SUM_SEMS
        + sum_scratch(experts, block, single, halves_of(experts, False), made=True)
        + [
            pltpu.SemaphoreType.DMA((2, 2)),
            pltpu.SemaphoreType.DMA((2, 2)),
            pltpu.SemaphoreType.DMA((width // TILE, 2)),
        ]
        + [
            pltpu.SemaphoreType.DMA((2, 1)),
            pltpu.SemaphoreType.DMA((2, 1)),
            pltpu.SemaphoreType.DMA((hidden // TILE, 1)),
        ]
        + [pltpu.SemaphoreType.DMA((2, 2)), pltpu.SemaphoreType.DMA((2,))]
        + [pltpu.VMEM((block, width), single), pltpu.SemaphoreType.DMA((1,))],
        compiler_params=pltpu.CompilerParams(
            collective_id=2, has_side_effects=True, vmem_limit_bytes=62 * 2**20
        ),
        name="experts",
    )(rows, ups, gates, win, wout, middle)


def by_kernels():
    return lax.axis_size("dp") == DEPTH and lax.axis_size("expert") == 2 * RING


def forward(tokens, gains, weight_qkv, weight_out, cosine, sine, allowed):
    rows, width = tokens.shape
    inputs = tokens.astype(single)
    normed_in = (normalize(inputs)[0] * gains[0]).astype(narrow)
    projected = jnp.dot(normed_in, weight_qkv, preferred_element_type=single)
    raw = jnp.stack([projected[:, :width], projected[:, width : 2 * width]])
    query_rows, key_rows = (
        rotate(normalize(raw[side])[0] * gains[side + 1], cosine, sine).astype(narrow) for side in range(2)
    )
    value_rows = projected[:, 2 * width :].astype(narrow)
    by_head = (rows, -1, HEAD)
    scores = jnp.einsum(
        "qhd,khd->hqk", query_rows.reshape(by_head), key_rows.reshape(by_head), preferred_element_type=single
    )
    scores = jnp.where(allowed[None], scores * HEAD ** (-0.5), masked_score)
    unnormed = jnp.exp(scores - jnp.max(scores, axis=-1, keepdims=True))
    probs = unnormed / jnp.sum(unnormed, axis=-1, keepdims=True)
    attended = jnp.einsum(
        "hqk,khd->qhd", probs.astype(narrow), value_rows.reshape(by_head), preferred_element_type=single
    )
    attended = attended.reshape(rows, width).astype(narrow)
    middle = inputs + jnp.dot(attended, weight_out, preferred_element_type=single)
    routed_in = (normalize(middle)[0] * gains[3]).astype(narrow)
    return (normed_in, raw, query_rows, key_rows, value_rows, probs, attended, middle, routed_in)


def wide_tables(cosine, sine):
    return (
        jnp.concatenate([cosine[:, 0], cosine[:, 0]], axis=1),
        jnp.concatenate([-sine[:, 0], sine[:, 0]], axis=1),
    )


def bring_all(w_qkv, w_out, upstream, dense, gain_rows, expert_in, expert_out, tokens, cosine, sine, allowed):
    width = upstream.shape[1]
    share = gain_rows.shape[1]
    if by_kernels():
        experts, rows = dense.shape[1], dense.shape[0]
        small = jnp.concatenate([dense.T, jnp.pad(gain_rows, ((0, 4), (0, rows - share)))], axis=0)
        tables = (*wide_tables(cosine, sine), allowed.astype(single))
        wq, wo, up, all_small, weight_in, weight_down, gains, *made = first_gather(
            w_qkv, w_out, upstream, small, expert_in, expert_out, tokens, *tables
        )
        core = lax.rem(lax.axis_index("expert"), 2)
        every_gate = lax.dynamic_index_in_dim(all_small, core, axis=2, keepdims=False)[:, :, :experts]
        return (
            wq.reshape(-1, w_qkv.shape[1]),
            wo.reshape(-1, w_out.shape[1]),
            up.reshape(-1, width),
            every_gate,
            gains,
            weight_in,
            weight_down.reshape(-1, width),
            made,
        )
    everyone = ("dp", "expert")
    weight_in, weight_down = fetch_weights(expert_in, expert_out)
    weight_qkv = lax.all_gather(w_qkv, everyone, axis=0, tiled=True)
    weight_out = lax.all_gather(w_out, everyone, axis=0, tiled=True)
    gains = lax.all_gather(gain_rows, everyone, axis=1, tiled=True)
    return (
        weight_qkv,
        weight_out,
        gather_alike(upstream).reshape(-1, width),
        gather_alike(dense.T),
        gains,
        weight_in,
        weight_down,
        forward(tokens, gains, weight_qkv, weight_out, cosine, sine, allowed),
    )


def experts_all(middle, routed_in, up_rows, every_gate, weight_in, weight_down, held):
    depth = lax.axis_size("dp")
    owners = lax.axis_size("expert")
    chips = owners // 2
    experts = owners * held
    chip_experts = 2 * held
    rows, width = routed_in.shape
    chip = lax.axis_index("expert") // 2
    mine = lax.dynamic_slice_in_dim(every_gate, chip * chip_experts, chip_experts, axis=2)
    gate = mine.transpose(0, 1, 3, 2)
    if by_kernels():
        gate = jnp.pad(gate.reshape(DEPTH, -1, chip_experts), ((0, 0), (0, 0), (0, 128 - chip_experts)))
        ups = up_rows.reshape(DEPTH, -1, width)
        grad_routed, table, results, grad_in, grad_down, grad_down_other = experts_round(
            routed_in, ups, gate, weight_in, weight_down, middle, experts
        )[:6]
        down = grad_down.astype(single) + grad_down_other.astype(single)
        return (results, grad_routed, table, (grad_in, down.reshape(held, -1, width)))
    mid_rows = gather_alike(routed_in).reshape(-1, width)
    out, mid, served, grad_in, grad_down = expert_rounds(
        mid_rows, up_rows, gate.reshape(-1, chip_experts), weight_in, weight_down
    )
    by_gate = served.reshape(depth, chips, rows, chip_experts).transpose(0, 1, 3, 2)
    spread = jnp.zeros((depth, chips, experts, rows), single)
    spread = lax.dynamic_update_slice_in_dim(spread, by_gate, chip * chip_experts, axis=2)
    mixture = scatter_alike(out.reshape(depth, chips, rows, width)).astype(single)
    return (
        (middle + mixture).astype(narrow),
        scatter_alike(mid.reshape(depth, chips, rows, width)).astype(single),
        scatter_alike(spread),
        return_weights(grad_in, grad_down, held),
    )


def backward(
    tokens, gains, grad_routed, upstream, normed, raw, queries, keys, values, probs, attended, middle, weight_qkv, weight_out,
    cosine, sine
):
    rows, width = tokens.shape
    by_head = (rows, -1, HEAD)
    grad_mid, piece_ffn = rms_back(grad_routed, *normalize(middle), gains[3])
    grad_middle = upstream.astype(single) + grad_mid
    branch = grad_middle.astype(narrow)
    grad_heads = contract_last(branch, weight_out).astype(narrow).reshape(by_head)
    grad_probs = jnp.einsum("qhd,khd->hqk", grad_heads, values.reshape(by_head), preferred_element_type=single)
    inner = jnp.sum(grad_probs * probs, axis=-1, keepdims=True)
    grad_scores = (probs * (grad_probs - inner)).astype(narrow)
    grads = (
        jnp.einsum("hqk,khd->qhd", grad_scores, keys.reshape(by_head), preferred_element_type=single),
        jnp.einsum("hqk,qhd->khd", grad_scores, queries.reshape(by_head), preferred_element_type=single),
    )
    grad_value = jnp.einsum("hqk,qhd->khd", probs.astype(narrow), grad_heads, preferred_element_type=single)
    (grad_q, piece_query), (grad_k, piece_key) = (
        rms_back(
            rotate(grads[side].reshape(rows, width) * HEAD ** (-0.5), cosine, -sine),
            *normalize(raw[side]),
            gains[side + 1],
        )
        for side in range(2)
    )
    grad_qkv = jnp.concatenate([grad_q, grad_k, grad_value.reshape(rows, width)], axis=1).astype(narrow)
    grad_input, piece_attn = rms_back(
        contract_last(grad_qkv, weight_qkv), *normalize(tokens.astype(single)), gains[0]
    )
    pieces = jnp.stack([piece_attn, piece_query, piece_key, piece_ffn])
    return (grad_middle + grad_input, pieces, (normed, grad_qkv), (attended, branch))


def deliver_all(tokens, gains, grad_routed, upstream, made, weight_qkv, weight_out, cosine, sine, share_in, held):
    normed, raw, queries, keys, values, probs, attended, middle, _ = made
    owners = lax.axis_size("dp") * lax.axis_size("expert")
    share = gains.shape[1] // owners
    if by_kernels():
        share_qkv, share_out, gain_sums, grad_tokens, share_in = last_sum(
            normed, attended, share_in, weight_qkv, weight_out, tokens, grad_routed, upstream, middle, raw, queries, keys,
            values, probs, *wide_tables(cosine, sine), gains, share, held
        )
        core = lax.rem(lax.axis_index("expert"), 2)
        gain_sums = lax.dynamic_slice_in_dim(gain_sums, core * share, share, axis=1)
        return (grad_tokens, gain_sums, share_qkv, share_out, share_in.astype(single))
    everyone = ("dp", "expert")
    grad_tokens, pieces, *pairs = backward(
        tokens, gains, grad_routed, upstream, normed, raw, queries, keys, values, probs, attended, middle, weight_qkv,
        weight_out, cosine, sine
    )
    return (
        grad_tokens,
        lax.psum_scatter(pieces, everyone, scatter_dimension=1, tiled=True),
        *(
            lax.psum_scatter(
                contract_rows(left, right, narrow), everyone, scatter_dimension=0, tiled=True
            ).astype(single)
            for left, right in pairs
        ),
        share_in.astype(single),
    )


def local(
    tokens,
    lengths,
    expert_ids,
    gates,
    attn_gain,
    w_qkv,
    q_gain,
    k_gain,
    w_out,
    ffn_gain,
    expert_in,
    expert_out,
    out_grad,
):
    micro_count, seq_len, model_width = tokens.shape
    rows = micro_count * seq_len
    held = expert_in.shape[0]
    experts = lax.axis_size("expert") * held
    own = tokens.reshape(rows, model_width)
    upstream = out_grad.reshape(rows, model_width)
    ids = expert_ids.reshape(rows, -1)
    gate_rows = gates.reshape(rows, -1)
    onehot = (ids[:, :, None] == jnp.arange(experts, dtype=jnp.int32)).astype(single)
    dense = jnp.sum(onehot * gate_rows[:, :, None], axis=1)
    gain_rows = jnp.stack([attn_gain, q_gain, k_gain, ffn_gain]).astype(single)
    document, position = layout(lengths[:, 0], seq_len)
    cosine, sine = angles(position)
    places = jnp.arange(rows, dtype=jnp.int32)
    allowed = (document[:, None] == document[None, :]) & (places[:, None] >= places[None, :])
    weight_qkv, weight_out, up_rows, every_gate, gains, weight_in, weight_down, made = bring_all(
        w_qkv, w_out, upstream, dense, gain_rows, expert_in, expert_out, own, cosine, sine, allowed
    )
    middle, routed_in = made[-2:]

    results, grad_routed, gate_table, (share_in, share_down) = experts_all(
        middle, routed_in, up_rows, every_gate, weight_in, weight_down, held
    )
    grad_gates = jnp.sum(onehot * gate_table.T[:, None, :], axis=2)

    grad_tokens, gain_sums, grad_qkv_share, grad_out_share, share_in = deliver_all(
        own, gains, grad_routed, upstream, made, weight_qkv, weight_out, cosine, sine, share_in, held
    )
    shape = (micro_count, seq_len, model_width)
    return (
        results.reshape(shape),
        grad_tokens.reshape(shape),
        grad_gates.reshape(expert_ids.shape),
        gain_sums[0],
        grad_qkv_share,
        gain_sums[1],
        gain_sums[2],
        grad_out_share,
        gain_sums[3],
        share_in,
        share_down.astype(single),
    )


def solution(mesh):
    by_rows = P(None, ("dp", "expert"), None)
    flat = P(("dp", "expert"))
    split = P(("dp", "expert"), None)
    held = P("expert", "dp", None)
    return jax.shard_map(
        local,
        mesh=mesh,
        in_specs=(
            by_rows, by_rows, by_rows, by_rows, flat, split, flat, flat, split, flat, held, held, by_rows,
        ),
        out_specs=(by_rows, by_rows, by_rows, flat, split, flat, flat, split, flat, held, held),
        check_vma=False,
    )
```
